32 devices in a mesh: rep: 8 (over z, x), grp: 4 (over y, core).
Axes of the slice: x: 2, y: 2, z: 4, core: 2. Of those that a mesh axis runs over, the one named last changes fastest.
Arguments:
- x_input: bfloat16 [8, 1024, 1024], P('rep', 'grp'), may hold values from -6 to 6
- norm_gain: bfloat16 [2, 2, 1024], P(None, None, 'grp'), may hold values from 0.5 to 1.5
- w_in: bfloat16 [2, 1024, 6144], P(None, 'grp'), may hold values from -0.1875 to 0.1875
- w_ab: bfloat16 [2, 1024, 16], P(None, 'grp'), may hold values from -0.1875 to 0.1875
- conv_w: bfloat16 [2, 4, 4096], P(None, None, 'grp'), may hold values from -3 to 3
- a_log: bfloat16 [2, 8], P(None, 'grp'), may hold values from -2.5 to 0
- dt_bias: bfloat16 [2, 8], P(None, 'grp'), may hold values from -5 to 0.5
- out_gain: bfloat16 [2, 256], P(None, 'grp'), may hold values from 0.5 to 1.5
- w_out: bfloat16 [2, 2048, 1024], P(None, 'grp'), may hold values from -0.25 to 0.25
- ffn_in: bfloat16 [2, 1024, 5632], P(None, 'grp'), may hold values from -0.1875 to 0.1875
- ffn_out: bfloat16 [2, 2816, 1024], P(None, 'grp'), may hold values from -0.21875 to 0.21875
- cotangent: bfloat16 [8, 1024, 1024], P('rep', 'grp'), may hold values from -6 to 6
Outputs:
- block_output: bfloat16 [8, 1024, 1024], P('rep', 'grp')
- input_grad: bfloat16 [8, 1024, 1024], P('rep', 'grp')
- grad_norm_gain: float32 [2, 2, 1024], P(None, None, 'grp')
- grad_w_in: float32 [2, 1024, 6144], P(None, 'grp')
- grad_w_ab: float32 [2, 1024, 16], P(None, 'grp')
- grad_conv_w: float32 [2, 4, 4096], P(None, None, 'grp')
- grad_a_log: float32 [2, 8], P(None, 'grp')
- grad_dt_bias: float32 [2, 8], P(None, 'grp')
- grad_out_gain: float32 [2, 256], P(None, 'grp')
- grad_w_out: float32 [2, 2048, 1024], P(None, 'grp')
- grad_ffn_in: float32 [2, 1024, 5632], P(None, 'grp')
- grad_ffn_out: float32 [2, 2816, 1024], P(None, 'grp')
The draws below stay inside these ranges and needn't reach their ends.
All inputs are finite; a program needn't handle non-finite values.
Results may differ from the reference program's by a relative error of at most 0.03.
Values may be sent and summed in bfloat16 or wider, within the bound.
A program may use at most 640 MiB of HBM per device.

```python
import math
import jax
import jax.numpy as jnp
from jax import lax

D = 1024
H = 8
DK = 128
DV = 256
FF = 2816
CONV = 4
BLOCK = 64
LEN = 1024
LAYERS = 2
HK = 1024
HV = 2048
CH = 4096
NSEQ = 8


def steps_of(key, extent, pieces, smallest, top_value):
    level, own = 1.0, jax.random.fold_in(key, 6)
    for dim, parts in pieces:
        draws = jnp.exp(jax.random.uniform(jax.random.fold_in(own, dim), (parts,), jnp.float32, smallest / len(pieces), top_value / len(pieces)))
        level = level * jnp.repeat(draws, extent[dim] // parts).reshape([-1 if axis == dim else 1 for axis in range(len(extent))])
    return level


def normal_values(rng, dims, width, limit, cuts=(), kind=jnp.bfloat16):
    drawn = width * jax.random.normal(rng, dims, jnp.float32)
    if cuts:
        drawn = drawn * steps_of(rng, dims, cuts, -0.22, 0.18)
    return jnp.clip(drawn, -limit, limit).astype(kind)


def setup_inputs(seed: int = 0) -> dict:
    key_list = jax.random.split(jax.random.key(seed), 13)
    x_input = normal_values(key_list[0], (NSEQ, LEN, D), 1.0, 6.0, ((0, 8), (1, 4)))
    norm_gain = jnp.clip(1.0 + 0.1 * jax.random.normal(key_list[1], (LAYERS, 2, D), jnp.float32), 0.5, 1.5).astype(jnp.bfloat16)
    w_in = normal_values(key_list[2], (LAYERS, D, 2 * HK + 2 * HV), D ** -0.5, 0.1875, ((1, 4),))
    w_ab = normal_values(key_list[3], (LAYERS, D, 2 * H), D ** -0.5, 0.1875, ((1, 4),))
    conv_w = normal_values(key_list[4], (LAYERS, CONV, CH), CONV ** -0.5, 3.0, ((2, 4),))
    a_log = jnp.clip(-2.5 + 2.5 * jax.random.uniform(key_list[5], (LAYERS, H), jnp.float32) ** steps_of(key_list[5], (LAYERS, H), ((1, 4),), -0.2, 0.2), -2.5, 0.0).astype(jnp.bfloat16)
    dt_bias = jnp.clip(-5.0 + 5.5 * jax.random.uniform(key_list[6], (LAYERS, H), jnp.float32) ** steps_of(key_list[6], (LAYERS, H), ((1, 4),), -0.2, 0.2), -5.0, 0.5).astype(jnp.bfloat16)
    out_gain = jnp.clip(1.0 + 0.1 * jax.random.normal(key_list[7], (LAYERS, DV), jnp.float32), 0.5, 1.5).astype(jnp.bfloat16)
    w_out = normal_values(key_list[8], (LAYERS, HV, D), (HV // 4) ** -0.5, 0.25, ((1, 4),))
    ffn_in = normal_values(key_list[9], (LAYERS, D, 2 * FF), D ** -0.5, 0.1875, ((1, 4),))
    ffn_out = normal_values(key_list[10], (LAYERS, FF, D), (FF // 4) ** -0.5, 0.21875, ((1, 4),))
    cotangent = normal_values(key_list[11], (NSEQ, LEN, D), 1.0, 6.0, ((0, 8), (1, 4)))
    return dict(x_input=x_input, norm_gain=norm_gain, w_in=w_in, w_ab=w_ab, conv_w=conv_w, a_log=a_log, dt_bias=dt_bias, out_gain=out_gain, w_out=w_out, ffn_in=ffn_in, ffn_out=ffn_out, cotangent=cotangent)


precise = lax.Precision.HIGHEST
epsilon = 1e-06
out_floor = 0.02

@jax.custom_vjp
def low(v):
    return lax.optimization_barrier(v.astype(jnp.bfloat16)).astype(jnp.float32)

@jax.custom_vjp
def low_back(v):
    return v

def low_keep(v):
    return (low(v), None)

def low_pass(kept, grad):
    return (grad,)

def back_keep(v):
    return (v, None)

def back_low(kept, grad):
    return (low(grad),)
low.defvjp(low_keep, low_pass)
low_back.defvjp(back_keep, back_low)

def matmul_high(left, right):
    return jnp.einsum('...i,ij->...j', left, right, precision=precise)

def rms_norm(residual, gain):
    return residual * lax.rsqrt(lax.optimization_barrier(jnp.mean(residual * residual, axis=-1, keepdims=True)) + epsilon) * gain

def conv_piece(extended, conv_weight):
    length = extended.shape[1] - (CONV - 1)
    convolved = sum((extended[:, tap_index:tap_index + length] * conv_weight[tap_index] for tap_index in range(CONV)))
    activated = jax.nn.silu(convolved)
    key_shape = activated.shape[:2] + (H, DK)
    queries = activated[..., :HK].reshape(key_shape)
    key_part = activated[..., HK:2 * HK].reshape(key_shape)
    values = activated[..., 2 * HK:].reshape(activated.shape[:2] + (H, DV))
    queries = queries * lax.rsqrt(lax.optimization_barrier(jnp.sum(queries * queries, axis=-1, keepdims=True)) + epsilon) / math.sqrt(DK)
    key_part = key_part * lax.rsqrt(lax.optimization_barrier(jnp.sum(key_part * key_part, axis=-1, keepdims=True)) + epsilon)
    return (queries, key_part, values)

def decay_piece(small_proj, alog_part, bias_part):
    strength = jax.nn.sigmoid(small_proj[..., :H])
    log_decay = -jnp.exp(alog_part) * jax.nn.softplus(small_proj[..., H:] + bias_part)
    return (strength, log_decay)

def gated_piece(mixed_heads, gate_part, gain_out):
    scaled = mixed_heads * lax.rsqrt(lax.optimization_barrier(jnp.mean(mixed_heads * mixed_heads, axis=-1, keepdims=True)) + out_floor)
    return scaled * gain_out * jax.nn.silu(gate_part)

def swiglu_piece(up_part):
    return jax.nn.silu(up_part[..., :FF]) * up_part[..., FF:]

def delta_rule(queries, key_part, values, strength, log_decay):
    seq_count, length = (queries.shape[0], queries.shape[1])
    block_count = length // BLOCK

    def blocks(tensor):
        return jnp.moveaxis(tensor.reshape((seq_count, block_count, BLOCK) + tensor.shape[2:]), 1, 0)

    def token_step(carried, inputs):
        query_now, key_now, value_now, strength_now, decay_now = inputs
        key_read = jnp.einsum('nhk,nhkv->nhv', key_now, carried, precision=precise)
        weighted = strength_now[..., None] * key_now
        carried = jnp.exp(decay_now)[..., None, None] * (carried - weighted[..., None] * key_read[..., None, :]) + weighted[..., None] * value_now[..., None, :]
        return (carried, jnp.einsum('nhk,nhkv->nhv', query_now, carried, precision=precise))

    def block_step(carried, inputs):
        carried, outputs = lax.scan(token_step, carried, tuple((jnp.moveaxis(tensor, 1, 0) for tensor in inputs)))
        return (carried, jnp.moveaxis(outputs, 0, 1))
    initial = jnp.zeros((seq_count, H, DK, DV), queries.dtype)
    inputs = tuple((blocks(tensor) for tensor in (queries, key_part, values, strength, log_decay)))
    final_state, outputs = lax.scan(jax.checkpoint(block_step), initial, inputs)
    return jnp.moveaxis(outputs, 0, 1).reshape(values.shape)

def layer(residual, norm_gains, in_weight, ab_weight, conv_weight, alog_part, bias_part, gain_out, out_weight, up_weight, down_weight):
    seq_count, length = (residual.shape[0], residual.shape[1])
    normed = low(rms_norm(residual, norm_gains[0]))
    projected = low(low_back(matmul_high(normed, in_weight)))
    small_proj = low_back(matmul_high(normed, ab_weight))
    padded = jnp.pad(projected[..., :CH], ((0, 0), (CONV - 1, 0), (0, 0)))
    queries, key_part, values = conv_piece(padded, conv_weight)
    queries, key_part, values = (low(queries), low(key_part), low(values))
    strength, log_decay = decay_piece(small_proj, alog_part, bias_part)
    mixed_heads = delta_rule(queries, key_part, values, strength, log_decay)
    gate_part = projected[..., CH:].reshape(seq_count, length, H, DV)
    gated_out = low(gated_piece(mixed_heads, gate_part, gain_out).reshape(seq_count, length, HV))
    residual_mid = residual + low_back(matmul_high(gated_out, out_weight))
    normed_two = low(rms_norm(residual_mid, norm_gains[1]))
    up_part = low_back(matmul_high(normed_two, up_weight))
    hidden = low(swiglu_piece(up_part))
    return residual_mid + low_back(matmul_high(hidden, down_weight))

def reference(x_input, norm_gain, w_in, w_ab, conv_w, a_log, dt_bias, out_gain, w_out, ffn_in, ffn_out, cotangent):
    weights = (norm_gain, w_in, w_ab, conv_w, a_log, dt_bias, out_gain, w_out, ffn_in, ffn_out)
    weights = tuple((weight.astype(jnp.float32) for weight in weights))

    def forward(residual, *layer_weights):
        for layer_index in range(LAYERS):
            residual = layer(residual, *(weight[layer_index] for weight in layer_weights))
        return residual
    block_output, pullback = jax.vjp(forward, x_input.astype(jnp.float32), *weights)
    gradients = pullback(cotangent.astype(jnp.float32))
    return (block_output.astype(jnp.bfloat16), gradients[0].astype(jnp.bfloat16), gradients[1], gradients[2], gradients[3], gradients[4], gradients[5], gradients[6], gradients[7], gradients[8], gradients[9], gradients[10])
```

```python
from functools import partial
import math

import jax
import jax.numpy as jnp
from jax import lax
from jax.sharding import PartitionSpec as P
from jax.experimental import pallas as pl
from jax.experimental.pallas import tpu as pltpu

H = 8
DK = 128
DV = 256
FF = 2816
CONV = 4
LAYERS = 2
HK = 1024
HV = 2048
CH = 4096
CHUNK = 128

f32 = jnp.float32
bf16 = jnp.bfloat16
HIGH = lax.Precision.HIGHEST
epsilon = 1e-06
out_floor = 0.02
NN = ((1,), (0,))
NT = ((1,), (1,))
TN = ((0,), (0,))


def mm(left, right, dims=NN, precision=None):
    return lax.dot_general(
        left, right, (dims, ((), ())), precision=precision, preferred_element_type=f32
    )


def mh(left, right, dims=NN):
    return mm(left, right, dims, HIGH)


def grid_of(shape, dim):
    return lax.broadcasted_iota(jnp.int32, shape, dim)


def conv_chunk(x_ext, taps):
    return sum(x_ext[5 + j : 5 + j + CHUNK] * taps[j : j + 1] for j in range(CONV))


def decay_chunk(small, heads_ref):
    lane = grid_of(small.shape, 1)
    strength = jax.nn.sigmoid(small)
    shifted_logit = small + heads_ref[1:2, :]
    soft = jnp.maximum(shifted_logit, 0.0) + jnp.log1p(jnp.exp(-jnp.abs(shifted_logit)))
    log_decay = -jnp.exp(heads_ref[0:1, :]) * soft
    row = grid_of((CHUNK, CHUNK), 0)
    col = grid_of((CHUNK, CHUNK), 1)
    lower_ones = jnp.where(row >= col, 1.0, 0.0).astype(f32)
    cumulative = mh(lower_ones, log_decay)
    turned = jnp.where(lane < 2, strength, cumulative).T
    return strength, shifted_logit, log_decay, cumulative, turned


def head_inputs(activated, h):
    qa = activated[:, 128 * h : 128 * h + 128]
    ka = activated[:, 256 + 128 * h : 384 + 128 * h]
    va = activated[:, 512 + 256 * h : 768 + 256 * h]
    q_norm = lax.rsqrt(jnp.sum(qa * qa, axis=-1, keepdims=True) + epsilon)
    k_norm = lax.rsqrt(jnp.sum(ka * ka, axis=-1, keepdims=True) + epsilon)
    q = (qa * q_norm * (1.0 / math.sqrt(DK))).astype(bf16)
    k = (ka * k_norm).astype(bf16)
    return qa, ka, q_norm, k_norm, q, k, va.astype(bf16)


def unit_inverse(system):
    size = system.shape[0]
    row = grid_of((size, size), 0)
    col = grid_of((size, size), 1)
    eye = jnp.where(row == col, 1.0, 0.0).astype(f32)
    powers = jnp.where((row >> 3) == (col >> 3), -system, 0.0)
    square = mh(powers, powers)
    total = eye + powers
    total = total + mh(total, square)
    total = total + mh(total, mh(square, square))
    for bits in (3, 4, 5, 6):
        joint = ((row >> (bits + 1)) == (col >> (bits + 1))) & ((row >> bits) != (col >> bits))
        link = jnp.where(joint, system, 0.0)
        total = total - mh(total, mh(link, total))
    return total


def mixer_forward_kernel(
    proj_ref, small_ref, taps_ref, heads_ref, gain_ref,
    gated_ref, start_ref, inv_ref, pseudo_ref, mixed_ref,
    halo, state,
):
    halo[...] = jnp.zeros_like(halo)
    state[...] = jnp.zeros_like(state)
    row = grid_of((CHUNK, CHUNK), 0)
    col = grid_of((CHUNK, CHUNK), 1)

    def body(c, carry):
        rows = pl.ds(pl.multiple_of(c * CHUNK, CHUNK), CHUNK)
        x = proj_ref[rows, 0:1024].astype(f32)
        x_ext = jnp.concatenate([halo[...], x], axis=0)
        halo[...] = x[CHUNK - 8 :]
        convolved = conv_chunk(x_ext, taps_ref[...])
        activated = convolved * jax.nn.sigmoid(convolved)
        strength, shifted_logit, log_decay, cumulative, turned = decay_chunk(
            small_ref[rows, :], heads_ref
        )
        parts = []
        systems = []
        for h in range(2):
            qa, ka, q_norm, k_norm, q, k, v = head_inputs(activated, h)
            c_col = cumulative[:, 2 + h : 3 + h]
            c_row = turned[2 + h : 3 + h, :]
            beta_row = turned[h : h + 1, :]
            ratio = jnp.exp(jnp.where(row >= col, c_col - c_row, -1e4)) * beta_row
            systems.append(jnp.where(row > col, ratio * mm(k, k, NT), 0.0))
            mixing = ratio * mm(q, k, NT)
            parts.append((q, k, v, c_col, mixing))
        zero = jnp.zeros((CHUNK, CHUNK), f32)
        joint = jnp.concatenate(
            [
                jnp.concatenate([systems[0], zero], axis=1),
                jnp.concatenate([zero, systems[1]], axis=1),
            ],
            axis=0,
        )
        inverse = unit_inverse(joint)
        for h in range(2):
            q, k, v, c_col, mixing = parts[h]
            inv = inverse[128 * h : 128 * h + 128, 128 * h : 128 * h + 128]
            growth = jnp.exp(c_col)
            last = c_col[CHUNK - 1 :, :]
            before = state[h]
            start_ref[c, h] = before
            inv_ref[c, h] = inv
            read = mh(jnp.concatenate([q, k], axis=0).astype(f32), before)
            pseudo = mh(inv, v.astype(f32) - growth * read[CHUNK:])
            pseudo_ref[c, h] = pseudo
            mixed = growth * read[:CHUNK] + mh(mixing, pseudo)
            tail = jnp.exp(last - c_col) * strength[:, h : h + 1]
            state[h] = jnp.exp(last) * before + mh(k.astype(f32), tail * pseudo, TN)
            mixed_ref[rows, 256 * h : 256 * h + 256] = mixed
            gate = proj_ref[rows, 1024 + 256 * h : 1280 + 256 * h].astype(f32)
            scale = lax.rsqrt(jnp.mean(mixed * mixed, axis=-1, keepdims=True) + out_floor)
            gated = mixed * scale * gain_ref[0:1, :] * (gate * jax.nn.sigmoid(gate))
            gated_ref[rows, 256 * h : 256 * h + 256] = gated.astype(bf16)
        return carry

    lax.fori_loop(0, proj_ref.shape[0] // CHUNK, body, 0)


def mixer_forward(projected, small, taps, heads, gain):
    tokens = projected.shape[0]
    chunks = tokens // CHUNK
    vmem = pl.BlockSpec(memory_space=pltpu.VMEM)
    return pl.pallas_call(
        mixer_forward_kernel,
        out_shape=(
            jax.ShapeDtypeStruct((tokens, 512), bf16),
            jax.ShapeDtypeStruct((chunks, 2, DK, DV), f32),
            jax.ShapeDtypeStruct((chunks, 2, CHUNK, CHUNK), f32),
            jax.ShapeDtypeStruct((chunks, 2, CHUNK, DV), f32),
            jax.ShapeDtypeStruct((tokens, 512), f32),
        ),
        in_specs=[vmem] * 5,
        out_specs=(vmem,) * 5,
        scratch_shapes=[pltpu.VMEM((8, 1024), f32), pltpu.VMEM((2, DK, DV), f32)],
        compiler_params=pltpu.CompilerParams(vmem_limit_bytes=48 << 20),
        name="mixer_forward",
    )(projected, small, taps, heads, gain)


def mixer_backward_kernel(
    proj_ref, small_ref, taps_ref, heads_ref, gain_ref,
    start_ref, inv_ref, pseudo_ref, mixed_ref, dgated_ref,
    dproj_ref, dsmall_ref, gtaps_ref, gheads_ref,
    halo, dstate,
):
    halo[...] = jnp.zeros_like(halo)
    dstate[...] = jnp.zeros_like(dstate)
    gtaps_ref[...] = jnp.zeros_like(gtaps_ref)
    gheads_ref[...] = jnp.zeros_like(gheads_ref)
    row = grid_of((CHUNK, CHUNK), 0)
    col = grid_of((CHUNK, CHUNK), 1)
    lane = col
    token = grid_of((CHUNK, 1), 0)
    chunks = proj_ref.shape[0] // CHUNK

    def body(step, carry):
        c = chunks - 1 - step
        rows = pl.ds(pl.multiple_of(c * CHUNK, CHUNK), CHUNK)
        x = proj_ref[rows, 0:1024].astype(f32)
        before_rows = pl.ds(pl.multiple_of(jnp.maximum(c * CHUNK - 16, 0), 16), 16)
        x_before = proj_ref[before_rows, 0:1024].astype(f32)[8:]
        x_before = jnp.where(c > 0, x_before, 0.0)
        x_ext = jnp.concatenate([x_before, x], axis=0)
        convolved = conv_chunk(x_ext, taps_ref[...])
        sig = jax.nn.sigmoid(convolved)
        activated = convolved * sig
        strength, shifted_logit, log_decay, cumulative, turned = decay_chunk(
            small_ref[rows, :], heads_ref
        )
        d_strength = jnp.zeros((CHUNK, CHUNK), f32)
        d_cumulative = jnp.zeros((CHUNK, CHUNK), f32)
        d_q_parts, d_k_parts, d_v_parts = [], [], []
        gain_sum = jnp.zeros((1, DV), f32)
        for h in range(2):
            qa, ka, q_norm, k_norm, q, k, v = head_inputs(activated, h)
            cols = slice(256 * h, 256 * h + 256)
            mixed = mixed_ref[rows, cols]
            gate = proj_ref[rows, 1024 + 256 * h : 1280 + 256 * h].astype(f32)
            d_gated = dgated_ref[rows, cols].astype(f32)
            gate_sig = jax.nn.sigmoid(gate)
            gate_silu = gate * gate_sig
            scale = lax.rsqrt(jnp.mean(mixed * mixed, axis=-1, keepdims=True) + out_floor)
            scaled = mixed * scale
            gain = gain_ref[0:1, :]
            gain_sum = gain_sum + jnp.sum(d_gated * scaled * gate_silu, axis=0, keepdims=True)
            d_gate = d_gated * scaled * gain * (gate_sig * (1.0 + gate * (1.0 - gate_sig)))
            dproj_ref[rows, 1024 + 256 * h : 1280 + 256 * h] = d_gate.astype(bf16)
            d_scaled = d_gated * gain * gate_silu
            d_mixed = scale * (
                d_scaled - scaled * jnp.mean(d_scaled * scaled, axis=-1, keepdims=True)
            )
            c_col = cumulative[:, 2 + h : 3 + h]
            c_row = turned[2 + h : 3 + h, :]
            beta_row = turned[h : h + 1, :]
            beta_col = strength[:, h : h + 1]
            growth = jnp.exp(c_col)
            last = c_col[CHUNK - 1 :, :]
            ratio = jnp.exp(jnp.where(row >= col, c_col - c_row, -1e4))
            key_gram = mm(k, k, NT)
            query_gram = mm(q, k, NT)
            mixing = ratio * beta_row * query_gram
            fade = jnp.exp(last - c_col)
            tail = fade * beta_col
            start = start_ref[c, h]
            inv = inv_ref[c, h]
            pseudo = pseudo_ref[c, h]
            d_end = dstate[h]
            kf = k.astype(f32)
            qf = q.astype(f32)
            d_pseudo = mh(mixing, d_mixed, TN) + tail * mh(kf, d_end)
            d_right = mh(inv, d_pseudo, TN)
            pair = jnp.concatenate([d_mixed, d_right], axis=0)
            reads = mh(pair, jnp.concatenate([start, pseudo], axis=0), NT)
            read_q = reads[:CHUNK, :DK]
            read_k = reads[CHUNK:, :DK]
            read_u = mh(pseudo, d_end, NT)
            d_mixing = jnp.where(row >= col, reads[:CHUNK, DK:], 0.0) * ratio
            d_system = jnp.where(row > col, -reads[CHUNK:, DK:], 0.0) * ratio
            raw = d_mixing * query_gram + d_system * key_gram
            x_pair = jnp.concatenate([d_mixing * beta_row, d_system * beta_row], axis=0)
            by_row = mh(x_pair, kf)
            by_col = mh(x_pair, jnp.concatenate([qf, kf], axis=0), TN)
            d_q = growth * read_q + by_row[:CHUNK]
            d_k = by_row[CHUNK:] + by_col - growth * read_k + tail * read_u
            dstate[h] = jnp.exp(last) * d_end + mh(
                jnp.concatenate([growth * qf, -growth * kf], axis=0), pair, TN
            )
            u_dot = jnp.sum(read_u * kf, axis=-1, keepdims=True)
            col_raw = jnp.sum(raw, axis=0, keepdims=True)
            col_raw = jnp.broadcast_to(col_raw, (CHUNK, CHUNK)).T[:, 0:1]
            d_beta = col_raw + fade * u_dot
            d_cum = (
                jnp.sum(raw * beta_row, axis=-1, keepdims=True)
                - beta_col * col_raw
                + growth
                * (
                    jnp.sum(read_q * qf, axis=-1, keepdims=True)
                    - jnp.sum(read_k * kf, axis=-1, keepdims=True)
                )
                - tail * u_dot
            )
            at_last = jnp.sum(tail * u_dot, axis=0, keepdims=True) + jnp.exp(last) * jnp.sum(
                jnp.sum(start * d_end, axis=-1, keepdims=True), axis=0, keepdims=True
            )
            d_cum = d_cum + jnp.where(token == CHUNK - 1, at_last, 0.0)
            d_strength = jnp.where(lane == h, d_beta, d_strength)
            d_cumulative = jnp.where(lane == 2 + h, d_cum, d_cumulative)
            d_qn = d_q * (1.0 / math.sqrt(DK))
            qn = qa * q_norm
            kn = ka * k_norm
            d_q_parts.append(
                q_norm * (d_qn - qn * jnp.sum(d_qn * qn, axis=-1, keepdims=True))
            )
            d_k_parts.append(k_norm * (d_k - kn * jnp.sum(d_k * kn, axis=-1, keepdims=True)))
            d_v_parts.append(d_right)
        upper_ones = jnp.where(row <= col, 1.0, 0.0).astype(f32)
        d_log = mh(upper_ones, d_cumulative)
        d_shifted = d_log * (-jnp.exp(heads_ref[0:1, :])) * jax.nn.sigmoid(shifted_logit)
        d_small = jnp.where(lane < 2, d_strength * strength * (1.0 - strength), d_shifted)
        dsmall_ref[rows, :] = jnp.where(lane < 4, d_small, 0.0).astype(bf16)
        gheads_ref[0:1, :] += gain_sum
        gheads_ref[1:2, 0:128] += jnp.sum(d_log * log_decay, axis=0, keepdims=True)
        gheads_ref[2:3, 0:128] += jnp.sum(d_shifted, axis=0, keepdims=True)
        d_activated = jnp.concatenate(d_q_parts + d_k_parts + d_v_parts, axis=1)
        d_conv = d_activated * (sig * (1.0 + convolved * (1.0 - sig)))
        for j in range(CONV):
            gtaps_ref[j : j + 1, :] += jnp.sum(
                d_conv * x_ext[5 + j : 5 + j + CHUNK], axis=0, keepdims=True
            )
        d_ext = jnp.concatenate([d_conv, halo[...]], axis=0)
        d_x = sum(
            d_ext[CONV - 1 - j : CONV - 1 - j + CHUNK] * taps_ref[j : j + 1] for j in range(CONV)
        )
        halo[...] = d_conv[:8]
        dproj_ref[rows, 0:1024] = d_x.astype(bf16)
        return carry

    lax.fori_loop(0, chunks, body, 0)


def mixer_backward(projected, small, taps, heads, gain, saved, d_gated):
    tokens = projected.shape[0]
    vmem = pl.BlockSpec(memory_space=pltpu.VMEM)
    return pl.pallas_call(
        mixer_backward_kernel,
        out_shape=(
            jax.ShapeDtypeStruct((tokens, 1536), bf16),
            jax.ShapeDtypeStruct((tokens, 128), bf16),
            jax.ShapeDtypeStruct((8, 1024), f32),
            jax.ShapeDtypeStruct((8, DV), f32),
        ),
        in_specs=[vmem] * 10,
        out_specs=(vmem,) * 4,
        scratch_shapes=[pltpu.VMEM((8, 1024), f32), pltpu.VMEM((2, DK, DV), f32)],
        compiler_params=pltpu.CompilerParams(vmem_limit_bytes=48 << 20),
        name="mixer_backward",
    )(projected, small, taps, heads, gain, *saved, d_gated)


def rms_norm(residual, gain):
    scale = lax.rsqrt(jnp.mean(residual * residual, axis=-1, keepdims=True) + epsilon)
    return residual * scale * gain


def norm_back(residual, gain, d_out):
    scale = lax.rsqrt(jnp.mean(residual * residual, axis=-1, keepdims=True) + epsilon)
    unit = residual * scale
    d_unit = d_out * gain
    d_residual = scale * (d_unit - unit * jnp.mean(d_unit * unit, axis=-1, keepdims=True))
    return d_residual, jnp.sum(d_out * unit, axis=0)


def gather_rows(x):
    return lax.all_gather(x, "grp", axis=0, tiled=True)


def scatter_rows(x):
    return lax.psum_scatter(x.astype(bf16), "grp", scatter_dimension=0, tiled=True).astype(f32)


def dot(left, right, dims=NN):
    return mm(left, right, dims)


def per_device(
    x_input, norm_gain, w_in, w_ab, conv_w, a_log, dt_bias, out_gain, w_out, ffn_in, ffn_out,
    cotangent,
):
    parts = lax.axis_size("grp")
    replicas = lax.axis_size("rep")
    mine = lax.axis_index("grp")
    rows, width = x_input.shape[1], x_input.shape[2]
    gains = lax.all_gather(norm_gain, "grp", axis=2, tiled=True).astype(f32)
    taps_all = lax.all_gather(conv_w, "grp", axis=2, tiled=True).astype(f32)
    out_gains = lax.all_gather(out_gain, "grp", axis=1, tiled=True).astype(f32)
    ab_all = lax.all_gather(w_ab, "grp", axis=1, tiled=True)

    def own(array, start, size):
        return lax.dynamic_slice_in_dim(array, start + mine * size, size, array.ndim - 1)

    layers = []
    for l in range(LAYERS):
        pieces = jnp.stack(
            [
                jnp.concatenate(
                    [
                        w_in[l][:, 256 * t : 256 * t + 256],
                        w_in[l][:, HK + 256 * t : HK + 256 * t + 256],
                        w_in[l][:, 2 * HK + 512 * t : 2 * HK + 512 * t + 512],
                        w_in[l][:, CH + 512 * t : CH + 512 * t + 512],
                    ],
                    axis=1,
                )
                for t in range(4)
            ]
        )
        in_weight = lax.all_to_all(pieces, "grp", 0, 0).reshape(width, 1536)
        pieces = jnp.stack(
            [
                jnp.concatenate(
                    [ffn_in[l][:, 704 * t : 704 * t + 704], ffn_in[l][:, FF + 704 * t : FF + 704 * t + 704]],
                    axis=1,
                )
                for t in range(4)
            ]
        )
        up_weight = lax.all_to_all(pieces, "grp", 0, 0).reshape(width, 1408)
        ab = jnp.concatenate([own(ab_all[l], 0, 2), own(ab_all[l], H, 2)], axis=1)
        ab = jnp.pad(ab, ((0, 0), (0, 124)))
        taps = jnp.concatenate(
            [own(taps_all[l], 0, 256), own(taps_all[l], HK, 256), own(taps_all[l], 2 * HK, 512)], axis=1
        )
        taps = jnp.pad(taps, ((0, 4), (0, 0)))
        heads = jnp.pad(
            jnp.stack([a_log[l], dt_bias[l]]).astype(f32), ((0, 6), (2, 124))
        )
        gain = jnp.pad(out_gains[l][None], ((0, 7), (0, 0)))
        layers.append((gains[l], in_weight, ab, taps, heads, gain, w_out[l], up_weight, ffn_out[l]))

    residual = x_input[0].astype(f32)
    kept = []
    for l in range(LAYERS):
        gain_pair, in_weight, ab, taps, heads, gain, out_weight, up_weight, down_weight = layers[l]
        normed = gather_rows(rms_norm(residual, gain_pair[0]).astype(bf16))
        projected = dot(normed, in_weight).astype(bf16)
        small = dot(normed, ab)
        gated, *saved = mixer_forward(projected, small, taps, heads, gain)
        residual_mid = residual + scatter_rows(dot(gated, out_weight))
        normed_two = gather_rows(rms_norm(residual_mid, gain_pair[1]).astype(bf16))
        up_part = dot(normed_two, up_weight)
        hidden = (jax.nn.silu(up_part[:, :704]) * up_part[:, 704:]).astype(bf16)
        residual_out = residual_mid + scatter_rows(dot(hidden, down_weight))
        kept.append((residual, normed, projected, small, gated, saved, residual_mid, normed_two, up_part, hidden))
        residual = residual_out
    block_output = residual.astype(bf16)[None]

    d_residual = cotangent[0].astype(f32)
    big = [None] * LAYERS
    small_grads = [None] * LAYERS
    for l in reversed(range(LAYERS)):
        gain_pair, in_weight, ab, taps, heads, gain, out_weight, up_weight, down_weight = layers[l]
        residual, normed, projected, small, gated, saved, residual_mid, normed_two, up_part, hidden = kept[l]
        d_down = gather_rows(d_residual.astype(bf16))
        g_down = dot(hidden, d_down, TN).astype(bf16)
        d_hidden = dot(d_down, down_weight, NT)
        gate, up = up_part[:, :704], up_part[:, 704:]
        sig = jax.nn.sigmoid(gate)
        d_up = jnp.concatenate(
            [d_hidden * up * (sig * (1.0 + gate * (1.0 - sig))), d_hidden * gate * sig], axis=1
        ).astype(bf16)
        g_up = dot(normed_two, d_up, TN).astype(bf16)
        d_normed_two = scatter_rows(dot(d_up, up_weight, NT))
        d_norm, g_gain_two = norm_back(residual_mid, gain_pair[1], d_normed_two)
        d_mid = d_residual + d_norm
        d_branch = gather_rows(d_mid.astype(bf16))
        g_out = dot(gated, d_branch, TN).astype(bf16)
        d_gated = dot(d_branch, out_weight, NT).astype(bf16)
        d_projected, d_small, g_taps, g_heads = mixer_backward(
            projected, small, taps, heads, gain, saved, d_gated
        )
        g_in = dot(normed, d_projected, TN).astype(bf16)
        g_ab = dot(normed, d_small, TN)[:, :4]
        d_normed = scatter_rows(dot(d_projected, in_weight, NT) + dot(d_small, ab, NT))
        d_norm, g_gain_one = norm_back(residual, gain_pair[0], d_normed)
        d_residual = d_mid + d_norm
        small_grads[l] = (g_gain_one, g_gain_two, g_ab, g_taps, g_heads)
        big[l] = (g_in, g_up, g_out, g_down)
    input_grad = d_residual.astype(bf16)[None]

    w_in_grads, up_grads, out_grads, down_grads = [], [], [], []
    for l in range(LAYERS):
        g_in, g_up, g_out, g_down = big[l]

        def columns(grad):
            part = rows // replicas
            grad = grad.reshape(parts, replicas, part, grad.shape[1])
            grad = lax.psum_scatter(jnp.moveaxis(grad, 1, 0), "rep", scatter_dimension=0, tiled=False)
            grad = lax.all_to_all(grad, "grp", 0, 0)
            grad = lax.all_gather(grad, "rep", axis=0)
            return jnp.moveaxis(grad, 1, 0).reshape(parts, rows, -1)

        def plain(grad):
            grad = lax.psum_scatter(grad, "rep", scatter_dimension=0, tiled=True)
            return lax.all_gather(grad, "rep", axis=0, tiled=True)

        blocks = columns(g_in)
        w_in_grads.append(
            jnp.concatenate(
                [blocks[t][:, 0:256] for t in range(4)]
                + [blocks[t][:, 256:512] for t in range(4)]
                + [blocks[t][:, 512:1024] for t in range(4)]
                + [blocks[t][:, 1024:1536] for t in range(4)],
                axis=1,
            ).astype(f32)
        )
        blocks = columns(g_up)
        up_grads.append(
            jnp.concatenate(
                [blocks[t][:, :704] for t in range(4)] + [blocks[t][:, 704:] for t in range(4)], axis=1
            ).astype(f32)
        )
        joint = plain(jnp.concatenate([g_out, g_down], axis=0))
        out_grads.append(joint[:512].astype(f32))
        down_grads.append(joint[512:].astype(f32))

    def spread(piece, full, at):
        zero = jnp.zeros(piece.shape[:-1] + (full,), f32)
        return lax.dynamic_update_slice_in_dim(zero, piece, at, piece.ndim - 1)

    packed = []
    for l in range(LAYERS):
        g_gain_one, g_gain_two, g_ab, g_taps, g_heads = small_grads[l]
        packed.append(g_gain_one)
        packed.append(g_gain_two)
        packed.append(g_heads[0])
        packed.append(spread(g_heads[1, 2:4], H, 2 * mine))
        packed.append(spread(g_heads[2, 2:4], H, 2 * mine))
        packed.append(spread(g_taps[:4, :256], HK, 256 * mine))
        packed.append(spread(g_taps[:4, 256:512], HK, 256 * mine))
        packed.append(spread(g_taps[:4, 512:], HV, 512 * mine))
        packed.append(spread(g_ab[:, :2], H, 2 * mine))
        packed.append(spread(g_ab[:, 2:], H, 2 * mine))
    flat = lax.psum(jnp.concatenate([piece.reshape(-1) for piece in packed]), ("rep", "grp"))
    sums, at = [], 0
    for piece in packed:
        sums.append(flat[at : at + piece.size].reshape(piece.shape))
        at += piece.size
    per_layer = [sums[10 * l : 10 * l + 10] for l in range(LAYERS)]

    def owned(array, dim):
        size = array.shape[dim] // parts
        return lax.dynamic_slice_in_dim(array, mine * size, size, dim)

    grad_gain = owned(jnp.stack([jnp.stack([p[0], p[1]]) for p in per_layer]), 2)
    grad_out_gain = owned(jnp.stack([p[2] for p in per_layer]), 1)
    grad_a_log = owned(jnp.stack([p[3] for p in per_layer]), 1)
    grad_dt = owned(jnp.stack([p[4] for p in per_layer]), 1)
    grad_conv = owned(jnp.stack([jnp.concatenate(p[5:8], axis=1) for p in per_layer]), 2)
    grad_ab = owned(jnp.stack([jnp.concatenate(p[8:10], axis=1) for p in per_layer]), 1)
    return (
        block_output,
        input_grad,
        grad_gain,
        jnp.stack(w_in_grads),
        grad_ab,
        grad_conv,
        grad_a_log,
        grad_dt,
        grad_out_gain,
        jnp.stack(out_grads),
        jnp.stack(up_grads),
        jnp.stack(down_grads),
    )


def solution(mesh):
    rows = P("rep", "grp", None)
    first = P(None, "grp")
    middle = P(None, "grp", None)
    last = P(None, None, "grp")
    in_specs = (rows, last, middle, middle, last, first, first, first, middle, middle, middle, rows)
    out_specs = (rows, rows, last, middle, middle, last, first, first, first, middle, middle, middle)
    return jax.shard_map(
        per_device, mesh=mesh, in_specs=in_specs, out_specs=out_specs, check_vma=False
    )
```

```python
from functools import partial
import math

import jax
import jax.numpy as jnp
from jax import lax
from jax.sharding import PartitionSpec as P
from jax.experimental import pallas as pl
from jax.experimental.pallas import tpu as pltpu

H = 8
DK = 128
DV = 256
FF = 2816
CONV = 4
LAYERS = 2
HK = 1024
HV = 2048
CH = 4096
CHUNK = 128

f32 = jnp.float32
bf16 = jnp.bfloat16
HIGH = lax.Precision.HIGHEST
epsilon = 1e-06
out_floor = 0.02
NN = ((1,), (0,))
NT = ((1,), (1,))
TN = ((0,), (0,))


def mm(left, right, dims=NN, precision=None):
    return lax.dot_general(
        left, right, (dims, ((), ())), precision=precision, preferred_element_type=f32
    )


def mh(left, right, dims=NN):
    return mm(left, right, dims, HIGH)


def grid_of(shape, dim):
    return lax.broadcasted_iota(jnp.int32, shape, dim)


def conv_chunk(x_ext, taps):
    return sum(x_ext[5 + j : 5 + j + CHUNK] * taps[j : j + 1] for j in range(CONV))


def decay_chunk(small, heads_ref):
    lane = grid_of(small.shape, 1)
    strength = jax.nn.sigmoid(small)
    shifted_logit = small + heads_ref[1:2, :]
    soft = jnp.maximum(shifted_logit, 0.0) + jnp.log1p(jnp.exp(-jnp.abs(shifted_logit)))
    log_decay = -jnp.exp(heads_ref[0:1, :]) * soft
    row = grid_of((CHUNK, CHUNK), 0)
    col = grid_of((CHUNK, CHUNK), 1)
    lower_ones = jnp.where(row >= col, 1.0, 0.0).astype(f32)
    cumulative = mm2(lower_ones.astype(bf16), log_decay)
    turned = jnp.where(lane < 2, strength, cumulative).T
    return strength, shifted_logit, log_decay, cumulative, turned


def head_inputs(activated, h):
    qa = activated[:, 128 * h : 128 * h + 128]
    ka = activated[:, 256 + 128 * h : 384 + 128 * h]
    va = activated[:, 512 + 256 * h : 768 + 256 * h]
    q_norm = lax.rsqrt(jnp.sum(qa * qa, axis=-1, keepdims=True) + epsilon)
    k_norm = lax.rsqrt(jnp.sum(ka * ka, axis=-1, keepdims=True) + epsilon)
    q = (qa * q_norm * (1.0 / math.sqrt(DK))).astype(bf16)
    k = (ka * k_norm).astype(bf16)
    return qa, ka, q_norm, k_norm, q, k, va.astype(bf16)


def split(x):
    high = x.astype(bf16)
    return high, (x - high.astype(f32)).astype(bf16)


def mm2(exact, right, dims=NN):
    high, low = split(right)
    return mm(exact, high, dims) + mm(exact, low, dims)


def mm3(left, right, dims=NN):
    lh, ll = split(left)
    rh, rl = split(right)
    return mm(lh, rh, dims) + (mm(lh, rl, dims) + mm(ll, rh, dims))


def mb(left, right, dims=NN):
    return mm(left.astype(bf16), right.astype(bf16), dims)


def unit_inverse(system):
    size = system.shape[0]
    row = grid_of((size, size), 0)
    col = grid_of((size, size), 1)
    eye = jnp.where(row == col, 1.0, 0.0).astype(f32)
    powers = jnp.where((row >> 2) == (col >> 2), -system, 0.0)
    square = mb(powers, powers)
    total = eye + powers
    total = total + mb(total, square)
    for bits in (2, 3, 4, 5, 6):
        joint = ((row >> (bits + 1)) == (col >> (bits + 1))) & ((row >> bits) != (col >> bits))
        link = jnp.where(joint, system, 0.0)
        total = total - mb(total, mb(link, total))
    return total


UNROLL = 2


def mixer_forward_kernel(
    proj_ref, small_ref, taps_ref, heads_ref, gain_ref,
    gated_ref, start_ref, inv_ref, pseudo_ref, mixed_ref,
    halo, state,
):
    halo[...] = jnp.zeros_like(halo)
    state[...] = jnp.zeros_like(state)
    row = grid_of((CHUNK, CHUNK), 0)
    col = grid_of((CHUNK, CHUNK), 1)
    zero = jnp.zeros((CHUNK, CHUNK), f32)

    def prepare(c):
        rows = pl.ds(pl.multiple_of(c * CHUNK, CHUNK), CHUNK)
        x = proj_ref[rows, 0:1024].astype(f32)
        x_ext = jnp.concatenate([halo[...], x], axis=0)
        halo[...] = x[CHUNK - 8 :]
        convolved = conv_chunk(x_ext, taps_ref[...])
        activated = convolved * jax.nn.sigmoid(convolved)
        strength, shifted_logit, log_decay, cumulative, turned = decay_chunk(
            small_ref[rows, :], heads_ref
        )
        parts = []
        systems = []
        for h in range(2):
            qa, ka, q_norm, k_norm, q, k, v = head_inputs(activated, h)
            c_col = cumulative[:, 2 + h : 3 + h]
            c_row = turned[2 + h : 3 + h, :]
            beta_row = turned[h : h + 1, :]
            ratio = jnp.exp(jnp.where(row >= col, c_col - c_row, -1e4)) * beta_row
            systems.append(jnp.where(row > col, ratio * mm(k, k, NT), 0.0))
            mixing = (ratio * mm(q, k, NT)).astype(bf16)
            parts.append((q, k, v, c_col, mixing, strength[:, h : h + 1]))
        joint = jnp.concatenate(
            [
                jnp.concatenate([systems[0], zero], axis=1),
                jnp.concatenate([zero, systems[1]], axis=1),
            ],
            axis=0,
        )
        return parts, unit_inverse(joint)

    def advance(c, parts, inverse):
        rows = pl.ds(pl.multiple_of(c * CHUNK, CHUNK), CHUNK)
        for h in range(2):
            q, k, v, c_col, mixing, beta_col = parts[h]
            inv = inverse[128 * h : 128 * h + 128, 128 * h : 128 * h + 128]
            growth = jnp.exp(c_col)
            last = c_col[CHUNK - 1 :, :]
            before = state[h]
            start_ref[c, h] = before
            inv_ref[c, h] = inv
            read = mm2(jnp.concatenate([q, k], axis=0), before)
            pseudo = mb(inv, v.astype(f32) - growth * read[CHUNK:])
            pseudo_ref[c, h] = pseudo
            tail = jnp.exp(last - c_col) * beta_col
            state[h] = jnp.exp(last) * before + mm2(k, tail * pseudo, TN)
            mixed = growth * read[:CHUNK] + mm(mixing, pseudo.astype(bf16))
            mixed_ref[rows, 256 * h : 256 * h + 256] = mixed
            gate = proj_ref[rows, 1024 + 256 * h : 1280 + 256 * h].astype(f32)
            scale = lax.rsqrt(jnp.mean(mixed * mixed, axis=-1, keepdims=True) + out_floor)
            gated = mixed * scale * gain_ref[0:1, :] * (gate * jax.nn.sigmoid(gate))
            gated_ref[rows, 256 * h : 256 * h + 256] = gated.astype(bf16)

    def body(step, carry):
        ready = [prepare(step * UNROLL + u) for u in range(UNROLL)]
        for u in range(UNROLL):
            advance(step * UNROLL + u, *ready[u])
        return carry

    lax.fori_loop(0, proj_ref.shape[0] // (CHUNK * UNROLL), body, 0)


def mixer_forward(projected, small, taps, heads, gain):
    tokens = projected.shape[0]
    chunks = tokens // CHUNK
    vmem = pl.BlockSpec(memory_space=pltpu.VMEM)
    return pl.pallas_call(
        mixer_forward_kernel,
        out_shape=(
            jax.ShapeDtypeStruct((tokens, 512), bf16),
            jax.ShapeDtypeStruct((chunks, 2, DK, DV), f32),
            jax.ShapeDtypeStruct((chunks, 2, CHUNK, CHUNK), f32),
            jax.ShapeDtypeStruct((chunks, 2, CHUNK, DV), f32),
            jax.ShapeDtypeStruct((tokens, 512), f32),
        ),
        in_specs=[vmem] * 5,
        out_specs=(vmem,) * 5,
        scratch_shapes=[pltpu.VMEM((8, 1024), f32), pltpu.VMEM((2, DK, DV), f32)],
        compiler_params=pltpu.CompilerParams(vmem_limit_bytes=48 << 20),
        name="mixer_forward",
    )(projected, small, taps, heads, gain)


def mixer_backward_kernel(
    proj_ref, small_ref, taps_ref, heads_ref, gain_ref,
    start_ref, inv_ref, pseudo_ref, mixed_ref, dgated_ref,
    dproj_ref, dsmall_ref, gtaps_ref, gheads_ref,
    halo, dstate,
):
    halo[...] = jnp.zeros_like(halo)
    dstate[...] = jnp.zeros_like(dstate)
    gtaps_ref[...] = jnp.zeros_like(gtaps_ref)
    gheads_ref[...] = jnp.zeros_like(gheads_ref)
    row = grid_of((CHUNK, CHUNK), 0)
    col = grid_of((CHUNK, CHUNK), 1)
    lane = col
    token = grid_of((CHUNK, 1), 0)
    chunks = proj_ref.shape[0] // CHUNK

    def body(step, carry):
        c = chunks - 1 - step
        rows = pl.ds(pl.multiple_of(c * CHUNK, CHUNK), CHUNK)
        x = proj_ref[rows, 0:1024].astype(f32)
        before_rows = pl.ds(pl.multiple_of(jnp.maximum(c * CHUNK - 16, 0), 16), 16)
        x_before = proj_ref[before_rows, 0:1024].astype(f32)[8:]
        x_before = jnp.where(c > 0, x_before, 0.0)
        x_ext = jnp.concatenate([x_before, x], axis=0)
        convolved = conv_chunk(x_ext, taps_ref[...])
        sig = jax.nn.sigmoid(convolved)
        activated = convolved * sig
        strength, shifted_logit, log_decay, cumulative, turned = decay_chunk(
            small_ref[rows, :], heads_ref
        )
        d_strength = jnp.zeros((CHUNK, CHUNK), f32)
        d_cumulative = jnp.zeros((CHUNK, CHUNK), f32)
        d_q_parts, d_k_parts, d_v_parts = [], [], []
        gain_sum = jnp.zeros((1, DV), f32)
        for h in range(2):
            qa, ka, q_norm, k_norm, q, k, v = head_inputs(activated, h)
            cols = slice(256 * h, 256 * h + 256)
            mixed = mixed_ref[rows, cols]
            gate = proj_ref[rows, 1024 + 256 * h : 1280 + 256 * h].astype(f32)
            d_gated = dgated_ref[rows, cols].astype(f32)
            gate_sig = jax.nn.sigmoid(gate)
            gate_silu = gate * gate_sig
            scale = lax.rsqrt(jnp.mean(mixed * mixed, axis=-1, keepdims=True) + out_floor)
            scaled = mixed * scale
            gain = gain_ref[0:1, :]
            gain_sum = gain_sum + jnp.sum(d_gated * scaled * gate_silu, axis=0, keepdims=True)
            d_gate = d_gated * scaled * gain * (gate_sig * (1.0 + gate * (1.0 - gate_sig)))
            dproj_ref[rows, 1024 + 256 * h : 1280 + 256 * h] = d_gate.astype(bf16)
            d_scaled = d_gated * gain * gate_silu
            d_mixed = scale * (
                d_scaled - scaled * jnp.mean(d_scaled * scaled, axis=-1, keepdims=True)
            )
            c_col = cumulative[:, 2 + h : 3 + h]
            c_row = turned[2 + h : 3 + h, :]
            beta_row = turned[h : h + 1, :]
            beta_col = strength[:, h : h + 1]
            growth = jnp.exp(c_col)
            last = c_col[CHUNK - 1 :, :]
            ratio = jnp.exp(jnp.where(row >= col, c_col - c_row, -1e4))
            key_gram = mm(k, k, NT)
            query_gram = mm(q, k, NT)
            mixing = ratio * beta_row * query_gram
            fade = jnp.exp(last - c_col)
            tail = fade * beta_col
            start = start_ref[c, h]
            inv = inv_ref[c, h]
            pseudo = pseudo_ref[c, h]
            d_end = dstate[h]
            kf = k.astype(f32)
            qf = q.astype(f32)
            d_pseudo = mh(mixing, d_mixed, TN) + tail * mh(kf, d_end)
            d_right = mh(inv, d_pseudo, TN)
            pair = jnp.concatenate([d_mixed, d_right], axis=0)
            reads = mh(pair, jnp.concatenate([start, pseudo], axis=0), NT)
            read_q = reads[:CHUNK, :DK]
            read_k = reads[CHUNK:, :DK]
            read_u = mh(pseudo, d_end, NT)
            d_mixing = jnp.where(row >= col, reads[:CHUNK, DK:], 0.0) * ratio
            d_system = jnp.where(row > col, -reads[CHUNK:, DK:], 0.0) * ratio
            raw = d_mixing * query_gram + d_system * key_gram
            x_pair = jnp.concatenate([d_mixing * beta_row, d_system * beta_row], axis=0)
            by_row = mh(x_pair, kf)
            by_col = mh(x_pair, jnp.concatenate([qf, kf], axis=0), TN)
            d_q = growth * read_q + by_row[:CHUNK]
            d_k = by_row[CHUNK:] + by_col - growth * read_k + tail * read_u
            dstate[h] = jnp.exp(last) * d_end + mh(
                jnp.concatenate([growth * qf, -growth * kf], axis=0), pair, TN
            )
            u_dot = jnp.sum(read_u * kf, axis=-1, keepdims=True)
            col_raw = jnp.sum(raw, axis=0, keepdims=True)
            col_raw = jnp.broadcast_to(col_raw, (CHUNK, CHUNK)).T[:, 0:1]
            d_beta = col_raw + fade * u_dot
            d_cum = (
                jnp.sum(raw * beta_row, axis=-1, keepdims=True)
                - beta_col * col_raw
                + growth
                * (
                    jnp.sum(read_q * qf, axis=-1, keepdims=True)
                    - jnp.sum(read_k * kf, axis=-1, keepdims=True)
                )
                - tail * u_dot
            )
            at_last = jnp.sum(tail * u_dot, axis=0, keepdims=True) + jnp.exp(last) * jnp.sum(
                jnp.sum(start * d_end, axis=-1, keepdims=True), axis=0, keepdims=True
            )
            d_cum = d_cum + jnp.where(token == CHUNK - 1, at_last, 0.0)
            d_strength = jnp.where(lane == h, d_beta, d_strength)
            d_cumulative = jnp.where(lane == 2 + h, d_cum, d_cumulative)
            d_qn = d_q * (1.0 / math.sqrt(DK))
            qn = qa * q_norm
            kn = ka * k_norm
            d_q_parts.append(
                q_norm * (d_qn - qn * jnp.sum(d_qn * qn, axis=-1, keepdims=True))
            )
            d_k_parts.append(k_norm * (d_k - kn * jnp.sum(d_k * kn, axis=-1, keepdims=True)))
            d_v_parts.append(d_right)
        upper_ones = jnp.where(row <= col, 1.0, 0.0).astype(f32)
        d_log = mh(upper_ones, d_cumulative)
        d_shifted = d_log * (-jnp.exp(heads_ref[0:1, :])) * jax.nn.sigmoid(shifted_logit)
        d_small = jnp.where(lane < 2, d_strength * strength * (1.0 - strength), d_shifted)
        dsmall_ref[rows, :] = jnp.where(lane < 4, d_small, 0.0).astype(bf16)
        gheads_ref[0:1, :] += gain_sum
        gheads_ref[1:2, 0:128] += jnp.sum(d_log * log_decay, axis=0, keepdims=True)
        gheads_ref[2:3, 0:128] += jnp.sum(d_shifted, axis=0, keepdims=True)
        d_activated = jnp.concatenate(d_q_parts + d_k_parts + d_v_parts, axis=1)
        d_conv = d_activated * (sig * (1.0 + convolved * (1.0 - sig)))
        for j in range(CONV):
            gtaps_ref[j : j + 1, :] += jnp.sum(
                d_conv * x_ext[5 + j : 5 + j + CHUNK], axis=0, keepdims=True
            )
        d_ext = jnp.concatenate([d_conv, halo[...]], axis=0)
        d_x = sum(
            d_ext[CONV - 1 - j : CONV - 1 - j + CHUNK] * taps_ref[j : j + 1] for j in range(CONV)
        )
        halo[...] = d_conv[:8]
        dproj_ref[rows, 0:1024] = d_x.astype(bf16)
        return carry

    lax.fori_loop(0, chunks, body, 0)


def mixer_backward(projected, small, taps, heads, gain, saved, d_gated):
    tokens = projected.shape[0]
    vmem = pl.BlockSpec(memory_space=pltpu.VMEM)
    return pl.pallas_call(
        mixer_backward_kernel,
        out_shape=(
            jax.ShapeDtypeStruct((tokens, 1536), bf16),
            jax.ShapeDtypeStruct((tokens, 128), bf16),
            jax.ShapeDtypeStruct((8, 1024), f32),
            jax.ShapeDtypeStruct((8, DV), f32),
        ),
        in_specs=[vmem] * 10,
        out_specs=(vmem,) * 4,
        scratch_shapes=[pltpu.VMEM((8, 1024), f32), pltpu.VMEM((2, DK, DV), f32)],
        compiler_params=pltpu.CompilerParams(vmem_limit_bytes=48 << 20),
        name="mixer_backward",
    )(projected, small, taps, heads, gain, *saved, d_gated)


SUB = 128
LIMIT = 56 << 20
MESH = pl.DeviceIdType.MESH


def place():
    me = lax.axis_index("grp")
    y, c = me // 2, me % 2
    return y, c


def shard_rows(y, c, i, size):
    return pl.ds(pl.multiple_of((2 * y + c) * size + i * SUB, SUB), SUB)


def greet(y, c):
    barrier = pltpu.get_barrier_semaphore()
    for target in (2 * y + 1 - c, 2 * (1 - y) + c):
        pl.semaphore_signal(barrier, inc=1, device_id={"grp": target}, device_id_type=MESH)
    return lambda: pl.semaphore_wait(barrier, 2)


def remote(src, dst, send, recv, target):
    return pltpu.make_async_remote_copy(
        src_ref=src, dst_ref=dst, send_sem=send, recv_sem=recv,
        device_id={"grp": target}, device_id_type=MESH,
    )


class Gather:
    def __init__(self, full, send, recv, size):
        self.full, self.send, self.recv, self.size = full, send, recv, size
        self.y, self.c = place()

    def piece(self, kind, i):
        y, c = self.y, self.c
        rows = shard_rows(1 - y if kind == 2 else y, c, i, self.size)
        target = 2 * (1 - y) + c if kind == 1 else 2 * y + 1 - c
        view = self.full.at[rows]
        return remote(view, view, self.send.at[kind, i], self.recv.at[kind, i], target)

    def own(self, i):
        return shard_rows(self.y, self.c, i, self.size)

    def start(self, i):
        self.piece(0, i).start()
        self.piece(1, i).start()

    def sibling(self, i):
        self.piece(0, i).wait_recv()
        return shard_rows(self.y, 1 - self.c, i, self.size)

    def across(self, i):
        self.piece(1, i).wait_recv()
        self.piece(2, i).start()
        return shard_rows(1 - self.y, self.c, i, self.size)

    def diagonal(self, i):
        self.piece(2, i).wait_recv()
        return shard_rows(1 - self.y, 1 - self.c, i, self.size)

    def finish(self):
        for kind in range(3):
            for i in range(self.size // SUB):
                self.piece(kind, i).wait_send()


class Scatter:
    def __init__(self, out, core, keep, relay, far, send, recv, size):
        self.out, self.core, self.keep, self.relayed, self.far = out, core, keep, relay, far
        self.send, self.recv, self.size = send, recv, size
        self.y, self.c = place()

    def to_sibling(self, part, i):
        rows = pl.ds(i * SUB, SUB)
        return remote(
            self.out.at[part, rows], self.core.at[part, rows],
            self.send.at[part, i], self.recv.at[part, i], 2 * self.y + 1 - self.c,
        )

    def to_across(self, i):
        rows = pl.ds(i * SUB, SUB)
        return remote(
            self.relayed.at[rows], self.far.at[rows],
            self.send.at[2, i], self.recv.at[2, i], 2 * (1 - self.y) + self.c,
        )

    def give(self, part, i, value):
        self.out[part, i * SUB : (i + 1) * SUB, :] = value.astype(bf16)
        self.to_sibling(part, i).start()

    def hold(self, part, i, value):
        self.keep[part, i * SUB : (i + 1) * SUB, :] = value

    def relay(self, i):
        rows = slice(i * SUB, (i + 1) * SUB)
        self.to_sibling(0, i).wait_recv()
        self.relayed[rows, :] = (self.keep[0, rows, :] + self.core[0, rows, :].astype(f32)).astype(bf16)
        self.to_across(i).start()

    def total(self, i):
        rows = slice(i * SUB, (i + 1) * SUB)
        self.to_sibling(1, i).wait_recv()
        near = self.keep[1, rows, :] + self.core[1, rows, :].astype(f32)
        self.to_across(i).wait_recv()
        return near + self.far[rows, :].astype(f32)

    def finish(self):
        for i in range(self.size // SUB):
            self.to_sibling(0, i).wait_send()
            self.to_sibling(1, i).wait_send()
            self.to_across(i).wait_send()

    @staticmethod
    def scratch(size, width):
        return [
            pltpu.VMEM((2, size, width), bf16),
            pltpu.VMEM((2, size, width), bf16),
            pltpu.VMEM((2, size, width), f32),
            pltpu.VMEM((size, width), bf16),
            pltpu.VMEM((size, width), bf16),
            pltpu.SemaphoreType.DMA((3, size // SUB)),
            pltpu.SemaphoreType.DMA((3, size // SUB)),
        ]


def gather_sems(size):
    return [pltpu.SemaphoreType.DMA((3, size // SUB)), pltpu.SemaphoreType.DMA((3, size // SUB))]


def in_order(gather):
    count = gather.size // SUB
    for i in range(count):
        yield gather.own(i)
    for i in range(count):
        yield gather.sibling(i)
    for i in range(count):
        yield gather.across(i)
        yield gather.diagonal(i)


def call(kernel, out_shape, inputs, scratch, collective, name, spots=()):
    vmem = pl.BlockSpec(memory_space=pltpu.VMEM)
    spot = pl.BlockSpec(memory_space=pl.ANY)
    return pl.pallas_call(
        kernel,
        out_shape=out_shape,
        in_specs=[vmem] * len(inputs) + [spot] * len(spots),
        out_specs=tuple(vmem for _ in out_shape),
        scratch_shapes=scratch,
        compiler_params=pltpu.CompilerParams(
            collective_id=collective, has_side_effects=True, vmem_limit_bytes=LIMIT
        ),
        cost_estimate=pl.CostEstimate(flops=1000, bytes_accessed=1000, transcendentals=0),
        name=name,
    )(*inputs, *spots)


def relative(y, c, d):
    dy, dc = d // 2, d % 2
    return 2 * (y + dy - 2 * y * dy) + c + dc - 2 * c * dc


def load_weight(own, sibling, far, whole, sems):
    y, c = place()
    size = own.shape[0]
    copies = []

    def add(src, d, start, count):
        rows = pl.ds(pl.multiple_of(relative(y, c, d) * size + start, count), count)
        copies.append(pltpu.make_async_copy(src, whole.at[rows], sems.at[len(copies)]))

    add(own, 0, 0, size)
    add(sibling, 1, 0, size)
    if len(far.shape) == 4:
        part = far.shape[2]
        for k in range(far.shape[0]):
            for d in (2, 3):
                add(far.at[k, d - 2], d, k * part, part)
    else:
        for d in (2, 3):
            add(far.at[d - 2], d, 0, size)
    for copy in copies:
        copy.start()

    def wait():
        for copy in copies:
            copy.wait()

    return wait


def load_down(src, whole, sem):
    rows = src.shape[0]
    copy = pltpu.make_async_copy(src, whole.at[pl.ds(0, rows)], sem)
    copy.start()
    whole[rows:, :] = jnp.zeros((whole.shape[0] - rows, whole.shape[1]), bf16)
    return copy.wait


def like(*shape, dtype=f32):
    return jax.ShapeDtypeStruct(shape, dtype)


def normalise(x, gain):
    return x * lax.rsqrt(jnp.mean(x * x, axis=-1, keepdims=True) + epsilon) * gain


def normalise_back(x, gain, d_out):
    scale = lax.rsqrt(jnp.mean(x * x, axis=-1, keepdims=True) + epsilon)
    unit = x * scale
    d_unit = d_out * gain
    d_x = scale * (d_unit - unit * jnp.mean(d_unit * unit, axis=-1, keepdims=True))
    return d_x, jnp.sum(d_out * unit, axis=0, keepdims=True)


def project_kernel(
    res_ref, gain_ref, ab_ref, own_ref, sibling_ref, far_ref,
    normed_ref, proj_ref, small_ref, w_ref, loads, send, recv,
):
    loaded = load_weight(own_ref, sibling_ref, far_ref, w_ref, loads)
    size = res_ref.shape[0]
    y, c = place()
    ready = greet(y, c)
    gather = Gather(normed_ref, send, recv, size)
    for i in range(size // SUB):
        rows = slice(i * SUB, (i + 1) * SUB)
        normed_ref[gather.own(i), :] = normalise(res_ref[rows, :], gain_ref[...]).astype(bf16)
        if i == 0:
            ready()
        gather.start(i)
    loaded()
    for rows in in_order(gather):
        normed = normed_ref[rows, :]
        proj_ref[rows, :] = mm(normed, w_ref[...]).astype(bf16)
        small_ref[rows, :] = mm(normed, ab_ref[...])
    gather.finish()


def project(residual, gain, weight, ab):
    size, width = residual.shape
    tokens = 4 * size
    return call(
        project_kernel,
        (like(tokens, width, dtype=bf16), like(tokens, 1536, dtype=bf16), like(tokens, 128)),
        (residual, gain, ab),
        [pltpu.VMEM((width, 1536), bf16), pltpu.SemaphoreType.DMA((10,))] + gather_sems(size),
        1 if len(weight[2].shape) == 4 else 6,
        "project",
        weight,
    )


def swiglu(up):
    lane = grid_of((SUB, 128), 1)
    gate, value, tail = up[:, :640], up[:, 640:1280], up[:, 1280:]
    turned = pltpu.roll(tail, 64, 1)
    head = gate * jax.nn.sigmoid(gate) * value
    last = jnp.where(lane < 64, tail * jax.nn.sigmoid(tail) * turned, 0.0)
    return jnp.concatenate([head, last], axis=1)


def swiglu_back(up, d_hidden):
    lane = grid_of((SUB, 128), 1)
    gate, value, tail = up[:, :640], up[:, 640:1280], up[:, 1280:]
    turned = pltpu.roll(tail, 64, 1)
    d_head, d_tail = d_hidden[:, :640], d_hidden[:, 640:]
    d_tail = d_tail + pltpu.roll(d_tail, 64, 1)
    sig = jax.nn.sigmoid(gate)
    d_gate = d_head * value * (sig * (1.0 + gate * (1.0 - sig)))
    d_value = d_head * gate * sig
    sig = jax.nn.sigmoid(tail)
    side = jnp.where(
        lane < 64,
        turned * (sig * (1.0 + tail * (1.0 - sig))),
        turned * jax.nn.sigmoid(turned),
    )
    return jnp.concatenate([d_gate, d_value, d_tail * side], axis=1)


def ffn_forward_kernel(
    gated_ref, wout_ref, res_ref, gain_ref, down_ref, own_ref, sibling_ref, far_ref,
    mid_ref, normed_ref, up_ref, hidden_ref, out_ref,
    wup_ref, wdown_ref, loads, *scratch,
):
    loaded = load_weight(own_ref, sibling_ref, far_ref, wup_ref, loads)
    loaded_down = load_down(down_ref, wdown_ref, loads.at[10])
    size = res_ref.shape[0]
    count = size // SUB
    y, c = place()
    ready = greet(y, c)
    first = Scatter(*scratch[:7], size)
    second = Scatter(*scratch[7:14], size)
    gather = Gather(normed_ref, *scratch[14:], size)

    def branch(rows):
        return mm(gated_ref[rows, :], wout_ref[...])

    for part in range(2):
        yy = 1 - y if part == 0 else y
        for i in range(count):
            value = branch(shard_rows(yy, 1 - c, i, size))
            if part == 0 and i == 0:
                ready()
            first.give(part, i, value)
            first.hold(part, i, branch(shard_rows(yy, c, i, size)))
            if part == 0:
                first.relay(i)
    for i in range(count):
        rows = slice(i * SUB, (i + 1) * SUB)
        mid = res_ref[rows, :] + first.total(i)
        mid_ref[rows, :] = mid
        normed_ref[gather.own(i), :] = normalise(mid, gain_ref[...]).astype(bf16)
        gather.start(i)

    def feed(rows):
        up = mm(normed_ref[rows, :], wup_ref[...])
        up_ref[rows, :] = up.astype(bf16)
        hidden = swiglu(up).astype(bf16)
        hidden_ref[rows, :] = hidden
        return mm(hidden, wdown_ref[...])

    loaded()
    loaded_down()
    for i in range(count):
        second.hold(1, i, feed(gather.own(i)))
    for i in range(count):
        second.give(1, i, feed(gather.sibling(i)))
    for i in range(count):
        near = gather.across(i)
        second.hold(0, i, feed(near))
        second.give(0, i, feed(gather.diagonal(i)))
        second.relay(i)
    for i in range(count):
        rows = slice(i * SUB, (i + 1) * SUB)
        out_ref[rows, :] = mid_ref[rows, :] + second.total(i)
    first.finish()
    second.finish()
    gather.finish()


def ffn_forward(gated, w_out, residual, gain, w_down, w_up):
    size, width = residual.shape
    tokens = 4 * size
    return call(
        ffn_forward_kernel,
        (
            like(size, width),
            like(tokens, width, dtype=bf16),
            like(tokens, 1408, dtype=bf16),
            like(tokens, 768, dtype=bf16),
            like(size, width),
        ),
        (gated, w_out, residual, gain),
        [
            pltpu.VMEM((width, 1408), bf16),
            pltpu.VMEM((768, width), bf16),
            pltpu.SemaphoreType.DMA((11,)),
        ]
        + Scatter.scratch(size, width)
        + Scatter.scratch(size, width)
        + gather_sems(size),
        2,
        "ffn_forward",
        (w_down,) + tuple(w_up),
    )


def grad_place():
    rank = lax.axis_index("rep") % 8
    x = rank % 2
    y, c = place()

    def slot(r):
        return r % 2 + x - 2 * (r % 2) * x

    def target(d):
        dy, dc = d // 2, d % 2
        return 2 * (y + dy - 2 * y * dy) + c + dc - 2 * c * dc

    return slot, target


def store_columns(buf, value, row, base, slot):
    for r in range(8):
        buf[slot(r), r // 2, base + row : base + row + value.shape[0], :] = value[
            :, 128 * r : 128 * r + 128
        ].astype(bf16)


def store_rows(buf, value, d, base, slot):
    blocks = value.shape[1] // 128
    for r in range(8):
        for j in range(blocks):
            at = base + (d * blocks + j) * 32
            buf[slot(r), r // 2, at : at + 32, :] = value[
                32 * r : 32 * r + 32, 128 * j : 128 * j + 128
            ].astype(bf16)


DOWN_AT, OUT_AT, UP_AT, FFN_ROWS = 0, 704, 1216, 2624
SMALL_AT, IN_ROWS = 1536, 1552


def ffn_backward_kernel(
    dres_ref, up_ref, hidden_ref, normed_ref, mid_ref, gain_ref, gated_ref, wout_ref,
    down_ref, own_ref, sibling_ref, far_ref,
    dmid_ref, dgated_ref, ggain_ref, buf_ref,
    wup_ref, wdown_ref, loads, ddown_ref, dup_ref, dbranch_ref, *scratch,
):
    loaded = load_weight(own_ref, sibling_ref, far_ref, wup_ref, loads)
    loaded_down = load_down(down_ref, wdown_ref, loads.at[10])
    size = dres_ref.shape[0]
    count = size // SUB
    y, c = place()
    ready = greet(y, c)
    slot, target = grad_place()
    first = Gather(ddown_ref, *scratch[:2], size)
    second = Gather(dbranch_ref, *scratch[2:4], size)
    scatter = Scatter(*scratch[4:], size)
    for i in range(count):
        ddown_ref[first.own(i), :] = dres_ref[i * SUB : (i + 1) * SUB, :].astype(bf16)
        if i == 0:
            ready()
        first.start(i)

    def feed(rows):
        d_hidden = mm(ddown_ref[rows, :], wdown_ref[...], NT)
        d_up = swiglu_back(up_ref[rows, :].astype(f32), d_hidden).astype(bf16)
        dup_ref[rows, :] = d_up
        return mm(d_up, wup_ref[...], NT)

    loaded()
    loaded_down()
    for i in range(count):
        scatter.hold(1, i, feed(first.own(i)))
    for i in range(count):
        scatter.give(1, i, feed(first.sibling(i)))
    for i in range(count):
        near = first.across(i)
        scatter.hold(0, i, feed(near))
        scatter.give(0, i, feed(first.diagonal(i)))
        scatter.relay(i)
    for m in range(6):
        wide = 128 if m < 5 else 64
        value = mm(hidden_ref[:, 128 * m : 128 * m + 128], ddown_ref[...], TN)
        store_columns(buf_ref, value[:wide], 128 * m, DOWN_AT, slot)
    ggain_ref[...] = jnp.zeros_like(ggain_ref)
    for i in range(count):
        rows = slice(i * SUB, (i + 1) * SUB)
        d_norm, g_gain = normalise_back(mid_ref[rows, :], gain_ref[...], scatter.total(i))
        d_mid = dres_ref[rows, :] + d_norm
        dmid_ref[rows, :] = d_mid
        ggain_ref[0:1, :] += g_gain
        dbranch_ref[second.own(i), :] = d_mid.astype(bf16)
        second.start(i)
    for d in range(4):
        lanes = pl.ds(pl.multiple_of(target(d) * 256, 256), 256)
        value = mm(normed_ref[:, lanes], dup_ref[...], TN)
        store_rows(buf_ref, value, d, UP_AT, slot)
    for rows in in_order(second):
        dgated_ref[rows, :] = mm(dbranch_ref[rows, :], wout_ref[...], NT).astype(bf16)
    for m in range(4):
        value = mm(gated_ref[:, 128 * m : 128 * m + 128], dbranch_ref[...], TN)
        store_columns(buf_ref, value, 128 * m, OUT_AT, slot)
    first.finish()
    second.finish()
    scatter.finish()


def ffn_backward(d_res, up, hidden, normed, mid, gain, gated, w_out, w_down, w_up):
    size, width = d_res.shape
    tokens = 4 * size
    return call(
        ffn_backward_kernel,
        (
            like(size, width),
            like(tokens, 512, dtype=bf16),
            like(8, width),
            like(2, 4, FFN_ROWS, 128, dtype=bf16),
        ),
        (d_res, up, hidden, normed, mid, gain, gated, w_out),
        [
            pltpu.VMEM((width, 1408), bf16),
            pltpu.VMEM((768, width), bf16),
            pltpu.SemaphoreType.DMA((11,)),
            pltpu.VMEM((tokens, width), bf16),
            pltpu.VMEM((tokens, 1408), bf16),
            pltpu.VMEM((tokens, width), bf16),
        ]
        + gather_sems(size)
        + gather_sems(size)
        + Scatter.scratch(size, width),
        3,
        "ffn_backward",
        (w_down,) + tuple(w_up),
    )


def project_backward_kernel(
    dproj_ref, dsmall_ref, ab_ref, normed_ref, res_ref, gain_ref, dmid_ref,
    gtwo_ref, gtaps_ref, gheads_ref, own_ref, sibling_ref, far_ref,
    dres_ref, buf_ref,
    w_ref, loads, table, *scratch,
):
    loaded = load_weight(own_ref, sibling_ref, far_ref, w_ref, loads)
    size = res_ref.shape[0]
    count = size // SUB
    y, c = place()
    ready = greet(y, c)
    slot, target = grad_place()
    scatter = Scatter(*scratch, size)

    def back(rows):
        return mm(dproj_ref[rows, :], w_ref[...], NT) + mm(dsmall_ref[rows, :], ab_ref[...], NT)

    def weight_grad(d):
        lanes = pl.ds(pl.multiple_of(target(d) * 256, 256), 256)
        value = mm(normed_ref[:, lanes], dproj_ref[...], TN)
        store_rows(buf_ref, value, d, 0, slot)

    loaded()
    for part in range(2):
        yy = 1 - y if part == 0 else y
        for i in range(count):
            value = back(shard_rows(yy, 1 - c, i, size))
            if part == 0 and i == 0:
                ready()
            scatter.give(part, i, value)
            scatter.hold(part, i, back(shard_rows(yy, c, i, size)))
            if part == 0:
                scatter.relay(i)
    for d in range(4):
        weight_grad(d)
    ab_grad = mm(dsmall_ref[...], normed_ref[...], TN)
    table[...] = jnp.zeros_like(table)
    for k in range(8):
        lanes = slice(128 * k, 128 * k + 128)
        for j in range(4):
            table[8 * j + k : 8 * j + k + 1, :] = gtaps_ref[j : j + 1, lanes]
            table[32 + 8 * j + k : 33 + 8 * j + k, :] = ab_grad[j : j + 1, lanes]
        table[72 + k : 73 + k, :] = gtwo_ref[0:1, lanes]
    table[80:81, :] = gheads_ref[0:1, 0:128]
    table[81:82, :] = gheads_ref[0:1, 128:256]
    table[82:83, :] = gheads_ref[1:2, 0:128]
    table[83:84, :] = gheads_ref[2:3, 0:128]
    gain_sum = jnp.zeros((1, res_ref.shape[1]), f32)
    for i in range(count):
        rows = slice(i * SUB, (i + 1) * SUB)
        d_norm, g_gain = normalise_back(res_ref[rows, :], gain_ref[...], scatter.total(i))
        dres_ref[rows, :] = dmid_ref[rows, :] + d_norm
        gain_sum = gain_sum + g_gain
    for k in range(8):
        table[64 + k : 65 + k, :] = gain_sum[:, 128 * k : 128 * k + 128]
    for r in range(8):
        buf_ref[slot(r), r // 2, SMALL_AT:IN_ROWS, :] = table[16 * r : 16 * r + 16, :].astype(bf16)
    scatter.finish()


def project_backward(d_proj, d_small, weight, ab, normed, residual, gain, d_mid, g_two, g_taps, g_heads):
    size, width = residual.shape
    return call(
        project_backward_kernel,
        (like(size, width), like(2, 4, IN_ROWS, 128, dtype=bf16)),
        (d_proj, d_small, ab, normed, residual, gain, d_mid, g_two, g_taps, g_heads),
        [
            pltpu.VMEM((width, 1536), bf16),
            pltpu.SemaphoreType.DMA((10,)),
            pltpu.VMEM((128, 128), f32),
        ]
        + Scatter.scratch(size, width),
        4 if len(weight[2].shape) == 4 else 7,
        "project_backward",
        weight,
    )


def collect(final_ref, pieces, sems):
    copy = pltpu.make_async_copy(final_ref, pieces, sems.at[0])
    copy.start()
    copy.wait()


def offset_of(s):
    y, c = place()
    sy, sc = s // 2, s % 2
    return 2 * (y + sy - 2 * y * sy) + c + sc - 2 * c * sc


def assemble_ffn_kernel(layer, earlier, final_ref, *refs):
    down_ref, out_ref, up_ref, pieces, down, out, up, sems = refs[earlier:]
    collect(final_ref, pieces, sems)
    stores = [
        pltpu.make_async_copy(down, down_ref.at[layer], sems.at[8]),
        pltpu.make_async_copy(out, out_ref.at[layer], sems.at[9]),
        pltpu.make_async_copy(up, up_ref.at[layer], sems.at[10]),
    ]
    for r in range(8):
        lanes = slice(128 * r, 128 * r + 128)
        down[:, lanes] = pieces[r, DOWN_AT:OUT_AT, :].astype(f32)
    stores[0].start()
    for r in range(8):
        lanes = slice(128 * r, 128 * r + 128)
        out[:, lanes] = pieces[r, OUT_AT:UP_AT, :].astype(f32)
    stores[1].start()
    left = grid_of((32, 128), 1) < 64

    def turn(tile):
        return pltpu.roll(tile, 64, 1)

    def body(r, carry):
        rows = pl.ds(pl.multiple_of(32 * r, 32), 32)
        for m in range(2):
            tiles = []
            for s in (2 * m, 2 * m + 1):
                at = UP_AT + offset_of(s) * 352
                tiles.append(
                    [
                        pieces[r, pl.ds(pl.multiple_of(at + 32 * j, 32), 32), :].astype(f32)
                        for j in range(11)
                    ]
                )
            for side in range(2):
                even = tiles[0][5 * side : 5 * side + 5]
                odd = [turn(tile) for tile in tiles[1][5 * side : 5 * side + 5]]
                even_tail = tiles[0][10] if side == 0 else turn(tiles[0][10])
                odd_tail = turn(tiles[1][10]) if side == 0 else tiles[1][10]
                row = even + [jnp.where(left, even_tail, odd[0])]
                row += [jnp.where(left, odd[j - 1], odd[j]) for j in range(1, 5)]
                row += [jnp.where(left, odd[4], odd_tail)]
                base = FF * side + 1408 * m
                for j, tile in enumerate(row):
                    up[rows, base + 128 * j : base + 128 * j + 128] = tile
        return carry

    lax.fori_loop(0, 8, body, 0)
    stores[2].start()
    for store in stores:
        store.wait()


def assemble_in_kernel(layer, earlier, final_ref, *refs):
    in_ref, table_ref, pieces, whole, sems = refs[earlier:]
    collect(final_ref, pieces, sems)
    store = pltpu.make_async_copy(whole, in_ref.at[layer], sems.at[8])

    def body(r, carry):
        rows = pl.ds(pl.multiple_of(32 * r, 32), 32)
        for s in range(4):
            at = offset_of(s) * 384
            for j in range(12):
                if j < 2:
                    column = 256 * s + 128 * j
                elif j < 4:
                    column = HK + 256 * s + 128 * (j - 2)
                elif j < 8:
                    column = 2 * HK + 512 * s + 128 * (j - 4)
                else:
                    column = CH + 512 * s + 128 * (j - 8)
                tile = pieces[r, pl.ds(pl.multiple_of(at + 32 * j, 32), 32), :]
                whole[rows, column : column + 128] = tile.astype(f32)
        return carry

    lax.fori_loop(0, 8, body, 0)
    store.start()
    for r in range(8):
        table_ref[16 * r : 16 * r + 16, :] = pieces[r, SMALL_AT:IN_ROWS, :].astype(f32)
    store.wait()


def assemble(kernel, layer, final, earlier, shapes, table, scratch, name):
    spot = pl.BlockSpec(memory_space=pl.ANY)
    out_shape = tuple(like(LAYERS, *shape) for shape in shapes)
    out_specs = (spot,) * len(shapes)
    if table:
        out_shape += (like(128, 128),)
        out_specs += (pl.BlockSpec(memory_space=pltpu.VMEM),)
    return pl.pallas_call(
        partial(kernel, layer, len(earlier)),
        out_shape=out_shape,
        in_specs=[spot] * (1 + len(earlier)),
        out_specs=out_specs,
        scratch_shapes=[pltpu.VMEM(final.shape, bf16)]
        + [pltpu.VMEM(shape, f32) for shape in scratch]
        + [pltpu.SemaphoreType.DMA((11,))],
        input_output_aliases={1 + k: k for k in range(len(earlier))},
        compiler_params=pltpu.CompilerParams(vmem_limit_bytes=LIMIT),
        name=name,
    )(final, *earlier)


def assemble_ffn(layer, final, earlier):
    shapes = [(704, 1024), (512, 1024), (256, 2 * FF)]
    return assemble(
        assemble_ffn_kernel, layer, final, earlier, shapes, False, shapes, "assemble_ffn"
    )


def assemble_in(layer, final, earlier):
    shapes = [(256, CH + HV)]
    return assemble(
        assemble_in_kernel, layer, final, earlier, shapes, True, shapes, "assemble_in"
    )


FFN_MOVE, IN_MOVE = (UP_AT, 352), (0, 384)


def add_into(dst, left, right):
    dst[...] = (left[...].astype(f32) + right[...].astype(f32)).astype(bf16)


class Group:
    def __init__(self, number, piece, moved, final, move, sems):
        self.number, self.piece, self.moved, self.final = number, piece, moved, final
        self.at, self.part = move
        self.send, self.recv, self.local = sems
        rank = lax.axis_index("rep")
        self.rank, self.x, self.z = rank, rank % 2, (rank % 8) // 2
        self.y, self.c = place()

    def swap(self, d):
        dy, dc = d // 2, d % 2
        target = 2 * (self.y + dy - 2 * self.y * dy) + self.c + dc - 2 * self.c * dc
        rows = pl.ds(self.at + d * self.part, self.part)
        return pltpu.make_async_remote_copy(
            src_ref=self.piece.at[rows], dst_ref=self.moved.at[rows],
            send_sem=self.send.at[self.number, d], recv_sem=self.recv.at[self.number, d],
            device_id={"grp": target}, device_id_type=MESH,
        )

    def start_swap(self):
        for d in range(1, 4):
            self.swap(d).start()
        first = self.at + self.part
        self.moved[0:first, :] = self.piece[0:first, :]
        rest = self.at + 4 * self.part
        if rest < self.piece.shape[0]:
            self.moved[rest:, :] = self.piece[rest:, :]

    def wait_swap(self):
        for d in range(1, 4):
            self.swap(d).wait_recv()

    def move(self, step, source_z, kind):
        owner = 2 * source_z + self.x
        src = self.moved if step == 0 else self.final.at[owner]
        side = 4 * kind if kind < 2 else 8
        slot = side + (abs(step) if kind < 2 else step + 3)
        target = (self.rank + 2, self.rank - 2, self.rank + 1 - 2 * self.x)[kind]
        return pltpu.make_async_remote_copy(
            src_ref=src, dst_ref=self.final.at[owner],
            send_sem=self.send.at[self.number, 4 + slot],
            recv_sem=self.recv.at[self.number, 4 + (slot if kind < 2 else 8)],
            device_id={"rep": target}, device_id_type=MESH,
        )

    def x_move(self, step, source_z):
        owner = 2 * source_z + self.x
        src = self.moved if step == 0 else self.final.at[owner]
        return pltpu.make_async_remote_copy(
            src_ref=src, dst_ref=self.final.at[owner],
            send_sem=self.send.at[self.number, 12 + step + 3],
            recv_sem=self.recv.at[self.number, 12 + source_z],
            device_id={"rep": self.rank + 1 - 2 * self.x}, device_id_type=MESH,
        )

    def own_copy(self):
        return pltpu.make_async_copy(
            self.moved, self.final.at[2 * self.z + self.x], self.local.at[self.number]
        )

    def begin(self):
        self.x_move(0, self.z).start()

        @pl.when(self.z < 3)
        def _():
            self.move(0, self.z, 0).start()

        @pl.when(self.z > 0)
        def _():
            self.move(0, self.z, 1).start()

        self.own_copy().start()

    def forward(self, k, act):
        z = self.z

        @pl.when(z >= k)
        def _():
            source = z - k
            act(self, k, source, 0)

            @pl.when(z < 3)
            def _():
                act(self, k, source, 2)

        @pl.when(z + k <= 3)
        def _():
            source = z + k
            act(self, -k, source, 1)

            @pl.when(z > 0)
            def _():
                act(self, -k, source, 3)

    def relay(self, k):
        def act(self, step, source, what):
            if what == 0:
                self.move(step - 1, source, 0).wait_recv()
                self.x_move(step, source).start()
            elif what == 1:
                self.move(step + 1, source, 1).wait_recv()
                self.x_move(step, source).start()
            elif what == 2:
                self.move(step, source, 0).start()
            else:
                self.move(step, source, 1).start()

        self.forward(k, act)

    def finish(self):
        def act(self, step, source, what):
            if what < 2:
                self.x_move(step, source).wait_send()
            elif what == 2:
                self.move(step, source, 0).wait_send()
            else:
                self.move(step, source, 1).wait_send()

        for k in range(1, 4):
            self.forward(k, act)
        self.x_move(0, self.z).wait_send()

        @pl.when(self.z < 3)
        def _():
            self.move(0, self.z, 0).wait_send()

        @pl.when(self.z > 0)
        def _():
            self.move(0, self.z, 1).wait_send()

        for source in range(4):
            self.x_move(0, source).wait_recv()
        self.own_copy().wait()
        for d in range(1, 4):
            self.swap(d).wait_send()


class Line:
    def __init__(self, values, right, left, send, recv):
        self.values, self.right, self.left = values, right, left
        self.send, self.recv = send, recv
        self.rank = lax.axis_index("rep")
        self.z = (self.rank % 8) // 2

    def go(self, o, toward):
        land = self.right if toward == 0 else self.left
        return pltpu.make_async_remote_copy(
            src_ref=self.values.at[o], dst_ref=land.at[o],
            send_sem=self.send.at[toward, o], recv_sem=self.recv.at[toward, o],
            device_id={"rep": self.rank + 2 - 4 * toward}, device_id_type=MESH,
        )

    def edges(self):
        @pl.when(self.z == 0)
        def _():
            for o in (3, 2, 1):
                self.go(o, 0).start()

        @pl.when(self.z == 3)
        def _():
            for o in (0, 1, 2):
                self.go(o, 1).start()

    def inner(self):
        z = self.z
        for o in (3, 2):

            @pl.when((z > 0) & (z < o))
            def _():
                self.go(o, 0).wait_recv()
                add_into(self.values.at[o], self.values.at[o], self.right.at[o])
                self.go(o, 0).start()

            @pl.when((z < 3) & (z > 3 - o))
            def _():
                self.go(3 - o, 1).wait_recv()
                add_into(self.values.at[3 - o], self.values.at[3 - o], self.left.at[3 - o])
                self.go(3 - o, 1).start()

    def total(self, out):
        z = self.z
        for o in range(4):

            @pl.when(z == o)
            def _():
                value = self.values[o].astype(f32)
                if o > 0:
                    self.go(o, 0).wait_recv()
                    value = value + self.right[o].astype(f32)
                if o < 3:
                    self.go(o, 1).wait_recv()
                    value = value + self.left[o].astype(f32)
                out[...] = value.astype(bf16)

    def finish(self):
        for o in range(4):

            @pl.when(self.z < o)
            def _():
                self.go(o, 0).wait_send()

            @pl.when(self.z > o)
            def _():
                self.go(o, 1).wait_send()


def finish_kernel(
    p1, p2, s3, b4, f1, f2, f3, f4,
    q1, q2, q3, q4, e1, e2, e3, e4, v3, r3, l3, v4, x4, r4, l4,
    send, recv, local, send3, recv3, send4, recv4, send5, recv5, loads,
):
    rank = lax.axis_index("rep")
    x, z = rank % 2, (rank % 8) // 2
    y, c = place()
    loaded = [
        pltpu.make_async_copy(p1, q1, loads.at[0]),
        pltpu.make_async_copy(p2, q2, loads.at[1]),
        pltpu.make_async_copy(s3, v3, loads.at[2]),
        pltpu.make_async_copy(b4.at[0], v4, loads.at[3]),
    ]
    for load in loaded:
        load.start()
    barrier = pltpu.get_barrier_semaphore()
    pl.semaphore_signal(
        barrier, inc=1, device_id={"rep": rank + 1 - 2 * x}, device_id_type=MESH
    )
    for d in range(1, 4):
        dy, dc = d // 2, d % 2
        target = 2 * (y + dy - 2 * y * dy) + c + dc - 2 * c * dc
        pl.semaphore_signal(barrier, inc=1, device_id={"grp": target}, device_id_type=MESH)

    @pl.when(z > 0)
    def _():
        pl.semaphore_signal(barrier, inc=1, device_id={"rep": rank - 2}, device_id_type=MESH)

    @pl.when(z < 3)
    def _():
        pl.semaphore_signal(barrier, inc=1, device_id={"rep": rank + 2}, device_id_type=MESH)

    @pl.when((z > 0) & (z < 3))
    def _():
        pl.semaphore_wait(barrier, 6)

    @pl.when((z == 0) | (z == 3))
    def _():
        pl.semaphore_wait(barrier, 5)

    def halves(o):
        return pltpu.make_async_remote_copy(
            src_ref=b4.at[1, o], dst_ref=x4.at[o], send_sem=send5.at[o], recv_sem=recv5.at[o],
            device_id={"rep": rank + 1 - 2 * x}, device_id_type=MESH,
        )

    for o in (3, 0, 2, 1):
        halves(o).start()
    sems = (send, recv, local)
    g1 = Group(0, q1, e1, f1, FFN_MOVE, sems)
    g2 = Group(1, q2, e2, f2, IN_MOVE, sems)
    g3 = Group(2, q3, e3, f3, FFN_MOVE, sems)
    g4 = Group(3, q4, e4, f4, IN_MOVE, sems)
    line3 = Line(v3, r3, l3, send3, recv3)
    line4 = Line(v4, r4, l4, send4, recv4)
    loaded[0].wait()
    g1.start_swap()
    loaded[1].wait()
    g2.start_swap()
    loaded[2].wait()
    line3.edges()
    g1.wait_swap()
    g1.begin()
    g2.wait_swap()
    g2.begin()
    line3.inner()
    loaded[3].wait()
    for o in (3, 0, 2, 1):
        halves(o).wait_recv()
        add_into(v4.at[o], v4.at[o], x4.at[o])
    line4.edges()
    line3.total(q3)
    g3.start_swap()
    g1.relay(1)
    g3.wait_swap()
    g3.begin()
    line4.inner()
    g2.relay(1)
    line4.total(q4)
    g4.start_swap()
    g1.relay(2)
    g4.wait_swap()
    g4.begin()
    g2.relay(2)
    g3.relay(1)
    g1.relay(3)
    g4.relay(1)
    g2.relay(3)
    g3.relay(2)
    g4.relay(2)
    g3.relay(3)
    g4.relay(3)
    for group in (g1, g2, g3, g4):
        group.finish()
    line3.finish()
    line4.finish()
    for o in range(4):
        halves(o).wait_send()


def finish_reduction(p1, p2, s3, b4):
    spot = pl.BlockSpec(memory_space=pl.ANY)
    big, small = p1.shape, p2.shape
    dma = pltpu.SemaphoreType.DMA
    return pl.pallas_call(
        finish_kernel,
        out_shape=tuple(like(8, *shape, dtype=bf16) for shape in (big, small, big, small)),
        in_specs=[spot] * 4,
        out_specs=(spot,) * 4,
        scratch_shapes=[
            pltpu.VMEM(shape, bf16)
            for shape in [big, small] * 4
            + [(4,) + big] * 3
            + [(4,) + small] * 4
        ]
        + [dma((4, 20)), dma((4, 20)), dma((4,))]
        + [dma((2, 4))] * 4
        + [dma((4,)), dma((4,)), dma((4,))],
        compiler_params=pltpu.CompilerParams(
            collective_id=5, has_side_effects=True, vmem_limit_bytes=LIMIT
        ),
        cost_estimate=pl.CostEstimate(flops=1000, bytes_accessed=1000, transcendentals=0),
        name="finish_reduction",
    )(p1, p2, s3, b4)


def swap_route(bit, count):
    return [(i, i ^ bit) for i in range(count)]


def planes_of(replicas):
    return [
        [8 * b + 2 * z + x for z in range(4)] for b in range(replicas // 8) for x in range(2)
    ]


def swap_x(array, replicas):
    return lax.ppermute(array, "rep", swap_route(1, replicas))


def add_arrived(kept, arrived):
    return (kept.astype(f32) + arrived.astype(f32)).astype(bf16)


def reduce_z(summed, replicas):
    piece = lax.psum_scatter(
        summed, "rep", scatter_dimension=0, tiled=False, axis_index_groups=planes_of(replicas)
    )
    blocks = replicas // 8
    if blocks > 1:
        piece = lax.psum(
            piece, "rep", axis_index_groups=[[8 * b + r for b in range(blocks)] for r in range(8)]
        )
    return piece


def exchange(piece, at, part):
    moved = [piece[: at + part]]
    for d in range(1, 4):
        moved.append(
            lax.ppermute(piece[at + d * part : at + (d + 1) * part], "grp", swap_route(d, 4))
        )
    moved.append(piece[at + 4 * part :])
    return jnp.concatenate(moved, axis=0)


def gather_z(piece, replicas):
    return lax.all_gather(piece, "rep", axis=0, axis_index_groups=planes_of(replicas))


def spread(piece, replicas):
    owned = gather_z(piece, replicas)
    other = swap_x(owned, replicas)
    odd = lax.axis_index("rep") % 2 == 1
    pair = jnp.stack([jnp.where(odd, other, owned), jnp.where(odd, owned, other)], axis=1)
    return pair.reshape((8,) + piece.shape)


def finish_all(piece1, piece2, summed3, buf4, replicas):
    if replicas == 8:
        return finish_reduction(piece1, piece2, summed3, buf4)
    piece3 = reduce_z(summed3, replicas)
    piece4 = reduce_z(add_arrived(buf4[0], swap_x(buf4[1], replicas)), replicas)
    return [
        spread(exchange(piece, *move), replicas)
        for piece, move in (
            (piece1, FFN_MOVE), (piece2, IN_MOVE), (piece3, FFN_MOVE), (piece4, IN_MOVE)
        )
    ]


def tie(*values):
    return lax.optimization_barrier(values)


def by_source(blocks, mine):
    y, c = mine // 2 == 1, mine % 2 == 1
    blocks = jnp.where(c, jnp.stack([blocks[k ^ 1] for k in range(4)]), blocks)
    return jnp.where(y, jnp.stack([blocks[k ^ 2] for k in range(4)]), blocks)


def swap(array, d):
    return lax.ppermute(array, "grp", swap_route(d, 4))


def reshard_near(pieces_of, mine):
    pieces = [pieces_of(mine ^ d, 0, None) for d in range(4)]
    return pieces[0], swap(pieces[1], 1), jnp.stack([swap(pieces[2], 2), swap(pieces[3], 3)])


def reshard_wide(pieces_of, mine, replicas):
    z = (lax.axis_index("rep") % 8) // 2
    own, sibling = pieces_of(mine, 0, None), swap(pieces_of(mine ^ 1, 0, None), 1)
    part = own.shape[0] // 4
    far = [swap(pieces_of(mine ^ d, part * z, part), d) for d in (2, 3)]
    far = lax.all_gather(jnp.stack(far), "rep", axis=0, axis_index_groups=planes_of(replicas))
    return own, sibling, far


def per_device(
    x_input, norm_gain, w_in, w_ab, conv_w, a_log, dt_bias, out_gain, w_out, ffn_in, ffn_out,
    cotangent,
):
    parts = lax.axis_size("grp")
    replicas = lax.axis_size("rep")
    mine = lax.axis_index("grp")
    rows, width = x_input.shape[1], x_input.shape[2]
    shard = w_in.shape[1]

    def cut(array, start, size):
        return lax.dynamic_slice_in_dim(array, start, size, array.ndim - 1)

    small_sizes = [part.size for part in (norm_gain, conv_w, out_gain, w_ab)]
    packed = jnp.concatenate(
        [part.reshape(-1) for part in (norm_gain, conv_w, out_gain, w_ab)]
    )
    packed = jnp.stack([packed] + [swap(packed, d) for d in range(1, 4)])
    packed = by_source(packed, mine)
    at = [sum(small_sizes[:k]) for k in range(5)]

    def unpack(k, shape, dim):
        part = packed[:, at[k] : at[k + 1]].reshape((parts,) + shape)
        part = jnp.moveaxis(part, 0, dim)
        return part.reshape(shape[:dim] + (parts * shape[dim],) + shape[dim + 1 :])

    gains = unpack(0, norm_gain.shape, 2).astype(f32)
    taps_all = unpack(1, conv_w.shape, 2).astype(f32)
    out_gains = unpack(2, out_gain.shape, 1).astype(f32)
    ab_all = unpack(3, w_ab.shape, 1)

    def in_pieces(l):
        def piece(t, start, count):
            rows = w_in[l] if count is None else lax.dynamic_slice_in_dim(w_in[l], start, count, 0)
            return jnp.concatenate(
                [
                    cut(rows, 256 * t, 256),
                    cut(rows, HK + 256 * t, 256),
                    cut(rows, 2 * HK + 512 * t, 512),
                    cut(rows, CH + 512 * t, 512),
                ],
                axis=1,
            )

        return piece

    def up_pieces(l):
        def piece(t, start, count):
            rows = ffn_in[l]
            if count is not None:
                rows = lax.dynamic_slice_in_dim(rows, start, count, 0)
            gate = cut(rows, 704 * t, 704)
            value = cut(rows, FF + 704 * t, 704)
            return jnp.concatenate(
                [gate[:, :640], value[:, :640], gate[:, 640:], value[:, 640:]], axis=1
            )

        return piece

    small_weights = []
    for l in range(LAYERS):
        ab = jnp.concatenate([cut(ab_all[l], 2 * mine, 2), cut(ab_all[l], H + 2 * mine, 2)], axis=1)
        ab = jnp.pad(ab, ((0, 0), (0, 124)))
        taps = jnp.concatenate(
            [
                cut(taps_all[l], 256 * mine, 256),
                cut(taps_all[l], HK + 256 * mine, 256),
                cut(taps_all[l], 2 * HK + 512 * mine, 512),
            ],
            axis=1,
        )
        taps = jnp.pad(taps, ((0, 4), (0, 0)))
        heads = jnp.pad(jnp.stack([a_log[l], dt_bias[l]]).astype(f32), ((0, 6), (2, 124)))
        gain = jnp.pad(out_gains[l][None], ((0, 7), (0, 0)))
        small_weights.append((gains[l, 0:1], gains[l, 1:2], ab, taps, heads, gain, w_out[l], ffn_out[l]))

    residual = x_input[0].astype(f32)
    kept = []
    in_weights = [reshard_near(in_pieces(0), mine)]
    up_weights = [reshard_wide(up_pieces(0), mine, replicas)]
    in_weights.append(reshard_wide(in_pieces(1), mine, replicas))
    up_weights.append(reshard_wide(up_pieces(1), mine, replicas))
    for l in range(LAYERS):
        gain_one, gain_two, ab, taps, heads, gain, out_weight, down_weight = small_weights[l]
        normed, projected, small = project(residual, gain_one, in_weights[l], ab)
        gated, *saved = mixer_forward(projected, small, taps, heads, gain)
        mid, normed_two, up, hidden, residual_out = ffn_forward(
            gated, out_weight, residual, gain_two, down_weight, up_weights[l]
        )
        kept.append((residual, normed, projected, small, gated, saved, mid, normed_two, up, hidden))
        residual = residual_out
    block_output = residual.astype(bf16)[None]

    d_residual = cotangent[0].astype(f32)

    def ffn_part(l, d_residual):
        gain_one, gain_two, ab, taps, heads, gain, out_weight, down_weight = small_weights[l]
        residual, normed, projected, small, gated, saved, mid, normed_two, up, hidden = kept[l]
        return ffn_backward(
            d_residual, up, hidden, normed_two, mid, gain_two, gated, out_weight, down_weight,
            up_weights[l],
        )

    def mixer_part(l, d_gated):
        gain_one, gain_two, ab, taps, heads, gain, out_weight, down_weight = small_weights[l]
        residual, normed, projected, small, gated, saved, mid, normed_two, up, hidden = kept[l]
        return mixer_backward(projected, small, taps, heads, gain, saved, d_gated)

    def project_part(l, d_mid, g_gain_two, mixed):
        gain_one, gain_two, ab, taps, heads, gain, out_weight, down_weight = small_weights[l]
        residual, normed, projected, small, gated, saved, mid, normed_two, up, hidden = kept[l]
        d_projected, d_small, g_taps, g_heads = mixed
        return project_backward(
            d_projected, d_small, in_weights[l], ab, normed, residual, gain_one, d_mid,
            g_gain_two, g_taps, g_heads,
        )

    d_mid, d_gated, g_gain_two, buf1 = ffn_part(1, d_residual)
    arrived1 = swap_x(buf1[1], replicas)
    mixed = mixer_part(1, d_gated)
    d_residual, buf2 = project_part(1, d_mid, g_gain_two, mixed)
    d_residual, arrived1 = tie(d_residual, arrived1)
    piece1 = reduce_z(add_arrived(buf1[0], arrived1), replicas)
    arrived2 = swap_x(buf2[1], replicas)
    d_mid, d_gated, g_gain_two, buf3 = ffn_part(0, d_residual)
    d_gated, piece1, arrived2 = tie(d_gated, piece1, arrived2)
    piece2 = reduce_z(add_arrived(buf2[0], arrived2), replicas)
    arrived3 = swap_x(buf3[1], replicas)
    mixed = mixer_part(0, d_gated)
    d_residual, buf4 = project_part(0, d_mid, g_gain_two, mixed)
    d_residual, arrived3 = tie(d_residual, arrived3)
    summed3 = add_arrived(buf3[0], arrived3)
    final1, final2, final3, final4 = finish_all(piece1, piece2, summed3, buf4, replicas)
    ffn_grads = assemble_ffn(1, final1, ())
    *in_grads, table_one = assemble_in(1, final2, ())
    down_grads, out_grads, up_grads = assemble_ffn(0, final3, tuple(ffn_grads))
    w_in_grads, table_zero = assemble_in(0, final4, tuple(in_grads))
    input_grad = d_residual.astype(bf16)[None]

    tables = jnp.stack([table_zero, table_one])
    everyone = lax.all_gather(tables, "grp", axis=0)
    sums = jnp.sum(everyone[:, :, 64:82], axis=0)
    grad_gain = lax.dynamic_slice_in_dim(
        sums[:, :16].reshape(LAYERS, 2, width), mine * shard, shard, 2
    )
    grad_out_gain = lax.dynamic_slice_in_dim(
        sums[:, 16:18].reshape(LAYERS, DV), mine * (DV // 4), DV // 4, 1
    )
    grad_a_log = tables[:, 82, 2:4]
    grad_dt = tables[:, 83, 2:4]
    taps_sum = everyone[:, :, 0:32].reshape(4, LAYERS, 4, 1024)

    def side_by_side(array):
        return jnp.moveaxis(array, 0, 2).reshape(LAYERS, 4, -1)

    conv_full = jnp.concatenate(
        [
            side_by_side(taps_sum[..., :256]),
            side_by_side(taps_sum[..., 256:512]),
            side_by_side(taps_sum[..., 512:]),
        ],
        axis=2,
    )
    grad_conv = lax.dynamic_slice_in_dim(conv_full, mine * 1024, 1024, 2)
    ab_sum = everyone[:, :, 32:64].reshape(4, LAYERS, 4, width)
    ab_sum = lax.dynamic_slice_in_dim(ab_sum, mine * shard, shard, 3)
    grad_ab = jnp.transpose(ab_sum.reshape(4, LAYERS, 2, 2, shard), (1, 4, 2, 0, 3)).reshape(
        LAYERS, shard, 2 * H
    )
    return (
        block_output,
        input_grad,
        grad_gain,
        w_in_grads,
        grad_ab,
        grad_conv,
        grad_a_log,
        grad_dt,
        grad_out_gain,
        out_grads,
        up_grads,
        down_grads,
    )


def solution(mesh):
    rows = P("rep", "grp", None)
    first = P(None, "grp")
    middle = P(None, "grp", None)
    last = P(None, None, "grp")
    in_specs = (rows, last, middle, middle, last, first, first, first, middle, middle, middle, rows)
    out_specs = (rows, rows, last, middle, middle, last, first, first, first, middle, middle, middle)
    return jax.shard_map(
        per_device, mesh=mesh, in_specs=in_specs, out_specs=out_specs, check_vma=False
    )
```

```python
from functools import partial
import math

import jax
import jax.numpy as jnp
from jax import lax
from jax.sharding import PartitionSpec as P
from jax.experimental import pallas as pl
from jax.experimental.pallas import tpu as pltpu

H = 8
DK = 128
DV = 256
FF = 2816
CONV = 4
LAYERS = 2
HK = 1024
HV = 2048
CH = 4096
CHUNK = 128

f32 = jnp.float32
bf16 = jnp.bfloat16
HIGH = lax.Precision.HIGHEST
epsilon = 1e-06
out_floor = 0.02
NN = ((1,), (0,))
NT = ((1,), (1,))
TN = ((0,), (0,))


def mm(left, right, dims=NN, precision=None):
    return lax.dot_general(
        left, right, (dims, ((), ())), precision=precision, preferred_element_type=f32
    )


def mh(left, right, dims=NN):
    return mm(left, right, dims, HIGH)


def grid_of(shape, dim):
    return lax.broadcasted_iota(jnp.int32, shape, dim)


def conv_chunk(x_ext, taps):
    return sum(x_ext[5 + j : 5 + j + CHUNK] * taps[j : j + 1] for j in range(CONV))


def decay_chunk(small, heads_ref):
    lane = grid_of(small.shape, 1)
    strength = jax.nn.sigmoid(small)
    shifted_logit = small + heads_ref[1:2, :]
    soft = jnp.maximum(shifted_logit, 0.0) + jnp.log1p(jnp.exp(-jnp.abs(shifted_logit)))
    log_decay = -jnp.exp(heads_ref[0:1, :]) * soft
    row = grid_of((CHUNK, CHUNK), 0)
    col = grid_of((CHUNK, CHUNK), 1)
    lower_ones = jnp.where(row >= col, 1.0, 0.0).astype(f32)
    cumulative = mm2(lower_ones.astype(bf16), log_decay)
    turned = jnp.where(lane < 2, strength, cumulative).T
    return strength, shifted_logit, log_decay, cumulative, turned


def head_inputs(activated, h):
    qa = activated[:, 128 * h : 128 * h + 128]
    ka = activated[:, 256 + 128 * h : 384 + 128 * h]
    va = activated[:, 512 + 256 * h : 768 + 256 * h]
    q_norm = lax.rsqrt(jnp.sum(qa * qa, axis=-1, keepdims=True) + epsilon)
    k_norm = lax.rsqrt(jnp.sum(ka * ka, axis=-1, keepdims=True) + epsilon)
    q = (qa * q_norm * (1.0 / math.sqrt(DK))).astype(bf16)
    k = (ka * k_norm).astype(bf16)
    return qa, ka, q_norm, k_norm, q, k, va.astype(bf16)


def split(x):
    high = x.astype(bf16)
    return high, (x - high.astype(f32)).astype(bf16)


def mm2(exact, right, dims=NN):
    high, low = split(right)
    return mm(exact, high, dims) + mm(exact, low, dims)


def mm3(left, right, dims=NN):
    lh, ll = split(left)
    rh, rl = split(right)
    return mm(lh, rh, dims) + (mm(lh, rl, dims) + mm(ll, rh, dims))


def mb(left, right, dims=NN):
    return mm(left.astype(bf16), right.astype(bf16), dims)


def unit_inverse(system):
    size = system.shape[0]
    row = grid_of((size, size), 0)
    col = grid_of((size, size), 1)
    eye = jnp.where(row == col, 1.0, 0.0).astype(f32)
    powers = jnp.where((row >> 2) == (col >> 2), -system, 0.0)
    square = mb(powers, powers)
    total = eye + powers
    total = total + mb(total, square)
    for bits in (2, 3, 4, 5, 6):
        joint = ((row >> (bits + 1)) == (col >> (bits + 1))) & ((row >> bits) != (col >> bits))
        link = jnp.where(joint, system, 0.0)
        total = total - mb(total, mb(link, total))
    return total


UNROLL = 2


def mixer_forward_kernel(
    layer, proj_ref, small_ref, taps_ref, heads_ref, gain_ref, *refs
):
    if layer == 0:
        up_source, in_source, *refs = refs
        *outs, up_whole, near, far = refs[:8]
        halo, state, *sems = refs[8:]
    else:
        up_source, *refs = refs
        *outs, up_whole = refs[:6]
        halo, state, *sems = refs[6:]
    gated_ref, start_ref, inv_ref, pseudo_ref, mixed_ref = outs
    ready = greet_wide(*place())
    shard = Reshard(up_source.at[layer], up_lanes, up_whole, *sems[:5])
    if layer == 0:
        quarter = Quarter(in_source.at[1], in_lanes, near, far, *sems[5:])
    ready()
    shard.start_far(0)
    shard.start_near()
    halo[...] = jnp.zeros_like(halo)
    state[...] = jnp.zeros_like(state)
    row = grid_of((CHUNK, CHUNK), 0)
    col = grid_of((CHUNK, CHUNK), 1)
    zero = jnp.zeros((CHUNK, CHUNK), f32)

    def prepare(c):
        rows = pl.ds(pl.multiple_of(c * CHUNK, CHUNK), CHUNK)
        x = proj_ref[rows, 0:1024].astype(f32)
        x_ext = jnp.concatenate([halo[...], x], axis=0)
        halo[...] = x[CHUNK - 8 :]
        convolved = conv_chunk(x_ext, taps_ref[...])
        activated = convolved * jax.nn.sigmoid(convolved)
        strength, shifted_logit, log_decay, cumulative, turned = decay_chunk(
            small_ref[rows, :], heads_ref
        )
        parts = []
        systems = []
        for h in range(2):
            qa, ka, q_norm, k_norm, q, k, v = head_inputs(activated, h)
            c_col = cumulative[:, 2 + h : 3 + h]
            c_row = turned[2 + h : 3 + h, :]
            beta_row = turned[h : h + 1, :]
            ratio = jnp.exp(jnp.where(row >= col, c_col - c_row, -1e4)) * beta_row
            systems.append(jnp.where(row > col, ratio * mm(k, k, NT), 0.0))
            mixing = (ratio * mm(q, k, NT)).astype(bf16)
            parts.append((q, k, v, c_col, mixing, strength[:, h : h + 1]))
        joint = jnp.concatenate(
            [
                jnp.concatenate([systems[0], zero], axis=1),
                jnp.concatenate([zero, systems[1]], axis=1),
            ],
            axis=0,
        )
        return parts, unit_inverse(joint)

    def advance(c, parts, inverse):
        rows = pl.ds(pl.multiple_of(c * CHUNK, CHUNK), CHUNK)
        for h in range(2):
            q, k, v, c_col, mixing, beta_col = parts[h]
            inv = inverse[128 * h : 128 * h + 128, 128 * h : 128 * h + 128]
            growth = jnp.exp(c_col)
            last = c_col[CHUNK - 1 :, :]
            before = state[h]
            start_ref[c, h] = before
            inv_ref[c, h] = inv
            read = mm2(jnp.concatenate([q, k], axis=0), before)
            pseudo = mb(inv, v.astype(f32) - growth * read[CHUNK:])
            pseudo_ref[c, h] = pseudo
            tail = jnp.exp(last - c_col) * beta_col
            state[h] = jnp.exp(last) * before + mm2(k, tail * pseudo, TN)
            mixed = growth * read[:CHUNK] + mm(mixing, pseudo.astype(bf16))
            mixed_ref[rows, 256 * h : 256 * h + 256] = mixed
            gate = proj_ref[rows, 1024 + 256 * h : 1280 + 256 * h].astype(f32)
            scale = lax.rsqrt(jnp.mean(mixed * mixed, axis=-1, keepdims=True) + out_floor)
            gated = mixed * scale * gain_ref[0:1, :] * (gate * jax.nn.sigmoid(gate))
            gated_ref[rows, 256 * h : 256 * h + 256] = gated.astype(bf16)

    def body(step, carry):
        ready = [prepare(step * UNROLL + u) for u in range(UNROLL)]
        for u in range(UNROLL):
            advance(step * UNROLL + u, *ready[u])
        @pl.when(step == 0)
        def _():
            shard.start_far(1)
            if layer == 0:
                quarter.start_near()

        @pl.when(step == 1)
        def _():
            shard.forward(0)
            if layer == 0:
                quarter.start_quarter()

        @pl.when(step == 2)
        def _():
            shard.forward(1)

        return carry

    lax.fori_loop(0, proj_ref.shape[0] // (CHUNK * UNROLL), body, 0)
    shard.wait()
    shard.finish()
    if layer == 0:
        quarter.wait_quarter()


def mixer_forward(layer, projected, small, taps, heads, gain, sources):
    tokens = projected.shape[0]
    chunks = tokens // CHUNK
    vmem = pl.BlockSpec(memory_space=pltpu.VMEM)
    spot = pl.BlockSpec(memory_space=pl.ANY)
    wholes = (jax.ShapeDtypeStruct((1024, 1536), bf16),)
    if layer == 0:
        wholes = wholes * 2 + (jax.ShapeDtypeStruct((2, PART, 1536), bf16),)
    return pl.pallas_call(
        partial(mixer_forward_kernel, layer),
        out_shape=(
            jax.ShapeDtypeStruct((tokens, 512), bf16),
            jax.ShapeDtypeStruct((chunks, 2, DK, DV), f32),
            jax.ShapeDtypeStruct((chunks, 2, CHUNK, CHUNK), f32),
            jax.ShapeDtypeStruct((chunks, 2, CHUNK, DV), f32),
            jax.ShapeDtypeStruct((tokens, 512), f32),
        )
        + wholes,
        in_specs=[vmem] * 5 + [spot] * len(sources),
        out_specs=(vmem,) * 5 + (spot,) * len(wholes),
        scratch_shapes=[pltpu.VMEM((8, 1024), f32), pltpu.VMEM((2, DK, DV), f32)]
        + Reshard.scratch() * len(sources),
        compiler_params=pltpu.CompilerParams(
            collective_id=8 + layer, has_side_effects=True, vmem_limit_bytes=LIMIT
        ),
        name="mixer_forward",
    )(projected, small, taps, heads, gain, *sources)


def mixer_backward_kernel(
    proj_ref, small_ref, taps_ref, heads_ref, gain_ref,
    start_ref, inv_ref, pseudo_ref, mixed_ref, dgated_ref,
    dproj_ref, dsmall_ref, gtaps_ref, gheads_ref,
    halo, dstate,
):
    halo[...] = jnp.zeros_like(halo)
    dstate[...] = jnp.zeros_like(dstate)
    gtaps_ref[...] = jnp.zeros_like(gtaps_ref)
    gheads_ref[...] = jnp.zeros_like(gheads_ref)
    row = grid_of((CHUNK, CHUNK), 0)
    col = grid_of((CHUNK, CHUNK), 1)
    lane = col
    token = grid_of((CHUNK, 1), 0)
    chunks = proj_ref.shape[0] // CHUNK

    def body(step, carry):
        c = chunks - 1 - step
        rows = pl.ds(pl.multiple_of(c * CHUNK, CHUNK), CHUNK)
        x = proj_ref[rows, 0:1024].astype(f32)
        before_rows = pl.ds(pl.multiple_of(jnp.maximum(c * CHUNK - 16, 0), 16), 16)
        x_before = proj_ref[before_rows, 0:1024].astype(f32)[8:]
        x_before = jnp.where(c > 0, x_before, 0.0)
        x_ext = jnp.concatenate([x_before, x], axis=0)
        convolved = conv_chunk(x_ext, taps_ref[...])
        sig = jax.nn.sigmoid(convolved)
        activated = convolved * sig
        strength, shifted_logit, log_decay, cumulative, turned = decay_chunk(
            small_ref[rows, :], heads_ref
        )
        d_strength = jnp.zeros((CHUNK, CHUNK), f32)
        d_cumulative = jnp.zeros((CHUNK, CHUNK), f32)
        d_q_parts, d_k_parts, d_v_parts = [], [], []
        gain_sum = jnp.zeros((1, DV), f32)
        for h in range(2):
            qa, ka, q_norm, k_norm, q, k, v = head_inputs(activated, h)
            cols = slice(256 * h, 256 * h + 256)
            mixed = mixed_ref[rows, cols]
            gate = proj_ref[rows, 1024 + 256 * h : 1280 + 256 * h].astype(f32)
            d_gated = dgated_ref[rows, cols].astype(f32)
            gate_sig = jax.nn.sigmoid(gate)
            gate_silu = gate * gate_sig
            scale = lax.rsqrt(jnp.mean(mixed * mixed, axis=-1, keepdims=True) + out_floor)
            scaled = mixed * scale
            gain = gain_ref[0:1, :]
            gain_sum = gain_sum + jnp.sum(d_gated * scaled * gate_silu, axis=0, keepdims=True)
            d_gate = d_gated * scaled * gain * (gate_sig * (1.0 + gate * (1.0 - gate_sig)))
            dproj_ref[rows, 1024 + 256 * h : 1280 + 256 * h] = d_gate.astype(bf16)
            d_scaled = d_gated * gain * gate_silu
            d_mixed = scale * (
                d_scaled - scaled * jnp.mean(d_scaled * scaled, axis=-1, keepdims=True)
            )
            c_col = cumulative[:, 2 + h : 3 + h]
            c_row = turned[2 + h : 3 + h, :]
            beta_row = turned[h : h + 1, :]
            beta_col = strength[:, h : h + 1]
            growth = jnp.exp(c_col)
            last = c_col[CHUNK - 1 :, :]
            ratio = jnp.exp(jnp.where(row >= col, c_col - c_row, -1e4))
            key_gram = mm(k, k, NT)
            query_gram = mm(q, k, NT)
            mixing = ratio * beta_row * query_gram
            fade = jnp.exp(last - c_col)
            tail = fade * beta_col
            start = start_ref[c, h]
            inv = inv_ref[c, h]
            pseudo = pseudo_ref[c, h]
            d_end = dstate[h]
            kf = k.astype(f32)
            qf = q.astype(f32)
            d_pseudo = mb(mixing, d_mixed, TN) + tail * mm(k, d_end.astype(bf16))
            d_right = mm3(inv, d_pseudo, TN)
            pair = jnp.concatenate([d_mixed, d_right], axis=0)
            reads = mm3(pair, jnp.concatenate([start, pseudo], axis=0), NT)
            read_q = reads[:CHUNK, :DK]
            read_k = reads[CHUNK:, :DK]
            read_u = mm3(pseudo, d_end, NT)
            d_mixing = jnp.where(row >= col, reads[:CHUNK, DK:], 0.0) * ratio
            d_system = jnp.where(row > col, -reads[CHUNK:, DK:], 0.0) * ratio
            raw = d_mixing * query_gram + d_system * key_gram
            x_pair = jnp.concatenate([d_mixing * beta_row, d_system * beta_row], axis=0)
            by_row = mm(x_pair.astype(bf16), k)
            by_col = mm(x_pair.astype(bf16), jnp.concatenate([q, k], axis=0), TN)
            d_q = growth * read_q + by_row[:CHUNK]
            d_k = by_row[CHUNK:] + by_col - growth * read_k + tail * read_u
            dstate[h] = jnp.exp(last) * d_end + mb(
                jnp.concatenate([growth * qf, -growth * kf], axis=0), pair, TN
            )
            u_dot = jnp.sum(read_u * kf, axis=-1, keepdims=True)
            col_raw = jnp.sum(raw, axis=0, keepdims=True)
            col_raw = jnp.broadcast_to(col_raw, (CHUNK, CHUNK)).T[:, 0:1]
            d_beta = col_raw + fade * u_dot
            d_cum = (
                jnp.sum(raw * beta_row, axis=-1, keepdims=True)
                - beta_col * col_raw
                + growth
                * (
                    jnp.sum(read_q * qf, axis=-1, keepdims=True)
                    - jnp.sum(read_k * kf, axis=-1, keepdims=True)
                )
                - tail * u_dot
            )
            at_last = jnp.sum(tail * u_dot, axis=0, keepdims=True) + jnp.exp(last) * jnp.sum(
                jnp.sum(start * d_end, axis=-1, keepdims=True), axis=0, keepdims=True
            )
            d_cum = d_cum + jnp.where(token == CHUNK - 1, at_last, 0.0)
            d_strength = jnp.where(lane == h, d_beta, d_strength)
            d_cumulative = jnp.where(lane == 2 + h, d_cum, d_cumulative)
            d_qn = d_q * (1.0 / math.sqrt(DK))
            qn = qa * q_norm
            kn = ka * k_norm
            d_q_parts.append(
                q_norm * (d_qn - qn * jnp.sum(d_qn * qn, axis=-1, keepdims=True))
            )
            d_k_parts.append(k_norm * (d_k - kn * jnp.sum(d_k * kn, axis=-1, keepdims=True)))
            d_v_parts.append(d_right)
        upper_ones = jnp.where(row <= col, 1.0, 0.0).astype(f32)
        d_log = mm2(upper_ones.astype(bf16), d_cumulative)
        d_shifted = d_log * (-jnp.exp(heads_ref[0:1, :])) * jax.nn.sigmoid(shifted_logit)
        d_small = jnp.where(lane < 2, d_strength * strength * (1.0 - strength), d_shifted)
        dsmall_ref[rows, :] = jnp.where(lane < 4, d_small, 0.0).astype(bf16)
        gheads_ref[0:1, :] += gain_sum
        gheads_ref[1:2, 0:128] += jnp.sum(d_log * log_decay, axis=0, keepdims=True)
        gheads_ref[2:3, 0:128] += jnp.sum(d_shifted, axis=0, keepdims=True)
        d_activated = jnp.concatenate(d_q_parts + d_k_parts + d_v_parts, axis=1)
        d_conv = d_activated * (sig * (1.0 + convolved * (1.0 - sig)))
        for j in range(CONV):
            gtaps_ref[j : j + 1, :] += jnp.sum(
                d_conv * x_ext[5 + j : 5 + j + CHUNK], axis=0, keepdims=True
            )
        d_ext = jnp.concatenate([d_conv, halo[...]], axis=0)
        d_x = sum(
            d_ext[CONV - 1 - j : CONV - 1 - j + CHUNK] * taps_ref[j : j + 1] for j in range(CONV)
        )
        halo[...] = d_conv[:8]
        dproj_ref[rows, 0:1024] = d_x.astype(bf16)
        return carry

    lax.fori_loop(0, chunks, body, 0)


def mixer_backward(projected, small, taps, heads, gain, saved, d_gated):
    tokens = projected.shape[0]
    vmem = pl.BlockSpec(memory_space=pltpu.VMEM)
    return pl.pallas_call(
        mixer_backward_kernel,
        out_shape=(
            jax.ShapeDtypeStruct((tokens, 1536), bf16),
            jax.ShapeDtypeStruct((tokens, 128), bf16),
            jax.ShapeDtypeStruct((8, 1024), f32),
            jax.ShapeDtypeStruct((8, DV), f32),
        ),
        in_specs=[vmem] * 10,
        out_specs=(vmem,) * 4,
        scratch_shapes=[pltpu.VMEM((8, 1024), f32), pltpu.VMEM((2, DK, DV), f32)],
        compiler_params=pltpu.CompilerParams(vmem_limit_bytes=48 << 20),
        name="mixer_backward",
    )(projected, small, taps, heads, gain, *saved, d_gated)


SUB = 128
LIMIT = 56 << 20
MESH = pl.DeviceIdType.MESH


def place():
    me = lax.axis_index("grp")
    y, c = me // 2, me % 2
    return y, c


def shard_rows(y, c, i, size):
    return pl.ds(pl.multiple_of((2 * y + c) * size + i * SUB, SUB), SUB)


def greet(y, c):
    barrier = pltpu.get_barrier_semaphore()
    for target in (2 * y + 1 - c, 2 * (1 - y) + c):
        pl.semaphore_signal(barrier, inc=1, device_id={"grp": target}, device_id_type=MESH)
    return lambda: pl.semaphore_wait(barrier, 2)


def remote(src, dst, send, recv, target):
    return pltpu.make_async_remote_copy(
        src_ref=src, dst_ref=dst, send_sem=send, recv_sem=recv,
        device_id={"grp": target}, device_id_type=MESH,
    )


class Gather:
    def __init__(self, full, send, recv, size):
        self.full, self.send, self.recv, self.size = full, send, recv, size
        self.y, self.c = place()

    def piece(self, kind, i):
        y, c = self.y, self.c
        rows = shard_rows(1 - y if kind == 2 else y, c, i, self.size)
        target = 2 * (1 - y) + c if kind == 1 else 2 * y + 1 - c
        view = self.full.at[rows]
        return remote(view, view, self.send.at[kind, i], self.recv.at[kind, i], target)

    def own(self, i):
        return shard_rows(self.y, self.c, i, self.size)

    def start(self, i):
        self.piece(0, i).start()
        self.piece(1, i).start()

    def sibling(self, i):
        self.piece(0, i).wait_recv()
        return shard_rows(self.y, 1 - self.c, i, self.size)

    def across(self, i):
        self.piece(1, i).wait_recv()
        self.piece(2, i).start()
        return shard_rows(1 - self.y, self.c, i, self.size)

    def diagonal(self, i):
        self.piece(2, i).wait_recv()
        return shard_rows(1 - self.y, 1 - self.c, i, self.size)

    def finish(self):
        for kind in range(3):
            for i in range(self.size // SUB):
                self.piece(kind, i).wait_send()


class Scatter:
    def __init__(self, out, core, keep, relay, far, send, recv, size):
        self.out, self.core, self.keep, self.relayed, self.far = out, core, keep, relay, far
        self.send, self.recv, self.size = send, recv, size
        self.y, self.c = place()

    def to_sibling(self, part, i):
        rows = pl.ds(i * SUB, SUB)
        return remote(
            self.out.at[part, rows], self.core.at[part, rows],
            self.send.at[part, i], self.recv.at[part, i], 2 * self.y + 1 - self.c,
        )

    def to_across(self, i):
        rows = pl.ds(i * SUB, SUB)
        return remote(
            self.relayed.at[rows], self.far.at[rows],
            self.send.at[2, i], self.recv.at[2, i], 2 * (1 - self.y) + self.c,
        )

    def give(self, part, i, value):
        self.out[part, i * SUB : (i + 1) * SUB, :] = value.astype(bf16)
        self.to_sibling(part, i).start()

    def hold(self, part, i, value):
        self.keep[part, i * SUB : (i + 1) * SUB, :] = value

    def relay(self, i):
        rows = slice(i * SUB, (i + 1) * SUB)
        self.to_sibling(0, i).wait_recv()
        self.relayed[rows, :] = (self.keep[0, rows, :] + self.core[0, rows, :].astype(f32)).astype(bf16)
        self.to_across(i).start()

    def total(self, i):
        rows = slice(i * SUB, (i + 1) * SUB)
        self.to_sibling(1, i).wait_recv()
        near = self.keep[1, rows, :] + self.core[1, rows, :].astype(f32)
        self.to_across(i).wait_recv()
        return near + self.far[rows, :].astype(f32)

    def finish(self):
        for i in range(self.size // SUB):
            self.to_sibling(0, i).wait_send()
            self.to_sibling(1, i).wait_send()
            self.to_across(i).wait_send()

    @staticmethod
    def scratch(size, width):
        return [
            pltpu.VMEM((2, size, width), bf16),
            pltpu.VMEM((2, size, width), bf16),
            pltpu.VMEM((2, size, width), f32),
            pltpu.VMEM((size, width), bf16),
            pltpu.VMEM((size, width), bf16),
            pltpu.SemaphoreType.DMA((3, size // SUB)),
            pltpu.SemaphoreType.DMA((3, size // SUB)),
        ]


def gather_sems(size):
    return [pltpu.SemaphoreType.DMA((3, size // SUB)), pltpu.SemaphoreType.DMA((3, size // SUB))]


def in_order(gather):
    count = gather.size // SUB
    for i in range(count):
        yield gather.own(i)
    for i in range(count):
        yield gather.sibling(i)
    for i in range(count):
        yield gather.across(i)
        yield gather.diagonal(i)


def call(kernel, out_shape, inputs, scratch, collective, name, spots=()):
    vmem = pl.BlockSpec(memory_space=pltpu.VMEM)
    spot = pl.BlockSpec(memory_space=pl.ANY)
    return pl.pallas_call(
        kernel,
        out_shape=out_shape,
        in_specs=[vmem] * len(inputs) + [spot] * len(spots),
        out_specs=tuple(vmem for _ in out_shape),
        scratch_shapes=scratch,
        compiler_params=pltpu.CompilerParams(
            collective_id=collective, has_side_effects=True, vmem_limit_bytes=LIMIT
        ),
        cost_estimate=pl.CostEstimate(flops=1000, bytes_accessed=1000, transcendentals=0),
        name=name,
    )(*inputs, *spots)


def relative(y, c, d):
    dy, dc = d // 2, d % 2
    return 2 * (y + dy - 2 * y * dy) + c + dc - 2 * c * dc


def load_whole(src, whole, sem):
    copy = pltpu.make_async_copy(src, whole, sem)
    copy.start()
    return copy.wait


def load_down(src, whole, sem):
    y, c = place()
    rows, extra = src.shape[0], whole.shape[0] - src.shape[0]
    whole[:extra, :] = jnp.zeros((extra, whole.shape[1]), bf16)
    whole[rows:, :] = jnp.zeros((extra, whole.shape[1]), bf16)
    spot = pl.ds(pl.multiple_of(extra * c, extra), rows)
    copy = pltpu.make_async_copy(src, whole.at[spot], sem)
    copy.start()
    return copy.wait


def flip(rank):
    return rank + 1 - 2 * (rank % 2)


def greet_wide(y, c):
    barrier = pltpu.get_barrier_semaphore()
    for d in range(1, 4):
        pl.semaphore_signal(
            barrier, inc=1, device_id={"grp": relative(y, c, d)}, device_id_type=MESH
        )
    pl.semaphore_signal(
        barrier, inc=1, device_id={"rep": flip(lax.axis_index("rep"))}, device_id_type=MESH
    )
    return lambda: pl.semaphore_wait(barrier, 4)


PART = 64


def in_lanes(t):
    return (
        (256 * t, 256, 0),
        (HK + 256 * t, 256, 256),
        (2 * HK + 512 * t, 512, 512),
        (CH + 512 * t, 512, 1024),
    )


def up_lanes(t):
    first = 1408 * (t // 2) + 640 * (t % 2)
    return ((first, 768, 0), (FF + first, 768, 768))


class Reshard:
    def __init__(self, source, lanes, whole, send, recv, passed, arrived, local):
        self.source, self.lanes, self.whole = source, lanes, whole
        self.send, self.recv, self.passed, self.arrived = send, recv, passed, arrived
        self.local = local
        self.y, self.c = place()
        rank = lax.axis_index("rep")
        self.x, self.other = rank % 2, flip(rank)
        self.size = source.shape[0]

    def at(self, index, offset, count):
        return pl.ds(pl.multiple_of(index * self.size + offset, PART), count)

    def pieces(self, d, q):
        y, c = self.y, self.c
        target = relative(y, c, d)
        start = 0 if d < 2 else self.size // 2 * self.x + PART * q
        count = self.size if d < 2 else PART
        copies = []
        for k, (lane, wide, to) in enumerate(self.lanes(target)):
            src = self.source.at[
                pl.ds(pl.multiple_of(start, PART), count) if d >= 2 else pl.ds(0, count),
                pl.ds(pl.multiple_of(lane, 128), wide),
            ]
            dst = self.whole.at[self.at(2 * y + c, start, count), pl.ds(to, wide)]
            if d == 0:
                copies.append(pltpu.make_async_copy(src, dst, self.local.at[k]))
            else:
                copies.append(
                    pltpu.make_async_remote_copy(
                        src_ref=src, dst_ref=dst,
                        send_sem=self.send.at[d, q, k], recv_sem=self.recv.at[d, q, k],
                        device_id={"grp": target}, device_id_type=MESH,
                    )
                )
        return copies

    def onward(self, d, q):
        source = relative(self.y, self.c, d)
        rows = self.at(source, self.size // 2 * self.x + PART * q, PART)
        return pltpu.make_async_remote_copy(
            src_ref=self.whole.at[rows], dst_ref=self.whole.at[rows],
            send_sem=self.passed.at[d - 2, q], recv_sem=self.arrived.at[d - 2, q],
            device_id={"rep": self.other}, device_id_type=MESH,
        )

    def parts(self):
        return range(self.size // 2 // PART)

    def start_far(self, q):
        for d in (2, 3):
            for copy in self.pieces(d, q):
                copy.start()

    def start_near(self):
        for copy in self.pieces(1, 0):
            copy.start()

    def start_own(self):
        for copy in self.pieces(0, 0):
            copy.start()

    def forward(self, q):
        for d in (2, 3):
            for copy in self.pieces(d, q):
                copy.wait_recv()
            self.onward(d, q).start()

    def wait_own(self):
        for copy in self.pieces(0, 0):
            copy.wait()

    def wait(self):
        for copy in self.pieces(1, 0):
            copy.wait_recv()
        for q in self.parts():
            for d in (2, 3):
                self.onward(d, q).wait_recv()

    def finish(self):
        for copy in self.pieces(1, 0):
            copy.wait_send()
        for q in self.parts():
            for d in (2, 3):
                for copy in self.pieces(d, q):
                    copy.wait_send()
                self.onward(d, q).wait_send()

    @staticmethod
    def scratch():
        dma = pltpu.SemaphoreType.DMA
        return [dma((4, 2, 4)), dma((4, 2, 4)), dma((2, 2)), dma((2, 2)), dma((4,))]


def like(*shape, dtype=f32):
    return jax.ShapeDtypeStruct(shape, dtype)


def normalise(x, gain):
    return x * lax.rsqrt(jnp.mean(x * x, axis=-1, keepdims=True) + epsilon) * gain


def normalise_back(x, gain, d_out):
    scale = lax.rsqrt(jnp.mean(x * x, axis=-1, keepdims=True) + epsilon)
    unit = x * scale
    d_unit = d_out * gain
    d_x = scale * (d_unit - unit * jnp.mean(d_unit * unit, axis=-1, keepdims=True))
    return d_x, jnp.sum(d_out * unit, axis=0, keepdims=True)


class Quarter(Reshard):
    def __init__(self, source, lanes, whole, far, *sems):
        super().__init__(source, lanes, whole, *sems)
        self.far = far
        self.z = (lax.axis_index("rep") % 8) // 2

    def quarters(self, d):
        target = relative(self.y, self.c, d)
        copies = []
        for k, (lane, wide, to) in enumerate(self.lanes(target)):
            copies.append(
                pltpu.make_async_remote_copy(
                    src_ref=self.source.at[
                        pl.ds(pl.multiple_of(PART * self.z, PART), PART),
                        pl.ds(pl.multiple_of(lane, 128), wide),
                    ],
                    dst_ref=self.far.at[d - 2, :, pl.ds(to, wide)],
                    send_sem=self.send.at[d, 0, k], recv_sem=self.recv.at[d, 0, k],
                    device_id={"grp": target}, device_id_type=MESH,
                )
            )
        return copies

    def start_quarter(self):
        for d in (2, 3):
            for copy in self.quarters(d):
                copy.start()

    def wait_quarter(self):
        for copy in self.pieces(1, 0):
            copy.wait_recv()
            copy.wait_send()
        for d in (2, 3):
            for copy in self.quarters(d):
                copy.wait_recv()
                copy.wait_send()


def load_shard(parts, whole, sems):
    y, c = place()
    copies = []

    def add(src, dst):
        copies.append(pltpu.make_async_copy(src, dst, sems.at[len(copies)]))

    if len(parts) == 1:
        add(parts[0], whole)
    else:
        raw, lanes, near, *far = parts
        size = whole.shape[0] // 4

        def block(index, count):
            return pl.ds(pl.multiple_of(index * size, size), count * size)

        own, sibling, across = block(2 * y + c, 1), block(2 * y + 1 - c, 1), block(2 - 2 * y, 2)
        for lane, wide, to in lanes(2 * y + c):
            src = raw.at[pl.ds(0, size), pl.ds(pl.multiple_of(lane, 128), wide)]
            add(src, whole.at[own, pl.ds(to, wide)])
        add(near.at[sibling], whole.at[sibling])
        if not far:
            add(near.at[across], whole.at[across])
        else:
            for z in range(4):
                for d in (2, 3):
                    at = relative(y, c, d) * size + PART * z
                    spot = pl.ds(pl.multiple_of(at, PART), PART)
                    add(far[0].at[z, d - 2], whole.at[spot])
    for copy in copies:
        copy.start()

    def wait():
        for copy in copies:
            copy.wait()

    return wait


def in_parts(parts):
    return parts if len(parts) == 1 else (parts[0].at[1], in_lanes) + tuple(parts[1:])


GAIN_AT, TAPS_AT, AB_AT, OUT_GAIN_AT, PACK_ROWS = 0, 8, 72, 136, 144


def start_kernel(
    x_ref, pack_ref, win_ref,
    normed_ref, proj_ref, small_ref, whole_ref,
    gain0, gain1, gain2, gain3, taps0, taps1, ab0, ab1, out0, out1,
    everyone, ab_rows, *scratch,
):
    size = x_ref.shape[0]
    y, c = place()
    me = 2 * y + c
    ready = greet_wide(y, c)
    shard = Reshard(win_ref.at[0], in_lanes, whole_ref, *scratch[:5])
    psend, precv = scratch[5:7]
    gather = Gather(normed_ref, *scratch[7:], size)
    everyone[me] = pack_ref[...]
    ready()

    def share(d):
        return pltpu.make_async_remote_copy(
            src_ref=pack_ref, dst_ref=everyone.at[me],
            send_sem=psend.at[d], recv_sem=precv.at[d],
            device_id={"grp": relative(y, c, d)}, device_id_type=MESH,
        )

    for d in (2, 3, 1):
        share(d).start()
    for q in shard.parts():
        shard.start_far(q)
    shard.start_near()
    shard.start_own()
    for d in (1, 2, 3):
        share(d).wait_recv()
    for k, ref in enumerate((gain0, gain1, gain2, gain3)):
        for s in range(4):
            for b in range(2):
                row = GAIN_AT + 2 * k + b
                ref[0:1, 256 * s + 128 * b : 256 * s + 128 * b + 128] = everyone[s, row : row + 1, :]
    for i in range(size // SUB):
        rows = slice(i * SUB, (i + 1) * SUB)
        normed = normalise(x_ref[rows, :].astype(f32), gain0[...])
        normed_ref[gather.own(i), :] = normed.astype(bf16)
        gather.start(i)
    for l, (taps, ab, out) in enumerate(((taps0, ab0, out0), (taps1, ab1, out1))):
        taps[...] = jnp.zeros_like(taps)
        out[...] = jnp.zeros_like(out)
        ab_rows[...] = jnp.zeros_like(ab_rows)
        for j in range(4):
            base = TAPS_AT + (4 * l + j) * 8
            for b in range(8):
                if b < 2:
                    s, row = 0, base + 2 * me + b
                elif b < 4:
                    s, row = 1, base + 2 * me + b - 2
                else:
                    s, row = 2 + y, base + 4 * c + b - 4
                taps[j : j + 1, 128 * b : 128 * b + 128] = everyone[s, pl.ds(row, 1), :]
            column = 2 * me + j if j < 2 else H + 2 * me + j - 2
            for s in range(4):
                for b in range(2):
                    row = AB_AT + (16 * l + column) * 2 + b
                    ab_rows[j : j + 1, 256 * s + 128 * b : 256 * s + 128 * b + 128] = everyone[
                        s, pl.ds(row, 1), :
                    ]
        ab[...] = ab_rows[...].T.astype(bf16)
        for s in range(4):
            out[0:1, 64 * s : 64 * s + 64] = everyone[
                s, OUT_GAIN_AT : OUT_GAIN_AT + 1, 64 * l : 64 * l + 64
            ]
    for q in shard.parts():
        shard.forward(q)
    shard.wait()
    shard.wait_own()
    for rows in in_order(gather):
        normed = normed_ref[rows, :]
        proj_ref[rows, :] = mm(normed, whole_ref[...]).astype(bf16)
        small_ref[rows, :] = mm(normed, ab0[...])
    gather.finish()
    shard.finish()
    for d in (1, 2, 3):
        share(d).wait_send()


def start(x, pack, w_in):
    size, width = x.shape
    tokens = 4 * size
    row = like(1, width)
    dma = pltpu.SemaphoreType.DMA
    return call(
        start_kernel,
        (
            like(tokens, width, dtype=bf16),
            like(tokens, 1536, dtype=bf16),
            like(tokens, 128),
            like(width, 1536, dtype=bf16),
            row, row, row, row,
            like(8, width), like(8, width),
            like(width, 128, dtype=bf16), like(width, 128, dtype=bf16),
            like(8, DV), like(8, DV),
        ),
        (x, pack),
        [pltpu.VMEM((4, PACK_ROWS, 128), f32), pltpu.VMEM((128, width), f32)]
        + Reshard.scratch()
        + [dma((4,)), dma((4,))]
        + gather_sems(size),
        1,
        "start",
        (w_in,),
    )


def project_kernel(count, res_ref, gain_ref, ab_ref, *refs):
    parts, refs = refs[:count], refs[count:]
    normed_ref, proj_ref, small_ref, w_ref, loads, send, recv = refs
    loaded = load_shard(in_parts(parts), w_ref, loads)
    size = res_ref.shape[0]
    y, c = place()
    ready = greet(y, c)
    gather = Gather(normed_ref, send, recv, size)
    for i in range(size // SUB):
        rows = slice(i * SUB, (i + 1) * SUB)
        normed_ref[gather.own(i), :] = normalise(res_ref[rows, :], gain_ref[...]).astype(bf16)
        if i == 0:
            ready()
        gather.start(i)
    loaded()
    for rows in in_order(gather):
        normed = normed_ref[rows, :]
        proj_ref[rows, :] = mm(normed, w_ref[...]).astype(bf16)
        small_ref[rows, :] = mm(normed, ab_ref[...])
    gather.finish()


def project(residual, gain, ab, weight):
    size, width = residual.shape
    tokens = 4 * size
    return call(
        partial(project_kernel, len(weight)),
        (like(tokens, width, dtype=bf16), like(tokens, 1536, dtype=bf16), like(tokens, 128)),
        (residual, gain, ab),
        [pltpu.VMEM((width, 1536), bf16), pltpu.SemaphoreType.DMA((13,))] + gather_sems(size),
        6,
        "project",
        weight,
    )


def swiglu(up):
    gate, value = up[:, :768], up[:, 768:]
    return gate * jax.nn.sigmoid(gate) * value


def swiglu_back(up, d_hidden):
    gate, value = up[:, :768], up[:, 768:]
    sig = jax.nn.sigmoid(gate)
    d_gate = d_hidden * value * (sig * (1.0 + gate * (1.0 - sig)))
    return jnp.concatenate([d_gate, d_hidden * gate * sig], axis=1)


def ffn_forward_kernel(
    layer, gated_ref, res_ref, gain_ref, raw_ref, down_ref, ffn_ref, whole_ref,
    mid_ref, normed_ref, up_ref, hidden_ref, out_ref,
    wup_ref, wdown_ref, wout_ref, loads, shard_loads, *scratch,
):
    loaded_out = load_whole(raw_ref.at[layer], wout_ref, loads.at[2])
    loaded = load_shard((ffn_ref.at[layer], up_lanes, whole_ref), wup_ref, shard_loads)
    loaded_down = load_down(down_ref.at[layer], wdown_ref, loads.at[1])
    size = res_ref.shape[0]
    count = size // SUB
    y, c = place()
    ready = greet(y, c)
    first = Scatter(*scratch[:7], size)
    second = Scatter(*scratch[7:14], size)
    gather = Gather(normed_ref, *scratch[14:], size)

    loaded_out()

    def branch(rows):
        return mm(gated_ref[rows, :], wout_ref[...])

    for part in range(2):
        yy = 1 - y if part == 0 else y
        for i in range(count):
            value = branch(shard_rows(yy, 1 - c, i, size))
            if part == 0 and i == 0:
                ready()
            first.give(part, i, value)
            first.hold(part, i, branch(shard_rows(yy, c, i, size)))
            if part == 0:
                first.relay(i)
    for i in range(count):
        rows = slice(i * SUB, (i + 1) * SUB)
        mid = res_ref[rows, :] + first.total(i)
        mid_ref[rows, :] = mid
        normed_ref[gather.own(i), :] = normalise(mid, gain_ref[...]).astype(bf16)
        gather.start(i)

    def feed(rows):
        up = mm(normed_ref[rows, :], wup_ref[...])
        up_ref[rows, :] = up.astype(bf16)
        hidden = swiglu(up).astype(bf16)
        hidden_ref[rows, :] = hidden
        return mm(hidden, wdown_ref[...])

    loaded()
    loaded_down()
    for i in range(count):
        second.hold(1, i, feed(gather.own(i)))
    for i in range(count):
        second.give(1, i, feed(gather.sibling(i)))
    for i in range(count):
        near = gather.across(i)
        second.hold(0, i, feed(near))
        second.give(0, i, feed(gather.diagonal(i)))
        second.relay(i)
    for i in range(count):
        rows = slice(i * SUB, (i + 1) * SUB)
        out_ref[rows, :] = mid_ref[rows, :] + second.total(i)
    first.finish()
    second.finish()
    gather.finish()


def ffn_forward(layer, gated, residual, gain, w_out, w_down, w_up):
    size, width = residual.shape
    tokens = 4 * size
    return call(
        partial(ffn_forward_kernel, layer),
        (
            like(size, width),
            like(tokens, width, dtype=bf16),
            like(tokens, 1536, dtype=bf16),
            like(tokens, 768, dtype=bf16),
            like(size, width),
        ),
        (gated, residual, gain),
        [
            pltpu.VMEM((width, 1536), bf16),
            pltpu.VMEM((768, width), bf16),
            pltpu.VMEM((512, width), bf16),
            pltpu.SemaphoreType.DMA((3,)),
            pltpu.SemaphoreType.DMA((13,)),
        ]
        + Scatter.scratch(size, width)
        + Scatter.scratch(size, width)
        + gather_sems(size),
        (2, 12)[layer],
        "ffn_forward",
        (w_out, w_down) + w_up,
    )


class Owners:
    def __init__(self, keep, send):
        self.keep, self.send = keep, send
        self.x = lax.axis_index("rep") % 2

    def put(self, r, store):
        @pl.when(self.x == r % 2)
        def _():
            store(self.keep.at[r // 2])

        @pl.when(self.x != r % 2)
        def _():
            store(self.send.at[r // 2])


def store_columns(buf, value, at):
    rows = pl.ds(at, value.shape[0])
    for r in range(8):

        def store(ref):
            ref[rows, :] = value[:, 128 * r : 128 * r + 128].astype(bf16)

        buf.put(r, store)


def store_up(buf, staged, d, c):
    own_half = (grid_of((32, 128), 1) >> 6) == c
    for r in range(8):
        rows = slice(32 * r, 32 * r + 32)

        def tile(side, j):
            lane = pl.multiple_of(768 * side + 128 * j, 128)
            return staged[rows, pl.ds(lane, 128)]

        tiles = [tile(j // 5, j % 5 + c) for j in range(10)]
        turned = pltpu.roll(tile(1, 5 - 5 * c), 64, 1)
        tiles.append(jnp.where(own_half, tile(0, 5 - 5 * c), turned))

        def store(ref):
            for j, value in enumerate(tiles):
                at = UP_AT + (d * 11 + j) * 32
                ref[at : at + 32, :] = value.astype(bf16)

        buf.put(r, store)


def store_rows(buf, value, d, base):
    blocks = value.shape[1] // 128
    for r in range(8):

        def store(ref):
            for j in range(blocks):
                at = base + (d * blocks + j) * 32
                ref[at : at + 32, :] = value[
                    32 * r : 32 * r + 32, 128 * j : 128 * j + 128
                ].astype(bf16)

        buf.put(r, store)


UP_AT, DOWN_AT, OUT_AT, FFN_ROWS = 0, 1408, 2112, 2624
SMALL_AT, IN_ROWS = 1536, 1552


def ffn_backward_kernel(
    layer, dres_ref, up_ref, hidden_ref, normed_ref, mid_ref, gain_ref, gated_ref,
    raw_ref, down_ref, ffn_ref, whole_ref,
    dmid_ref, dgated_ref, ggain_ref, keep_ref, send_ref,
    wup_ref, wdown_ref, wout_ref, loads, shard_loads, ddown_ref, dup_ref, dbranch_ref, staged, *scratch,
):
    buf_ref = Owners(keep_ref, send_ref)
    loaded_out = load_whole(raw_ref.at[layer], wout_ref, loads.at[2])
    loaded = load_shard((ffn_ref.at[layer], up_lanes, whole_ref), wup_ref, shard_loads)
    loaded_down = load_down(down_ref.at[layer], wdown_ref, loads.at[1])
    size = dres_ref.shape[0]
    count = size // SUB
    y, c = place()
    ready = greet(y, c)
    first = Gather(ddown_ref, *scratch[:2], size)
    second = Gather(dbranch_ref, *scratch[2:4], size)
    scatter = Scatter(*scratch[4:], size)
    for i in range(count):
        ddown_ref[first.own(i), :] = dres_ref[i * SUB : (i + 1) * SUB, :].astype(bf16)
        if i == 0:
            ready()
        first.start(i)

    def feed(rows):
        d_hidden = mm(ddown_ref[rows, :], wdown_ref[...], NT)
        d_up = swiglu_back(up_ref[rows, :].astype(f32), d_hidden).astype(bf16)
        dup_ref[rows, :] = d_up
        return mm(d_up, wup_ref[...], NT)

    loaded()
    loaded_down()
    for i in range(count):
        scatter.hold(1, i, feed(first.own(i)))
    for i in range(count):
        scatter.give(1, i, feed(first.sibling(i)))
    for i in range(count):
        near = first.across(i)
        scatter.hold(0, i, feed(near))
        scatter.give(0, i, feed(first.diagonal(i)))
        scatter.relay(i)
    for m in range(6):
        value = mm(hidden_ref[:, 128 * m : 128 * m + 128], ddown_ref[...], TN)
        store_columns(buf_ref, value, pl.multiple_of(DOWN_AT + 128 * m - 64 * c, 64))
    ggain_ref[...] = jnp.zeros_like(ggain_ref)
    for i in range(count):
        rows = slice(i * SUB, (i + 1) * SUB)
        d_norm, g_gain = normalise_back(mid_ref[rows, :], gain_ref[...], scatter.total(i))
        d_mid = dres_ref[rows, :] + d_norm
        dmid_ref[rows, :] = d_mid
        ggain_ref[0:1, :] += g_gain
        dbranch_ref[second.own(i), :] = d_mid.astype(bf16)
        second.start(i)
    for d in range(4):
        lanes = pl.ds(pl.multiple_of(relative(y, c, d) * 256, 256), 256)
        staged[...] = mm(normed_ref[:, lanes], dup_ref[...], TN)
        store_up(buf_ref, staged, d, c)
    loaded_out()
    for rows in in_order(second):
        dgated_ref[rows, :] = mm(dbranch_ref[rows, :], wout_ref[...], NT).astype(bf16)
    for m in range(4):
        value = mm(gated_ref[:, 128 * m : 128 * m + 128], dbranch_ref[...], TN)
        store_columns(buf_ref, value, OUT_AT + 128 * m)
    first.finish()
    second.finish()
    scatter.finish()


def ffn_backward(layer, d_res, up, hidden, normed, mid, gain, gated, w_out, w_down, w_up):
    size, width = d_res.shape
    tokens = 4 * size
    return call(
        partial(ffn_backward_kernel, layer),
        (
            like(size, width),
            like(tokens, 512, dtype=bf16),
            like(8, width),
            like(4, FFN_ROWS, 128, dtype=bf16),
            like(4, FFN_ROWS, 128, dtype=bf16),
        ),
        (d_res, up, hidden, normed, mid, gain, gated),
        [
            pltpu.VMEM((width, 1536), bf16),
            pltpu.VMEM((768, width), bf16),
            pltpu.VMEM((512, width), bf16),
            pltpu.SemaphoreType.DMA((3,)),
            pltpu.SemaphoreType.DMA((13,)),
            pltpu.VMEM((tokens, width), bf16),
            pltpu.VMEM((tokens, 1536), bf16),
            pltpu.VMEM((tokens, width), bf16),
            pltpu.VMEM((256, 1536), f32),
        ]
        + gather_sems(size)
        + gather_sems(size)
        + Scatter.scratch(size, width),
        (3, 13)[layer],
        "ffn_backward",
        (w_out, w_down) + w_up,
    )


def project_backward_kernel(
    parts, dproj_ref, dsmall_ref, ab_ref, normed_ref, res_ref, gain_ref, dmid_ref,
    gtwo_ref, gtaps_ref, gheads_ref, *refs
):
    parts, refs = refs[:parts], refs[parts:]
    dres_ref, keep_ref, send_ref, w_ref, loads, table, *scratch = refs
    buf_ref = Owners(keep_ref, send_ref)
    loaded = load_shard(in_parts(parts), w_ref, loads)
    size = res_ref.shape[0]
    count = size // SUB
    y, c = place()
    ready = greet(y, c)
    scatter = Scatter(*scratch, size)

    def back(rows):
        return mm(dproj_ref[rows, :], w_ref[...], NT) + mm(dsmall_ref[rows, :], ab_ref[...], NT)

    def weight_grad(d):
        lanes = pl.ds(pl.multiple_of(relative(y, c, d) * 256, 256), 256)
        value = mm(normed_ref[:, lanes], dproj_ref[...], TN)
        store_rows(buf_ref, value, d, 0)

    loaded()
    for part in range(2):
        yy = 1 - y if part == 0 else y
        for i in range(count):
            value = back(shard_rows(yy, 1 - c, i, size))
            if part == 0 and i == 0:
                ready()
            scatter.give(part, i, value)
            scatter.hold(part, i, back(shard_rows(yy, c, i, size)))
            if part == 0:
                scatter.relay(i)
    for d in range(4):
        weight_grad(d)
    ab_grad = mm(dsmall_ref[...], normed_ref[...], TN)
    table[...] = jnp.zeros_like(table)
    for k in range(8):
        lanes = slice(128 * k, 128 * k + 128)
        for j in range(4):
            table[8 * j + k : 8 * j + k + 1, :] = gtaps_ref[j : j + 1, lanes]
            table[32 + 8 * j + k : 33 + 8 * j + k, :] = ab_grad[j : j + 1, lanes]
        table[72 + k : 73 + k, :] = gtwo_ref[0:1, lanes]
    table[80:81, :] = gheads_ref[0:1, 0:128]
    table[81:82, :] = gheads_ref[0:1, 128:256]
    table[82:83, :] = gheads_ref[1:2, 0:128]
    table[83:84, :] = gheads_ref[2:3, 0:128]
    gain_sum = jnp.zeros((1, res_ref.shape[1]), f32)
    for i in range(count):
        rows = slice(i * SUB, (i + 1) * SUB)
        d_norm, g_gain = normalise_back(res_ref[rows, :], gain_ref[...], scatter.total(i))
        dres_ref[rows, :] = dmid_ref[rows, :] + d_norm
        gain_sum = gain_sum + g_gain
    for k in range(8):
        table[64 + k : 65 + k, :] = gain_sum[:, 128 * k : 128 * k + 128]
    for r in range(8):

        def store(ref):
            ref[SMALL_AT:IN_ROWS, :] = table[16 * r : 16 * r + 16, :].astype(bf16)

        buf_ref.put(r, store)
    scatter.finish()


def project_backward(d_proj, d_small, weight, ab, normed, residual, gain, d_mid, g_two, g_taps, g_heads):
    size, width = residual.shape
    return call(
        partial(project_backward_kernel, len(weight)),
        (like(size, width),) + (like(4, IN_ROWS, 128, dtype=bf16),) * 2,
        (d_proj, d_small, ab, normed, residual, gain, d_mid, g_two, g_taps, g_heads),
        [
            pltpu.VMEM((width, 1536), bf16),
            pltpu.SemaphoreType.DMA((13,)),
            pltpu.VMEM((128, 128), f32),
        ]
        + Scatter.scratch(size, width),
        4 if len(weight) == 1 else 7,
        "project_backward",
        weight,
    )


def assemble_kernel(
    f1, f2, f3, f4, down_ref, out_ref, up_ref, in_ref, table_ref,
    p1, p2, p3, p4, down, out, up, whole, loads, stores,
):
    y, c = place()
    copies = [
        pltpu.make_async_copy(src, dst, loads.at[k])
        for k, (src, dst) in enumerate(((f1, p1), (f2, p2), (f3, p3), (f4, p4)))
    ]
    for copy in copies:
        copy.start()
    left = grid_of((32, 128), 1) < 64

    def ffn(layer, pieces):
        def up_rows(r, carry):
            rows = pl.ds(pl.multiple_of(32 * r, 32), 32)
            for m in range(2):
                tiles = []
                for s in (2 * m, 2 * m + 1):
                    at = UP_AT + offset_of(y, c, s) * 352
                    tiles.append(
                        [
                            pieces[r, pl.ds(pl.multiple_of(at + 32 * j, 32), 32), :].astype(f32)
                            for j in range(11)
                        ]
                    )
                even, odd = tiles
                middle = (
                    jnp.where(left, even[10], odd[10]),
                    pltpu.roll(jnp.where(left, odd[10], even[10]), 64, 1),
                )
                for side in range(2):
                    part = slice(5 * side, 5 * side + 5)
                    base = FF * side + 1408 * m
                    for j, tile in enumerate(even[part] + [middle[side]] + odd[part]):
                        up[layer, rows, base + 128 * j : base + 128 * j + 128] = tile
            return carry

        lax.fori_loop(0, 8, up_rows, 0)
        done = [pltpu.make_async_copy(up.at[layer], up_ref.at[layer], stores.at[layer, 0])]
        done[0].start()
        for r in range(8):
            lanes = slice(128 * r, 128 * r + 128)
            down[layer, :, lanes] = pieces[r, DOWN_AT:OUT_AT, :].astype(f32)
            out[layer, :, lanes] = pieces[r, OUT_AT:FFN_ROWS, :].astype(f32)
        done.append(pltpu.make_async_copy(down.at[layer], down_ref.at[layer], stores.at[layer, 1]))
        done.append(pltpu.make_async_copy(out.at[layer], out_ref.at[layer], stores.at[layer, 2]))
        done[1].start()
        done[2].start()
        return done

    def projection(layer, pieces):
        def in_rows(r, carry):
            rows = pl.ds(pl.multiple_of(32 * r, 32), 32)
            for s in range(4):
                at = offset_of(y, c, s) * 384
                for lane, wide, to in in_lanes(s):
                    for k in range(wide // 128):
                        j = to // 128 + k
                        tile = pieces[r, pl.ds(pl.multiple_of(at + 32 * j, 32), 32), :]
                        column = lane + 128 * k
                        whole[layer, rows, column : column + 128] = tile.astype(f32)
            return carry

        lax.fori_loop(0, 8, in_rows, 0)
        done = pltpu.make_async_copy(whole.at[layer], in_ref.at[layer], stores.at[layer, 3])
        done.start()
        for s in range(4):
            at = pl.ds(pl.multiple_of(SMALL_AT + 16 * offset_of(y, c, s), 16), 16)
            for r in range(8):
                table_ref[s, layer, 16 * r : 16 * r + 16, :] = pieces[r, at, :].astype(f32)
        return [done]

    waiting = []
    copies[0].wait()
    waiting += ffn(1, p1)
    copies[1].wait()
    waiting += projection(1, p2)
    copies[2].wait()
    waiting += ffn(0, p3)
    copies[3].wait()
    waiting += projection(0, p4)
    for store in waiting:
        store.wait()


def offset_of(y, c, s):
    sy, sc = s // 2, s % 2
    return 2 * (y + sy - 2 * y * sy) + c + sc - 2 * c * sc


def assemble(finals):
    spot = pl.BlockSpec(memory_space=pl.ANY)
    shapes = [(LAYERS, 704, 1024), (LAYERS, 512, 1024), (LAYERS, 256, 2 * FF), (LAYERS, 256, CH + HV)]
    return pl.pallas_call(
        assemble_kernel,
        out_shape=tuple(like(*shape) for shape in shapes) + (like(4, LAYERS, 128, 128),),
        in_specs=[spot] * 4,
        out_specs=(spot,) * 4 + (pl.BlockSpec(memory_space=pltpu.VMEM),),
        scratch_shapes=[pltpu.VMEM(final.shape, bf16) for final in finals]
        + [pltpu.VMEM(shape, f32) for shape in shapes]
        + [pltpu.SemaphoreType.DMA((4,)), pltpu.SemaphoreType.DMA((2, 4))],
        compiler_params=pltpu.CompilerParams(vmem_limit_bytes=LIMIT),
        name="assemble",
    )(*finals)


FFN_MOVE, IN_MOVE = (UP_AT, 352), (0, 384)
GATHERED_ROWS = SMALL_AT + 4 * 16


def add_into(dst, left, right):
    dst[...] = (left[...].astype(f32) + right[...].astype(f32)).astype(bf16)


class Group:
    def __init__(self, number, piece, moved, final, move, sems, x_first=False):
        self.number, self.piece, self.moved, self.final = number, piece, moved, final
        self.at, self.part = move
        self.send, self.recv, self.local = sems
        self.x_first = x_first
        rank = lax.axis_index("rep")
        self.rank, self.x, self.z = rank, rank % 2, (rank % 8) // 2
        self.y, self.c = place()
        self.extra = moved.shape[0] > piece.shape[0]

    def swaps(self, d):
        target = relative(self.y, self.c, d)
        rows = pl.ds(self.at + d * self.part, self.part)
        spans = [(rows, rows, d)]
        if self.extra:
            spans.append((pl.ds(SMALL_AT, 16), pl.ds(SMALL_AT + 16 * d, 16), 20 + d))
        return [
            pltpu.make_async_remote_copy(
                src_ref=self.piece.at[src], dst_ref=self.moved.at[dst],
                send_sem=self.send.at[self.number, k], recv_sem=self.recv.at[self.number, k],
                device_id={"grp": target}, device_id_type=MESH,
            )
            for src, dst, k in spans
        ]

    def start_swap(self):
        for d in range(1, 4):
            for copy in self.swaps(d):
                copy.start()
        first = self.at + self.part
        self.moved[0:first, :] = self.piece[0:first, :]
        rest, last = self.at + 4 * self.part, self.piece.shape[0]
        if rest < last:
            self.moved[rest:last, :] = self.piece[rest:last, :]

    def wait_swap(self):
        for d in range(1, 4):
            for copy in self.swaps(d):
                copy.wait_recv()

    def owner(self, source_z, which):
        return 2 * source_z + (self.x if which == 0 else 1 - self.x)

    def move(self, step, source_z, kind, which=0):
        owner = self.owner(source_z, which)
        src = self.moved if step == 0 and which == 0 else self.final.at[owner]
        number = self.number if which == 0 else 4
        slot = 4 + 4 * kind + step
        return pltpu.make_async_remote_copy(
            src_ref=src, dst_ref=self.final.at[owner],
            send_sem=self.send.at[number, slot], recv_sem=self.recv.at[number, slot],
            device_id={"rep": self.rank + 2 - 4 * kind}, device_id_type=MESH,
        )

    def x_move(self, step, source_z):
        owner = self.owner(source_z, 0)
        src = self.moved if step == 0 else self.final.at[owner]
        return pltpu.make_async_remote_copy(
            src_ref=src, dst_ref=self.final.at[owner],
            send_sem=self.send.at[self.number, 12 + step + 3],
            recv_sem=self.recv.at[self.number, 12 + source_z],
            device_id={"rep": flip(self.rank)}, device_id_type=MESH,
        )

    def own_copy(self):
        return pltpu.make_async_copy(
            self.moved, self.final.at[self.owner(self.z, 0)], self.local.at[self.number]
        )

    def both_ways(self, which, act):
        @pl.when(self.z < 3)
        def _():
            act(self.move(0, self.z, 0, which))

        @pl.when(self.z > 0)
        def _():
            act(self.move(0, self.z, 1, which))

    def begin(self):
        self.both_ways(0, lambda copy: copy.start())
        self.x_move(0, self.z).start()
        self.own_copy().start()

    def begin_other(self):
        self.x_move(0, self.z).wait_recv()
        self.both_ways(1, lambda copy: copy.start())

    def passes(self, k, which, arrive, onward):
        z = self.z

        @pl.when(z >= k)
        def _():
            arrive(k, z - k, 0)

            @pl.when(z < 3)
            def _():
                onward(self.move(k, z - k, 0, which))

        @pl.when(z + k <= 3)
        def _():
            arrive(-k, z + k, 1)

            @pl.when(z > 0)
            def _():
                onward(self.move(k, z + k, 1, which))

    def relay(self, k):
        for which in range(2 if self.x_first else 1):

            def arrive(step, source, kind):
                self.move(abs(step) - 1, source, kind, which).wait_recv()
                if not self.x_first:
                    self.x_move(step, source).start()

            self.passes(k, which, arrive, lambda copy: copy.start())

    def finish(self):
        for which in range(2 if self.x_first else 1):

            def arrive(step, source, kind):
                if not self.x_first:
                    self.x_move(step, source).wait_send()

            for k in range(1, 4):
                self.passes(k, which, arrive, lambda copy: copy.wait_send())
            self.both_ways(which, lambda copy: copy.wait_send())
        self.x_move(0, self.z).wait_send()
        if not self.x_first:
            for source in range(4):
                self.x_move(0, source).wait_recv()
        self.own_copy().wait()
        for d in range(1, 4):
            for copy in self.swaps(d):
                copy.wait_send()


class Line:
    def __init__(self, values, right, left, send, recv):
        self.values, self.right, self.left = values, right, left
        self.send, self.recv = send, recv
        self.rank = lax.axis_index("rep")
        self.z = (self.rank % 8) // 2

    def go(self, o, toward):
        land = self.right if toward == 0 else self.left
        return pltpu.make_async_remote_copy(
            src_ref=self.values.at[o], dst_ref=land.at[o],
            send_sem=self.send.at[toward, o], recv_sem=self.recv.at[toward, o],
            device_id={"rep": self.rank + 2 - 4 * toward}, device_id_type=MESH,
        )

    def edge(self, step, act):
        @pl.when(self.z == 0)
        def _():
            act(self.go(3 - step, 0))

        @pl.when(self.z == 3)
        def _():
            act(self.go(step, 1))

    def start_edge(self, step):
        if step > 0:
            self.edge(step - 1, lambda copy: copy.wait_send())
        self.edge(step, lambda copy: copy.start())

    def inner(self, step):
        z, o = self.z, 3 - step

        @pl.when((z > 0) & (z < o))
        def _():
            self.go(o, 0).wait_recv()
            add_into(self.values.at[o], self.values.at[o], self.right.at[o])
            self.go(o, 0).start()

        @pl.when((z < 3) & (z > step))
        def _():
            self.go(step, 1).wait_recv()
            add_into(self.values.at[step], self.values.at[step], self.left.at[step])
            self.go(step, 1).start()

    def total(self, out):
        z = self.z
        for o in range(4):

            @pl.when(z == o)
            def _():
                value = self.values[o].astype(f32)
                if o > 0:
                    self.go(o, 0).wait_recv()
                    value = value + self.right[o].astype(f32)
                if o < 3:
                    self.go(o, 1).wait_recv()
                    value = value + self.left[o].astype(f32)
                out[...] = value.astype(bf16)

    def finish(self):
        self.edge(2, lambda copy: copy.wait_send())
        for o in range(4):

            @pl.when((self.z > 0) & (self.z < o))
            def _():
                self.go(o, 0).wait_send()

            @pl.when((self.z < 3) & (self.z > o))
            def _():
                self.go(o, 1).wait_send()


def finish_kernel(
    p1, p2, s3, k4, b4, f1, f2, f3, f4,
    q1, q2, q3, q4, e1, e2, e3, e4, v3, r3, l3, v4, x4, r4, l4,
    send, recv, local, send3, recv3, send4, recv4, send5, recv5, loads,
):
    rank = lax.axis_index("rep")
    x, z = rank % 2, (rank % 8) // 2
    y, c = place()
    loaded = [
        pltpu.make_async_copy(p1, q1, loads.at[0]),
        pltpu.make_async_copy(p2, q2, loads.at[1]),
        pltpu.make_async_copy(s3, v3, loads.at[2]),
        pltpu.make_async_copy(k4, v4, loads.at[3]),
    ]
    for load in loaded:
        load.start()
    barrier = pltpu.get_barrier_semaphore()
    pl.semaphore_signal(
        barrier, inc=1, device_id={"rep": rank + 1 - 2 * x}, device_id_type=MESH
    )
    for d in range(1, 4):
        dy, dc = d // 2, d % 2
        target = 2 * (y + dy - 2 * y * dy) + c + dc - 2 * c * dc
        pl.semaphore_signal(barrier, inc=1, device_id={"grp": target}, device_id_type=MESH)

    @pl.when(z > 0)
    def _():
        pl.semaphore_signal(barrier, inc=1, device_id={"rep": rank - 2}, device_id_type=MESH)

    @pl.when(z < 3)
    def _():
        pl.semaphore_signal(barrier, inc=1, device_id={"rep": rank + 2}, device_id_type=MESH)

    @pl.when((z > 0) & (z < 3))
    def _():
        pl.semaphore_wait(barrier, 6)

    @pl.when((z == 0) | (z == 3))
    def _():
        pl.semaphore_wait(barrier, 5)

    def halves(o):
        return pltpu.make_async_remote_copy(
            src_ref=b4.at[o], dst_ref=x4.at[o], send_sem=send5.at[o], recv_sem=recv5.at[o],
            device_id={"rep": rank + 1 - 2 * x}, device_id_type=MESH,
        )

    for o in (3, 0, 2, 1):
        halves(o).start()
    sems = (send, recv, local)
    g1 = Group(0, q1, e1, f1, FFN_MOVE, sems)
    g2 = Group(1, q2, e2, f2, IN_MOVE, sems, x_first=True)
    g3 = Group(2, q3, e3, f3, FFN_MOVE, sems)
    g4 = Group(3, q4, e4, f4, IN_MOVE, sems)
    line3 = Line(v3, r3, l3, send3, recv3)
    line4 = Line(v4, r4, l4, send4, recv4)
    loaded[0].wait()
    g1.start_swap()
    loaded[2].wait()
    line3.start_edge(0)
    loaded[1].wait()
    g2.start_swap()
    g1.wait_swap()
    g1.begin()
    line3.inner(0)
    line3.start_edge(1)
    g2.wait_swap()
    g2.begin()
    loaded[3].wait()
    for o in (3, 0, 2, 1):
        halves(o).wait_recv()
        add_into(v4.at[o], v4.at[o], x4.at[o])
    line4.start_edge(0)
    line3.inner(1)
    line3.start_edge(2)
    g1.relay(1)
    line4.inner(0)
    line4.start_edge(1)
    line3.total(q3)
    g3.start_swap()
    line4.inner(1)
    line4.start_edge(2)
    g1.relay(2)
    g3.wait_swap()
    g3.begin()
    line4.total(q4)
    g4.start_swap()
    g2.begin_other()
    g1.relay(3)
    g4.wait_swap()
    g4.begin()
    g2.relay(1)
    g3.relay(1)
    g4.relay(1)
    g2.relay(2)
    g3.relay(2)
    g4.relay(2)
    g3.relay(3)
    g4.relay(3)
    g2.relay(3)
    for group in (g1, g2, g3, g4):
        group.finish()
    line3.finish()
    line4.finish()
    for o in range(4):
        halves(o).wait_send()


def finish_reduction(p1, p2, s3, k4, b4):
    spot = pl.BlockSpec(memory_space=pl.ANY)
    big, small = p1.shape, p2.shape
    wide = (GATHERED_ROWS, 128)
    dma = pltpu.SemaphoreType.DMA
    return pl.pallas_call(
        finish_kernel,
        out_shape=tuple(like(8, *shape, dtype=bf16) for shape in (big, wide, big, wide)),
        in_specs=[spot] * 5,
        out_specs=(spot,) * 4,
        scratch_shapes=[
            pltpu.VMEM(shape, bf16)
            for shape in [big, small] * 2 + [big, wide] * 2
            + [(4,) + big] * 3
            + [(4,) + small] * 4
        ]
        + [dma((5, 24)), dma((5, 24)), dma((4,))]
        + [dma((2, 4))] * 4
        + [dma((4,)), dma((4,)), dma((4,))],
        compiler_params=pltpu.CompilerParams(
            collective_id=5, has_side_effects=True, vmem_limit_bytes=LIMIT
        ),
        cost_estimate=pl.CostEstimate(flops=1000, bytes_accessed=1000, transcendentals=0),
        name="finish_reduction",
    )(p1, p2, s3, k4, b4)


def swap_route(bit, count):
    return [(i, i ^ bit) for i in range(count)]


def planes_of(replicas):
    return [
        [8 * b + 2 * z + x for z in range(4)] for b in range(replicas // 8) for x in range(2)
    ]


def swap_x(array, replicas):
    return lax.ppermute(array, "rep", swap_route(1, replicas))


def add_arrived(kept, arrived):
    return (kept.astype(f32) + arrived.astype(f32)).astype(bf16)


def reduce_z(summed, replicas):
    piece = lax.psum_scatter(
        summed, "rep", scatter_dimension=0, tiled=False, axis_index_groups=planes_of(replicas)
    )
    blocks = replicas // 8
    if blocks > 1:
        piece = lax.psum(
            piece, "rep", axis_index_groups=[[8 * b + r for b in range(blocks)] for r in range(8)]
        )
    return piece


def exchange(piece, at, part):
    moved = [piece[: at + part]]
    for d in range(1, 4):
        moved.append(swap(piece[at + d * part : at + (d + 1) * part], d))
    moved.append(piece[at + 4 * part :])
    if piece.shape[0] == IN_ROWS:
        moved += [swap(piece[SMALL_AT:], d) for d in range(1, 4)]
    return jnp.concatenate(moved, axis=0)


def gather_z(piece, replicas):
    return lax.all_gather(piece, "rep", axis=0, axis_index_groups=planes_of(replicas))


def spread(piece, replicas):
    owned = gather_z(piece, replicas)
    other = swap_x(owned, replicas)
    odd = lax.axis_index("rep") % 2 == 1
    pair = jnp.stack([jnp.where(odd, other, owned), jnp.where(odd, owned, other)], axis=1)
    return pair.reshape((8,) + piece.shape)


def finish_all(piece1, piece2, summed3, keep4, send4, replicas):
    if replicas == 8:
        return finish_reduction(piece1, piece2, summed3, keep4, send4)
    piece3 = reduce_z(summed3, replicas)
    piece4 = reduce_z(add_arrived(keep4, swap_x(send4, replicas)), replicas)
    return [
        spread(exchange(piece, *move), replicas)
        for piece, move in (
            (piece1, FFN_MOVE), (piece2, IN_MOVE), (piece3, FFN_MOVE), (piece4, IN_MOVE)
        )
    ]


def tie(*values):
    return lax.optimization_barrier(values)


def swap(array, d):
    return lax.ppermute(array, "grp", swap_route(d, 4))


def per_device(
    x_input, norm_gain, w_in, w_ab, conv_w, a_log, dt_bias, out_gain, w_out, ffn_in, ffn_out,
    cotangent,
):
    parts = lax.axis_size("grp")
    replicas = lax.axis_size("rep")
    mine = lax.axis_index("grp")
    rows, width = x_input.shape[1], x_input.shape[2]
    shard = w_in.shape[1]

    pack = jnp.concatenate(
        [
            norm_gain.reshape(-1, 128),
            conv_w.reshape(-1, 128),
            jnp.swapaxes(w_ab, 1, 2).reshape(-1, 128),
            out_gain.reshape(-1, 128),
            jnp.zeros((PACK_ROWS - OUT_GAIN_AT - 1, 128), bf16),
        ]
    ).astype(f32)
    normed, projected, small, in_weight, *rest = start(x_input[0], pack, w_in)
    gains, taps_pair, ab_pair, out_pair = rest[0:4], rest[4:6], rest[6:8], rest[8:10]
    small_weights = []
    for l in range(LAYERS):
        heads = jnp.pad(jnp.stack([a_log[l], dt_bias[l]]).astype(f32), ((0, 6), (2, 124)))
        small_weights.append(
            (
                gains[2 * l], gains[2 * l + 1], ab_pair[l], taps_pair[l], heads, out_pair[l],
            )
        )

    residual = x_input[0].astype(f32)
    kept = []
    in_weights, up_weights = [(in_weight,)], []
    for l in range(LAYERS):
        gain_one, gain_two, ab, taps, heads, gain = small_weights[l]
        if l > 0:
            normed, projected, small = project(residual, gain_one, ab, in_weights[l])
        gated, *saved = mixer_forward(
            l, projected, small, taps, heads, gain, (ffn_in, w_in)[: LAYERS - l]
        )
        up_weights.append((ffn_in, saved[4]))
        if l == 0:
            near, far = saved[5:]
            in_weights.append(
                (
                    w_in,
                    near,
                    lax.all_gather(far, "rep", axis=0, axis_index_groups=planes_of(replicas)),
                )
            )
        saved = saved[:4]
        mid, normed_two, up, hidden, residual_out = ffn_forward(
            l, gated, residual, gain_two, w_out, ffn_out, up_weights[l]
        )
        kept.append((residual, normed, projected, small, gated, saved, mid, normed_two, up, hidden))
        residual = residual_out
    block_output = residual.astype(bf16)[None]

    d_residual = cotangent[0].astype(f32)

    def ffn_part(l, d_residual):
        gain_one, gain_two, ab, taps, heads, gain = small_weights[l]
        residual, normed, projected, small, gated, saved, mid, normed_two, up, hidden = kept[l]
        return ffn_backward(
            l, d_residual, up, hidden, normed_two, mid, gain_two, gated, w_out, ffn_out,
            up_weights[l],
        )

    def mixer_part(l, d_gated):
        gain_one, gain_two, ab, taps, heads, gain = small_weights[l]
        residual, normed, projected, small, gated, saved, mid, normed_two, up, hidden = kept[l]
        return mixer_backward(projected, small, taps, heads, gain, saved, d_gated)

    def project_part(l, d_mid, g_gain_two, mixed):
        gain_one, gain_two, ab, taps, heads, gain = small_weights[l]
        residual, normed, projected, small, gated, saved, mid, normed_two, up, hidden = kept[l]
        d_projected, d_small, g_taps, g_heads = mixed
        return project_backward(
            d_projected, d_small, in_weights[l], ab, normed, residual, gain_one, d_mid,
            g_gain_two, g_taps, g_heads,
        )

    d_mid, d_gated, g_gain_two, keep1, send1 = ffn_part(1, d_residual)
    arrived1 = swap_x(send1, replicas)
    mixed = mixer_part(1, d_gated)
    d_residual, keep2, send2 = project_part(1, d_mid, g_gain_two, mixed)
    d_residual, arrived1 = tie(d_residual, arrived1)
    piece1 = reduce_z(add_arrived(keep1, arrived1), replicas)
    arrived2 = swap_x(send2, replicas)
    d_mid, d_gated, g_gain_two, keep3, send3 = ffn_part(0, d_residual)
    d_gated, piece1, arrived2 = tie(d_gated, piece1, arrived2)
    piece2 = reduce_z(add_arrived(keep2, arrived2), replicas)
    arrived3 = swap_x(send3, replicas)
    mixed = mixer_part(0, d_gated)
    d_residual, keep4, send4 = project_part(0, d_mid, g_gain_two, mixed)
    d_residual, arrived3 = tie(d_residual, arrived3)
    summed3 = add_arrived(keep3, arrived3)
    final1, final2, final3, final4 = finish_all(piece1, piece2, summed3, keep4, send4, replicas)
    down_grads, out_grads, up_grads, w_in_grads, everyone = assemble(
        (final1, final2, final3, final4)
    )
    input_grad = d_residual.astype(bf16)[None]

    tables = lax.dynamic_index_in_dim(everyone, mine, 0, keepdims=False)
    sums = jnp.sum(everyone[:, :, 64:82], axis=0)
    grad_gain = lax.dynamic_slice_in_dim(
        sums[:, :16].reshape(LAYERS, 2, width), mine * shard, shard, 2
    )
    grad_out_gain = lax.dynamic_slice_in_dim(
        sums[:, 16:18].reshape(LAYERS, DV), mine * (DV // 4), DV // 4, 1
    )
    grad_a_log = tables[:, 82, 2:4]
    grad_dt = tables[:, 83, 2:4]
    taps_sum = everyone[:, :, 0:32].reshape(4, LAYERS, 4, 1024)

    def side_by_side(array):
        return jnp.moveaxis(array, 0, 2).reshape(LAYERS, 4, -1)

    conv_full = jnp.concatenate(
        [
            side_by_side(taps_sum[..., :256]),
            side_by_side(taps_sum[..., 256:512]),
            side_by_side(taps_sum[..., 512:]),
        ],
        axis=2,
    )
    grad_conv = lax.dynamic_slice_in_dim(conv_full, mine * 1024, 1024, 2)
    ab_sum = everyone[:, :, 32:64].reshape(4, LAYERS, 4, width)
    ab_sum = lax.dynamic_slice_in_dim(ab_sum, mine * shard, shard, 3)
    grad_ab = jnp.transpose(ab_sum.reshape(4, LAYERS, 2, 2, shard), (1, 4, 2, 0, 3)).reshape(
        LAYERS, shard, 2 * H
    )
    return (
        block_output,
        input_grad,
        grad_gain,
        w_in_grads,
        grad_ab,
        grad_conv,
        grad_a_log,
        grad_dt,
        grad_out_gain,
        out_grads,
        up_grads,
        down_grads,
    )


def solution(mesh):
    rows = P("rep", "grp", None)
    first = P(None, "grp")
    middle = P(None, "grp", None)
    last = P(None, None, "grp")
    in_specs = (rows, last, middle, middle, last, first, first, first, middle, middle, middle, rows)
    out_specs = (rows, rows, last, middle, middle, last, first, first, first, middle, middle, middle)
    return jax.shard_map(
        per_device, mesh=mesh, in_specs=in_specs, out_specs=out_specs, check_vma=False
    )
```

```python
from functools import partial
import math

import jax
import jax.numpy as jnp
from jax import lax
from jax.sharding import PartitionSpec as P
from jax.experimental import pallas as pl
from jax.experimental.pallas import tpu as pltpu

H = 8
DK = 128
DV = 256
FF = 2816
CONV = 4
LAYERS = 2
HK = 1024
HV = 2048
CH = 4096
CHUNK = 128

f32 = jnp.float32
bf16 = jnp.bfloat16
HIGH = lax.Precision.HIGHEST
epsilon = 1e-06
out_floor = 0.02
NN = ((1,), (0,))
NT = ((1,), (1,))
TN = ((0,), (0,))


def mm(left, right, dims=NN, precision=None):
    return lax.dot_general(
        left, right, (dims, ((), ())), precision=precision, preferred_element_type=f32
    )


def mh(left, right, dims=NN):
    return mm(left, right, dims, HIGH)


def grid_of(shape, dim):
    return lax.broadcasted_iota(jnp.int32, shape, dim)


def conv_chunk(x_ext, taps):
    return sum(x_ext[5 + j : 5 + j + CHUNK] * taps[j : j + 1] for j in range(CONV))


def decay_chunk(small, heads_ref):
    lane = grid_of(small.shape, 1)
    strength = jax.nn.sigmoid(small)
    shifted_logit = small + heads_ref[1:2, :]
    soft = jnp.maximum(shifted_logit, 0.0) + jnp.log1p(jnp.exp(-jnp.abs(shifted_logit)))
    log_decay = -jnp.exp(heads_ref[0:1, :]) * soft
    row = grid_of((CHUNK, CHUNK), 0)
    col = grid_of((CHUNK, CHUNK), 1)
    lower_ones = jnp.where(row >= col, 1.0, 0.0).astype(f32)
    cumulative = mm2(lower_ones.astype(bf16), log_decay)
    turned = jnp.where(lane < 2, strength, cumulative).T
    return strength, shifted_logit, log_decay, cumulative, turned


def head_inputs(activated, h):
    qa = activated[:, 128 * h : 128 * h + 128]
    ka = activated[:, 256 + 128 * h : 384 + 128 * h]
    va = activated[:, 512 + 256 * h : 768 + 256 * h]
    q_norm = lax.rsqrt(jnp.sum(qa * qa, axis=-1, keepdims=True) + epsilon)
    k_norm = lax.rsqrt(jnp.sum(ka * ka, axis=-1, keepdims=True) + epsilon)
    q = (qa * q_norm * (1.0 / math.sqrt(DK))).astype(bf16)
    k = (ka * k_norm).astype(bf16)
    return qa, ka, q_norm, k_norm, q, k, va.astype(bf16)


def split(x):
    high = x.astype(bf16)
    return high, (x - high.astype(f32)).astype(bf16)


def mm2(exact, right, dims=NN):
    high, low = split(right)
    return mm(exact, high, dims) + mm(exact, low, dims)


def mm3(left, right, dims=NN):
    lh, ll = split(left)
    rh, rl = split(right)
    return mm(lh, rh, dims) + (mm(lh, rl, dims) + mm(ll, rh, dims))


def mb(left, right, dims=NN):
    return mm(left.astype(bf16), right.astype(bf16), dims)


def unit_inverse(system):
    size = system.shape[0]
    row = grid_of((size, size), 0)
    col = grid_of((size, size), 1)
    eye = jnp.where(row == col, 1.0, 0.0).astype(f32)
    powers = jnp.where((row >> 2) == (col >> 2), -system, 0.0)
    square = mb(powers, powers)
    total = eye + powers
    total = total + mb(total, square)
    for bits in (2, 3, 4, 5, 6):
        joint = ((row >> (bits + 1)) == (col >> (bits + 1))) & ((row >> bits) != (col >> bits))
        link = jnp.where(joint, system, 0.0)
        total = total - mb(total, mb(link, total))
    return total


def mixer_forward_kernel(
    layer, proj_hbm, small_ref, taps_ref, heads_ref, gain_ref, *refs
):
    if layer == 0:
        up_source, in_source, *refs = refs
        *outs, up_whole, near, far = refs[:8]
        refs = refs[8:]
    else:
        up_source, *refs = refs
        *outs, up_whole = refs[:6]
        refs = refs[6:]
    proj_ref, gated_ref, start_ref, inv_ref, pseudo_ref, mixed_ref = refs[:6]
    load_sem, store_sem, halo, state, *sems = refs[6:]

    def chunk_rows(c):
        return pl.ds(pl.multiple_of(c * CHUNK, CHUNK), CHUNK)

    def load(c):
        rows = chunk_rows(c)
        return pltpu.make_async_copy(proj_hbm.at[rows], proj_ref.at[rows], load_sem.at[c])

    def stores(c):
        rows = chunk_rows(c)
        pairs = zip(refs[1:6], outs, (rows, c, c, c, rows))
        return [
            pltpu.make_async_copy(src.at[at], dst.at[at], store_sem.at[k, c])
            for k, (src, dst, at) in enumerate(pairs)
        ]

    chunks = proj_ref.shape[0] // CHUNK
    for c in range(chunks):
        load(c).start()
    ready = greet_wide(*place())
    shard = Reshard(up_source.at[layer], up_lanes, up_whole, *sems[:5])
    if layer == 0:
        quarter = Quarter(in_source.at[1], in_lanes, near, far, *sems[5:])
    ready()
    shard.start_far(0)
    shard.start_near()
    halo[...] = jnp.zeros_like(halo)
    state[...] = jnp.zeros_like(state)
    row = grid_of((CHUNK, CHUNK), 0)
    col = grid_of((CHUNK, CHUNK), 1)
    zero = jnp.zeros((CHUNK, CHUNK), f32)

    def prepare(c):
        rows = pl.ds(pl.multiple_of(c * CHUNK, CHUNK), CHUNK)
        x = proj_ref[rows, 0:1024].astype(f32)
        x_ext = jnp.concatenate([halo[...], x], axis=0)
        halo[...] = x[CHUNK - 8 :]
        convolved = conv_chunk(x_ext, taps_ref[...])
        activated = convolved * jax.nn.sigmoid(convolved)
        strength, shifted_logit, log_decay, cumulative, turned = decay_chunk(
            small_ref[rows, :], heads_ref
        )
        parts = []
        systems = []
        for h in range(2):
            qa, ka, q_norm, k_norm, q, k, v = head_inputs(activated, h)
            c_col = cumulative[:, 2 + h : 3 + h]
            c_row = turned[2 + h : 3 + h, :]
            beta_row = turned[h : h + 1, :]
            ratio = jnp.exp(jnp.where(row >= col, c_col - c_row, -1e4)) * beta_row
            systems.append(jnp.where(row > col, ratio * mm(k, k, NT), 0.0))
            mixing = (ratio * mm(q, k, NT)).astype(bf16)
            parts.append((q, k, v, c_col, mixing, strength[:, h : h + 1]))
        joint = jnp.concatenate(
            [
                jnp.concatenate([systems[0], zero], axis=1),
                jnp.concatenate([zero, systems[1]], axis=1),
            ],
            axis=0,
        )
        return parts, unit_inverse(joint)

    def advance(c, parts, inverse):
        rows = pl.ds(pl.multiple_of(c * CHUNK, CHUNK), CHUNK)
        for h in range(2):
            q, k, v, c_col, mixing, beta_col = parts[h]
            inv = inverse[128 * h : 128 * h + 128, 128 * h : 128 * h + 128]
            growth = jnp.exp(c_col)
            last = c_col[CHUNK - 1 :, :]
            before = state[h]
            start_ref[c, h] = before
            inv = inv.astype(bf16)
            inv_ref[c, h] = inv
            read = mm2(jnp.concatenate([q, k], axis=0), before)
            pseudo = mm(inv, (v.astype(f32) - growth * read[CHUNK:]).astype(bf16))
            pseudo_ref[c, h] = pseudo
            tail = jnp.exp(last - c_col) * beta_col
            state[h] = jnp.exp(last) * before + mm2(k, tail * pseudo, TN)
            mixed = growth * read[:CHUNK] + mm(mixing, pseudo.astype(bf16))
            mixed_ref[rows, 256 * h : 256 * h + 256] = mixed
            gate = proj_ref[rows, 1024 + 256 * h : 1280 + 256 * h].astype(f32)
            scale = lax.rsqrt(jnp.mean(mixed * mixed, axis=-1, keepdims=True) + out_floor)
            gated = mixed * scale * gain_ref[0:1, :] * (gate * jax.nn.sigmoid(gate))
            gated_ref[rows, 256 * h : 256 * h + 256] = gated.astype(bf16)

    def body(step, carry):
        load(step).wait()
        advance(step, *prepare(step))
        for store in stores(step):
            store.start()
        @pl.when(step == 0)
        def _():
            shard.start_far(1)
            if layer == 0:
                quarter.start_near()

        @pl.when(step == 2)
        def _():
            shard.forward(0)
            if layer == 0:
                quarter.start_quarter()

        @pl.when(step == 4)
        def _():
            shard.forward(1)

        return carry

    lax.fori_loop(0, chunks, body, 0)
    shard.wait()
    shard.finish()
    if layer == 0:
        quarter.wait_quarter()
    for c in range(chunks):
        for store in stores(c):
            store.wait()


def mixer_forward(layer, projected, small, taps, heads, gain, sources):
    tokens = projected.shape[0]
    chunks = tokens // CHUNK
    vmem = pl.BlockSpec(memory_space=pltpu.VMEM)
    spot = pl.BlockSpec(memory_space=pl.ANY)
    wholes = (jax.ShapeDtypeStruct((1024, 1536), bf16),)
    if layer == 0:
        wholes = wholes * 2 + (jax.ShapeDtypeStruct((2, PART, 1536), bf16),)
    return pl.pallas_call(
        partial(mixer_forward_kernel, layer),
        out_shape=(
            jax.ShapeDtypeStruct((tokens, 512), bf16),
            jax.ShapeDtypeStruct((chunks, 2, DK, DV), f32),
            jax.ShapeDtypeStruct((chunks, 2, CHUNK, CHUNK), bf16),
            jax.ShapeDtypeStruct((chunks, 2, CHUNK, DV), f32),
            jax.ShapeDtypeStruct((tokens, 512), f32),
        )
        + wholes,
        in_specs=[spot] + [vmem] * 4 + [spot] * len(sources),
        out_specs=(spot,) * (5 + len(wholes)),
        scratch_shapes=[
            pltpu.VMEM((tokens, 1536), bf16),
            pltpu.VMEM((tokens, 512), bf16),
            pltpu.VMEM((chunks, 2, DK, DV), f32),
            pltpu.VMEM((chunks, 2, CHUNK, CHUNK), bf16),
            pltpu.VMEM((chunks, 2, CHUNK, DV), f32),
            pltpu.VMEM((tokens, 512), f32),
            pltpu.SemaphoreType.DMA((chunks,)),
            pltpu.SemaphoreType.DMA((5, chunks)),
        ]
        + [pltpu.VMEM((8, 1024), f32), pltpu.VMEM((2, DK, DV), f32)]
        + Reshard.scratch() * len(sources),
        compiler_params=pltpu.CompilerParams(
            collective_id=8 + layer, has_side_effects=True, vmem_limit_bytes=LIMIT
        ),
        name="mixer_forward",
    )(projected, small, taps, heads, gain, *sources)


def mixer_backward_kernel(
    small_ref, taps_ref, heads_ref, gain_ref, *refs
):
    sources, refs = refs[:6], refs[6:]
    dproj_hbm, dsmall_ref, gtaps_ref, gheads_ref, *refs = refs
    held, refs = refs[:6], refs[6:]
    proj_ref, start_ref, inv_ref, pseudo_ref, mixed_ref, dgated_ref = held
    dproj_ref, load_sem, store_sem, halo, dstate = refs

    def chunk_rows(c):
        return pl.ds(pl.multiple_of(c * CHUNK, CHUNK), CHUNK)

    def load(k, c):
        at = c if k in (1, 2, 3) else chunk_rows(c)
        return pltpu.make_async_copy(sources[k].at[at], held[k].at[at], load_sem.at[k, c])

    def store(c):
        rows = chunk_rows(c)
        return pltpu.make_async_copy(dproj_ref.at[rows], dproj_hbm.at[rows], store_sem.at[c])

    halo[...] = jnp.zeros_like(halo)
    dstate[...] = jnp.zeros_like(dstate)
    gtaps_ref[...] = jnp.zeros_like(gtaps_ref)
    gheads_ref[...] = jnp.zeros_like(gheads_ref)
    row = grid_of((CHUNK, CHUNK), 0)
    col = grid_of((CHUNK, CHUNK), 1)
    lane = col
    token = grid_of((CHUNK, 1), 0)
    chunks = proj_ref.shape[0] // CHUNK
    for c in reversed(range(chunks)):
        for k in range(6):
            load(k, c).start()
    load(0, chunks - 1).wait()

    def body(step, carry):
        c = chunks - 1 - step
        for k in range(1, 6):
            load(k, c).wait()

        @pl.when(c > 0)
        def _():
            load(0, c - 1).wait()

        rows = pl.ds(pl.multiple_of(c * CHUNK, CHUNK), CHUNK)
        x = proj_ref[rows, 0:1024].astype(f32)
        before_rows = pl.ds(pl.multiple_of(jnp.maximum(c * CHUNK - 16, 0), 16), 16)
        x_before = proj_ref[before_rows, 0:1024].astype(f32)[8:]
        x_before = jnp.where(c > 0, x_before, 0.0)
        x_ext = jnp.concatenate([x_before, x], axis=0)
        convolved = conv_chunk(x_ext, taps_ref[...])
        sig = jax.nn.sigmoid(convolved)
        activated = convolved * sig
        strength, shifted_logit, log_decay, cumulative, turned = decay_chunk(
            small_ref[rows, :], heads_ref
        )
        d_strength = jnp.zeros((CHUNK, CHUNK), f32)
        d_cumulative = jnp.zeros((CHUNK, CHUNK), f32)
        d_q_parts, d_k_parts, d_v_parts = [], [], []
        gain_sum = jnp.zeros((1, DV), f32)
        for h in range(2):
            qa, ka, q_norm, k_norm, q, k, v = head_inputs(activated, h)
            cols = slice(256 * h, 256 * h + 256)
            mixed = mixed_ref[rows, cols]
            gate = proj_ref[rows, 1024 + 256 * h : 1280 + 256 * h].astype(f32)
            d_gated = dgated_ref[rows, cols].astype(f32)
            gate_sig = jax.nn.sigmoid(gate)
            gate_silu = gate * gate_sig
            scale = lax.rsqrt(jnp.mean(mixed * mixed, axis=-1, keepdims=True) + out_floor)
            scaled = mixed * scale
            gain = gain_ref[0:1, :]
            gain_sum = gain_sum + jnp.sum(d_gated * scaled * gate_silu, axis=0, keepdims=True)
            d_gate = d_gated * scaled * gain * (gate_sig * (1.0 + gate * (1.0 - gate_sig)))
            dproj_ref[rows, 1024 + 256 * h : 1280 + 256 * h] = d_gate.astype(bf16)
            d_scaled = d_gated * gain * gate_silu
            d_mixed = scale * (
                d_scaled - scaled * jnp.mean(d_scaled * scaled, axis=-1, keepdims=True)
            )
            c_col = cumulative[:, 2 + h : 3 + h]
            c_row = turned[2 + h : 3 + h, :]
            beta_row = turned[h : h + 1, :]
            beta_col = strength[:, h : h + 1]
            growth = jnp.exp(c_col)
            last = c_col[CHUNK - 1 :, :]
            ratio = jnp.exp(jnp.where(row >= col, c_col - c_row, -1e4))
            key_gram = mm(k, k, NT)
            query_gram = mm(q, k, NT)
            mixing = ratio * beta_row * query_gram
            fade = jnp.exp(last - c_col)
            tail = fade * beta_col
            start = start_ref[c, h]
            inv = inv_ref[c, h]
            pseudo = pseudo_ref[c, h]
            d_end = dstate[h]
            kf = k.astype(f32)
            qf = q.astype(f32)
            d_pseudo = mb(mixing, d_mixed, TN) + tail * mm(k, d_end.astype(bf16))
            d_right = mm2(inv, d_pseudo, TN)
            pair = jnp.concatenate([d_mixed, d_right], axis=0)
            reads = mm3(pair, jnp.concatenate([start, pseudo], axis=0), NT)
            read_q = reads[:CHUNK, :DK]
            read_k = reads[CHUNK:, :DK]
            read_u = mm3(pseudo, d_end, NT)
            d_mixing = jnp.where(row >= col, reads[:CHUNK, DK:], 0.0) * ratio
            d_system = jnp.where(row > col, -reads[CHUNK:, DK:], 0.0) * ratio
            raw = d_mixing * query_gram + d_system * key_gram
            x_pair = jnp.concatenate([d_mixing * beta_row, d_system * beta_row], axis=0)
            by_row = mm(x_pair.astype(bf16), k)
            by_col = mm(x_pair.astype(bf16), jnp.concatenate([q, k], axis=0), TN)
            d_q = growth * read_q + by_row[:CHUNK]
            d_k = by_row[CHUNK:] + by_col - growth * read_k + tail * read_u
            dstate[h] = jnp.exp(last) * d_end + mb(
                jnp.concatenate([growth * qf, -growth * kf], axis=0), pair, TN
            )
            u_dot = jnp.sum(read_u * kf, axis=-1, keepdims=True)
            col_raw = jnp.sum(raw, axis=0, keepdims=True)
            col_raw = jnp.broadcast_to(col_raw, (CHUNK, CHUNK)).T[:, 0:1]
            d_beta = col_raw + fade * u_dot
            d_cum = (
                jnp.sum(raw * beta_row, axis=-1, keepdims=True)
                - beta_col * col_raw
                + growth
                * (
                    jnp.sum(read_q * qf, axis=-1, keepdims=True)
                    - jnp.sum(read_k * kf, axis=-1, keepdims=True)
                )
                - tail * u_dot
            )
            at_last = jnp.sum(tail * u_dot, axis=0, keepdims=True) + jnp.exp(last) * jnp.sum(
                jnp.sum(start * d_end, axis=-1, keepdims=True), axis=0, keepdims=True
            )
            d_cum = d_cum + jnp.where(token == CHUNK - 1, at_last, 0.0)
            d_strength = jnp.where(lane == h, d_beta, d_strength)
            d_cumulative = jnp.where(lane == 2 + h, d_cum, d_cumulative)
            d_qn = d_q * (1.0 / math.sqrt(DK))
            qn = qa * q_norm
            kn = ka * k_norm
            d_q_parts.append(
                q_norm * (d_qn - qn * jnp.sum(d_qn * qn, axis=-1, keepdims=True))
            )
            d_k_parts.append(k_norm * (d_k - kn * jnp.sum(d_k * kn, axis=-1, keepdims=True)))
            d_v_parts.append(d_right)
        upper_ones = jnp.where(row <= col, 1.0, 0.0).astype(f32)
        d_log = mm2(upper_ones.astype(bf16), d_cumulative)
        d_shifted = d_log * (-jnp.exp(heads_ref[0:1, :])) * jax.nn.sigmoid(shifted_logit)
        d_small = jnp.where(lane < 2, d_strength * strength * (1.0 - strength), d_shifted)
        dsmall_ref[rows, :] = jnp.where(lane < 4, d_small, 0.0).astype(bf16)
        gheads_ref[0:1, :] += gain_sum
        gheads_ref[1:2, 0:128] += jnp.sum(d_log * log_decay, axis=0, keepdims=True)
        gheads_ref[2:3, 0:128] += jnp.sum(d_shifted, axis=0, keepdims=True)
        d_activated = jnp.concatenate(d_q_parts + d_k_parts + d_v_parts, axis=1)
        d_conv = d_activated * (sig * (1.0 + convolved * (1.0 - sig)))
        for j in range(CONV):
            gtaps_ref[j : j + 1, :] += jnp.sum(
                d_conv * x_ext[5 + j : 5 + j + CHUNK], axis=0, keepdims=True
            )
        d_ext = jnp.concatenate([d_conv, halo[...]], axis=0)
        d_x = sum(
            d_ext[CONV - 1 - j : CONV - 1 - j + CHUNK] * taps_ref[j : j + 1] for j in range(CONV)
        )
        halo[...] = d_conv[:8]
        dproj_ref[rows, 0:1024] = d_x.astype(bf16)
        store(c).start()
        return carry

    lax.fori_loop(0, chunks, body, 0)
    for c in range(chunks):
        store(c).wait()


def mixer_backward(projected, small, taps, heads, gain, saved, d_gated):
    tokens = projected.shape[0]
    vmem = pl.BlockSpec(memory_space=pltpu.VMEM)
    spot = pl.BlockSpec(memory_space=pl.ANY)
    held = (projected, *saved, d_gated)
    chunks = tokens // CHUNK
    return pl.pallas_call(
        mixer_backward_kernel,
        out_shape=(
            jax.ShapeDtypeStruct((tokens, 1536), bf16),
            jax.ShapeDtypeStruct((tokens, 128), bf16),
            jax.ShapeDtypeStruct((8, 1024), f32),
            jax.ShapeDtypeStruct((8, DV), f32),
        ),
        in_specs=[vmem] * 4 + [spot] * 6,
        out_specs=(spot,) + (vmem,) * 3,
        scratch_shapes=[pltpu.VMEM(array.shape, array.dtype) for array in held]
        + [
            pltpu.VMEM((tokens, 1536), bf16),
            pltpu.SemaphoreType.DMA((6, chunks)),
            pltpu.SemaphoreType.DMA((chunks,)),
        ]
        + [pltpu.VMEM((8, 1024), f32), pltpu.VMEM((2, DK, DV), f32)],
        compiler_params=pltpu.CompilerParams(vmem_limit_bytes=LIMIT),
        name="mixer_backward",
    )(small, taps, heads, gain, *held)


SUB = 128
LIMIT = 56 << 20
MESH = pl.DeviceIdType.MESH


def place():
    me = lax.axis_index("grp")
    y, c = me // 2, me % 2
    return y, c


def shard_rows(y, c, i, size):
    return pl.ds(pl.multiple_of((2 * y + c) * size + i * SUB, SUB), SUB)


def greet(y, c):
    barrier = pltpu.get_barrier_semaphore()
    for target in (2 * y + 1 - c, 2 * (1 - y) + c):
        pl.semaphore_signal(barrier, inc=1, device_id={"grp": target}, device_id_type=MESH)
    return lambda: pl.semaphore_wait(barrier, 2)


def remote(src, dst, send, recv, target):
    return pltpu.make_async_remote_copy(
        src_ref=src, dst_ref=dst, send_sem=send, recv_sem=recv,
        device_id={"grp": target}, device_id_type=MESH,
    )


class Gather:
    def __init__(self, full, send, recv, size):
        self.full, self.send, self.recv, self.size = full, send, recv, size
        self.y, self.c = place()

    def piece(self, kind, i):
        y, c = self.y, self.c
        rows = shard_rows(1 - y if kind == 2 else y, c, i, self.size)
        target = 2 * (1 - y) + c if kind == 1 else 2 * y + 1 - c
        view = self.full.at[rows]
        return remote(view, view, self.send.at[kind, i], self.recv.at[kind, i], target)

    def own(self, i):
        return shard_rows(self.y, self.c, i, self.size)

    def start(self, i):
        self.piece(0, i).start()
        self.piece(1, i).start()

    def sibling(self, i):
        self.piece(0, i).wait_recv()
        return shard_rows(self.y, 1 - self.c, i, self.size)

    def across(self, i):
        self.piece(1, i).wait_recv()
        self.piece(2, i).start()
        return shard_rows(1 - self.y, self.c, i, self.size)

    def diagonal(self, i):
        self.piece(2, i).wait_recv()
        return shard_rows(1 - self.y, 1 - self.c, i, self.size)

    def finish(self):
        for kind in range(3):
            for i in range(self.size // SUB):
                self.piece(kind, i).wait_send()


class Scatter:
    def __init__(self, out, core, keep, relay, far, send, recv, size):
        self.out, self.core, self.keep, self.relayed, self.far = out, core, keep, relay, far
        self.send, self.recv, self.size = send, recv, size
        self.y, self.c = place()

    def to_sibling(self, part, i):
        rows = pl.ds(i * SUB, SUB)
        return remote(
            self.out.at[part, rows], self.core.at[part, rows],
            self.send.at[part, i], self.recv.at[part, i], 2 * self.y + 1 - self.c,
        )

    def to_across(self, i):
        rows = pl.ds(i * SUB, SUB)
        return remote(
            self.relayed.at[rows], self.far.at[rows],
            self.send.at[2, i], self.recv.at[2, i], 2 * (1 - self.y) + self.c,
        )

    def give(self, part, i, value):
        self.out[part, i * SUB : (i + 1) * SUB, :] = value.astype(bf16)
        self.to_sibling(part, i).start()

    def hold(self, part, i, value):
        self.keep[part, i * SUB : (i + 1) * SUB, :] = value

    def relay(self, i):
        rows = slice(i * SUB, (i + 1) * SUB)
        self.to_sibling(0, i).wait_recv()
        self.relayed[rows, :] = (self.keep[0, rows, :] + self.core[0, rows, :].astype(f32)).astype(bf16)
        self.to_across(i).start()

    def total(self, i):
        rows = slice(i * SUB, (i + 1) * SUB)
        self.to_sibling(1, i).wait_recv()
        near = self.keep[1, rows, :] + self.core[1, rows, :].astype(f32)
        self.to_across(i).wait_recv()
        return near + self.far[rows, :].astype(f32)

    def finish(self):
        for i in range(self.size // SUB):
            self.to_sibling(0, i).wait_send()
            self.to_sibling(1, i).wait_send()
            self.to_across(i).wait_send()

    @staticmethod
    def scratch(size, width):
        return [
            pltpu.VMEM((2, size, width), bf16),
            pltpu.VMEM((2, size, width), bf16),
            pltpu.VMEM((2, size, width), f32),
            pltpu.VMEM((size, width), bf16),
            pltpu.VMEM((size, width), bf16),
            pltpu.SemaphoreType.DMA((3, size // SUB)),
            pltpu.SemaphoreType.DMA((3, size // SUB)),
        ]


def gather_sems(size):
    return [pltpu.SemaphoreType.DMA((3, size // SUB)), pltpu.SemaphoreType.DMA((3, size // SUB))]


def in_order(gather):
    count = gather.size // SUB
    for i in range(count):
        yield gather.own(i)
    for i in range(count):
        yield gather.sibling(i)
    for i in range(count):
        yield gather.across(i)
        yield gather.diagonal(i)


def call(kernel, out_shape, inputs, scratch, collective, name, spots=(), out_spots=()):
    vmem = pl.BlockSpec(memory_space=pltpu.VMEM)
    spot = pl.BlockSpec(memory_space=pl.ANY)
    return pl.pallas_call(
        kernel,
        out_shape=out_shape,
        in_specs=[vmem] * len(inputs) + [spot] * len(spots),
        out_specs=tuple(spot if k in out_spots else vmem for k in range(len(out_shape))),
        scratch_shapes=scratch,
        compiler_params=pltpu.CompilerParams(
            collective_id=collective, has_side_effects=True, vmem_limit_bytes=LIMIT
        ),
        cost_estimate=pl.CostEstimate(flops=1000, bytes_accessed=1000, transcendentals=0),
        name=name,
    )(*inputs, *spots)


def relative(y, c, d):
    dy, dc = d // 2, d % 2
    return 2 * (y + dy - 2 * y * dy) + c + dc - 2 * c * dc


def load_whole(src, whole, sem):
    copy = pltpu.make_async_copy(src, whole, sem)
    copy.start()
    return copy.wait


class Outgoing:
    def __init__(self, sems):
        self.sems, self.copies = sems, []

    def put(self, src, dst):
        copy = pltpu.make_async_copy(src, dst, self.sems.at[len(self.copies)])
        copy.start()
        self.copies.append(copy)

    def wait(self):
        for copy in self.copies:
            copy.wait()


def load_down(src, whole, sem):
    y, c = place()
    rows, extra = src.shape[0], whole.shape[0] - src.shape[0]
    whole[:extra, :] = jnp.zeros((extra, whole.shape[1]), bf16)
    whole[rows:, :] = jnp.zeros((extra, whole.shape[1]), bf16)
    spot = pl.ds(pl.multiple_of(extra * c, extra), rows)
    copy = pltpu.make_async_copy(src, whole.at[spot], sem)
    copy.start()
    return copy.wait


def flip(rank):
    return rank + 1 - 2 * (rank % 2)


def greet_wide(y, c):
    barrier = pltpu.get_barrier_semaphore()
    for d in range(1, 4):
        pl.semaphore_signal(
            barrier, inc=1, device_id={"grp": relative(y, c, d)}, device_id_type=MESH
        )
    pl.semaphore_signal(
        barrier, inc=1, device_id={"rep": flip(lax.axis_index("rep"))}, device_id_type=MESH
    )
    return lambda: pl.semaphore_wait(barrier, 4)


PART = 64


def in_lanes(t):
    return (
        (256 * t, 256, 0),
        (HK + 256 * t, 256, 256),
        (2 * HK + 512 * t, 512, 512),
        (CH + 512 * t, 512, 1024),
    )


def up_lanes(t):
    first = 1408 * (t // 2) + 640 * (t % 2)
    return ((first, 768, 0), (FF + first, 768, 768))


class Reshard:
    def __init__(self, source, lanes, whole, send, recv, passed, arrived, local):
        self.source, self.lanes, self.whole = source, lanes, whole
        self.send, self.recv, self.passed, self.arrived = send, recv, passed, arrived
        self.local = local
        self.y, self.c = place()
        rank = lax.axis_index("rep")
        self.x, self.other = rank % 2, flip(rank)
        self.size = source.shape[0]

    def at(self, index, offset, count):
        return pl.ds(pl.multiple_of(index * self.size + offset, PART), count)

    def pieces(self, d, q):
        y, c = self.y, self.c
        target = relative(y, c, d)
        start = 0 if d < 2 else self.size // 2 * self.x + PART * q
        count = self.size if d < 2 else PART
        copies = []
        for k, (lane, wide, to) in enumerate(self.lanes(target)):
            src = self.source.at[
                pl.ds(pl.multiple_of(start, PART), count) if d >= 2 else pl.ds(0, count),
                pl.ds(pl.multiple_of(lane, 128), wide),
            ]
            dst = self.whole.at[self.at(2 * y + c, start, count), pl.ds(to, wide)]
            if d == 0:
                copies.append(pltpu.make_async_copy(src, dst, self.local.at[k]))
            else:
                copies.append(
                    pltpu.make_async_remote_copy(
                        src_ref=src, dst_ref=dst,
                        send_sem=self.send.at[d, q, k], recv_sem=self.recv.at[d, q, k],
                        device_id={"grp": target}, device_id_type=MESH,
                    )
                )
        return copies

    def onward(self, d, q):
        source = relative(self.y, self.c, d)
        rows = self.at(source, self.size // 2 * self.x + PART * q, PART)
        return pltpu.make_async_remote_copy(
            src_ref=self.whole.at[rows], dst_ref=self.whole.at[rows],
            send_sem=self.passed.at[d - 2, q], recv_sem=self.arrived.at[d - 2, q],
            device_id={"rep": self.other}, device_id_type=MESH,
        )

    def parts(self):
        return range(self.size // 2 // PART)

    def start_far(self, q):
        for d in (2, 3):
            for copy in self.pieces(d, q):
                copy.start()

    def start_near(self):
        for copy in self.pieces(1, 0):
            copy.start()

    def start_own(self):
        for copy in self.pieces(0, 0):
            copy.start()

    def forward(self, q):
        for d in (2, 3):
            for copy in self.pieces(d, q):
                copy.wait_recv()
            self.onward(d, q).start()

    def wait_own(self):
        for copy in self.pieces(0, 0):
            copy.wait()

    def wait(self):
        for copy in self.pieces(1, 0):
            copy.wait_recv()
        for q in self.parts():
            for d in (2, 3):
                self.onward(d, q).wait_recv()

    def finish(self):
        for copy in self.pieces(1, 0):
            copy.wait_send()
        for q in self.parts():
            for d in (2, 3):
                for copy in self.pieces(d, q):
                    copy.wait_send()
                self.onward(d, q).wait_send()

    @staticmethod
    def scratch():
        dma = pltpu.SemaphoreType.DMA
        return [dma((4, 2, 4)), dma((4, 2, 4)), dma((2, 2)), dma((2, 2)), dma((4,))]


def like(*shape, dtype=f32):
    return jax.ShapeDtypeStruct(shape, dtype)


def normalise(x, gain):
    return x * lax.rsqrt(jnp.mean(x * x, axis=-1, keepdims=True) + epsilon) * gain


def normalise_back(x, gain, d_out):
    scale = lax.rsqrt(jnp.mean(x * x, axis=-1, keepdims=True) + epsilon)
    unit = x * scale
    d_unit = d_out * gain
    d_x = scale * (d_unit - unit * jnp.mean(d_unit * unit, axis=-1, keepdims=True))
    return d_x, jnp.sum(d_out * unit, axis=0, keepdims=True)


class Quarter(Reshard):
    def __init__(self, source, lanes, whole, far, *sems):
        super().__init__(source, lanes, whole, *sems)
        self.far = far
        self.z = (lax.axis_index("rep") % 8) // 2

    def quarters(self, d):
        target = relative(self.y, self.c, d)
        copies = []
        for k, (lane, wide, to) in enumerate(self.lanes(target)):
            copies.append(
                pltpu.make_async_remote_copy(
                    src_ref=self.source.at[
                        pl.ds(pl.multiple_of(PART * self.z, PART), PART),
                        pl.ds(pl.multiple_of(lane, 128), wide),
                    ],
                    dst_ref=self.far.at[d - 2, :, pl.ds(to, wide)],
                    send_sem=self.send.at[d, 0, k], recv_sem=self.recv.at[d, 0, k],
                    device_id={"grp": target}, device_id_type=MESH,
                )
            )
        return copies

    def start_quarter(self):
        for d in (2, 3):
            for copy in self.quarters(d):
                copy.start()

    def wait_quarter(self):
        for copy in self.pieces(1, 0):
            copy.wait_recv()
            copy.wait_send()
        for d in (2, 3):
            for copy in self.quarters(d):
                copy.wait_recv()
                copy.wait_send()


def load_shard(parts, whole, sems):
    y, c = place()
    copies = []

    def add(src, dst):
        copies.append(pltpu.make_async_copy(src, dst, sems.at[len(copies)]))

    if len(parts) == 1:
        add(parts[0], whole)
    else:
        raw, lanes, near, *far = parts
        size = whole.shape[0] // 4

        def block(index, count):
            return pl.ds(pl.multiple_of(index * size, size), count * size)

        own, sibling, across = block(2 * y + c, 1), block(2 * y + 1 - c, 1), block(2 - 2 * y, 2)
        for lane, wide, to in lanes(2 * y + c):
            src = raw.at[pl.ds(0, size), pl.ds(pl.multiple_of(lane, 128), wide)]
            add(src, whole.at[own, pl.ds(to, wide)])
        add(near.at[sibling], whole.at[sibling])
        if not far:
            add(near.at[across], whole.at[across])
        else:
            for z in range(4):
                for d in (2, 3):
                    at = relative(y, c, d) * size + PART * z
                    spot = pl.ds(pl.multiple_of(at, PART), PART)
                    add(far[0].at[z, d - 2], whole.at[spot])
    for copy in copies:
        copy.start()

    def wait():
        for copy in copies:
            copy.wait()

    return wait


def in_parts(parts):
    return parts if len(parts) == 1 else (parts[0].at[1], in_lanes) + tuple(parts[1:])


GAIN_AT, TAPS_AT, AB_AT, OUT_GAIN_AT, PACK_ROWS = 0, 8, 72, 136, 144


def start_kernel(
    x_ref, pack_ref, win_ref,
    normed_hbm, proj_hbm, small_ref, whole_hbm,
    gain0, gain1, gain2, gain3, taps0, taps1, ab0, ab1, out0, out1,
    everyone, ab_rows, normed_ref, proj_ref, whole_ref, out_sems, *scratch,
):
    outgoing = Outgoing(out_sems)
    size = x_ref.shape[0]
    y, c = place()
    me = 2 * y + c
    ready = greet_wide(y, c)
    shard = Reshard(win_ref.at[0], in_lanes, whole_ref, *scratch[:5])
    psend, precv = scratch[5:7]
    gather = Gather(normed_ref, *scratch[7:], size)
    everyone[me] = pack_ref[...]
    ready()

    def share(d):
        return pltpu.make_async_remote_copy(
            src_ref=pack_ref, dst_ref=everyone.at[me],
            send_sem=psend.at[d], recv_sem=precv.at[d],
            device_id={"grp": relative(y, c, d)}, device_id_type=MESH,
        )

    for d in (2, 3, 1):
        share(d).start()
    for q in shard.parts():
        shard.start_far(q)
    shard.start_near()
    shard.start_own()
    for d in (1, 2, 3):
        share(d).wait_recv()
    for k, ref in enumerate((gain0, gain1, gain2, gain3)):
        for s in range(4):
            for b in range(2):
                row = GAIN_AT + 2 * k + b
                ref[0:1, 256 * s + 128 * b : 256 * s + 128 * b + 128] = everyone[s, row : row + 1, :]
    for i in range(size // SUB):
        rows = slice(i * SUB, (i + 1) * SUB)
        normed = normalise(x_ref[rows, :].astype(f32), gain0[...])
        normed_ref[gather.own(i), :] = normed.astype(bf16)
        gather.start(i)
    for l, (taps, ab, out) in enumerate(((taps0, ab0, out0), (taps1, ab1, out1))):
        taps[...] = jnp.zeros_like(taps)
        out[...] = jnp.zeros_like(out)
        ab_rows[...] = jnp.zeros_like(ab_rows)
        for j in range(4):
            base = TAPS_AT + (4 * l + j) * 8
            for b in range(8):
                if b < 2:
                    s, row = 0, base + 2 * me + b
                elif b < 4:
                    s, row = 1, base + 2 * me + b - 2
                else:
                    s, row = 2 + y, base + 4 * c + b - 4
                taps[j : j + 1, 128 * b : 128 * b + 128] = everyone[s, pl.ds(row, 1), :]
            column = 2 * me + j if j < 2 else H + 2 * me + j - 2
            for s in range(4):
                for b in range(2):
                    row = AB_AT + (16 * l + column) * 2 + b
                    ab_rows[j : j + 1, 256 * s + 128 * b : 256 * s + 128 * b + 128] = everyone[
                        s, pl.ds(row, 1), :
                    ]
        ab[...] = ab_rows[...].T.astype(bf16)
        for s in range(4):
            out[0:1, 64 * s : 64 * s + 64] = everyone[
                s, OUT_GAIN_AT : OUT_GAIN_AT + 1, 64 * l : 64 * l + 64
            ]
    for q in shard.parts():
        shard.forward(q)
    shard.wait()
    shard.wait_own()
    outgoing.put(whole_ref, whole_hbm)
    for rows in in_order(gather):
        normed = normed_ref[rows, :]
        proj_ref[rows, :] = mm(normed, whole_ref[...]).astype(bf16)
        small_ref[rows, :] = mm(normed, ab0[...])
        outgoing.put(proj_ref.at[rows], proj_hbm.at[rows])
        outgoing.put(normed_ref.at[rows], normed_hbm.at[rows])
    gather.finish()
    outgoing.wait()
    shard.finish()
    for d in (1, 2, 3):
        share(d).wait_send()


def start(x, pack, w_in):
    size, width = x.shape
    tokens = 4 * size
    row = like(1, width)
    dma = pltpu.SemaphoreType.DMA
    return call(
        start_kernel,
        (
            like(tokens, width, dtype=bf16),
            like(tokens, 1536, dtype=bf16),
            like(tokens, 128),
            like(width, 1536, dtype=bf16),
            row, row, row, row,
            like(8, width), like(8, width),
            like(width, 128, dtype=bf16), like(width, 128, dtype=bf16),
            like(8, DV), like(8, DV),
        ),
        (x, pack),
        [
            pltpu.VMEM((4, PACK_ROWS, 128), f32),
            pltpu.VMEM((128, width), f32),
            pltpu.VMEM((tokens, width), bf16),
            pltpu.VMEM((tokens, 1536), bf16),
            pltpu.VMEM((width, 1536), bf16),
            dma((17,)),
        ]
        + Reshard.scratch()
        + [dma((4,)), dma((4,))]
        + gather_sems(size),
        1,
        "start",
        (w_in,),
        (0, 1, 3),
    )


def project_kernel(count, res_ref, gain_ref, ab_ref, *refs):
    parts, refs = refs[:count], refs[count:]
    normed_hbm, proj_hbm, small_ref, w_ref, loads, normed_ref, proj_ref, out_sems, send, recv = refs
    outgoing = Outgoing(out_sems)
    loaded = load_shard(in_parts(parts), w_ref, loads)
    size = res_ref.shape[0]
    y, c = place()
    ready = greet(y, c)
    gather = Gather(normed_ref, send, recv, size)
    for i in range(size // SUB):
        rows = slice(i * SUB, (i + 1) * SUB)
        normed_ref[gather.own(i), :] = normalise(res_ref[rows, :], gain_ref[...]).astype(bf16)
        if i == 0:
            ready()
        gather.start(i)
    loaded()
    for rows in in_order(gather):
        normed = normed_ref[rows, :]
        proj_ref[rows, :] = mm(normed, w_ref[...]).astype(bf16)
        small_ref[rows, :] = mm(normed, ab_ref[...])
        outgoing.put(proj_ref.at[rows], proj_hbm.at[rows])
        outgoing.put(normed_ref.at[rows], normed_hbm.at[rows])
    gather.finish()
    outgoing.wait()


def project(residual, gain, ab, weight):
    size, width = residual.shape
    tokens = 4 * size
    return call(
        partial(project_kernel, len(weight)),
        (like(tokens, width, dtype=bf16), like(tokens, 1536, dtype=bf16), like(tokens, 128)),
        (residual, gain, ab),
        [
            pltpu.VMEM((width, 1536), bf16),
            pltpu.SemaphoreType.DMA((13,)),
            pltpu.VMEM((tokens, width), bf16),
            pltpu.VMEM((tokens, 1536), bf16),
            pltpu.SemaphoreType.DMA((16,)),
        ]
        + gather_sems(size),
        6,
        "project",
        weight,
        (0, 1),
    )


def swiglu(up):
    gate, value = up[:, :768], up[:, 768:]
    return gate * jax.nn.sigmoid(gate) * value


def swiglu_back(up, d_hidden):
    gate, value = up[:, :768], up[:, 768:]
    sig = jax.nn.sigmoid(gate)
    d_gate = d_hidden * value * (sig * (1.0 + gate * (1.0 - sig)))
    return jnp.concatenate([d_gate, d_hidden * gate * sig], axis=1)


def ffn_forward_kernel(
    layer, gated_ref, res_ref, gain_ref, raw_ref, down_ref, ffn_ref, whole_ref,
    mid_hbm, normed_hbm, up_hbm, hidden_hbm, out_ref,
    wup_ref, wdown_ref, wout_ref, loads, shard_loads,
    mid_ref, normed_ref, up_ref, hidden_ref, out_sems, *scratch,
):
    outgoing = Outgoing(out_sems)
    loaded_out = load_whole(raw_ref.at[layer], wout_ref, loads.at[2])
    loaded = load_shard((ffn_ref.at[layer], up_lanes, whole_ref), wup_ref, shard_loads)
    loaded_down = load_down(down_ref.at[layer], wdown_ref, loads.at[1])
    size = res_ref.shape[0]
    count = size // SUB
    y, c = place()
    ready = greet(y, c)
    first = Scatter(*scratch[:7], size)
    second = Scatter(*scratch[7:14], size)
    gather = Gather(normed_ref, *scratch[14:], size)

    loaded_out()

    def branch(rows):
        return mm(gated_ref[rows, :], wout_ref[...])

    for part in range(2):
        yy = 1 - y if part == 0 else y
        for i in range(count):
            value = branch(shard_rows(yy, 1 - c, i, size))
            if part == 0 and i == 0:
                ready()
            first.give(part, i, value)
            first.hold(part, i, branch(shard_rows(yy, c, i, size)))
            if part == 0:
                first.relay(i)
    for i in range(count):
        rows = slice(i * SUB, (i + 1) * SUB)
        mid = res_ref[rows, :] + first.total(i)
        mid_ref[rows, :] = mid
        normed_ref[gather.own(i), :] = normalise(mid, gain_ref[...]).astype(bf16)
        gather.start(i)

    def feed(rows):
        up = mm(normed_ref[rows, :], wup_ref[...])
        up_ref[rows, :] = up.astype(bf16)
        hidden = swiglu(up).astype(bf16)
        hidden_ref[rows, :] = hidden
        outgoing.put(normed_ref.at[rows], normed_hbm.at[rows])
        outgoing.put(up_ref.at[rows], up_hbm.at[rows])
        outgoing.put(hidden_ref.at[rows], hidden_hbm.at[rows])
        return mm(hidden, wdown_ref[...])

    outgoing.put(mid_ref, mid_hbm)
    loaded()
    loaded_down()
    for i in range(count):
        second.hold(1, i, feed(gather.own(i)))
    for i in range(count):
        second.give(1, i, feed(gather.sibling(i)))
    for i in range(count):
        near = gather.across(i)
        second.hold(0, i, feed(near))
        second.give(0, i, feed(gather.diagonal(i)))
        second.relay(i)
    for i in range(count):
        rows = slice(i * SUB, (i + 1) * SUB)
        out_ref[rows, :] = mid_ref[rows, :] + second.total(i)
    first.finish()
    second.finish()
    gather.finish()
    outgoing.wait()


def ffn_forward(layer, gated, residual, gain, w_out, w_down, w_up):
    size, width = residual.shape
    tokens = 4 * size
    return call(
        partial(ffn_forward_kernel, layer),
        (
            like(size, width),
            like(tokens, width, dtype=bf16),
            like(tokens, 1536, dtype=bf16),
            like(tokens, 768, dtype=bf16),
            like(size, width),
        ),
        (gated, residual, gain),
        [
            pltpu.VMEM((width, 1536), bf16),
            pltpu.VMEM((768, width), bf16),
            pltpu.VMEM((512, width), bf16),
            pltpu.SemaphoreType.DMA((3,)),
            pltpu.SemaphoreType.DMA((13,)),
            pltpu.VMEM((size, width), f32),
            pltpu.VMEM((tokens, width), bf16),
            pltpu.VMEM((tokens, 1536), bf16),
            pltpu.VMEM((tokens, 768), bf16),
            pltpu.SemaphoreType.DMA((25,)),
        ]
        + Scatter.scratch(size, width)
        + Scatter.scratch(size, width)
        + gather_sems(size),
        (2, 12)[layer],
        "ffn_forward",
        (w_out, w_down) + w_up,
        (0, 1, 2, 3),
    )


class Owners:
    def __init__(self, keep, send):
        self.keep, self.send = keep, send
        self.x = lax.axis_index("rep") % 2

    def put(self, r, store):
        @pl.when(self.x == r % 2)
        def _():
            store(self.keep.at[r // 2])

        @pl.when(self.x != r % 2)
        def _():
            store(self.send.at[r // 2])


def store_columns(buf, value, at):
    rows = pl.ds(at, value.shape[0])
    for r in range(8):

        def store(ref):
            ref[rows, :] = value[:, 128 * r : 128 * r + 128].astype(bf16)

        buf.put(r, store)


def store_up(buf, staged, d, c):
    own_half = (grid_of((32, 128), 1) >> 6) == c
    for r in range(8):
        rows = slice(32 * r, 32 * r + 32)

        def tile(side, j):
            lane = pl.multiple_of(768 * side + 128 * j, 128)
            return staged[rows, pl.ds(lane, 128)]

        tiles = [tile(j // 5, j % 5 + c) for j in range(10)]
        turned = pltpu.roll(tile(1, 5 - 5 * c), 64, 1)
        tiles.append(jnp.where(own_half, tile(0, 5 - 5 * c), turned))

        def store(ref):
            for j, value in enumerate(tiles):
                at = UP_AT + (d * 11 + j) * 32
                ref[at : at + 32, :] = value.astype(bf16)

        buf.put(r, store)


def store_rows(buf, value, d, base):
    blocks = value.shape[1] // 128
    for r in range(8):

        def store(ref):
            for j in range(blocks):
                at = base + (d * blocks + j) * 32
                ref[at : at + 32, :] = value[
                    32 * r : 32 * r + 32, 128 * j : 128 * j + 128
                ].astype(bf16)

        buf.put(r, store)


UP_AT, DOWN_AT, OUT_AT, FFN_ROWS = 0, 1408, 2112, 2624
SMALL_AT, IN_ROWS = 1536, 1552


def ffn_backward_kernel(
    layer, dres_ref, gain_ref, up_hbm, hidden_hbm, normed_hbm, mid_hbm, gated_hbm,
    raw_ref, down_ref, ffn_ref, whole_ref,
    dmid_ref, dgated_hbm, ggain_ref, keep_hbm, send_hbm,
    wup_ref, wdown_ref, wout_ref, loads, shard_loads, ddown_ref, dup_ref, dbranch_ref, staged,
    up_ref, hidden_ref, normed_ref, mid_ref, gated_ref, dgated_ref, keep_ref, send_ref,
    late_sems, out_sems, *scratch,
):
    buf_ref = Owners(keep_ref, send_ref)
    outgoing = Outgoing(out_sems)
    loaded_out = load_whole(raw_ref.at[layer], wout_ref, loads.at[2])
    loaded = load_shard((ffn_ref.at[layer], up_lanes, whole_ref), wup_ref, shard_loads)
    loaded_down = load_down(down_ref.at[layer], wdown_ref, loads.at[1])
    size = dres_ref.shape[0]
    count = size // SUB
    y, c = place()
    ready = greet(y, c)
    first = Gather(ddown_ref, *scratch[:2], size)
    second = Gather(dbranch_ref, *scratch[2:4], size)
    scatter = Scatter(*scratch[4:], size)
    late = [
        load_whole(src, dst, late_sems.at[k])
        for k, (src, dst) in enumerate(
            (
                (up_hbm, up_ref),
                (hidden_hbm, hidden_ref),
                (mid_hbm, mid_ref),
                (normed_hbm, normed_ref),
                (gated_hbm, gated_ref),
            )
        )
    ]
    for i in range(count):
        ddown_ref[first.own(i), :] = dres_ref[i * SUB : (i + 1) * SUB, :].astype(bf16)
        if i == 0:
            ready()
        first.start(i)

    def feed(rows):
        d_hidden = mm(ddown_ref[rows, :], wdown_ref[...], NT)
        d_up = swiglu_back(up_ref[rows, :].astype(f32), d_hidden).astype(bf16)
        dup_ref[rows, :] = d_up
        return mm(d_up, wup_ref[...], NT)

    loaded()
    loaded_down()
    late[0]()
    for i in range(count):
        scatter.hold(1, i, feed(first.own(i)))
    for i in range(count):
        scatter.give(1, i, feed(first.sibling(i)))
    for i in range(count):
        near = first.across(i)
        scatter.hold(0, i, feed(near))
        scatter.give(0, i, feed(first.diagonal(i)))
        scatter.relay(i)
    late[1]()
    for m in range(6):
        value = mm(hidden_ref[:, 128 * m : 128 * m + 128], ddown_ref[...], TN)
        store_columns(buf_ref, value, pl.multiple_of(DOWN_AT + 128 * m - 64 * c, 64))
    ggain_ref[...] = jnp.zeros_like(ggain_ref)
    late[2]()
    for i in range(count):
        rows = slice(i * SUB, (i + 1) * SUB)
        d_norm, g_gain = normalise_back(mid_ref[rows, :], gain_ref[...], scatter.total(i))
        d_mid = dres_ref[rows, :] + d_norm
        dmid_ref[rows, :] = d_mid
        ggain_ref[0:1, :] += g_gain
        dbranch_ref[second.own(i), :] = d_mid.astype(bf16)
        second.start(i)
    late[3]()
    for d in range(4):
        lanes = pl.ds(pl.multiple_of(relative(y, c, d) * 256, 256), 256)
        staged[...] = mm(normed_ref[:, lanes], dup_ref[...], TN)
        store_up(buf_ref, staged, d, c)
    for keep, hbm in ((keep_ref, keep_hbm), (send_ref, send_hbm)):
        rows = pl.ds(0, OUT_AT)
        outgoing.put(keep.at[:, rows], hbm.at[:, rows])
    loaded_out()
    for rows in in_order(second):
        dgated_ref[rows, :] = mm(dbranch_ref[rows, :], wout_ref[...], NT).astype(bf16)
    outgoing.put(dgated_ref, dgated_hbm)
    late[4]()
    for m in range(4):
        value = mm(gated_ref[:, 128 * m : 128 * m + 128], dbranch_ref[...], TN)
        store_columns(buf_ref, value, OUT_AT + 128 * m)
    for keep, hbm in ((keep_ref, keep_hbm), (send_ref, send_hbm)):
        rows = pl.ds(OUT_AT, FFN_ROWS - OUT_AT)
        outgoing.put(keep.at[:, rows], hbm.at[:, rows])
    first.finish()
    second.finish()
    scatter.finish()
    outgoing.wait()


def ffn_backward(layer, d_res, up, hidden, normed, mid, gain, gated, w_out, w_down, w_up):
    size, width = d_res.shape
    tokens = 4 * size
    return call(
        partial(ffn_backward_kernel, layer),
        (
            like(size, width),
            like(tokens, 512, dtype=bf16),
            like(8, width),
            like(4, FFN_ROWS, 128, dtype=bf16),
            like(4, FFN_ROWS, 128, dtype=bf16),
        ),
        (d_res, gain),
        [
            pltpu.VMEM((width, 1536), bf16),
            pltpu.VMEM((768, width), bf16),
            pltpu.VMEM((512, width), bf16),
            pltpu.SemaphoreType.DMA((3,)),
            pltpu.SemaphoreType.DMA((13,)),
            pltpu.VMEM((tokens, width), bf16),
            pltpu.VMEM((tokens, 1536), bf16),
            pltpu.VMEM((tokens, width), bf16),
            pltpu.VMEM((256, 1536), f32),
        ]
        + [pltpu.VMEM(array.shape, array.dtype) for array in (up, hidden, normed, mid, gated, gated)]
        + [pltpu.VMEM((4, FFN_ROWS, 128), bf16)] * 2
        + [pltpu.SemaphoreType.DMA((5,)), pltpu.SemaphoreType.DMA((5,))]
        + gather_sems(size)
        + gather_sems(size)
        + Scatter.scratch(size, width),
        (3, 13)[layer],
        "ffn_backward",
        (up, hidden, normed, mid, gated, w_out, w_down) + w_up,
        (1, 3, 4),
    )


def project_backward_kernel(
    parts, dproj_ref, dsmall_ref, ab_ref, gain_ref, gtwo_ref, gtaps_ref, gheads_ref, *refs
):
    normed_hbm, res_hbm, dmid_hbm, *refs = refs
    parts, refs = refs[:parts], refs[parts:]
    dres_ref, keep_hbm, send_hbm, w_ref, loads, table, *refs = refs
    normed_ref, res_ref, dmid_ref, keep_ref, send_ref, late_sems, out_sems, *scratch = refs
    buf_ref = Owners(keep_ref, send_ref)
    outgoing = Outgoing(out_sems)
    loaded = load_shard(in_parts(parts), w_ref, loads)
    late = [
        load_whole(src, dst, late_sems.at[k])
        for k, (src, dst) in enumerate(
            ((normed_hbm, normed_ref), (res_hbm, res_ref), (dmid_hbm, dmid_ref))
        )
    ]
    size = res_ref.shape[0]
    count = size // SUB
    y, c = place()
    ready = greet(y, c)
    scatter = Scatter(*scratch, size)

    def back(rows):
        return mm(dproj_ref[rows, :], w_ref[...], NT) + mm(dsmall_ref[rows, :], ab_ref[...], NT)

    def weight_grad(d):
        lanes = pl.ds(pl.multiple_of(relative(y, c, d) * 256, 256), 256)
        value = mm(normed_ref[:, lanes], dproj_ref[...], TN)
        store_rows(buf_ref, value, d, 0)

    loaded()
    for part in range(2):
        yy = 1 - y if part == 0 else y
        for i in range(count):
            value = back(shard_rows(yy, 1 - c, i, size))
            if part == 0 and i == 0:
                ready()
            scatter.give(part, i, value)
            scatter.hold(part, i, back(shard_rows(yy, c, i, size)))
            if part == 0:
                scatter.relay(i)
    late[0]()
    for d in range(4):
        weight_grad(d)
    for keep, hbm in ((keep_ref, keep_hbm), (send_ref, send_hbm)):
        rows = pl.ds(0, SMALL_AT)
        outgoing.put(keep.at[:, rows], hbm.at[:, rows])
    ab_grad = mm(dsmall_ref[...], normed_ref[...], TN)
    table[...] = jnp.zeros_like(table)
    for k in range(8):
        lanes = slice(128 * k, 128 * k + 128)
        for j in range(4):
            table[8 * j + k : 8 * j + k + 1, :] = gtaps_ref[j : j + 1, lanes]
            table[32 + 8 * j + k : 33 + 8 * j + k, :] = ab_grad[j : j + 1, lanes]
        table[72 + k : 73 + k, :] = gtwo_ref[0:1, lanes]
    table[80:81, :] = gheads_ref[0:1, 0:128]
    table[81:82, :] = gheads_ref[0:1, 128:256]
    table[82:83, :] = gheads_ref[1:2, 0:128]
    table[83:84, :] = gheads_ref[2:3, 0:128]
    gain_sum = jnp.zeros((1, res_ref.shape[1]), f32)
    late[1]()
    late[2]()
    for i in range(count):
        rows = slice(i * SUB, (i + 1) * SUB)
        d_norm, g_gain = normalise_back(res_ref[rows, :], gain_ref[...], scatter.total(i))
        dres_ref[rows, :] = dmid_ref[rows, :] + d_norm
        gain_sum = gain_sum + g_gain
    for k in range(8):
        table[64 + k : 65 + k, :] = gain_sum[:, 128 * k : 128 * k + 128]
    for r in range(8):

        def store(ref):
            ref[SMALL_AT:IN_ROWS, :] = table[16 * r : 16 * r + 16, :].astype(bf16)

        buf_ref.put(r, store)
    for keep, hbm in ((keep_ref, keep_hbm), (send_ref, send_hbm)):
        rows = pl.ds(SMALL_AT, IN_ROWS - SMALL_AT)
        outgoing.put(keep.at[:, rows], hbm.at[:, rows])
    scatter.finish()
    outgoing.wait()


def project_backward(d_proj, d_small, weight, ab, normed, residual, gain, d_mid, g_two, g_taps, g_heads):
    size, width = residual.shape
    return call(
        partial(project_backward_kernel, len(weight)),
        (like(size, width),) + (like(4, IN_ROWS, 128, dtype=bf16),) * 2,
        (d_proj, d_small, ab, gain, g_two, g_taps, g_heads),
        [
            pltpu.VMEM((width, 1536), bf16),
            pltpu.SemaphoreType.DMA((13,)),
            pltpu.VMEM((128, 128), f32),
        ]
        + [pltpu.VMEM(array.shape, array.dtype) for array in (normed, residual, d_mid)]
        + [pltpu.VMEM((4, IN_ROWS, 128), bf16)] * 2
        + [pltpu.SemaphoreType.DMA((3,)), pltpu.SemaphoreType.DMA((4,))]
        + Scatter.scratch(size, width),
        4 if len(weight) == 1 else 7,
        "project_backward",
        (normed, residual, d_mid) + tuple(weight),
        (1, 2),
    )


def assemble_kernel(
    f1, f2, f3, f4, last_ref, grad_ref,
    down_ref, out_ref, up_ref, in_ref, table_ref, block_ref, input_ref,
    p1, p2, p3, p4, down, out, up, whole, loads, stores,
):
    y, c = place()
    copies = [
        pltpu.make_async_copy(src, dst, loads.at[k])
        for k, (src, dst) in enumerate(((f1, p1), (f2, p2), (f3, p3), (f4, p4)))
    ]
    for copy in copies:
        copy.start()
    block_ref[...] = last_ref[...].astype(bf16)
    input_ref[...] = grad_ref[...].astype(bf16)
    left = grid_of((32, 128), 1) < 64

    def ffn(layer, pieces):
        def up_rows(r, carry):
            rows = pl.ds(pl.multiple_of(32 * r, 32), 32)
            for m in range(2):
                tiles = []
                for s in (2 * m, 2 * m + 1):
                    at = UP_AT + offset_of(y, c, s) * 352
                    tiles.append(
                        [
                            pieces[r, pl.ds(pl.multiple_of(at + 32 * j, 32), 32), :].astype(f32)
                            for j in range(11)
                        ]
                    )
                even, odd = tiles
                middle = (
                    jnp.where(left, even[10], odd[10]),
                    pltpu.roll(jnp.where(left, odd[10], even[10]), 64, 1),
                )
                for side in range(2):
                    part = slice(5 * side, 5 * side + 5)
                    base = FF * side + 1408 * m
                    for j, tile in enumerate(even[part] + [middle[side]] + odd[part]):
                        up[layer, rows, base + 128 * j : base + 128 * j + 128] = tile
            return carry

        lax.fori_loop(0, 8, up_rows, 0)
        done = [pltpu.make_async_copy(up.at[layer], up_ref.at[layer], stores.at[layer, 0])]
        done[0].start()
        for r in range(8):
            lanes = slice(128 * r, 128 * r + 128)
            down[layer, :, lanes] = pieces[r, DOWN_AT:OUT_AT, :].astype(f32)
            out[layer, :, lanes] = pieces[r, OUT_AT:FFN_ROWS, :].astype(f32)
        done.append(pltpu.make_async_copy(down.at[layer], down_ref.at[layer], stores.at[layer, 1]))
        done.append(pltpu.make_async_copy(out.at[layer], out_ref.at[layer], stores.at[layer, 2]))
        done[1].start()
        done[2].start()
        return done

    def projection(layer, pieces):
        def in_rows(r, carry):
            rows = pl.ds(pl.multiple_of(32 * r, 32), 32)
            for s in range(4):
                at = offset_of(y, c, s) * 384
                for lane, wide, to in in_lanes(s):
                    for k in range(wide // 128):
                        j = to // 128 + k
                        tile = pieces[r, pl.ds(pl.multiple_of(at + 32 * j, 32), 32), :]
                        column = lane + 128 * k
                        whole[layer, rows, column : column + 128] = tile.astype(f32)
            return carry

        lax.fori_loop(0, 8, in_rows, 0)
        done = pltpu.make_async_copy(whole.at[layer], in_ref.at[layer], stores.at[layer, 3])
        done.start()
        for s in range(4):
            at = pl.ds(pl.multiple_of(SMALL_AT + 16 * offset_of(y, c, s), 16), 16)
            for r in range(8):
                table_ref[s, layer, 16 * r : 16 * r + 16, :] = pieces[r, at, :].astype(f32)
        return [done]

    waiting = []
    copies[0].wait()
    waiting += ffn(1, p1)
    copies[1].wait()
    waiting += projection(1, p2)
    copies[2].wait()
    waiting += ffn(0, p3)
    copies[3].wait()
    waiting += projection(0, p4)
    for store in waiting:
        store.wait()


def offset_of(y, c, s):
    sy, sc = s // 2, s % 2
    return 2 * (y + sy - 2 * y * sy) + c + sc - 2 * c * sc


def assemble(finals, last, grad):
    spot = pl.BlockSpec(memory_space=pl.ANY)
    vmem = pl.BlockSpec(memory_space=pltpu.VMEM)
    shapes = [(LAYERS, 704, 1024), (LAYERS, 512, 1024), (LAYERS, 256, 2 * FF), (LAYERS, 256, CH + HV)]
    return pl.pallas_call(
        assemble_kernel,
        out_shape=tuple(like(*shape) for shape in shapes)
        + (like(4, LAYERS, 128, 128),)
        + (like(*last.shape, dtype=bf16),) * 2,
        in_specs=[spot] * 4 + [vmem] * 2,
        out_specs=(spot,) * 4 + (vmem,) * 3,
        scratch_shapes=[pltpu.VMEM(final.shape, bf16) for final in finals]
        + [pltpu.VMEM(shape, f32) for shape in shapes]
        + [pltpu.SemaphoreType.DMA((4,)), pltpu.SemaphoreType.DMA((2, 4))],
        compiler_params=pltpu.CompilerParams(vmem_limit_bytes=LIMIT),
        name="assemble",
    )(*finals, last, grad)


FFN_MOVE, IN_MOVE = (UP_AT, 352), (0, 384)
GATHERED_ROWS = SMALL_AT + 4 * 16


def add_into(dst, left, right):
    dst[...] = (left[...].astype(f32) + right[...].astype(f32)).astype(bf16)


class Group:
    def __init__(self, number, piece, moved, final, move, sems, x_first=False):
        self.number, self.piece, self.moved, self.final = number, piece, moved, final
        self.at, self.part = move
        self.send, self.recv, self.local = sems
        self.x_first = x_first
        rank = lax.axis_index("rep")
        self.rank, self.x, self.z = rank, rank % 2, (rank % 8) // 2
        self.y, self.c = place()
        self.extra = moved.shape[0] > piece.shape[0]

    def swaps(self, d):
        target = relative(self.y, self.c, d)
        rows = pl.ds(self.at + d * self.part, self.part)
        spans = [(rows, rows, d)]
        if self.extra:
            spans.append((pl.ds(SMALL_AT, 16), pl.ds(SMALL_AT + 16 * d, 16), 20 + d))
        return [
            pltpu.make_async_remote_copy(
                src_ref=self.piece.at[src], dst_ref=self.moved.at[dst],
                send_sem=self.send.at[self.number, k], recv_sem=self.recv.at[self.number, k],
                device_id={"grp": target}, device_id_type=MESH,
            )
            for src, dst, k in spans
        ]

    def start_swap(self):
        for d in range(1, 4):
            for copy in self.swaps(d):
                copy.start()
        first = self.at + self.part
        self.moved[0:first, :] = self.piece[0:first, :]
        rest, last = self.at + 4 * self.part, self.piece.shape[0]
        if rest < last:
            self.moved[rest:last, :] = self.piece[rest:last, :]

    def wait_swap(self):
        for d in range(1, 4):
            for copy in self.swaps(d):
                copy.wait_recv()

    def owner(self, source_z, which):
        return 2 * source_z + (self.x if which == 0 else 1 - self.x)

    def move(self, step, source_z, kind, which=0):
        owner = self.owner(source_z, which)
        src = self.moved if step == 0 and which == 0 else self.final.at[owner]
        number = self.number if which == 0 else 4
        slot = 4 + 4 * kind + step
        return pltpu.make_async_remote_copy(
            src_ref=src, dst_ref=self.final.at[owner],
            send_sem=self.send.at[number, slot], recv_sem=self.recv.at[number, slot],
            device_id={"rep": self.rank + 2 - 4 * kind}, device_id_type=MESH,
        )

    def x_move(self, step, source_z):
        owner = self.owner(source_z, 0)
        src = self.moved if step == 0 else self.final.at[owner]
        return pltpu.make_async_remote_copy(
            src_ref=src, dst_ref=self.final.at[owner],
            send_sem=self.send.at[self.number, 12 + step + 3],
            recv_sem=self.recv.at[self.number, 12 + source_z],
            device_id={"rep": flip(self.rank)}, device_id_type=MESH,
        )

    def own_copy(self):
        return pltpu.make_async_copy(
            self.moved, self.final.at[self.owner(self.z, 0)], self.local.at[self.number]
        )

    def both_ways(self, which, act):
        @pl.when(self.z < 3)
        def _():
            act(self.move(0, self.z, 0, which))

        @pl.when(self.z > 0)
        def _():
            act(self.move(0, self.z, 1, which))

    def begin(self):
        self.both_ways(0, lambda copy: copy.start())
        self.x_move(0, self.z).start()
        self.own_copy().start()

    def begin_other(self):
        self.x_move(0, self.z).wait_recv()
        self.both_ways(1, lambda copy: copy.start())

    def passes(self, k, which, arrive, onward):
        z = self.z

        @pl.when(z >= k)
        def _():
            arrive(k, z - k, 0)

            @pl.when(z < 3)
            def _():
                onward(self.move(k, z - k, 0, which))

        @pl.when(z + k <= 3)
        def _():
            arrive(-k, z + k, 1)

            @pl.when(z > 0)
            def _():
                onward(self.move(k, z + k, 1, which))

    def relay(self, k, which=0):
        def arrive(step, source, kind):
            self.move(abs(step) - 1, source, kind, which).wait_recv()
            if not self.x_first:
                self.x_move(step, source).start()

        self.passes(k, which, arrive, lambda copy: copy.start())

    def finish(self):
        for which in range(2 if self.x_first else 1):

            def arrive(step, source, kind):
                if not self.x_first:
                    self.x_move(step, source).wait_send()

            for k in range(1, 4):
                self.passes(k, which, arrive, lambda copy: copy.wait_send())
            self.both_ways(which, lambda copy: copy.wait_send())
        self.x_move(0, self.z).wait_send()
        if not self.x_first:
            for source in range(4):
                self.x_move(0, source).wait_recv()
        self.own_copy().wait()
        for d in range(1, 4):
            for copy in self.swaps(d):
                copy.wait_send()


class Line:
    def __init__(self, values, right, left, send, recv):
        self.values, self.right, self.left = values, right, left
        self.send, self.recv = send, recv
        self.rank = lax.axis_index("rep")
        self.z = (self.rank % 8) // 2

    def go(self, o, toward):
        land = self.right if toward == 0 else self.left
        return pltpu.make_async_remote_copy(
            src_ref=self.values.at[o], dst_ref=land.at[o],
            send_sem=self.send.at[toward, o], recv_sem=self.recv.at[toward, o],
            device_id={"rep": self.rank + 2 - 4 * toward}, device_id_type=MESH,
        )

    def edge(self, step, act):
        @pl.when(self.z == 0)
        def _():
            act(self.go(3 - step, 0))

        @pl.when(self.z == 3)
        def _():
            act(self.go(step, 1))

    def start_edge(self, step):
        if step > 0:
            self.edge(step - 1, lambda copy: copy.wait_send())
        self.edge(step, lambda copy: copy.start())

    def inner(self, step):
        z, o = self.z, 3 - step

        @pl.when((z > 0) & (z < o))
        def _():
            self.go(o, 0).wait_recv()
            add_into(self.values.at[o], self.values.at[o], self.right.at[o])
            self.go(o, 0).start()

        @pl.when((z < 3) & (z > step))
        def _():
            self.go(step, 1).wait_recv()
            add_into(self.values.at[step], self.values.at[step], self.left.at[step])
            self.go(step, 1).start()

    def total(self, out):
        z = self.z
        for o in range(4):

            @pl.when(z == o)
            def _():
                value = self.values[o].astype(f32)
                if o > 0:
                    self.go(o, 0).wait_recv()
                    value = value + self.right[o].astype(f32)
                if o < 3:
                    self.go(o, 1).wait_recv()
                    value = value + self.left[o].astype(f32)
                out[...] = value.astype(bf16)

    def finish(self):
        self.edge(2, lambda copy: copy.wait_send())
        for o in range(4):

            @pl.when((self.z > 0) & (self.z < o))
            def _():
                self.go(o, 0).wait_send()

            @pl.when((self.z < 3) & (self.z > o))
            def _():
                self.go(o, 1).wait_send()


def finish_kernel(
    p1, p2, k3, a3, k4, b4, f1, f2, f3, f4,
    q1, q2, q3, q4, e1, e2, e3, e4, v3, x3, r3, l3, v4, x4, r4, l4,
    send, recv, local, send3, recv3, send4, recv4, send5, recv5, loads,
):
    rank = lax.axis_index("rep")
    x, z = rank % 2, (rank % 8) // 2
    y, c = place()
    loaded = [
        pltpu.make_async_copy(p1, q1, loads.at[0]),
        pltpu.make_async_copy(p2, q2, loads.at[1]),
        pltpu.make_async_copy(k3, v3, loads.at[2]),
        pltpu.make_async_copy(k4, v4, loads.at[3]),
        pltpu.make_async_copy(a3, x3, loads.at[4]),
    ]
    for load in loaded:
        load.start()
    barrier = pltpu.get_barrier_semaphore()
    pl.semaphore_signal(
        barrier, inc=1, device_id={"rep": rank + 1 - 2 * x}, device_id_type=MESH
    )
    for d in range(1, 4):
        dy, dc = d // 2, d % 2
        target = 2 * (y + dy - 2 * y * dy) + c + dc - 2 * c * dc
        pl.semaphore_signal(barrier, inc=1, device_id={"grp": target}, device_id_type=MESH)

    @pl.when(z > 0)
    def _():
        pl.semaphore_signal(barrier, inc=1, device_id={"rep": rank - 2}, device_id_type=MESH)

    @pl.when(z < 3)
    def _():
        pl.semaphore_signal(barrier, inc=1, device_id={"rep": rank + 2}, device_id_type=MESH)

    @pl.when((z > 0) & (z < 3))
    def _():
        pl.semaphore_wait(barrier, 6)

    @pl.when((z == 0) | (z == 3))
    def _():
        pl.semaphore_wait(barrier, 5)

    def halves(o):
        return pltpu.make_async_remote_copy(
            src_ref=b4.at[o], dst_ref=x4.at[o], send_sem=send5.at[o], recv_sem=recv5.at[o],
            device_id={"rep": rank + 1 - 2 * x}, device_id_type=MESH,
        )

    for o in (3, 0, 2, 1):
        halves(o).start()
    sems = (send, recv, local)

    def merge(*owners):
        for o in owners:
            add_into(v3.at[o], v3.at[o], x3.at[o])

    def arrive(*owners):
        for o in owners:
            halves(o).wait_recv()
            add_into(v4.at[o], v4.at[o], x4.at[o])

    g1 = Group(0, q1, e1, f1, FFN_MOVE, sems)
    g2 = Group(1, q2, e2, f2, IN_MOVE, sems)
    g3 = Group(2, q3, e3, f3, FFN_MOVE, sems)
    g4 = Group(3, q4, e4, f4, IN_MOVE, sems)
    line3 = Line(v3, r3, l3, send3, recv3)
    line4 = Line(v4, r4, l4, send4, recv4)
    loaded[0].wait()
    g1.start_swap()
    loaded[1].wait()
    g2.start_swap()
    g1.wait_swap()
    g1.begin()
    loaded[3].wait()
    arrive(3, 0)
    loaded[2].wait()
    loaded[4].wait()
    merge(3, 0)
    line3.start_edge(0)
    g2.wait_swap()
    g2.begin()
    merge(2, 1)
    line3.start_edge(1)
    g1.relay(1)
    line3.inner(0)
    line3.inner(1)
    line4.start_edge(0)
    g2.relay(1)
    g1.relay(2)
    line3.start_edge(2)
    arrive(2, 1)
    line3.total(q3)
    g3.start_swap()
    g2.relay(2)
    g3.wait_swap()
    g3.begin()
    line4.inner(0)
    line4.start_edge(1)
    line4.inner(1)
    line4.start_edge(2)
    g2.relay(3)
    g1.relay(3)
    g3.relay(1)
    line4.total(q4)
    g4.start_swap()
    g4.wait_swap()
    g4.begin()
    g3.relay(2)
    g4.relay(1)
    g4.relay(2)
    g3.relay(3)
    g4.relay(3)
    for group in (g1, g2, g3, g4):
        group.finish()
    line3.finish()
    line4.finish()
    for o in range(4):
        halves(o).wait_send()


def finish_reduction(p1, p2, k3, a3, k4, b4):
    spot = pl.BlockSpec(memory_space=pl.ANY)
    big, small = p1.shape, p2.shape
    wide = (GATHERED_ROWS, 128)
    dma = pltpu.SemaphoreType.DMA
    return pl.pallas_call(
        finish_kernel,
        out_shape=tuple(like(8, *shape, dtype=bf16) for shape in (big, wide, big, wide)),
        in_specs=[spot] * 6,
        out_specs=(spot,) * 4,
        scratch_shapes=[
            pltpu.VMEM(shape, bf16)
            for shape in [big, small] * 2 + [big, wide] * 2
            + [(4,) + big] * 4
            + [(4,) + small] * 4
        ]
        + [dma((5, 24)), dma((5, 24)), dma((4,))]
        + [dma((2, 4))] * 4
        + [dma((4,)), dma((4,)), dma((5,))],
        compiler_params=pltpu.CompilerParams(
            collective_id=5, has_side_effects=True, vmem_limit_bytes=LIMIT
        ),
        cost_estimate=pl.CostEstimate(flops=1000, bytes_accessed=1000, transcendentals=0),
        name="finish_reduction",
    )(p1, p2, k3, a3, k4, b4)


def swap_route(bit, count):
    return [(i, i ^ bit) for i in range(count)]


def planes_of(replicas):
    return [
        [8 * b + 2 * z + x for z in range(4)] for b in range(replicas // 8) for x in range(2)
    ]


def swap_x(array, replicas):
    return lax.ppermute(array, "rep", swap_route(1, replicas))


def add_arrived(kept, arrived):
    return (kept.astype(f32) + arrived.astype(f32)).astype(bf16)


def reduce_z(summed, replicas):
    piece = lax.psum_scatter(
        summed, "rep", scatter_dimension=0, tiled=False, axis_index_groups=planes_of(replicas)
    )
    blocks = replicas // 8
    if blocks > 1:
        piece = lax.psum(
            piece, "rep", axis_index_groups=[[8 * b + r for b in range(blocks)] for r in range(8)]
        )
    return piece


def exchange(piece, at, part):
    moved = [piece[: at + part]]
    for d in range(1, 4):
        moved.append(swap(piece[at + d * part : at + (d + 1) * part], d))
    moved.append(piece[at + 4 * part :])
    if piece.shape[0] == IN_ROWS:
        moved += [swap(piece[SMALL_AT:], d) for d in range(1, 4)]
    return jnp.concatenate(moved, axis=0)


def gather_z(piece, replicas):
    return lax.all_gather(piece, "rep", axis=0, axis_index_groups=planes_of(replicas))


def spread(piece, replicas):
    owned = gather_z(piece, replicas)
    other = swap_x(owned, replicas)
    odd = lax.axis_index("rep") % 2 == 1
    pair = jnp.stack([jnp.where(odd, other, owned), jnp.where(odd, owned, other)], axis=1)
    return pair.reshape((8,) + piece.shape)


def finish_all(piece1, piece2, keep3, arrived3, keep4, send4, replicas):
    if replicas == 8:
        return finish_reduction(piece1, piece2, keep3, arrived3, keep4, send4)
    piece3 = reduce_z(add_arrived(keep3, arrived3), replicas)
    piece4 = reduce_z(add_arrived(keep4, swap_x(send4, replicas)), replicas)
    return [
        spread(exchange(piece, *move), replicas)
        for piece, move in (
            (piece1, FFN_MOVE), (piece2, IN_MOVE), (piece3, FFN_MOVE), (piece4, IN_MOVE)
        )
    ]


def tie(*values):
    return lax.optimization_barrier(values)


def swap(array, d):
    return lax.ppermute(array, "grp", swap_route(d, 4))


def per_device(
    x_input, norm_gain, w_in, w_ab, conv_w, a_log, dt_bias, out_gain, w_out, ffn_in, ffn_out,
    cotangent,
):
    parts = lax.axis_size("grp")
    replicas = lax.axis_size("rep")
    mine = lax.axis_index("grp")
    rows, width = x_input.shape[1], x_input.shape[2]
    shard = w_in.shape[1]

    pack = jnp.concatenate(
        [
            norm_gain.reshape(-1, 128),
            conv_w.reshape(-1, 128),
            jnp.swapaxes(w_ab, 1, 2).reshape(-1, 128),
            out_gain.reshape(-1, 128),
            jnp.zeros((PACK_ROWS - OUT_GAIN_AT - 1, 128), bf16),
        ]
    ).astype(f32)
    normed, projected, small, in_weight, *rest = start(x_input[0], pack, w_in)
    gains, taps_pair, ab_pair, out_pair = rest[0:4], rest[4:6], rest[6:8], rest[8:10]
    small_weights = []
    for l in range(LAYERS):
        heads = jnp.pad(jnp.stack([a_log[l], dt_bias[l]]).astype(f32), ((0, 6), (2, 124)))
        small_weights.append(
            (
                gains[2 * l], gains[2 * l + 1], ab_pair[l], taps_pair[l], heads, out_pair[l],
            )
        )

    residual = x_input[0].astype(f32)
    kept = []
    in_weights, up_weights = [(in_weight,)], []
    for l in range(LAYERS):
        gain_one, gain_two, ab, taps, heads, gain = small_weights[l]
        if l > 0:
            normed, projected, small = project(residual, gain_one, ab, in_weights[l])
        gated, *saved = mixer_forward(
            l, projected, small, taps, heads, gain, (ffn_in, w_in)[: LAYERS - l]
        )
        up_weights.append((ffn_in, saved[4]))
        if l == 0:
            near, far = saved[5:]
            in_weights.append(
                (
                    w_in,
                    near,
                    lax.all_gather(far, "rep", axis=0, axis_index_groups=planes_of(replicas)),
                )
            )
        saved = saved[:4]
        mid, normed_two, up, hidden, residual_out = ffn_forward(
            l, gated, residual, gain_two, w_out, ffn_out, up_weights[l]
        )
        kept.append((residual, normed, projected, small, gated, saved, mid, normed_two, up, hidden))
        residual = residual_out

    d_residual = cotangent[0].astype(f32)

    def ffn_part(l, d_residual):
        gain_one, gain_two, ab, taps, heads, gain = small_weights[l]
        residual, normed, projected, small, gated, saved, mid, normed_two, up, hidden = kept[l]
        return ffn_backward(
            l, d_residual, up, hidden, normed_two, mid, gain_two, gated, w_out, ffn_out,
            up_weights[l],
        )

    def mixer_part(l, d_gated):
        gain_one, gain_two, ab, taps, heads, gain = small_weights[l]
        residual, normed, projected, small, gated, saved, mid, normed_two, up, hidden = kept[l]
        return mixer_backward(projected, small, taps, heads, gain, saved, d_gated)

    def project_part(l, d_mid, g_gain_two, mixed):
        gain_one, gain_two, ab, taps, heads, gain = small_weights[l]
        residual, normed, projected, small, gated, saved, mid, normed_two, up, hidden = kept[l]
        d_projected, d_small, g_taps, g_heads = mixed
        return project_backward(
            d_projected, d_small, in_weights[l], ab, normed, residual, gain_one, d_mid,
            g_gain_two, g_taps, g_heads,
        )

    d_mid, d_gated, g_gain_two, keep1, send1 = ffn_part(1, d_residual)
    arrived1 = swap_x(send1, replicas)
    mixed = mixer_part(1, d_gated)
    d_residual, keep2, send2 = project_part(1, d_mid, g_gain_two, mixed)
    d_residual, arrived1 = tie(d_residual, arrived1)
    piece1 = reduce_z(add_arrived(keep1, arrived1), replicas)
    arrived2 = swap_x(send2, replicas)
    d_mid, d_gated, g_gain_two, keep3, send3 = ffn_part(0, d_residual)
    d_gated, piece1, arrived2 = tie(d_gated, piece1, arrived2)
    piece2 = reduce_z(add_arrived(keep2, arrived2), replicas)
    arrived3 = swap_x(send3, replicas)
    mixed = mixer_part(0, d_gated)
    d_residual, keep4, send4 = project_part(0, d_mid, g_gain_two, mixed)
    d_residual, arrived3 = tie(d_residual, arrived3)
    final1, final2, final3, final4 = finish_all(piece1, piece2, keep3, arrived3, keep4, send4, replicas)
    finals = (final1, final2, final3, final4)
    down_grads, out_grads, up_grads, w_in_grads, everyone, *ends = assemble(
        finals, residual, d_residual
    )
    block_output, input_grad = (end[None] for end in ends)

    tables = lax.dynamic_index_in_dim(everyone, mine, 0, keepdims=False)
    sums = jnp.sum(everyone[:, :, 64:82], axis=0)
    grad_gain = lax.dynamic_slice_in_dim(
        sums[:, :16].reshape(LAYERS, 2, width), mine * shard, shard, 2
    )
    grad_out_gain = lax.dynamic_slice_in_dim(
        sums[:, 16:18].reshape(LAYERS, DV), mine * (DV // 4), DV // 4, 1
    )
    grad_a_log = tables[:, 82, 2:4]
    grad_dt = tables[:, 83, 2:4]
    taps_sum = everyone[:, :, 0:32].reshape(4, LAYERS, 4, 1024)

    def side_by_side(array):
        return jnp.moveaxis(array, 0, 2).reshape(LAYERS, 4, -1)

    conv_full = jnp.concatenate(
        [
            side_by_side(taps_sum[..., :256]),
            side_by_side(taps_sum[..., 256:512]),
            side_by_side(taps_sum[..., 512:]),
        ],
        axis=2,
    )
    grad_conv = lax.dynamic_slice_in_dim(conv_full, mine * 1024, 1024, 2)
    ab_sum = everyone[:, :, 32:64].reshape(4, LAYERS, 4, width)
    ab_sum = lax.dynamic_slice_in_dim(ab_sum, mine * shard, shard, 3)
    grad_ab = jnp.transpose(ab_sum.reshape(4, LAYERS, 2, 2, shard), (1, 4, 2, 0, 3)).reshape(
        LAYERS, shard, 2 * H
    )
    return (
        block_output,
        input_grad,
        grad_gain,
        w_in_grads,
        grad_ab,
        grad_conv,
        grad_a_log,
        grad_dt,
        grad_out_gain,
        out_grads,
        up_grads,
        down_grads,
    )


def solution(mesh):
    rows = P("rep", "grp", None)
    first = P(None, "grp")
    middle = P(None, "grp", None)
    last = P(None, None, "grp")
    in_specs = (rows, last, middle, middle, last, first, first, first, middle, middle, middle, rows)
    out_specs = (rows, rows, last, middle, middle, last, first, first, first, middle, middle, middle)
    return jax.shard_map(
        per_device, mesh=mesh, in_specs=in_specs, out_specs=out_specs, check_vma=False
    )
```

```python
from functools import partial
import math

import jax
import jax.numpy as jnp
from jax import lax
from jax.sharding import PartitionSpec as P
from jax.experimental import pallas as pl
from jax.experimental.pallas import tpu as pltpu

H = 8
DK = 128
DV = 256
FF = 2816
CONV = 4
LAYERS = 2
HK = 1024
HV = 2048
CH = 4096
CHUNK = 128

f32 = jnp.float32
bf16 = jnp.bfloat16
HIGH = lax.Precision.HIGHEST
epsilon = 1e-06
out_floor = 0.02
NN = ((1,), (0,))
NT = ((1,), (1,))
TN = ((0,), (0,))


def mm(left, right, dims=NN, precision=None):
    return lax.dot_general(
        left, right, (dims, ((), ())), precision=precision, preferred_element_type=f32
    )


def mh(left, right, dims=NN):
    return mm(left, right, dims, HIGH)


def grid_of(shape, dim):
    return lax.broadcasted_iota(jnp.int32, shape, dim)


def conv_chunk(x_ext, taps):
    return sum(x_ext[5 + j : 5 + j + CHUNK] * taps[j : j + 1] for j in range(CONV))


def decay_chunk(small, heads_ref):
    lane = grid_of(small.shape, 1)
    strength = jax.nn.sigmoid(small)
    shifted_logit = small + heads_ref[1:2, :]
    soft = jnp.maximum(shifted_logit, 0.0) + jnp.log1p(jnp.exp(-jnp.abs(shifted_logit)))
    log_decay = -jnp.exp(heads_ref[0:1, :]) * soft
    row = grid_of((CHUNK, CHUNK), 0)
    col = grid_of((CHUNK, CHUNK), 1)
    lower_ones = jnp.where(row >= col, 1.0, 0.0).astype(f32)
    cumulative = mm2(lower_ones.astype(bf16), log_decay)
    turned = jnp.where(lane < 2, strength, cumulative).T
    return strength, shifted_logit, log_decay, cumulative, turned


def head_inputs(activated, h):
    qa = activated[:, 128 * h : 128 * h + 128]
    ka = activated[:, 256 + 128 * h : 384 + 128 * h]
    va = activated[:, 512 + 256 * h : 768 + 256 * h]
    q_norm = lax.rsqrt(jnp.sum(qa * qa, axis=-1, keepdims=True) + epsilon)
    k_norm = lax.rsqrt(jnp.sum(ka * ka, axis=-1, keepdims=True) + epsilon)
    q = (qa * q_norm * (1.0 / math.sqrt(DK))).astype(bf16)
    k = (ka * k_norm).astype(bf16)
    return qa, ka, q_norm, k_norm, q, k, va.astype(bf16)


def split(x):
    high = x.astype(bf16)
    return high, (x - high.astype(f32)).astype(bf16)


def mm2(exact, right, dims=NN):
    high, low = split(right)
    return mm(exact, high, dims) + mm(exact, low, dims)


def mm3(left, right, dims=NN):
    lh, ll = split(left)
    rh, rl = split(right)
    return mm(lh, rh, dims) + (mm(lh, rl, dims) + mm(ll, rh, dims))


def mb(left, right, dims=NN):
    return mm(left.astype(bf16), right.astype(bf16), dims)


def unit_inverse(system):
    size = system.shape[0]
    row = grid_of((size, size), 0)
    col = grid_of((size, size), 1)
    eye = jnp.where(row == col, 1.0, 0.0).astype(f32)
    powers = jnp.where((row >> 2) == (col >> 2), -system, 0.0)
    square = mb(powers, powers)
    total = eye + powers
    total = total + mb(total, square)
    for bits in (2, 3, 4, 5, 6):
        joint = ((row >> (bits + 1)) == (col >> (bits + 1))) & ((row >> bits) != (col >> bits))
        link = jnp.where(joint, system, 0.0)
        total = total - mb(total, mb(link, total))
    return total


def mixer_forward_kernel(
    layer, proj_hbm, small_ref, taps_ref, heads_ref, gain_ref, *refs
):
    if layer == 0:
        up_source, in_source, *refs = refs
        *outs, up_whole, near, far = refs[:8]
        refs = refs[8:]
    else:
        up_source, cotangent_hbm, *refs = refs
        *outs, up_whole, ddown_hbm = refs[:7]
        refs = refs[7:]
    proj_ref, gated_ref, start_ref, inv_ref, pseudo_ref, mixed_ref = refs[:6]
    load_sem, store_sem, halo, state, *sems = refs[6:]

    def chunk_rows(c):
        return pl.ds(pl.multiple_of(c * CHUNK, CHUNK), CHUNK)

    def load(c):
        rows = chunk_rows(c)
        return pltpu.make_async_copy(proj_hbm.at[rows], proj_ref.at[rows], load_sem.at[c])

    def stores(c):
        rows = chunk_rows(c)
        pairs = zip(refs[1:6], outs, (rows, c, c, c, rows))
        return [
            pltpu.make_async_copy(src.at[at], dst.at[at], store_sem.at[k, c])
            for k, (src, dst, at) in enumerate(pairs)
        ]

    chunks = proj_ref.shape[0] // CHUNK
    for c in range(chunks):
        load(c).start()
    ready = greet_wide(*place())
    shard = Reshard(up_source.at[layer], up_lanes, up_whole, *sems[:5])
    if layer == 0:
        quarter = Quarter(in_source.at[1], in_lanes, near, far, *sems[5:])
    ready()
    shard.start_far(0)
    shard.start_near()
    if layer == 1:
        ddown, ddown_sems, *gather_refs = sems[5:]
        gather = Gather(ddown, *gather_refs, cotangent_hbm.shape[0])
        count = gather.size // SUB
        own_rows = ddown.at[block_rows(gather.y, gather.c, gather.size)]
        pltpu.make_async_copy(cotangent_hbm, own_rows, ddown_sems.at[0]).start()
    halo[...] = jnp.zeros_like(halo)
    state[...] = jnp.zeros_like(state)
    row = grid_of((CHUNK, CHUNK), 0)
    col = grid_of((CHUNK, CHUNK), 1)
    zero = jnp.zeros((CHUNK, CHUNK), f32)

    def prepare(c):
        rows = pl.ds(pl.multiple_of(c * CHUNK, CHUNK), CHUNK)
        x = proj_ref[rows, 0:1024].astype(f32)
        x_ext = jnp.concatenate([halo[...], x], axis=0)
        halo[...] = x[CHUNK - 8 :]
        convolved = conv_chunk(x_ext, taps_ref[...])
        activated = convolved * jax.nn.sigmoid(convolved)
        strength, shifted_logit, log_decay, cumulative, turned = decay_chunk(
            small_ref[rows, :], heads_ref
        )
        parts = []
        systems = []
        for h in range(2):
            qa, ka, q_norm, k_norm, q, k, v = head_inputs(activated, h)
            c_col = cumulative[:, 2 + h : 3 + h]
            c_row = turned[2 + h : 3 + h, :]
            beta_row = turned[h : h + 1, :]
            ratio = jnp.exp(jnp.where(row >= col, c_col - c_row, -1e4)) * beta_row
            systems.append(jnp.where(row > col, ratio * mm(k, k, NT), 0.0))
            mixing = (ratio * mm(q, k, NT)).astype(bf16)
            parts.append((q, k, v, c_col, mixing, strength[:, h : h + 1]))
        joint = jnp.concatenate(
            [
                jnp.concatenate([systems[0], zero], axis=1),
                jnp.concatenate([zero, systems[1]], axis=1),
            ],
            axis=0,
        )
        return parts, unit_inverse(joint)

    def advance(c, parts, inverse):
        rows = pl.ds(pl.multiple_of(c * CHUNK, CHUNK), CHUNK)
        for h in range(2):
            q, k, v, c_col, mixing, beta_col = parts[h]
            inv = inverse[128 * h : 128 * h + 128, 128 * h : 128 * h + 128]
            growth = jnp.exp(c_col)
            last = c_col[CHUNK - 1 :, :]
            before = state[h]
            start_ref[c, h] = before
            inv = inv.astype(bf16)
            inv_ref[c, h] = inv
            read = mm2(jnp.concatenate([q, k], axis=0), before)
            pseudo = mm(inv, (v.astype(f32) - growth * read[CHUNK:]).astype(bf16))
            pseudo_ref[c, h] = pseudo
            tail = jnp.exp(last - c_col) * beta_col
            state[h] = jnp.exp(last) * before + mm2(k, tail * pseudo, TN)
            mixed = growth * read[:CHUNK] + mm(mixing, pseudo.astype(bf16))
            mixed_ref[rows, 256 * h : 256 * h + 256] = mixed
            gate = proj_ref[rows, 1024 + 256 * h : 1280 + 256 * h].astype(f32)
            scale = lax.rsqrt(jnp.mean(mixed * mixed, axis=-1, keepdims=True) + out_floor)
            gated = mixed * scale * gain_ref[0:1, :] * (gate * jax.nn.sigmoid(gate))
            gated_ref[rows, 256 * h : 256 * h + 256] = gated.astype(bf16)

    def body(step, carry):
        load(step).wait()
        advance(step, *prepare(step))
        for store in stores(step):
            store.start()
        @pl.when(step == 0)
        def _():
            shard.start_far(1)
            if layer == 0:
                quarter.start_near()

        @pl.when(step == 2)
        def _():
            shard.forward(0)
            if layer == 0:
                quarter.start_quarter()
            else:
                pltpu.make_async_copy(cotangent_hbm, own_rows, ddown_sems.at[0]).wait()
                for i in range(count):
                    gather.start(i)

        @pl.when(step == 4)
        def _():
            shard.forward(1)

        return carry

    lax.fori_loop(0, chunks, body, 0)
    shard.wait()
    shard.finish()
    if layer == 0:
        quarter.wait_quarter()
    else:
        for i in range(count):
            gather.across(i)
        for i in range(count):
            gather.sibling(i)
            gather.diagonal(i)
        whole_out = pltpu.make_async_copy(ddown, ddown_hbm, ddown_sems.at[1])
        whole_out.start()
        gather.finish()
        whole_out.wait()
    for c in range(chunks):
        for store in stores(c):
            store.wait()


def mixer_forward(layer, projected, small, taps, heads, gain, sources):
    tokens = projected.shape[0]
    chunks = tokens // CHUNK
    vmem = pl.BlockSpec(memory_space=pltpu.VMEM)
    spot = pl.BlockSpec(memory_space=pl.ANY)
    wholes = (jax.ShapeDtypeStruct((1024, 1536), bf16),)
    if layer == 0:
        wholes = wholes * 2 + (jax.ShapeDtypeStruct((2, PART, 1536), bf16),)
        carried = Reshard.scratch() * 2
    else:
        wholes = wholes + (jax.ShapeDtypeStruct((tokens, 1024), bf16),)
        carried = Reshard.scratch() + [
            pltpu.VMEM((tokens, 1024), bf16),
            pltpu.SemaphoreType.DMA((2,)),
        ]
        carried += gather_sems(tokens // 4)
    return pl.pallas_call(
        partial(mixer_forward_kernel, layer),
        out_shape=(
            jax.ShapeDtypeStruct((tokens, 512), bf16),
            jax.ShapeDtypeStruct((chunks, 2, DK, DV), f32),
            jax.ShapeDtypeStruct((chunks, 2, CHUNK, CHUNK), bf16),
            jax.ShapeDtypeStruct((chunks, 2, CHUNK, DV), f32),
            jax.ShapeDtypeStruct((tokens, 512), f32),
        )
        + wholes,
        in_specs=[spot] + [vmem] * 4 + [spot] * len(sources),
        out_specs=(spot,) * (5 + len(wholes)),
        scratch_shapes=[
            pltpu.VMEM((tokens, 1536), bf16),
            pltpu.VMEM((tokens, 512), bf16),
            pltpu.VMEM((chunks, 2, DK, DV), f32),
            pltpu.VMEM((chunks, 2, CHUNK, CHUNK), bf16),
            pltpu.VMEM((chunks, 2, CHUNK, DV), f32),
            pltpu.VMEM((tokens, 512), f32),
            pltpu.SemaphoreType.DMA((chunks,)),
            pltpu.SemaphoreType.DMA((5, chunks)),
        ]
        + [pltpu.VMEM((8, 1024), f32), pltpu.VMEM((2, DK, DV), f32)]
        + carried,
        compiler_params=pltpu.CompilerParams(
            collective_id=8 + layer, has_side_effects=True, vmem_limit_bytes=LIMIT
        ),
        name="mixer_forward",
    )(projected, small, taps, heads, gain, *sources)


def mixer_backward_kernel(
    small_ref, taps_ref, heads_ref, gain_ref, *refs
):
    sources, refs = refs[:6], refs[6:]
    dproj_hbm, dsmall_ref, gtaps_ref, gheads_ref, *refs = refs
    held, refs = refs[:6], refs[6:]
    proj_ref, start_ref, inv_ref, pseudo_ref, mixed_ref, dgated_ref = held
    dproj_ref, load_sem, store_sem, halo, dstate = refs

    def chunk_rows(c):
        return pl.ds(pl.multiple_of(c * CHUNK, CHUNK), CHUNK)

    def load(k, c):
        at = c if k in (1, 2, 3) else chunk_rows(c)
        return pltpu.make_async_copy(sources[k].at[at], held[k].at[at], load_sem.at[k, c])

    def store(c):
        rows = chunk_rows(c)
        return pltpu.make_async_copy(dproj_ref.at[rows], dproj_hbm.at[rows], store_sem.at[c])

    halo[...] = jnp.zeros_like(halo)
    dstate[...] = jnp.zeros_like(dstate)
    gtaps_ref[...] = jnp.zeros_like(gtaps_ref)
    gheads_ref[...] = jnp.zeros_like(gheads_ref)
    row = grid_of((CHUNK, CHUNK), 0)
    col = grid_of((CHUNK, CHUNK), 1)
    lane = col
    token = grid_of((CHUNK, 1), 0)
    chunks = proj_ref.shape[0] // CHUNK
    for c in reversed(range(chunks)):
        for k in range(6):
            load(k, c).start()
    load(0, chunks - 1).wait()

    def body(step, carry):
        c = chunks - 1 - step
        for k in range(1, 6):
            load(k, c).wait()

        @pl.when(c > 0)
        def _():
            load(0, c - 1).wait()

        rows = pl.ds(pl.multiple_of(c * CHUNK, CHUNK), CHUNK)
        x = proj_ref[rows, 0:1024].astype(f32)
        before_rows = pl.ds(pl.multiple_of(jnp.maximum(c * CHUNK - 16, 0), 16), 16)
        x_before = proj_ref[before_rows, 0:1024].astype(f32)[8:]
        x_before = jnp.where(c > 0, x_before, 0.0)
        x_ext = jnp.concatenate([x_before, x], axis=0)
        convolved = conv_chunk(x_ext, taps_ref[...])
        sig = jax.nn.sigmoid(convolved)
        activated = convolved * sig
        strength, shifted_logit, log_decay, cumulative, turned = decay_chunk(
            small_ref[rows, :], heads_ref
        )
        d_strength = jnp.zeros((CHUNK, CHUNK), f32)
        d_cumulative = jnp.zeros((CHUNK, CHUNK), f32)
        d_q_parts, d_k_parts, d_v_parts = [], [], []
        gain_sum = jnp.zeros((1, DV), f32)
        for h in range(2):
            qa, ka, q_norm, k_norm, q, k, v = head_inputs(activated, h)
            cols = slice(256 * h, 256 * h + 256)
            mixed = mixed_ref[rows, cols]
            gate = proj_ref[rows, 1024 + 256 * h : 1280 + 256 * h].astype(f32)
            d_gated = dgated_ref[rows, cols].astype(f32)
            gate_sig = jax.nn.sigmoid(gate)
            gate_silu = gate * gate_sig
            scale = lax.rsqrt(jnp.mean(mixed * mixed, axis=-1, keepdims=True) + out_floor)
            scaled = mixed * scale
            gain = gain_ref[0:1, :]
            gain_sum = gain_sum + jnp.sum(d_gated * scaled * gate_silu, axis=0, keepdims=True)
            d_gate = d_gated * scaled * gain * (gate_sig * (1.0 + gate * (1.0 - gate_sig)))
            dproj_ref[rows, 1024 + 256 * h : 1280 + 256 * h] = d_gate.astype(bf16)
            d_scaled = d_gated * gain * gate_silu
            d_mixed = scale * (
                d_scaled - scaled * jnp.mean(d_scaled * scaled, axis=-1, keepdims=True)
            )
            c_col = cumulative[:, 2 + h : 3 + h]
            c_row = turned[2 + h : 3 + h, :]
            beta_row = turned[h : h + 1, :]
            beta_col = strength[:, h : h + 1]
            growth = jnp.exp(c_col)
            last = c_col[CHUNK - 1 :, :]
            ratio = jnp.exp(jnp.where(row >= col, c_col - c_row, -1e4))
            key_gram = mm(k, k, NT)
            query_gram = mm(q, k, NT)
            mixing = ratio * beta_row * query_gram
            fade = jnp.exp(last - c_col)
            tail = fade * beta_col
            start = start_ref[c, h]
            inv = inv_ref[c, h]
            pseudo = pseudo_ref[c, h]
            d_end = dstate[h]
            kf = k.astype(f32)
            qf = q.astype(f32)
            d_pseudo = mb(mixing, d_mixed, TN) + tail * mm(k, d_end.astype(bf16))
            d_right = mm2(inv, d_pseudo, TN)
            pair = jnp.concatenate([d_mixed, d_right], axis=0)
            reads = mm3(pair, jnp.concatenate([start, pseudo], axis=0), NT)
            read_q = reads[:CHUNK, :DK]
            read_k = reads[CHUNK:, :DK]
            read_u = mm3(pseudo, d_end, NT)
            d_mixing = jnp.where(row >= col, reads[:CHUNK, DK:], 0.0) * ratio
            d_system = jnp.where(row > col, -reads[CHUNK:, DK:], 0.0) * ratio
            raw = d_mixing * query_gram + d_system * key_gram
            x_pair = jnp.concatenate([d_mixing * beta_row, d_system * beta_row], axis=0)
            by_row = mm(x_pair.astype(bf16), k)
            by_col = mm(x_pair.astype(bf16), jnp.concatenate([q, k], axis=0), TN)
            d_q = growth * read_q + by_row[:CHUNK]
            d_k = by_row[CHUNK:] + by_col - growth * read_k + tail * read_u
            dstate[h] = jnp.exp(last) * d_end + mb(
                jnp.concatenate([growth * qf, -growth * kf], axis=0), pair, TN
            )
            u_dot = jnp.sum(read_u * kf, axis=-1, keepdims=True)
            col_raw = jnp.sum(raw, axis=0, keepdims=True)
            col_raw = jnp.broadcast_to(col_raw, (CHUNK, CHUNK)).T[:, 0:1]
            d_beta = col_raw + fade * u_dot
            d_cum = (
                jnp.sum(raw * beta_row, axis=-1, keepdims=True)
                - beta_col * col_raw
                + growth
                * (
                    jnp.sum(read_q * qf, axis=-1, keepdims=True)
                    - jnp.sum(read_k * kf, axis=-1, keepdims=True)
                )
                - tail * u_dot
            )
            at_last = jnp.sum(tail * u_dot, axis=0, keepdims=True) + jnp.exp(last) * jnp.sum(
                jnp.sum(start * d_end, axis=-1, keepdims=True), axis=0, keepdims=True
            )
            d_cum = d_cum + jnp.where(token == CHUNK - 1, at_last, 0.0)
            d_strength = jnp.where(lane == h, d_beta, d_strength)
            d_cumulative = jnp.where(lane == 2 + h, d_cum, d_cumulative)
            d_qn = d_q * (1.0 / math.sqrt(DK))
            qn = qa * q_norm
            kn = ka * k_norm
            d_q_parts.append(
                q_norm * (d_qn - qn * jnp.sum(d_qn * qn, axis=-1, keepdims=True))
            )
            d_k_parts.append(k_norm * (d_k - kn * jnp.sum(d_k * kn, axis=-1, keepdims=True)))
            d_v_parts.append(d_right)
        upper_ones = jnp.where(row <= col, 1.0, 0.0).astype(f32)
        d_log = mm2(upper_ones.astype(bf16), d_cumulative)
        d_shifted = d_log * (-jnp.exp(heads_ref[0:1, :])) * jax.nn.sigmoid(shifted_logit)
        d_small = jnp.where(lane < 2, d_strength * strength * (1.0 - strength), d_shifted)
        dsmall_ref[rows, :] = jnp.where(lane < 4, d_small, 0.0).astype(bf16)
        gheads_ref[0:1, :] += gain_sum
        gheads_ref[1:2, 0:128] += jnp.sum(d_log * log_decay, axis=0, keepdims=True)
        gheads_ref[2:3, 0:128] += jnp.sum(d_shifted, axis=0, keepdims=True)
        d_activated = jnp.concatenate(d_q_parts + d_k_parts + d_v_parts, axis=1)
        d_conv = d_activated * (sig * (1.0 + convolved * (1.0 - sig)))
        for j in range(CONV):
            gtaps_ref[j : j + 1, :] += jnp.sum(
                d_conv * x_ext[5 + j : 5 + j + CHUNK], axis=0, keepdims=True
            )
        d_ext = jnp.concatenate([d_conv, halo[...]], axis=0)
        d_x = sum(
            d_ext[CONV - 1 - j : CONV - 1 - j + CHUNK] * taps_ref[j : j + 1] for j in range(CONV)
        )
        halo[...] = d_conv[:8]
        dproj_ref[rows, 0:1024] = d_x.astype(bf16)
        store(c).start()
        return carry

    lax.fori_loop(0, chunks, body, 0)
    for c in range(chunks):
        store(c).wait()


def mixer_backward(projected, small, taps, heads, gain, saved, d_gated):
    tokens = projected.shape[0]
    vmem = pl.BlockSpec(memory_space=pltpu.VMEM)
    spot = pl.BlockSpec(memory_space=pl.ANY)
    held = (projected, *saved, d_gated)
    chunks = tokens // CHUNK
    return pl.pallas_call(
        mixer_backward_kernel,
        out_shape=(
            jax.ShapeDtypeStruct((tokens, 1536), bf16),
            jax.ShapeDtypeStruct((tokens, 128), bf16),
            jax.ShapeDtypeStruct((8, 1024), f32),
            jax.ShapeDtypeStruct((8, DV), f32),
        ),
        in_specs=[vmem] * 4 + [spot] * 6,
        out_specs=(spot,) + (vmem,) * 3,
        scratch_shapes=[pltpu.VMEM(array.shape, array.dtype) for array in held]
        + [
            pltpu.VMEM((tokens, 1536), bf16),
            pltpu.SemaphoreType.DMA((6, chunks)),
            pltpu.SemaphoreType.DMA((chunks,)),
        ]
        + [pltpu.VMEM((8, 1024), f32), pltpu.VMEM((2, DK, DV), f32)],
        compiler_params=pltpu.CompilerParams(vmem_limit_bytes=LIMIT),
        name="mixer_backward",
    )(small, taps, heads, gain, *held)


SUB = 128
LIMIT = 56 << 20
MESH = pl.DeviceIdType.MESH


def place():
    me = lax.axis_index("grp")
    y, c = me // 2, me % 2
    return y, c


def shard_rows(y, c, i, size):
    return pl.ds(pl.multiple_of((2 * y + c) * size + i * SUB, SUB), SUB)


def block_rows(y, c, size):
    return pl.ds(pl.multiple_of((2 * y + c) * size, size), size)


def greet(y, c):
    barrier = pltpu.get_barrier_semaphore()
    for target in (2 * y + 1 - c, 2 * (1 - y) + c):
        pl.semaphore_signal(barrier, inc=1, device_id={"grp": target}, device_id_type=MESH)
    return lambda: pl.semaphore_wait(barrier, 2)


def remote(src, dst, send, recv, target):
    return pltpu.make_async_remote_copy(
        src_ref=src, dst_ref=dst, send_sem=send, recv_sem=recv,
        device_id={"grp": target}, device_id_type=MESH,
    )


class Gather:
    def __init__(self, full, send, recv, size):
        self.full, self.send, self.recv, self.size = full, send, recv, size
        self.y, self.c = place()

    def piece(self, kind, i):
        y, c = self.y, self.c
        rows = shard_rows(1 - y if kind == 2 else y, c, i, self.size)
        target = 2 * (1 - y) + c if kind == 1 else 2 * y + 1 - c
        view = self.full.at[rows]
        return remote(view, view, self.send.at[kind, i], self.recv.at[kind, i], target)

    def own(self, i):
        return shard_rows(self.y, self.c, i, self.size)

    def start(self, i):
        self.piece(0, i).start()
        self.piece(1, i).start()

    def sibling(self, i):
        self.piece(0, i).wait_recv()
        return shard_rows(self.y, 1 - self.c, i, self.size)

    def across(self, i):
        self.piece(1, i).wait_recv()
        self.piece(2, i).start()
        return shard_rows(1 - self.y, self.c, i, self.size)

    def diagonal(self, i):
        self.piece(2, i).wait_recv()
        return shard_rows(1 - self.y, 1 - self.c, i, self.size)

    def finish(self):
        for kind in range(3):
            for i in range(self.size // SUB):
                self.piece(kind, i).wait_send()


class Scatter:
    def __init__(self, out, core, keep, relay, far, send, recv, size):
        self.out, self.core, self.keep, self.relayed, self.far = out, core, keep, relay, far
        self.send, self.recv, self.size = send, recv, size
        self.y, self.c = place()

    def to_sibling(self, part, i):
        rows = pl.ds(i * SUB, SUB)
        return remote(
            self.out.at[part, rows], self.core.at[part, rows],
            self.send.at[part, i], self.recv.at[part, i], 2 * self.y + 1 - self.c,
        )

    def to_across(self, i):
        rows = pl.ds(i * SUB, SUB)
        return remote(
            self.relayed.at[rows], self.far.at[rows],
            self.send.at[2, i], self.recv.at[2, i], 2 * (1 - self.y) + self.c,
        )

    def give(self, part, i, value):
        self.out[part, i * SUB : (i + 1) * SUB, :] = value.astype(bf16)
        self.to_sibling(part, i).start()

    def hold(self, part, i, value):
        self.keep[part, i * SUB : (i + 1) * SUB, :] = value

    def relay(self, i):
        rows = slice(i * SUB, (i + 1) * SUB)
        self.to_sibling(0, i).wait_recv()
        self.relayed[rows, :] = (self.keep[0, rows, :] + self.core[0, rows, :].astype(f32)).astype(bf16)
        self.to_across(i).start()

    def total(self, i):
        rows = slice(i * SUB, (i + 1) * SUB)
        self.to_sibling(1, i).wait_recv()
        near = self.keep[1, rows, :] + self.core[1, rows, :].astype(f32)
        self.to_across(i).wait_recv()
        return near + self.far[rows, :].astype(f32)

    def finish(self):
        for i in range(self.size // SUB):
            self.to_sibling(0, i).wait_send()
            self.to_sibling(1, i).wait_send()
            self.to_across(i).wait_send()

    @staticmethod
    def scratch(size, width):
        return [
            pltpu.VMEM((2, size, width), bf16),
            pltpu.VMEM((2, size, width), bf16),
            pltpu.VMEM((2, size, width), f32),
            pltpu.VMEM((size, width), bf16),
            pltpu.VMEM((size, width), bf16),
            pltpu.SemaphoreType.DMA((3, size // SUB)),
            pltpu.SemaphoreType.DMA((3, size // SUB)),
        ]


def gather_sems(size):
    return [pltpu.SemaphoreType.DMA((3, size // SUB)), pltpu.SemaphoreType.DMA((3, size // SUB))]


def in_order(gather):
    count = gather.size // SUB
    for i in range(count):
        yield gather.own(i)
    for i in range(count):
        yield gather.sibling(i)
    for i in range(count):
        yield gather.across(i)
        yield gather.diagonal(i)


def call(kernel, out_shape, inputs, scratch, collective, name, spots=(), out_spots=()):
    vmem = pl.BlockSpec(memory_space=pltpu.VMEM)
    spot = pl.BlockSpec(memory_space=pl.ANY)
    return pl.pallas_call(
        kernel,
        out_shape=out_shape,
        in_specs=[vmem] * len(inputs) + [spot] * len(spots),
        out_specs=tuple(spot if k in out_spots else vmem for k in range(len(out_shape))),
        scratch_shapes=scratch,
        compiler_params=pltpu.CompilerParams(
            collective_id=collective, has_side_effects=True, vmem_limit_bytes=LIMIT
        ),
        cost_estimate=pl.CostEstimate(flops=1000, bytes_accessed=1000, transcendentals=0),
        name=name,
    )(*inputs, *spots)


def relative(y, c, d):
    dy, dc = d // 2, d % 2
    return 2 * (y + dy - 2 * y * dy) + c + dc - 2 * c * dc


def load_whole(src, whole, sem):
    copy = pltpu.make_async_copy(src, whole, sem)
    copy.start()
    return copy.wait


class Outgoing:
    def __init__(self, sems):
        self.sems, self.copies = sems, []

    def put(self, src, dst):
        copy = pltpu.make_async_copy(src, dst, self.sems.at[len(self.copies)])
        copy.start()
        self.copies.append(copy)

    def wait(self):
        for copy in self.copies:
            copy.wait()


def load_down(src, whole, sem):
    y, c = place()
    rows, extra = src.shape[0], whole.shape[0] - src.shape[0]
    whole[:extra, :] = jnp.zeros((extra, whole.shape[1]), bf16)
    whole[rows:, :] = jnp.zeros((extra, whole.shape[1]), bf16)
    spot = pl.ds(pl.multiple_of(extra * c, extra), rows)
    copy = pltpu.make_async_copy(src, whole.at[spot], sem)
    copy.start()
    return copy.wait


def flip(rank):
    return rank + 1 - 2 * (rank % 2)


def greet_wide(y, c):
    barrier = pltpu.get_barrier_semaphore()
    for d in range(1, 4):
        pl.semaphore_signal(
            barrier, inc=1, device_id={"grp": relative(y, c, d)}, device_id_type=MESH
        )
    pl.semaphore_signal(
        barrier, inc=1, device_id={"rep": flip(lax.axis_index("rep"))}, device_id_type=MESH
    )
    return lambda: pl.semaphore_wait(barrier, 4)


PART = 64


def in_lanes(t):
    return (
        (256 * t, 256, 0),
        (HK + 256 * t, 256, 256),
        (2 * HK + 512 * t, 512, 512),
        (CH + 512 * t, 512, 1024),
    )


def up_lanes(t):
    first = 1408 * (t // 2) + 640 * (t % 2)
    return ((first, 768, 0), (FF + first, 768, 768))


class Reshard:
    def __init__(self, source, lanes, whole, send, recv, passed, arrived, local):
        self.source, self.lanes, self.whole = source, lanes, whole
        self.send, self.recv, self.passed, self.arrived = send, recv, passed, arrived
        self.local = local
        self.y, self.c = place()
        rank = lax.axis_index("rep")
        self.x, self.other = rank % 2, flip(rank)
        self.size = source.shape[0]

    def at(self, index, offset, count):
        return pl.ds(pl.multiple_of(index * self.size + offset, PART), count)

    def pieces(self, d, q):
        y, c = self.y, self.c
        target = relative(y, c, d)
        start = 0 if d < 2 else self.size // 2 * self.x + PART * q
        count = self.size if d < 2 else PART
        copies = []
        for k, (lane, wide, to) in enumerate(self.lanes(target)):
            src = self.source.at[
                pl.ds(pl.multiple_of(start, PART), count) if d >= 2 else pl.ds(0, count),
                pl.ds(pl.multiple_of(lane, 128), wide),
            ]
            dst = self.whole.at[self.at(2 * y + c, start, count), pl.ds(to, wide)]
            if d == 0:
                copies.append(pltpu.make_async_copy(src, dst, self.local.at[k]))
            else:
                copies.append(
                    pltpu.make_async_remote_copy(
                        src_ref=src, dst_ref=dst,
                        send_sem=self.send.at[d, q, k], recv_sem=self.recv.at[d, q, k],
                        device_id={"grp": target}, device_id_type=MESH,
                    )
                )
        return copies

    def onward(self, d, q):
        source = relative(self.y, self.c, d)
        rows = self.at(source, self.size // 2 * self.x + PART * q, PART)
        return pltpu.make_async_remote_copy(
            src_ref=self.whole.at[rows], dst_ref=self.whole.at[rows],
            send_sem=self.passed.at[d - 2, q], recv_sem=self.arrived.at[d - 2, q],
            device_id={"rep": self.other}, device_id_type=MESH,
        )

    def parts(self):
        return range(self.size // 2 // PART)

    def start_far(self, q):
        for d in (2, 3):
            for copy in self.pieces(d, q):
                copy.start()

    def start_near(self):
        for copy in self.pieces(1, 0):
            copy.start()

    def start_own(self):
        for copy in self.pieces(0, 0):
            copy.start()

    def forward(self, q):
        for d in (2, 3):
            for copy in self.pieces(d, q):
                copy.wait_recv()
            self.onward(d, q).start()

    def wait_own(self):
        for copy in self.pieces(0, 0):
            copy.wait()

    def wait(self):
        for copy in self.pieces(1, 0):
            copy.wait_recv()
        for q in self.parts():
            for d in (2, 3):
                self.onward(d, q).wait_recv()

    def finish(self):
        for copy in self.pieces(1, 0):
            copy.wait_send()
        for q in self.parts():
            for d in (2, 3):
                for copy in self.pieces(d, q):
                    copy.wait_send()
                self.onward(d, q).wait_send()

    @staticmethod
    def scratch():
        dma = pltpu.SemaphoreType.DMA
        return [dma((4, 2, 4)), dma((4, 2, 4)), dma((2, 2)), dma((2, 2)), dma((4,))]


def like(*shape, dtype=f32):
    return jax.ShapeDtypeStruct(shape, dtype)


def normalise(x, gain):
    return x * lax.rsqrt(jnp.mean(x * x, axis=-1, keepdims=True) + epsilon) * gain


def normalise_back(x, gain, d_out):
    scale = lax.rsqrt(jnp.mean(x * x, axis=-1, keepdims=True) + epsilon)
    unit = x * scale
    d_unit = d_out * gain
    d_x = scale * (d_unit - unit * jnp.mean(d_unit * unit, axis=-1, keepdims=True))
    return d_x, jnp.sum(d_out * unit, axis=0, keepdims=True)


class Quarter(Reshard):
    def __init__(self, source, lanes, whole, far, *sems):
        super().__init__(source, lanes, whole, *sems)
        self.far = far
        self.z = (lax.axis_index("rep") % 8) // 2

    def quarters(self, d):
        target = relative(self.y, self.c, d)
        copies = []
        for k, (lane, wide, to) in enumerate(self.lanes(target)):
            copies.append(
                pltpu.make_async_remote_copy(
                    src_ref=self.source.at[
                        pl.ds(pl.multiple_of(PART * self.z, PART), PART),
                        pl.ds(pl.multiple_of(lane, 128), wide),
                    ],
                    dst_ref=self.far.at[d - 2, :, pl.ds(to, wide)],
                    send_sem=self.send.at[d, 0, k], recv_sem=self.recv.at[d, 0, k],
                    device_id={"grp": target}, device_id_type=MESH,
                )
            )
        return copies

    def start_quarter(self):
        for d in (2, 3):
            for copy in self.quarters(d):
                copy.start()

    def wait_quarter(self):
        for copy in self.pieces(1, 0):
            copy.wait_recv()
            copy.wait_send()
        for d in (2, 3):
            for copy in self.quarters(d):
                copy.wait_recv()
                copy.wait_send()


def load_shard(parts, whole, sems):
    y, c = place()
    copies = []

    def add(src, dst):
        copies.append(pltpu.make_async_copy(src, dst, sems.at[len(copies)]))

    if len(parts) == 1:
        add(parts[0], whole)
    else:
        raw, lanes, near, *far = parts
        size = whole.shape[0] // 4

        def block(index, count):
            return pl.ds(pl.multiple_of(index * size, size), count * size)

        own, sibling, across = block(2 * y + c, 1), block(2 * y + 1 - c, 1), block(2 - 2 * y, 2)
        for lane, wide, to in lanes(2 * y + c):
            src = raw.at[pl.ds(0, size), pl.ds(pl.multiple_of(lane, 128), wide)]
            add(src, whole.at[own, pl.ds(to, wide)])
        add(near.at[sibling], whole.at[sibling])
        if not far:
            add(near.at[across], whole.at[across])
        else:
            for z in range(4):
                for d in (2, 3):
                    at = relative(y, c, d) * size + PART * z
                    spot = pl.ds(pl.multiple_of(at, PART), PART)
                    add(far[0].at[z, d - 2], whole.at[spot])
    for copy in copies:
        copy.start()

    def wait():
        for copy in copies:
            copy.wait()

    return wait


def in_parts(parts):
    return parts if len(parts) == 1 else (parts[0].at[1], in_lanes) + tuple(parts[1:])


GAIN_AT, TAPS_AT, AB_AT, OUT_GAIN_AT, PACK_ROWS = 0, 8, 72, 136, 144


def start_kernel(
    x_ref, pack_ref, win_ref,
    normed_hbm, proj_hbm, small_ref, whole_hbm,
    gain0, gain1, gain2, gain3, taps0, taps1, ab0, ab1, out0, out1,
    everyone, ab_rows, normed_ref, proj_ref, whole_ref, out_sems, *scratch,
):
    outgoing = Outgoing(out_sems)
    size = x_ref.shape[0]
    y, c = place()
    me = 2 * y + c
    ready = greet_wide(y, c)
    shard = Reshard(win_ref.at[0], in_lanes, whole_ref, *scratch[:5])
    psend, precv = scratch[5:7]
    gather = Gather(normed_ref, *scratch[7:], size)
    everyone[me] = pack_ref[...]
    ready()

    def share(d):
        return pltpu.make_async_remote_copy(
            src_ref=pack_ref, dst_ref=everyone.at[me],
            send_sem=psend.at[d], recv_sem=precv.at[d],
            device_id={"grp": relative(y, c, d)}, device_id_type=MESH,
        )

    for d in (2, 3, 1):
        share(d).start()
    for q in shard.parts():
        shard.start_far(q)
    shard.start_near()
    shard.start_own()
    for d in (1, 2, 3):
        share(d).wait_recv()
    for k, ref in enumerate((gain0, gain1, gain2, gain3)):
        for s in range(4):
            for b in range(2):
                row = GAIN_AT + 2 * k + b
                ref[0:1, 256 * s + 128 * b : 256 * s + 128 * b + 128] = everyone[s, row : row + 1, :]
    for i in range(size // SUB):
        rows = slice(i * SUB, (i + 1) * SUB)
        normed = normalise(x_ref[rows, :].astype(f32), gain0[...])
        normed_ref[gather.own(i), :] = normed.astype(bf16)
        gather.start(i)
    for l, (taps, ab, out) in enumerate(((taps0, ab0, out0), (taps1, ab1, out1))):
        taps[...] = jnp.zeros_like(taps)
        out[...] = jnp.zeros_like(out)
        ab_rows[...] = jnp.zeros_like(ab_rows)
        for j in range(4):
            base = TAPS_AT + (4 * l + j) * 8
            for b in range(8):
                if b < 2:
                    s, row = 0, base + 2 * me + b
                elif b < 4:
                    s, row = 1, base + 2 * me + b - 2
                else:
                    s, row = 2 + y, base + 4 * c + b - 4
                taps[j : j + 1, 128 * b : 128 * b + 128] = everyone[s, pl.ds(row, 1), :]
            column = 2 * me + j if j < 2 else H + 2 * me + j - 2
            for s in range(4):
                for b in range(2):
                    row = AB_AT + (16 * l + column) * 2 + b
                    ab_rows[j : j + 1, 256 * s + 128 * b : 256 * s + 128 * b + 128] = everyone[
                        s, pl.ds(row, 1), :
                    ]
        ab[...] = ab_rows[...].T.astype(bf16)
        for s in range(4):
            out[0:1, 64 * s : 64 * s + 64] = everyone[
                s, OUT_GAIN_AT : OUT_GAIN_AT + 1, 64 * l : 64 * l + 64
            ]
    for q in shard.parts():
        shard.forward(q)
    shard.wait()
    shard.wait_own()
    outgoing.put(whole_ref, whole_hbm)
    for rows in in_order(gather):
        normed = normed_ref[rows, :]
        proj_ref[rows, :] = mm(normed, whole_ref[...]).astype(bf16)
        small_ref[rows, :] = mm(normed, ab0[...])
        outgoing.put(proj_ref.at[rows], proj_hbm.at[rows])
        outgoing.put(normed_ref.at[rows], normed_hbm.at[rows])
    gather.finish()
    outgoing.wait()
    shard.finish()
    for d in (1, 2, 3):
        share(d).wait_send()


def start(x, pack, w_in):
    size, width = x.shape
    tokens = 4 * size
    row = like(1, width)
    dma = pltpu.SemaphoreType.DMA
    return call(
        start_kernel,
        (
            like(tokens, width, dtype=bf16),
            like(tokens, 1536, dtype=bf16),
            like(tokens, 128),
            like(width, 1536, dtype=bf16),
            row, row, row, row,
            like(8, width), like(8, width),
            like(width, 128, dtype=bf16), like(width, 128, dtype=bf16),
            like(8, DV), like(8, DV),
        ),
        (x, pack),
        [
            pltpu.VMEM((4, PACK_ROWS, 128), f32),
            pltpu.VMEM((128, width), f32),
            pltpu.VMEM((tokens, width), bf16),
            pltpu.VMEM((tokens, 1536), bf16),
            pltpu.VMEM((width, 1536), bf16),
            dma((17,)),
        ]
        + Reshard.scratch()
        + [dma((4,)), dma((4,))]
        + gather_sems(size),
        1,
        "start",
        (w_in,),
        (0, 1, 3),
    )


def project_kernel(count, res_ref, gain_ref, ab_ref, *refs):
    parts, refs = refs[:count], refs[count:]
    normed_hbm, proj_hbm, small_ref, w_ref, loads, normed_ref, proj_ref, out_sems, send, recv = refs
    outgoing = Outgoing(out_sems)
    loaded = load_shard(in_parts(parts), w_ref, loads)
    size = res_ref.shape[0]
    y, c = place()
    ready = greet(y, c)
    gather = Gather(normed_ref, send, recv, size)
    for i in range(size // SUB):
        rows = slice(i * SUB, (i + 1) * SUB)
        normed_ref[gather.own(i), :] = normalise(res_ref[rows, :], gain_ref[...]).astype(bf16)
        if i == 0:
            ready()
        gather.start(i)
    loaded()
    for rows in in_order(gather):
        normed = normed_ref[rows, :]
        proj_ref[rows, :] = mm(normed, w_ref[...]).astype(bf16)
        small_ref[rows, :] = mm(normed, ab_ref[...])
        outgoing.put(proj_ref.at[rows], proj_hbm.at[rows])
        outgoing.put(normed_ref.at[rows], normed_hbm.at[rows])
    gather.finish()
    outgoing.wait()


def project(residual, gain, ab, weight):
    size, width = residual.shape
    tokens = 4 * size
    return call(
        partial(project_kernel, len(weight)),
        (like(tokens, width, dtype=bf16), like(tokens, 1536, dtype=bf16), like(tokens, 128)),
        (residual, gain, ab),
        [
            pltpu.VMEM((width, 1536), bf16),
            pltpu.SemaphoreType.DMA((13,)),
            pltpu.VMEM((tokens, width), bf16),
            pltpu.VMEM((tokens, 1536), bf16),
            pltpu.SemaphoreType.DMA((16,)),
        ]
        + gather_sems(size),
        6,
        "project",
        weight,
        (0, 1),
    )


def swiglu(up):
    gate, value = up[:, :768], up[:, 768:]
    return gate * jax.nn.sigmoid(gate) * value


def swiglu_back(up, d_hidden):
    gate, value = up[:, :768], up[:, 768:]
    sig = jax.nn.sigmoid(gate)
    d_gate = d_hidden * value * (sig * (1.0 + gate * (1.0 - sig)))
    return jnp.concatenate([d_gate, d_hidden * gate * sig], axis=1)


def ffn_forward_kernel(
    layer, gated_ref, res_ref, gain_ref, raw_ref, down_ref, ffn_ref, whole_ref,
    mid_hbm, normed_hbm, up_hbm, hidden_hbm, *refs
):
    last = layer == LAYERS - 1
    if not last:
        out_ref, *refs = refs
    wup_ref, wdown_ref, wout_ref, loads, shard_loads, *refs = refs
    mid_ref, normed_ref, up_ref, hidden_ref, out_sems, *scratch = refs
    outgoing = Outgoing(out_sems)
    loaded_out = load_whole(raw_ref.at[layer], wout_ref, loads.at[2])
    loaded = load_shard((ffn_ref.at[layer], up_lanes, whole_ref), wup_ref, shard_loads)
    if not last:
        loaded_down = load_down(down_ref.at[layer], wdown_ref, loads.at[1])
    size = res_ref.shape[0]
    count = size // SUB
    y, c = place()
    ready = greet(y, c)
    first = Scatter(*scratch[:7], size)
    second = Scatter(*scratch[7:14], size)
    gather = Gather(normed_ref, *scratch[14:], size)

    loaded_out()

    def branch(rows):
        return mm(gated_ref[rows, :], wout_ref[...])

    for part in range(2):
        yy = 1 - y if part == 0 else y
        for i in range(count):
            value = branch(shard_rows(yy, 1 - c, i, size))
            if part == 0 and i == 0:
                ready()
            first.give(part, i, value)
            first.hold(part, i, branch(shard_rows(yy, c, i, size)))
            if part == 0:
                first.relay(i)
    for i in range(count):
        rows = slice(i * SUB, (i + 1) * SUB)
        mid = res_ref[rows, :] + first.total(i)
        mid_ref[rows, :] = mid
        normed_ref[gather.own(i), :] = normalise(mid, gain_ref[...]).astype(bf16)
        gather.start(i)

    def feed(rows):
        up = mm(normed_ref[rows, :], wup_ref[...])
        up_ref[rows, :] = up.astype(bf16)
        hidden = swiglu(up).astype(bf16)
        hidden_ref[rows, :] = hidden
        outgoing.put(normed_ref.at[rows], normed_hbm.at[rows])
        outgoing.put(up_ref.at[rows], up_hbm.at[rows])
        outgoing.put(hidden_ref.at[rows], hidden_hbm.at[rows])
        return None if last else mm(hidden, wdown_ref[...])

    outgoing.put(mid_ref, mid_hbm)
    loaded()
    if last:
        for rows in in_order(gather):
            feed(rows)
    else:
        loaded_down()
        for i in range(count):
            second.hold(1, i, feed(gather.own(i)))
        for i in range(count):
            second.give(1, i, feed(gather.sibling(i)))
        for i in range(count):
            near = gather.across(i)
            second.hold(0, i, feed(near))
            second.give(0, i, feed(gather.diagonal(i)))
            second.relay(i)
        for i in range(count):
            rows = slice(i * SUB, (i + 1) * SUB)
            out_ref[rows, :] = mid_ref[rows, :] + second.total(i)
    first.finish()
    if not last:
        second.finish()
    gather.finish()
    outgoing.wait()


def ffn_forward(layer, gated, residual, gain, w_out, w_down, w_up):
    size, width = residual.shape
    tokens = 4 * size
    return call(
        partial(ffn_forward_kernel, layer),
        (
            like(size, width),
            like(tokens, width, dtype=bf16),
            like(tokens, 1536, dtype=bf16),
            like(tokens, 768, dtype=bf16),
        )
        + (like(size, width),) * (layer < LAYERS - 1),
        (gated, residual, gain),
        [
            pltpu.VMEM((width, 1536), bf16),
            pltpu.VMEM((768, width), bf16),
            pltpu.VMEM((512, width), bf16),
            pltpu.SemaphoreType.DMA((3,)),
            pltpu.SemaphoreType.DMA((13,)),
            pltpu.VMEM((size, width), f32),
            pltpu.VMEM((tokens, width), bf16),
            pltpu.VMEM((tokens, 1536), bf16),
            pltpu.VMEM((tokens, 768), bf16),
            pltpu.SemaphoreType.DMA((25,)),
        ]
        + Scatter.scratch(size, width)
        + Scatter.scratch(size, width)
        + gather_sems(size),
        (2, 12)[layer],
        "ffn_forward",
        (w_out, w_down) + w_up,
        (0, 1, 2, 3),
    )


class Owners:
    def __init__(self, keep, send):
        self.keep, self.send = keep, send
        self.x = lax.axis_index("rep") % 2

    def put(self, r, store):
        @pl.when(self.x == r % 2)
        def _():
            store(self.keep.at[r // 2])

        @pl.when(self.x != r % 2)
        def _():
            store(self.send.at[r // 2])


def store_columns(buf, value, at):
    rows = pl.ds(at, value.shape[0])
    for r in range(8):

        def store(ref):
            ref[rows, :] = value[:, 128 * r : 128 * r + 128].astype(bf16)

        buf.put(r, store)


def store_up(buf, staged, d, c):
    own_half = (grid_of((32, 128), 1) >> 6) == c
    for r in range(8):
        rows = slice(32 * r, 32 * r + 32)

        def tile(side, j):
            lane = pl.multiple_of(768 * side + 128 * j, 128)
            return staged[rows, pl.ds(lane, 128)]

        tiles = [tile(j // 5, j % 5 + c) for j in range(10)]
        turned = pltpu.roll(tile(1, 5 - 5 * c), 64, 1)
        tiles.append(jnp.where(own_half, tile(0, 5 - 5 * c), turned))

        def store(ref):
            for j, value in enumerate(tiles):
                at = UP_AT + (d * 11 + j) * 32
                ref[at : at + 32, :] = value.astype(bf16)

        buf.put(r, store)


def store_rows(buf, value, d, base):
    blocks = value.shape[1] // 128
    for r in range(8):

        def store(ref):
            for j in range(blocks):
                at = base + (d * blocks + j) * 32
                ref[at : at + 32, :] = value[
                    32 * r : 32 * r + 32, 128 * j : 128 * j + 128
                ].astype(bf16)

        buf.put(r, store)


UP_AT, DOWN_AT, OUT_AT, FFN_ROWS = 0, 1408, 2112, 2624
SMALL_AT, IN_ROWS = 1536, 1552


def ffn_backward_kernel(
    layer, dres_ref, gain_ref, ddown_hbm, up_hbm, hidden_hbm, normed_hbm, mid_hbm, gated_hbm,
    raw_ref, down_ref, ffn_ref, whole_ref,
    dmid_ref, dgated_hbm, ggain_ref, keep_hbm, send_hbm,
    wup_ref, wdown_ref, wout_ref, loads, shard_loads, ddown_ref, dup_ref, dbranch_ref, staged,
    up_ref, hidden_ref, normed_ref, mid_ref, gated_ref, dgated_ref, keep_ref, send_ref,
    late_sems, out_sems, *scratch,
):
    buf_ref = Owners(keep_ref, send_ref)
    outgoing = Outgoing(out_sems)
    loaded_out = load_whole(raw_ref.at[layer], wout_ref, loads.at[2])
    loaded = load_shard((ffn_ref.at[layer], up_lanes, whole_ref), wup_ref, shard_loads)
    loaded_down = load_down(down_ref.at[layer], wdown_ref, loads.at[1])
    size = dres_ref.shape[0]
    count = size // SUB
    y, c = place()
    ready = greet(y, c)
    gathered = layer == LAYERS - 1
    if gathered:
        loaded_rows = load_whole(ddown_hbm, ddown_ref, late_sems.at[5])
    else:
        first = Gather(ddown_ref, *scratch[:2], size)
    second = Gather(dbranch_ref, *scratch[2:4], size)
    scatter = Scatter(*scratch[4:], size)
    late = [
        load_whole(src, dst, late_sems.at[k])
        for k, (src, dst) in enumerate(
            (
                (up_hbm, up_ref),
                (hidden_hbm, hidden_ref),
                (mid_hbm, mid_ref),
                (normed_hbm, normed_ref),
                (gated_hbm, gated_ref),
            )
        )
    ]
    if not gathered:
        for i in range(count):
            ddown_ref[first.own(i), :] = dres_ref[i * SUB : (i + 1) * SUB, :].astype(bf16)
            if i == 0:
                ready()
            first.start(i)

    def feed(rows):
        d_hidden = mm(ddown_ref[rows, :], wdown_ref[...], NT)
        d_up = swiglu_back(up_ref[rows, :].astype(f32), d_hidden).astype(bf16)
        dup_ref[rows, :] = d_up
        return mm(d_up, wup_ref[...], NT)

    loaded()
    loaded_down()
    late[0]()
    if gathered:
        loaded_rows()
        for part in range(2):
            yy = 1 - y if part == 0 else y
            for i in range(count):
                value = feed(shard_rows(yy, 1 - c, i, size))
                if part == 0 and i == 0:
                    ready()
                scatter.give(part, i, value)
                scatter.hold(part, i, feed(shard_rows(yy, c, i, size)))
                if part == 0:
                    scatter.relay(i)
    else:
        for i in range(count):
            scatter.hold(1, i, feed(first.own(i)))
        for i in range(count):
            scatter.give(1, i, feed(first.sibling(i)))
        for i in range(count):
            near = first.across(i)
            scatter.hold(0, i, feed(near))
            scatter.give(0, i, feed(first.diagonal(i)))
            scatter.relay(i)
    late[1]()
    for m in range(6):
        value = mm(hidden_ref[:, 128 * m : 128 * m + 128], ddown_ref[...], TN)
        store_columns(buf_ref, value, pl.multiple_of(DOWN_AT + 128 * m - 64 * c, 64))
    ggain_ref[...] = jnp.zeros_like(ggain_ref)
    late[2]()
    for i in range(count):
        rows = slice(i * SUB, (i + 1) * SUB)
        d_norm, g_gain = normalise_back(mid_ref[rows, :], gain_ref[...], scatter.total(i))
        d_mid = dres_ref[rows, :] + d_norm
        dmid_ref[rows, :] = d_mid
        ggain_ref[0:1, :] += g_gain
        dbranch_ref[second.own(i), :] = d_mid.astype(bf16)
        second.start(i)
    late[3]()
    for d in range(4):
        lanes = pl.ds(pl.multiple_of(relative(y, c, d) * 256, 256), 256)
        staged[...] = mm(normed_ref[:, lanes], dup_ref[...], TN)
        store_up(buf_ref, staged, d, c)
    for keep, hbm in ((keep_ref, keep_hbm), (send_ref, send_hbm)):
        rows = pl.ds(0, OUT_AT)
        outgoing.put(keep.at[:, rows], hbm.at[:, rows])
    loaded_out()
    for rows in in_order(second):
        dgated_ref[rows, :] = mm(dbranch_ref[rows, :], wout_ref[...], NT).astype(bf16)
    outgoing.put(dgated_ref, dgated_hbm)
    late[4]()
    for m in range(4):
        value = mm(gated_ref[:, 128 * m : 128 * m + 128], dbranch_ref[...], TN)
        store_columns(buf_ref, value, OUT_AT + 128 * m)
    for keep, hbm in ((keep_ref, keep_hbm), (send_ref, send_hbm)):
        rows = pl.ds(OUT_AT, FFN_ROWS - OUT_AT)
        outgoing.put(keep.at[:, rows], hbm.at[:, rows])
    if not gathered:
        first.finish()
    second.finish()
    scatter.finish()
    outgoing.wait()


def ffn_backward(layer, d_res, d_down, up, hidden, normed, mid, gain, gated, w_out, w_down, w_up):
    size, width = d_res.shape
    tokens = 4 * size
    return call(
        partial(ffn_backward_kernel, layer),
        (
            like(size, width),
            like(tokens, 512, dtype=bf16),
            like(8, width),
            like(4, FFN_ROWS, 128, dtype=bf16),
            like(4, FFN_ROWS, 128, dtype=bf16),
        ),
        (d_res, gain),
        [
            pltpu.VMEM((width, 1536), bf16),
            pltpu.VMEM((768, width), bf16),
            pltpu.VMEM((512, width), bf16),
            pltpu.SemaphoreType.DMA((3,)),
            pltpu.SemaphoreType.DMA((13,)),
            pltpu.VMEM((tokens, width), bf16),
            pltpu.VMEM((tokens, 1536), bf16),
            pltpu.VMEM((tokens, width), bf16),
            pltpu.VMEM((256, 1536), f32),
        ]
        + [pltpu.VMEM(array.shape, array.dtype) for array in (up, hidden, normed, mid, gated, gated)]
        + [pltpu.VMEM((4, FFN_ROWS, 128), bf16)] * 2
        + [pltpu.SemaphoreType.DMA((6,)), pltpu.SemaphoreType.DMA((5,))]
        + gather_sems(size)
        + gather_sems(size)
        + Scatter.scratch(size, width),
        (3, 13)[layer],
        "ffn_backward",
        (d_down, up, hidden, normed, mid, gated, w_out, w_down) + w_up,
        (1, 3, 4),
    )


def project_backward_kernel(
    parts, dproj_ref, dsmall_ref, ab_ref, gain_ref, gtwo_ref, gtaps_ref, gheads_ref, *refs
):
    normed_hbm, res_hbm, dmid_hbm, *refs = refs
    parts, refs = refs[:parts], refs[parts:]
    dres_ref, keep_hbm, send_hbm, w_ref, loads, table, *refs = refs
    normed_ref, res_ref, dmid_ref, keep_ref, send_ref, late_sems, out_sems, *scratch = refs
    buf_ref = Owners(keep_ref, send_ref)
    outgoing = Outgoing(out_sems)
    loaded = load_shard(in_parts(parts), w_ref, loads)
    late = [
        load_whole(src, dst, late_sems.at[k])
        for k, (src, dst) in enumerate(
            ((normed_hbm, normed_ref), (res_hbm, res_ref), (dmid_hbm, dmid_ref))
        )
    ]
    size = res_ref.shape[0]
    count = size // SUB
    y, c = place()
    ready = greet(y, c)
    scatter = Scatter(*scratch, size)

    def back(rows):
        return mm(dproj_ref[rows, :], w_ref[...], NT) + mm(dsmall_ref[rows, :], ab_ref[...], NT)

    def weight_grad(d):
        lanes = pl.ds(pl.multiple_of(relative(y, c, d) * 256, 256), 256)
        value = mm(normed_ref[:, lanes], dproj_ref[...], TN)
        store_rows(buf_ref, value, d, 0)

    loaded()
    for part in range(2):
        yy = 1 - y if part == 0 else y
        for i in range(count):
            value = back(shard_rows(yy, 1 - c, i, size))
            if part == 0 and i == 0:
                ready()
            scatter.give(part, i, value)
            scatter.hold(part, i, back(shard_rows(yy, c, i, size)))
            if part == 0:
                scatter.relay(i)
    late[0]()
    for d in range(4):
        weight_grad(d)
    for keep, hbm in ((keep_ref, keep_hbm), (send_ref, send_hbm)):
        rows = pl.ds(0, SMALL_AT)
        outgoing.put(keep.at[:, rows], hbm.at[:, rows])
    ab_grad = mm(dsmall_ref[...], normed_ref[...], TN)
    table[...] = jnp.zeros_like(table)
    for k in range(8):
        lanes = slice(128 * k, 128 * k + 128)
        for j in range(4):
            table[8 * j + k : 8 * j + k + 1, :] = gtaps_ref[j : j + 1, lanes]
            table[32 + 8 * j + k : 33 + 8 * j + k, :] = ab_grad[j : j + 1, lanes]
        table[72 + k : 73 + k, :] = gtwo_ref[0:1, lanes]
    table[80:81, :] = gheads_ref[0:1, 0:128]
    table[81:82, :] = gheads_ref[0:1, 128:256]
    table[82:83, :] = gheads_ref[1:2, 0:128]
    table[83:84, :] = gheads_ref[2:3, 0:128]
    gain_sum = jnp.zeros((1, res_ref.shape[1]), f32)
    late[1]()
    late[2]()
    for i in range(count):
        rows = slice(i * SUB, (i + 1) * SUB)
        d_norm, g_gain = normalise_back(res_ref[rows, :], gain_ref[...], scatter.total(i))
        dres_ref[rows, :] = dmid_ref[rows, :] + d_norm
        gain_sum = gain_sum + g_gain
    for k in range(8):
        table[64 + k : 65 + k, :] = gain_sum[:, 128 * k : 128 * k + 128]
    for r in range(8):

        def store(ref):
            ref[SMALL_AT:IN_ROWS, :] = table[16 * r : 16 * r + 16, :].astype(bf16)

        buf_ref.put(r, store)
    for keep, hbm in ((keep_ref, keep_hbm), (send_ref, send_hbm)):
        rows = pl.ds(SMALL_AT, IN_ROWS - SMALL_AT)
        outgoing.put(keep.at[:, rows], hbm.at[:, rows])
    scatter.finish()
    outgoing.wait()


def project_backward(d_proj, d_small, weight, ab, normed, residual, gain, d_mid, g_two, g_taps, g_heads):
    size, width = residual.shape
    return call(
        partial(project_backward_kernel, len(weight)),
        (like(size, width),) + (like(4, IN_ROWS, 128, dtype=bf16),) * 2,
        (d_proj, d_small, ab, gain, g_two, g_taps, g_heads),
        [
            pltpu.VMEM((width, 1536), bf16),
            pltpu.SemaphoreType.DMA((13,)),
            pltpu.VMEM((128, 128), f32),
        ]
        + [pltpu.VMEM(array.shape, array.dtype) for array in (normed, residual, d_mid)]
        + [pltpu.VMEM((4, IN_ROWS, 128), bf16)] * 2
        + [pltpu.SemaphoreType.DMA((3,)), pltpu.SemaphoreType.DMA((4,))]
        + Scatter.scratch(size, width),
        4 if len(weight) == 1 else 7,
        "project_backward",
        (normed, residual, d_mid) + tuple(weight),
        (1, 2),
    )


def assemble_kernel(
    f1, f2, f3, f4, last_ref, grad_ref,
    down_ref, out_ref, up_ref, in_ref, table_ref, block_ref, input_ref,
    p1, p2, p3, p4, down, out, up, whole, loads, stores,
):
    y, c = place()
    copies = [
        pltpu.make_async_copy(src, dst, loads.at[k])
        for k, (src, dst) in enumerate(((f1, p1), (f2, p2), (f3, p3), (f4, p4)))
    ]
    for copy in copies:
        copy.start()
    block_ref[...] = last_ref[...].astype(bf16)
    input_ref[...] = grad_ref[...].astype(bf16)
    left = grid_of((32, 128), 1) < 64

    def ffn(layer, pieces):
        def up_rows(r, carry):
            rows = pl.ds(pl.multiple_of(32 * r, 32), 32)
            for m in range(2):
                tiles = []
                for s in (2 * m, 2 * m + 1):
                    at = UP_AT + offset_of(y, c, s) * 352
                    tiles.append(
                        [
                            pieces[r, pl.ds(pl.multiple_of(at + 32 * j, 32), 32), :].astype(f32)
                            for j in range(11)
                        ]
                    )
                even, odd = tiles
                middle = (
                    jnp.where(left, even[10], odd[10]),
                    pltpu.roll(jnp.where(left, odd[10], even[10]), 64, 1),
                )
                for side in range(2):
                    part = slice(5 * side, 5 * side + 5)
                    base = FF * side + 1408 * m
                    for j, tile in enumerate(even[part] + [middle[side]] + odd[part]):
                        up[layer, rows, base + 128 * j : base + 128 * j + 128] = tile
            return carry

        lax.fori_loop(0, 8, up_rows, 0)
        done = [pltpu.make_async_copy(up.at[layer], up_ref.at[layer], stores.at[layer, 0])]
        done[0].start()
        for r in range(8):
            lanes = slice(128 * r, 128 * r + 128)
            down[layer, :, lanes] = pieces[r, DOWN_AT:OUT_AT, :].astype(f32)
            out[layer, :, lanes] = pieces[r, OUT_AT:FFN_ROWS, :].astype(f32)
        done.append(pltpu.make_async_copy(down.at[layer], down_ref.at[layer], stores.at[layer, 1]))
        done.append(pltpu.make_async_copy(out.at[layer], out_ref.at[layer], stores.at[layer, 2]))
        done[1].start()
        done[2].start()
        return done

    def projection(layer, pieces):
        def in_rows(r, carry):
            rows = pl.ds(pl.multiple_of(32 * r, 32), 32)
            for s in range(4):
                at = offset_of(y, c, s) * 384
                for lane, wide, to in in_lanes(s):
                    for k in range(wide // 128):
                        j = to // 128 + k
                        tile = pieces[r, pl.ds(pl.multiple_of(at + 32 * j, 32), 32), :]
                        column = lane + 128 * k
                        whole[layer, rows, column : column + 128] = tile.astype(f32)
            return carry

        lax.fori_loop(0, 8, in_rows, 0)
        done = pltpu.make_async_copy(whole.at[layer], in_ref.at[layer], stores.at[layer, 3])
        done.start()
        for s in range(4):
            at = pl.ds(pl.multiple_of(SMALL_AT + 16 * offset_of(y, c, s), 16), 16)
            for r in range(8):
                table_ref[s, layer, 16 * r : 16 * r + 16, :] = pieces[r, at, :].astype(f32)
        return [done]

    waiting = []
    copies[0].wait()
    waiting += ffn(1, p1)
    copies[1].wait()
    waiting += projection(1, p2)
    copies[2].wait()
    waiting += ffn(0, p3)
    copies[3].wait()
    waiting += projection(0, p4)
    for store in waiting:
        store.wait()


def offset_of(y, c, s):
    sy, sc = s // 2, s % 2
    return 2 * (y + sy - 2 * y * sy) + c + sc - 2 * c * sc


def assemble(finals, last, grad):
    spot = pl.BlockSpec(memory_space=pl.ANY)
    vmem = pl.BlockSpec(memory_space=pltpu.VMEM)
    shapes = [(LAYERS, 704, 1024), (LAYERS, 512, 1024), (LAYERS, 256, 2 * FF), (LAYERS, 256, CH + HV)]
    return pl.pallas_call(
        assemble_kernel,
        out_shape=tuple(like(*shape) for shape in shapes)
        + (like(4, LAYERS, 128, 128),)
        + (like(*last.shape, dtype=bf16),) * 2,
        in_specs=[spot] * 4 + [vmem] * 2,
        out_specs=(spot,) * 4 + (vmem,) * 3,
        scratch_shapes=[pltpu.VMEM(final.shape, bf16) for final in finals]
        + [pltpu.VMEM(shape, f32) for shape in shapes]
        + [pltpu.SemaphoreType.DMA((4,)), pltpu.SemaphoreType.DMA((2, 4))],
        compiler_params=pltpu.CompilerParams(vmem_limit_bytes=LIMIT),
        name="assemble",
    )(*finals, last, grad)


FFN_MOVE, IN_MOVE = (UP_AT, 352), (0, 384)
GATHERED_ROWS = SMALL_AT + 4 * 16


def add_into(dst, left, right):
    dst[...] = (left[...].astype(f32) + right[...].astype(f32)).astype(bf16)


class Group:
    def __init__(self, number, piece, moved, final, move, sems, x_first=False):
        self.number, self.piece, self.moved, self.final = number, piece, moved, final
        self.at, self.part = move
        self.send, self.recv, self.local = sems
        self.x_first = x_first
        rank = lax.axis_index("rep")
        self.rank, self.x, self.z = rank, rank % 2, (rank % 8) // 2
        self.y, self.c = place()
        self.extra = moved.shape[0] > piece.shape[0]

    def swaps(self, d):
        target = relative(self.y, self.c, d)
        rows = pl.ds(self.at + d * self.part, self.part)
        spans = [(rows, rows, d)]
        if self.extra:
            spans.append((pl.ds(SMALL_AT, 16), pl.ds(SMALL_AT + 16 * d, 16), 20 + d))
        return [
            pltpu.make_async_remote_copy(
                src_ref=self.piece.at[src], dst_ref=self.moved.at[dst],
                send_sem=self.send.at[self.number, k], recv_sem=self.recv.at[self.number, k],
                device_id={"grp": target}, device_id_type=MESH,
            )
            for src, dst, k in spans
        ]

    def start_swap(self):
        for d in range(1, 4):
            for copy in self.swaps(d):
                copy.start()
        first = self.at + self.part
        self.moved[0:first, :] = self.piece[0:first, :]
        rest, last = self.at + 4 * self.part, self.piece.shape[0]
        if rest < last:
            self.moved[rest:last, :] = self.piece[rest:last, :]

    def wait_swap(self):
        for d in range(1, 4):
            for copy in self.swaps(d):
                copy.wait_recv()

    def owner(self, source_z, which):
        return 2 * source_z + (self.x if which == 0 else 1 - self.x)

    def move(self, step, source_z, kind, which=0):
        owner = self.owner(source_z, which)
        src = self.moved if step == 0 and which == 0 else self.final.at[owner]
        number = self.number if which == 0 else 4
        slot = 4 + 4 * kind + step
        return pltpu.make_async_remote_copy(
            src_ref=src, dst_ref=self.final.at[owner],
            send_sem=self.send.at[number, slot], recv_sem=self.recv.at[number, slot],
            device_id={"rep": self.rank + 2 - 4 * kind}, device_id_type=MESH,
        )

    def x_move(self, step, source_z):
        owner = self.owner(source_z, 0)
        src = self.moved if step == 0 else self.final.at[owner]
        return pltpu.make_async_remote_copy(
            src_ref=src, dst_ref=self.final.at[owner],
            send_sem=self.send.at[self.number, 12 + step + 3],
            recv_sem=self.recv.at[self.number, 12 + source_z],
            device_id={"rep": flip(self.rank)}, device_id_type=MESH,
        )

    def own_copy(self):
        return pltpu.make_async_copy(
            self.moved, self.final.at[self.owner(self.z, 0)], self.local.at[self.number]
        )

    def both_ways(self, which, act):
        @pl.when(self.z < 3)
        def _():
            act(self.move(0, self.z, 0, which))

        @pl.when(self.z > 0)
        def _():
            act(self.move(0, self.z, 1, which))

    def begin(self):
        self.both_ways(0, lambda copy: copy.start())
        self.x_move(0, self.z).start()
        self.own_copy().start()

    def begin_other(self):
        self.x_move(0, self.z).wait_recv()
        self.both_ways(1, lambda copy: copy.start())

    def passes(self, k, which, arrive, onward):
        z = self.z

        @pl.when(z >= k)
        def _():
            arrive(k, z - k, 0)

            @pl.when(z < 3)
            def _():
                onward(self.move(k, z - k, 0, which))

        @pl.when(z + k <= 3)
        def _():
            arrive(-k, z + k, 1)

            @pl.when(z > 0)
            def _():
                onward(self.move(k, z + k, 1, which))

    def relay(self, k, which=0):
        def arrive(step, source, kind):
            self.move(abs(step) - 1, source, kind, which).wait_recv()
            if not self.x_first:
                self.x_move(step, source).start()

        self.passes(k, which, arrive, lambda copy: copy.start())

    def finish(self):
        for which in range(2 if self.x_first else 1):

            def arrive(step, source, kind):
                if not self.x_first:
                    self.x_move(step, source).wait_send()

            for k in range(1, 4):
                self.passes(k, which, arrive, lambda copy: copy.wait_send())
            self.both_ways(which, lambda copy: copy.wait_send())
        self.x_move(0, self.z).wait_send()
        if not self.x_first:
            for source in range(4):
                self.x_move(0, source).wait_recv()
        self.own_copy().wait()
        for d in range(1, 4):
            for copy in self.swaps(d):
                copy.wait_send()


class Line:
    def __init__(self, values, right, left, send, recv):
        self.values, self.right, self.left = values, right, left
        self.send, self.recv = send, recv
        self.rank = lax.axis_index("rep")
        self.z = (self.rank % 8) // 2

    def go(self, o, toward):
        land = self.right if toward == 0 else self.left
        return pltpu.make_async_remote_copy(
            src_ref=self.values.at[o], dst_ref=land.at[o],
            send_sem=self.send.at[toward, o], recv_sem=self.recv.at[toward, o],
            device_id={"rep": self.rank + 2 - 4 * toward}, device_id_type=MESH,
        )

    def edge(self, step, act):
        @pl.when(self.z == 0)
        def _():
            act(self.go(3 - step, 0))

        @pl.when(self.z == 3)
        def _():
            act(self.go(step, 1))

    def start_edge(self, step):
        if step > 0:
            self.edge(step - 1, lambda copy: copy.wait_send())
        self.edge(step, lambda copy: copy.start())

    def inner(self, step):
        z, o = self.z, 3 - step

        @pl.when((z > 0) & (z < o))
        def _():
            self.go(o, 0).wait_recv()
            add_into(self.values.at[o], self.values.at[o], self.right.at[o])
            self.go(o, 0).start()

        @pl.when((z < 3) & (z > step))
        def _():
            self.go(step, 1).wait_recv()
            add_into(self.values.at[step], self.values.at[step], self.left.at[step])
            self.go(step, 1).start()

    def total(self, out):
        z = self.z
        for o in range(4):

            @pl.when(z == o)
            def _():
                value = self.values[o].astype(f32)
                if o > 0:
                    self.go(o, 0).wait_recv()
                    value = value + self.right[o].astype(f32)
                if o < 3:
                    self.go(o, 1).wait_recv()
                    value = value + self.left[o].astype(f32)
                out[...] = value.astype(bf16)

    def finish(self):
        self.edge(2, lambda copy: copy.wait_send())
        for o in range(4):

            @pl.when((self.z > 0) & (self.z < o))
            def _():
                self.go(o, 0).wait_send()

            @pl.when((self.z < 3) & (self.z > o))
            def _():
                self.go(o, 1).wait_send()


def finish_kernel(
    p1, p2, k3, a3, k4, b4, hidden_hbm, down_raw, mid_ref, f1, f2, f3, f4, last_ref,
    q1, q2, q3, q4, e1, e2, e3, e4, v3, x3, r3, l3, v4, x4, r4, l4,
    send, recv, local, send3, recv3, send4, recv4, send5, recv5, loads,
    hidden_ref, wdown_ref, down_loads, *scratch,
):
    loaded_hidden = load_whole(hidden_hbm, hidden_ref, down_loads.at[0])
    loaded_down = load_down(down_raw.at[LAYERS - 1], wdown_ref, down_loads.at[1])
    scatter = Scatter(*scratch, mid_ref.shape[0])
    count = scatter.size // SUB
    rank = lax.axis_index("rep")
    x, z = rank % 2, (rank % 8) // 2
    y, c = place()
    loaded = [
        pltpu.make_async_copy(p1, q1, loads.at[0]),
        pltpu.make_async_copy(p2, q2, loads.at[1]),
        pltpu.make_async_copy(k3, v3, loads.at[2]),
        pltpu.make_async_copy(k4, v4, loads.at[3]),
        pltpu.make_async_copy(a3, x3, loads.at[4]),
    ]
    for load in loaded:
        load.start()
    barrier = pltpu.get_barrier_semaphore()
    pl.semaphore_signal(
        barrier, inc=1, device_id={"rep": rank + 1 - 2 * x}, device_id_type=MESH
    )
    for d in range(1, 4):
        dy, dc = d // 2, d % 2
        target = 2 * (y + dy - 2 * y * dy) + c + dc - 2 * c * dc
        pl.semaphore_signal(barrier, inc=1, device_id={"grp": target}, device_id_type=MESH)

    @pl.when(z > 0)
    def _():
        pl.semaphore_signal(barrier, inc=1, device_id={"rep": rank - 2}, device_id_type=MESH)

    @pl.when(z < 3)
    def _():
        pl.semaphore_signal(barrier, inc=1, device_id={"rep": rank + 2}, device_id_type=MESH)

    @pl.when((z > 0) & (z < 3))
    def _():
        pl.semaphore_wait(barrier, 6)

    @pl.when((z == 0) | (z == 3))
    def _():
        pl.semaphore_wait(barrier, 5)

    def halves(o):
        return pltpu.make_async_remote_copy(
            src_ref=b4.at[o], dst_ref=x4.at[o], send_sem=send5.at[o], recv_sem=recv5.at[o],
            device_id={"rep": rank + 1 - 2 * x}, device_id_type=MESH,
        )

    for o in (3, 0, 2, 1):
        halves(o).start()
    sems = (send, recv, local)

    def down_begin():
        loaded_hidden()
        loaded_down()
        for part in range(2):
            yy = 1 - y if part == 0 else y
            for i in range(count):
                for cc, take in ((1 - c, scatter.give), (c, scatter.hold)):
                    rows = shard_rows(yy, cc, i, scatter.size)
                    take(part, i, mm(hidden_ref[rows, :], wdown_ref[...]))
                if part == 0:
                    scatter.relay(i)

    def down_end():
        for i in range(count):
            rows = slice(i * SUB, (i + 1) * SUB)
            last_ref[rows, :] = mid_ref[rows, :] + scatter.total(i)
        scatter.finish()

    def merge(*owners):
        for o in owners:
            add_into(v3.at[o], v3.at[o], x3.at[o])

    def arrive(*owners):
        for o in owners:
            halves(o).wait_recv()
            add_into(v4.at[o], v4.at[o], x4.at[o])

    g1 = Group(0, q1, e1, f1, FFN_MOVE, sems)
    g2 = Group(1, q2, e2, f2, IN_MOVE, sems)
    g3 = Group(2, q3, e3, f3, FFN_MOVE, sems)
    g4 = Group(3, q4, e4, f4, IN_MOVE, sems)
    line3 = Line(v3, r3, l3, send3, recv3)
    line4 = Line(v4, r4, l4, send4, recv4)
    loaded[0].wait()
    g1.start_swap()
    loaded[1].wait()
    g2.start_swap()
    g1.wait_swap()
    g1.begin()
    down_begin()
    loaded[3].wait()
    arrive(3, 0)
    loaded[2].wait()
    loaded[4].wait()
    merge(3, 0)
    line3.start_edge(0)
    g2.wait_swap()
    g2.begin()
    merge(2, 1)
    line3.start_edge(1)
    g1.relay(1)
    line3.inner(0)
    line3.inner(1)
    line4.start_edge(0)
    g2.relay(1)
    g1.relay(2)
    line3.start_edge(2)
    arrive(2, 1)
    line3.total(q3)
    g3.start_swap()
    g2.relay(2)
    g3.wait_swap()
    g3.begin()
    line4.inner(0)
    line4.start_edge(1)
    line4.inner(1)
    line4.start_edge(2)
    g2.relay(3)
    g1.relay(3)
    g3.relay(1)
    line4.total(q4)
    g4.start_swap()
    g4.wait_swap()
    g4.begin()
    down_end()
    g3.relay(2)
    g4.relay(1)
    g4.relay(2)
    g3.relay(3)
    g4.relay(3)
    for group in (g1, g2, g3, g4):
        group.finish()
    line3.finish()
    line4.finish()
    for o in range(4):
        halves(o).wait_send()


def finish_reduction(p1, p2, k3, a3, k4, b4, hidden, w_down, mid):
    spot = pl.BlockSpec(memory_space=pl.ANY)
    vmem = pl.BlockSpec(memory_space=pltpu.VMEM)
    big, small = p1.shape, p2.shape
    wide = (GATHERED_ROWS, 128)
    dma = pltpu.SemaphoreType.DMA
    return pl.pallas_call(
        finish_kernel,
        out_shape=tuple(like(8, *shape, dtype=bf16) for shape in (big, wide, big, wide))
        + (like(*mid.shape),),
        in_specs=[spot] * 8 + [vmem],
        out_specs=(spot,) * 4 + (vmem,),
        scratch_shapes=[
            pltpu.VMEM(shape, bf16)
            for shape in [big, small] * 2 + [big, wide] * 2
            + [(4,) + big] * 4
            + [(4,) + small] * 4
        ]
        + [dma((5, 24)), dma((5, 24)), dma((4,))]
        + [dma((2, 4))] * 4
        + [dma((4,)), dma((4,)), dma((5,))]
        + [pltpu.VMEM(hidden.shape, bf16), pltpu.VMEM((768, mid.shape[1]), bf16), dma((2,))]
        + Scatter.scratch(*mid.shape),
        compiler_params=pltpu.CompilerParams(
            collective_id=5, has_side_effects=True, vmem_limit_bytes=LIMIT
        ),
        cost_estimate=pl.CostEstimate(flops=1000, bytes_accessed=1000, transcendentals=0),
        name="finish_reduction",
    )(p1, p2, k3, a3, k4, b4, hidden, w_down, mid)


def swap_route(bit, count):
    return [(i, i ^ bit) for i in range(count)]


def planes_of(replicas):
    return [
        [8 * b + 2 * z + x for z in range(4)] for b in range(replicas // 8) for x in range(2)
    ]


def swap_x(array, replicas):
    return lax.ppermute(array, "rep", swap_route(1, replicas))


def add_arrived(kept, arrived):
    return (kept.astype(f32) + arrived.astype(f32)).astype(bf16)


def reduce_z(summed, replicas):
    piece = lax.psum_scatter(
        summed, "rep", scatter_dimension=0, tiled=False, axis_index_groups=planes_of(replicas)
    )
    blocks = replicas // 8
    if blocks > 1:
        piece = lax.psum(
            piece, "rep", axis_index_groups=[[8 * b + r for b in range(blocks)] for r in range(8)]
        )
    return piece


def exchange(piece, at, part):
    moved = [piece[: at + part]]
    for d in range(1, 4):
        moved.append(swap(piece[at + d * part : at + (d + 1) * part], d))
    moved.append(piece[at + 4 * part :])
    if piece.shape[0] == IN_ROWS:
        moved += [swap(piece[SMALL_AT:], d) for d in range(1, 4)]
    return jnp.concatenate(moved, axis=0)


def gather_z(piece, replicas):
    return lax.all_gather(piece, "rep", axis=0, axis_index_groups=planes_of(replicas))


def spread(piece, replicas):
    owned = gather_z(piece, replicas)
    other = swap_x(owned, replicas)
    odd = lax.axis_index("rep") % 2 == 1
    pair = jnp.stack([jnp.where(odd, other, owned), jnp.where(odd, owned, other)], axis=1)
    return pair.reshape((8,) + piece.shape)


def finish_all(
    piece1, piece2, keep3, arrived3, keep4, send4, hidden, w_down, mid, replicas
):
    if replicas == 8:
        return finish_reduction(
            piece1, piece2, keep3, arrived3, keep4, send4, hidden, w_down, mid
        )
    piece3 = reduce_z(add_arrived(keep3, arrived3), replicas)
    piece4 = reduce_z(add_arrived(keep4, swap_x(send4, replicas)), replicas)
    finals = [
        spread(exchange(piece, *move), replicas)
        for piece, move in (
            (piece1, FFN_MOVE), (piece2, IN_MOVE), (piece3, FFN_MOVE), (piece4, IN_MOVE)
        )
    ]
    padded = jnp.zeros((hidden.shape[1], mid.shape[1]), bf16)
    offset = 64 * (lax.axis_index("grp") % 2)
    padded = lax.dynamic_update_slice_in_dim(padded, w_down[LAYERS - 1], offset, 0)
    partial_sum = mm(hidden, padded).astype(bf16)
    down = lax.psum_scatter(partial_sum, "grp", scatter_dimension=0, tiled=True)
    return finals + [mid + down.astype(f32)]


def tie(*values):
    return lax.optimization_barrier(values)


def swap(array, d):
    return lax.ppermute(array, "grp", swap_route(d, 4))


def per_device(
    x_input, norm_gain, w_in, w_ab, conv_w, a_log, dt_bias, out_gain, w_out, ffn_in, ffn_out,
    cotangent,
):
    parts = lax.axis_size("grp")
    replicas = lax.axis_size("rep")
    mine = lax.axis_index("grp")
    rows, width = x_input.shape[1], x_input.shape[2]
    shard = w_in.shape[1]

    pack = jnp.concatenate(
        [
            norm_gain.reshape(-1, 128),
            conv_w.reshape(-1, 128),
            jnp.swapaxes(w_ab, 1, 2).reshape(-1, 128),
            out_gain.reshape(-1, 128),
            jnp.zeros((PACK_ROWS - OUT_GAIN_AT - 1, 128), bf16),
        ]
    ).astype(f32)
    normed, projected, small, in_weight, *rest = start(x_input[0], pack, w_in)
    gains, taps_pair, ab_pair, out_pair = rest[0:4], rest[4:6], rest[6:8], rest[8:10]
    small_weights = []
    for l in range(LAYERS):
        heads = jnp.pad(jnp.stack([a_log[l], dt_bias[l]]).astype(f32), ((0, 6), (2, 124)))
        small_weights.append(
            (
                gains[2 * l], gains[2 * l + 1], ab_pair[l], taps_pair[l], heads, out_pair[l],
            )
        )

    residual = x_input[0].astype(f32)
    kept = []
    in_weights, up_weights = [(in_weight,)], []
    for l in range(LAYERS):
        gain_one, gain_two, ab, taps, heads, gain = small_weights[l]
        if l > 0:
            normed, projected, small = project(residual, gain_one, ab, in_weights[l])
        gated, *saved = mixer_forward(
            l, projected, small, taps, heads, gain, (ffn_in, (w_in, cotangent[0])[l])
        )
        up_weights.append((ffn_in, saved[4]))
        if l == 0:
            near, far = saved[5:]
            in_weights.append(
                (
                    w_in,
                    near,
                    lax.all_gather(far, "rep", axis=0, axis_index_groups=planes_of(replicas)),
                )
            )
        else:
            d_down = saved[5]
        saved = saved[:4]
        mid, normed_two, up, hidden, *residual_out = ffn_forward(
            l, gated, residual, gain_two, w_out, ffn_out, up_weights[l]
        )
        kept.append((residual, normed, projected, small, gated, saved, mid, normed_two, up, hidden))
        if l == 0:
            (residual,) = residual_out

    d_residual = cotangent[0].astype(f32)

    def ffn_part(l, d_residual):
        gain_one, gain_two, ab, taps, heads, gain = small_weights[l]
        residual, normed, projected, small, gated, saved, mid, normed_two, up, hidden = kept[l]
        return ffn_backward(
            l, d_residual, d_down, up, hidden, normed_two, mid, gain_two, gated, w_out, ffn_out,
            up_weights[l],
        )

    def mixer_part(l, d_gated):
        gain_one, gain_two, ab, taps, heads, gain = small_weights[l]
        residual, normed, projected, small, gated, saved, mid, normed_two, up, hidden = kept[l]
        return mixer_backward(projected, small, taps, heads, gain, saved, d_gated)

    def project_part(l, d_mid, g_gain_two, mixed):
        gain_one, gain_two, ab, taps, heads, gain = small_weights[l]
        residual, normed, projected, small, gated, saved, mid, normed_two, up, hidden = kept[l]
        d_projected, d_small, g_taps, g_heads = mixed
        return project_backward(
            d_projected, d_small, in_weights[l], ab, normed, residual, gain_one, d_mid,
            g_gain_two, g_taps, g_heads,
        )

    d_mid, d_gated, g_gain_two, keep1, send1 = ffn_part(1, d_residual)
    arrived1 = swap_x(send1, replicas)
    mixed = mixer_part(1, d_gated)
    d_residual, keep2, send2 = project_part(1, d_mid, g_gain_two, mixed)
    d_residual, arrived1 = tie(d_residual, arrived1)
    piece1 = reduce_z(add_arrived(keep1, arrived1), replicas)
    arrived2 = swap_x(send2, replicas)
    d_mid, d_gated, g_gain_two, keep3, send3 = ffn_part(0, d_residual)
    d_gated, piece1, arrived2 = tie(d_gated, piece1, arrived2)
    piece2 = reduce_z(add_arrived(keep2, arrived2), replicas)
    arrived3 = swap_x(send3, replicas)
    mixed = mixer_part(0, d_gated)
    d_residual, keep4, send4 = project_part(0, d_mid, g_gain_two, mixed)
    d_residual, arrived3 = tie(d_residual, arrived3)
    final1, final2, final3, final4, last = finish_all(
        piece1, piece2, keep3, arrived3, keep4, send4, kept[-1][-1], ffn_out, kept[-1][6], replicas
    )
    finals = (final1, final2, final3, final4)
    residual = last
    down_grads, out_grads, up_grads, w_in_grads, everyone, *ends = assemble(
        finals, residual, d_residual
    )
    block_output, input_grad = (end[None] for end in ends)

    tables = lax.dynamic_index_in_dim(everyone, mine, 0, keepdims=False)
    sums = jnp.sum(everyone[:, :, 64:82], axis=0)
    grad_gain = lax.dynamic_slice_in_dim(
        sums[:, :16].reshape(LAYERS, 2, width), mine * shard, shard, 2
    )
    grad_out_gain = lax.dynamic_slice_in_dim(
        sums[:, 16:18].reshape(LAYERS, DV), mine * (DV // 4), DV // 4, 1
    )
    grad_a_log = tables[:, 82, 2:4]
    grad_dt = tables[:, 83, 2:4]
    taps_sum = everyone[:, :, 0:32].reshape(4, LAYERS, 4, 1024)

    def side_by_side(array):
        return jnp.moveaxis(array, 0, 2).reshape(LAYERS, 4, -1)

    conv_full = jnp.concatenate(
        [
            side_by_side(taps_sum[..., :256]),
            side_by_side(taps_sum[..., 256:512]),
            side_by_side(taps_sum[..., 512:]),
        ],
        axis=2,
    )
    grad_conv = lax.dynamic_slice_in_dim(conv_full, mine * 1024, 1024, 2)
    ab_sum = everyone[:, :, 32:64].reshape(4, LAYERS, 4, width)
    ab_sum = lax.dynamic_slice_in_dim(ab_sum, mine * shard, shard, 3)
    grad_ab = jnp.transpose(ab_sum.reshape(4, LAYERS, 2, 2, shard), (1, 4, 2, 0, 3)).reshape(
        LAYERS, shard, 2 * H
    )
    return (
        block_output,
        input_grad,
        grad_gain,
        w_in_grads,
        grad_ab,
        grad_conv,
        grad_a_log,
        grad_dt,
        grad_out_gain,
        out_grads,
        up_grads,
        down_grads,
    )


def solution(mesh):
    rows = P("rep", "grp", None)
    first = P(None, "grp")
    middle = P(None, "grp", None)
    last = P(None, None, "grp")
    in_specs = (rows, last, middle, middle, last, first, first, first, middle, middle, middle, rows)
    out_specs = (rows, rows, last, middle, middle, last, first, first, first, middle, middle, middle)
    return jax.shard_map(
        per_device, mesh=mesh, in_specs=in_specs, out_specs=out_specs, check_vma=False
    )
```

```python
from functools import partial
import math

import jax
import jax.numpy as jnp
from jax import lax
from jax.sharding import PartitionSpec as P
from jax.experimental import pallas as pl
from jax.experimental.pallas import tpu as pltpu

H = 8
DK = 128
DV = 256
FF = 2816
CONV = 4
LAYERS = 2
HK = 1024
HV = 2048
CH = 4096
CHUNK = 128

f32 = jnp.float32
bf16 = jnp.bfloat16
HIGH = lax.Precision.HIGHEST
epsilon = 1e-06
out_floor = 0.02
NN = ((1,), (0,))
NT = ((1,), (1,))
TN = ((0,), (0,))


def mm(left, right, dims=NN, precision=None):
    return lax.dot_general(
        left, right, (dims, ((), ())), precision=precision, preferred_element_type=f32
    )


def mh(left, right, dims=NN):
    return mm(left, right, dims, HIGH)


def grid_of(shape, dim):
    return lax.broadcasted_iota(jnp.int32, shape, dim)


def conv_chunk(x_ext, taps):
    return sum(x_ext[5 + j : 5 + j + CHUNK] * taps[j : j + 1] for j in range(CONV))


def decay_chunk(small, heads_ref):
    lane = grid_of(small.shape, 1)
    strength = jax.nn.sigmoid(small)
    shifted_logit = small + heads_ref[1:2, :]
    soft = jnp.maximum(shifted_logit, 0.0) + jnp.log1p(jnp.exp(-jnp.abs(shifted_logit)))
    log_decay = -jnp.exp(heads_ref[0:1, :]) * soft
    row = grid_of((CHUNK, CHUNK), 0)
    col = grid_of((CHUNK, CHUNK), 1)
    lower_ones = jnp.where(row >= col, 1.0, 0.0).astype(f32)
    cumulative = mm2(lower_ones.astype(bf16), log_decay)
    turned = jnp.where(lane < 2, strength, cumulative).T
    return strength, shifted_logit, log_decay, cumulative, turned


def head_inputs(activated, h):
    qa = activated[:, 128 * h : 128 * h + 128]
    ka = activated[:, 256 + 128 * h : 384 + 128 * h]
    va = activated[:, 512 + 256 * h : 768 + 256 * h]
    q_norm = lax.rsqrt(jnp.sum(qa * qa, axis=-1, keepdims=True) + epsilon)
    k_norm = lax.rsqrt(jnp.sum(ka * ka, axis=-1, keepdims=True) + epsilon)
    q = (qa * q_norm * (1.0 / math.sqrt(DK))).astype(bf16)
    k = (ka * k_norm).astype(bf16)
    return qa, ka, q_norm, k_norm, q, k, va.astype(bf16)


def split(x):
    high = x.astype(bf16)
    return high, (x - high.astype(f32)).astype(bf16)


def mm2(exact, right, dims=NN):
    high, low = split(right)
    return mm(exact, high, dims) + mm(exact, low, dims)


def mm3(left, right, dims=NN):
    lh, ll = split(left)
    rh, rl = split(right)
    return mm(lh, rh, dims) + (mm(lh, rl, dims) + mm(ll, rh, dims))


def mb(left, right, dims=NN):
    return mm(left.astype(bf16), right.astype(bf16), dims)


def unit_inverse(system):
    size = system.shape[0]
    row = grid_of((size, size), 0)
    col = grid_of((size, size), 1)
    eye = jnp.where(row == col, 1.0, 0.0).astype(f32)
    powers = jnp.where((row >> 2) == (col >> 2), -system, 0.0)
    square = mb(powers, powers)
    total = eye + powers
    total = total + mb(total, square)
    for bits in (2, 3, 4, 5, 6):
        joint = ((row >> (bits + 1)) == (col >> (bits + 1))) & ((row >> bits) != (col >> bits))
        link = jnp.where(joint, system, 0.0)
        total = total - mb(total, mb(link, total))
    return total


def mixer_forward_kernel(
    layer, proj_hbm, small_ref, taps_ref, heads_ref, gain_ref, *refs
):
    if layer == 0:
        up_source, in_source, *refs = refs
        *outs, up_whole, near, far = refs[:8]
        refs = refs[8:]
    else:
        up_source, cotangent_hbm, *refs = refs
        *outs, up_whole, ddown_hbm = refs[:7]
        refs = refs[7:]
    proj_ref, gated_ref, start_ref, inv_ref, pseudo_ref, mixed_ref = refs[:6]
    load_sem, store_sem, halo, state, *sems = refs[6:]

    def chunk_rows(c):
        return pl.ds(pl.multiple_of(c * CHUNK, CHUNK), CHUNK)

    def load(c):
        rows = chunk_rows(c)
        return pltpu.make_async_copy(proj_hbm.at[rows], proj_ref.at[rows], load_sem.at[c])

    def stores(c):
        rows = chunk_rows(c)
        pairs = zip(refs[1:6], outs, (rows, c, c, c, rows))
        return [
            pltpu.make_async_copy(src.at[at], dst.at[at], store_sem.at[k, c])
            for k, (src, dst, at) in enumerate(pairs)
        ]

    chunks = proj_ref.shape[0] // CHUNK
    for c in range(chunks):
        load(c).start()
    ready = greet_wide(*place())
    shard = Reshard(up_source.at[layer], up_lanes, up_whole, *sems[:5])
    if layer == 0:
        quarter = Quarter(in_source.at[1], in_lanes, near, far, *sems[5:])
    ready()
    shard.start_far(0)
    shard.start_near()
    if layer == 1:
        ddown, ddown_sems, *gather_refs = sems[5:]
        gather = Gather(ddown, *gather_refs, cotangent_hbm.shape[0])
        count = gather.size // SUB
        own_rows = ddown.at[block_rows(gather.y, gather.c, gather.size)]
        pltpu.make_async_copy(cotangent_hbm, own_rows, ddown_sems.at[0]).start()
    halo[...] = jnp.zeros_like(halo)
    state[...] = jnp.zeros_like(state)
    row = grid_of((CHUNK, CHUNK), 0)
    col = grid_of((CHUNK, CHUNK), 1)
    zero = jnp.zeros((CHUNK, CHUNK), f32)

    def prepare(c):
        rows = pl.ds(pl.multiple_of(c * CHUNK, CHUNK), CHUNK)
        x = proj_ref[rows, 0:1024].astype(f32)
        x_ext = jnp.concatenate([halo[...], x], axis=0)
        halo[...] = x[CHUNK - 8 :]
        convolved = conv_chunk(x_ext, taps_ref[...])
        activated = convolved * jax.nn.sigmoid(convolved)
        strength, shifted_logit, log_decay, cumulative, turned = decay_chunk(
            small_ref[rows, :], heads_ref
        )
        parts = []
        systems = []
        for h in range(2):
            qa, ka, q_norm, k_norm, q, k, v = head_inputs(activated, h)
            c_col = cumulative[:, 2 + h : 3 + h]
            c_row = turned[2 + h : 3 + h, :]
            beta_row = turned[h : h + 1, :]
            ratio = jnp.exp(jnp.where(row >= col, c_col - c_row, -1e4)) * beta_row
            systems.append(jnp.where(row > col, ratio * mm(k, k, NT), 0.0))
            mixing = (ratio * mm(q, k, NT)).astype(bf16)
            parts.append((q, k, v, c_col, mixing, strength[:, h : h + 1]))
        joint = jnp.concatenate(
            [
                jnp.concatenate([systems[0], zero], axis=1),
                jnp.concatenate([zero, systems[1]], axis=1),
            ],
            axis=0,
        )
        return parts, unit_inverse(joint)

    def advance(c, parts, inverse):
        rows = pl.ds(pl.multiple_of(c * CHUNK, CHUNK), CHUNK)
        for h in range(2):
            q, k, v, c_col, mixing, beta_col = parts[h]
            inv = inverse[128 * h : 128 * h + 128, 128 * h : 128 * h + 128]
            growth = jnp.exp(c_col)
            last = c_col[CHUNK - 1 :, :]
            before = state[h]
            start_ref[c, h] = before
            inv = inv.astype(bf16)
            inv_ref[c, h] = inv
            read = mm2(jnp.concatenate([q, k], axis=0), before)
            pseudo = mm(inv, (v.astype(f32) - growth * read[CHUNK:]).astype(bf16))
            pseudo_ref[c, h] = pseudo
            tail = jnp.exp(last - c_col) * beta_col
            state[h] = jnp.exp(last) * before + mm2(k, tail * pseudo, TN)
            mixed = growth * read[:CHUNK] + mm(mixing, pseudo.astype(bf16))
            mixed_ref[rows, 256 * h : 256 * h + 256] = mixed
            gate = proj_ref[rows, 1024 + 256 * h : 1280 + 256 * h].astype(f32)
            scale = lax.rsqrt(jnp.mean(mixed * mixed, axis=-1, keepdims=True) + out_floor)
            gated = mixed * scale * gain_ref[0:1, :] * (gate * jax.nn.sigmoid(gate))
            gated_ref[rows, 256 * h : 256 * h + 256] = gated.astype(bf16)

    def body(step, carry):
        load(step).wait()
        advance(step, *prepare(step))
        for store in stores(step):
            store.start()
        @pl.when(step == 0)
        def _():
            shard.start_far(1)
            if layer == 0:
                quarter.start_near()

        @pl.when(step == 2)
        def _():
            shard.forward(0)
            if layer == 0:
                quarter.start_quarter()
            else:
                pltpu.make_async_copy(cotangent_hbm, own_rows, ddown_sems.at[0]).wait()
                for i in range(count):
                    gather.start(i)

        @pl.when(step == 4)
        def _():
            shard.forward(1)

        return carry

    lax.fori_loop(0, chunks, body, 0)
    shard.wait()
    shard.finish()
    if layer == 0:
        quarter.wait_quarter()
    else:
        for i in range(count):
            gather.across(i)
        for i in range(count):
            gather.sibling(i)
            gather.diagonal(i)
        whole_out = pltpu.make_async_copy(ddown, ddown_hbm, ddown_sems.at[1])
        whole_out.start()
        gather.finish()
        whole_out.wait()
    for c in range(chunks):
        for store in stores(c):
            store.wait()


def mixer_forward(layer, projected, small, taps, heads, gain, sources):
    tokens = projected.shape[0]
    chunks = tokens // CHUNK
    vmem = pl.BlockSpec(memory_space=pltpu.VMEM)
    spot = pl.BlockSpec(memory_space=pl.ANY)
    wholes = (jax.ShapeDtypeStruct((1024, 1536), bf16),)
    if layer == 0:
        wholes = wholes * 2 + (jax.ShapeDtypeStruct((2, PART, 1536), bf16),)
        carried = Reshard.scratch() * 2
    else:
        wholes = wholes + (jax.ShapeDtypeStruct((tokens, 1024), bf16),)
        carried = Reshard.scratch() + [
            pltpu.VMEM((tokens, 1024), bf16),
            pltpu.SemaphoreType.DMA((2,)),
        ]
        carried += gather_sems(tokens // 4)
    return pl.pallas_call(
        partial(mixer_forward_kernel, layer),
        out_shape=(
            jax.ShapeDtypeStruct((tokens, 512), bf16),
            jax.ShapeDtypeStruct((chunks, 2, DK, DV), f32),
            jax.ShapeDtypeStruct((chunks, 2, CHUNK, CHUNK), bf16),
            jax.ShapeDtypeStruct((chunks, 2, CHUNK, DV), f32),
            jax.ShapeDtypeStruct((tokens, 512), f32),
        )
        + wholes,
        in_specs=[spot] + [vmem] * 4 + [spot] * len(sources),
        out_specs=(spot,) * (5 + len(wholes)),
        scratch_shapes=[
            pltpu.VMEM((tokens, 1536), bf16),
            pltpu.VMEM((tokens, 512), bf16),
            pltpu.VMEM((chunks, 2, DK, DV), f32),
            pltpu.VMEM((chunks, 2, CHUNK, CHUNK), bf16),
            pltpu.VMEM((chunks, 2, CHUNK, DV), f32),
            pltpu.VMEM((tokens, 512), f32),
            pltpu.SemaphoreType.DMA((chunks,)),
            pltpu.SemaphoreType.DMA((5, chunks)),
        ]
        + [pltpu.VMEM((8, 1024), f32), pltpu.VMEM((2, DK, DV), f32)]
        + carried,
        compiler_params=pltpu.CompilerParams(
            collective_id=8 + layer, has_side_effects=True, vmem_limit_bytes=LIMIT
        ),
        name="mixer_forward",
    )(projected, small, taps, heads, gain, *sources)


def mixer_backward_kernel(
    small_ref, taps_ref, heads_ref, gain_ref, *refs
):
    sources, refs = refs[:6], refs[6:]
    dproj_hbm, dsmall_ref, gtaps_ref, gheads_ref, *refs = refs
    held, refs = refs[:6], refs[6:]
    proj_ref, start_ref, inv_ref, pseudo_ref, mixed_ref, dgated_ref = held
    dproj_ref, load_sem, store_sem, halo, dstate = refs

    def chunk_rows(c):
        return pl.ds(pl.multiple_of(c * CHUNK, CHUNK), CHUNK)

    def load(k, c):
        at = c if k in (1, 2, 3) else chunk_rows(c)
        return pltpu.make_async_copy(sources[k].at[at], held[k].at[at], load_sem.at[k, c])

    def store(c):
        rows = chunk_rows(c)
        return pltpu.make_async_copy(dproj_ref.at[rows], dproj_hbm.at[rows], store_sem.at[c])

    halo[...] = jnp.zeros_like(halo)
    dstate[...] = jnp.zeros_like(dstate)
    gtaps_ref[...] = jnp.zeros_like(gtaps_ref)
    gheads_ref[...] = jnp.zeros_like(gheads_ref)
    row = grid_of((CHUNK, CHUNK), 0)
    col = grid_of((CHUNK, CHUNK), 1)
    lane = col
    token = grid_of((CHUNK, 1), 0)
    chunks = proj_ref.shape[0] // CHUNK
    for c in reversed(range(chunks)):
        for k in range(6):
            load(k, c).start()
    load(0, chunks - 1).wait()

    def body(step, carry):
        c = chunks - 1 - step
        for k in range(1, 6):
            load(k, c).wait()

        @pl.when(c > 0)
        def _():
            load(0, c - 1).wait()

        rows = pl.ds(pl.multiple_of(c * CHUNK, CHUNK), CHUNK)
        x = proj_ref[rows, 0:1024].astype(f32)
        before_rows = pl.ds(pl.multiple_of(jnp.maximum(c * CHUNK - 16, 0), 16), 16)
        x_before = proj_ref[before_rows, 0:1024].astype(f32)[8:]
        x_before = jnp.where(c > 0, x_before, 0.0)
        x_ext = jnp.concatenate([x_before, x], axis=0)
        convolved = conv_chunk(x_ext, taps_ref[...])
        sig = jax.nn.sigmoid(convolved)
        activated = convolved * sig
        strength, shifted_logit, log_decay, cumulative, turned = decay_chunk(
            small_ref[rows, :], heads_ref
        )
        d_strength = jnp.zeros((CHUNK, CHUNK), f32)
        d_cumulative = jnp.zeros((CHUNK, CHUNK), f32)
        d_q_parts, d_k_parts, d_v_parts = [], [], []
        gain_sum = jnp.zeros((1, DV), f32)
        for h in range(2):
            qa, ka, q_norm, k_norm, q, k, v = head_inputs(activated, h)
            cols = slice(256 * h, 256 * h + 256)
            mixed = mixed_ref[rows, cols]
            gate = proj_ref[rows, 1024 + 256 * h : 1280 + 256 * h].astype(f32)
            d_gated = dgated_ref[rows, cols].astype(f32)
            gate_sig = jax.nn.sigmoid(gate)
            gate_silu = gate * gate_sig
            scale = lax.rsqrt(jnp.mean(mixed * mixed, axis=-1, keepdims=True) + out_floor)
            scaled = mixed * scale
            gain = gain_ref[0:1, :]
            gain_sum = gain_sum + jnp.sum(d_gated * scaled * gate_silu, axis=0, keepdims=True)
            d_gate = d_gated * scaled * gain * (gate_sig * (1.0 + gate * (1.0 - gate_sig)))
            dproj_ref[rows, 1024 + 256 * h : 1280 + 256 * h] = d_gate.astype(bf16)
            d_scaled = d_gated * gain * gate_silu
            d_mixed = scale * (
                d_scaled - scaled * jnp.mean(d_scaled * scaled, axis=-1, keepdims=True)
            )
            c_col = cumulative[:, 2 + h : 3 + h]
            c_row = turned[2 + h : 3 + h, :]
            beta_row = turned[h : h + 1, :]
            beta_col = strength[:, h : h + 1]
            growth = jnp.exp(c_col)
            last = c_col[CHUNK - 1 :, :]
            ratio = jnp.exp(jnp.where(row >= col, c_col - c_row, -1e4))
            key_gram = mm(k, k, NT)
            query_gram = mm(q, k, NT)
            mixing = ratio * beta_row * query_gram
            fade = jnp.exp(last - c_col)
            tail = fade * beta_col
            start = start_ref[c, h]
            inv = inv_ref[c, h]
            pseudo = pseudo_ref[c, h]
            d_end = dstate[h]
            kf = k.astype(f32)
            qf = q.astype(f32)
            d_pseudo = mb(mixing, d_mixed, TN) + tail * mm(k, d_end.astype(bf16))
            d_right = mm2(inv, d_pseudo, TN)
            pair = jnp.concatenate([d_mixed, d_right], axis=0)
            reads = mm3(pair, jnp.concatenate([start, pseudo], axis=0), NT)
            read_q = reads[:CHUNK, :DK]
            read_k = reads[CHUNK:, :DK]
            read_u = mm3(pseudo, d_end, NT)
            d_mixing = jnp.where(row >= col, reads[:CHUNK, DK:], 0.0) * ratio
            d_system = jnp.where(row > col, -reads[CHUNK:, DK:], 0.0) * ratio
            raw = d_mixing * query_gram + d_system * key_gram
            x_pair = jnp.concatenate([d_mixing * beta_row, d_system * beta_row], axis=0)
            by_row = mm(x_pair.astype(bf16), k)
            by_col = mm(x_pair.astype(bf16), jnp.concatenate([q, k], axis=0), TN)
            d_q = growth * read_q + by_row[:CHUNK]
            d_k = by_row[CHUNK:] + by_col - growth * read_k + tail * read_u
            dstate[h] = jnp.exp(last) * d_end + mb(
                jnp.concatenate([growth * qf, -growth * kf], axis=0), pair, TN
            )
            u_dot = jnp.sum(read_u * kf, axis=-1, keepdims=True)
            col_raw = jnp.sum(raw, axis=0, keepdims=True)
            col_raw = jnp.broadcast_to(col_raw, (CHUNK, CHUNK)).T[:, 0:1]
            d_beta = col_raw + fade * u_dot
            d_cum = (
                jnp.sum(raw * beta_row, axis=-1, keepdims=True)
                - beta_col * col_raw
                + growth
                * (
                    jnp.sum(read_q * qf, axis=-1, keepdims=True)
                    - jnp.sum(read_k * kf, axis=-1, keepdims=True)
                )
                - tail * u_dot
            )
            at_last = jnp.sum(tail * u_dot, axis=0, keepdims=True) + jnp.exp(last) * jnp.sum(
                jnp.sum(start * d_end, axis=-1, keepdims=True), axis=0, keepdims=True
            )
            d_cum = d_cum + jnp.where(token == CHUNK - 1, at_last, 0.0)
            d_strength = jnp.where(lane == h, d_beta, d_strength)
            d_cumulative = jnp.where(lane == 2 + h, d_cum, d_cumulative)
            d_qn = d_q * (1.0 / math.sqrt(DK))
            qn = qa * q_norm
            kn = ka * k_norm
            d_q_parts.append(
                q_norm * (d_qn - qn * jnp.sum(d_qn * qn, axis=-1, keepdims=True))
            )
            d_k_parts.append(k_norm * (d_k - kn * jnp.sum(d_k * kn, axis=-1, keepdims=True)))
            d_v_parts.append(d_right)
        upper_ones = jnp.where(row <= col, 1.0, 0.0).astype(f32)
        d_log = mm2(upper_ones.astype(bf16), d_cumulative)
        d_shifted = d_log * (-jnp.exp(heads_ref[0:1, :])) * jax.nn.sigmoid(shifted_logit)
        d_small = jnp.where(lane < 2, d_strength * strength * (1.0 - strength), d_shifted)
        dsmall_ref[rows, :] = jnp.where(lane < 4, d_small, 0.0).astype(bf16)
        gheads_ref[0:1, :] += gain_sum
        gheads_ref[1:2, 0:128] += jnp.sum(d_log * log_decay, axis=0, keepdims=True)
        gheads_ref[2:3, 0:128] += jnp.sum(d_shifted, axis=0, keepdims=True)
        d_activated = jnp.concatenate(d_q_parts + d_k_parts + d_v_parts, axis=1)
        d_conv = d_activated * (sig * (1.0 + convolved * (1.0 - sig)))
        for j in range(CONV):
            gtaps_ref[j : j + 1, :] += jnp.sum(
                d_conv * x_ext[5 + j : 5 + j + CHUNK], axis=0, keepdims=True
            )
        d_ext = jnp.concatenate([d_conv, halo[...]], axis=0)
        d_x = sum(
            d_ext[CONV - 1 - j : CONV - 1 - j + CHUNK] * taps_ref[j : j + 1] for j in range(CONV)
        )
        halo[...] = d_conv[:8]
        dproj_ref[rows, 0:1024] = d_x.astype(bf16)
        store(c).start()
        return carry

    lax.fori_loop(0, chunks, body, 0)
    for c in range(chunks):
        store(c).wait()


def mixer_backward(projected, small, taps, heads, gain, saved, d_gated):
    tokens = projected.shape[0]
    vmem = pl.BlockSpec(memory_space=pltpu.VMEM)
    spot = pl.BlockSpec(memory_space=pl.ANY)
    held = (projected, *saved, d_gated)
    chunks = tokens // CHUNK
    return pl.pallas_call(
        mixer_backward_kernel,
        out_shape=(
            jax.ShapeDtypeStruct((tokens, 1536), bf16),
            jax.ShapeDtypeStruct((tokens, 128), bf16),
            jax.ShapeDtypeStruct((8, 1024), f32),
            jax.ShapeDtypeStruct((8, DV), f32),
        ),
        in_specs=[vmem] * 4 + [spot] * 6,
        out_specs=(spot,) + (vmem,) * 3,
        scratch_shapes=[pltpu.VMEM(array.shape, array.dtype) for array in held]
        + [
            pltpu.VMEM((tokens, 1536), bf16),
            pltpu.SemaphoreType.DMA((6, chunks)),
            pltpu.SemaphoreType.DMA((chunks,)),
        ]
        + [pltpu.VMEM((8, 1024), f32), pltpu.VMEM((2, DK, DV), f32)],
        compiler_params=pltpu.CompilerParams(vmem_limit_bytes=LIMIT),
        name="mixer_backward",
    )(small, taps, heads, gain, *held)


SUB = 128
LIMIT = 56 << 20
MESH = pl.DeviceIdType.MESH


def place():
    me = lax.axis_index("grp")
    y, c = me // 2, me % 2
    return y, c


def shard_rows(y, c, i, size):
    return pl.ds(pl.multiple_of((2 * y + c) * size + i * SUB, SUB), SUB)


def block_rows(y, c, size):
    return pl.ds(pl.multiple_of((2 * y + c) * size, size), size)


def greet(y, c):
    barrier = pltpu.get_barrier_semaphore()
    for target in (2 * y + 1 - c, 2 * (1 - y) + c):
        pl.semaphore_signal(barrier, inc=1, device_id={"grp": target}, device_id_type=MESH)
    return lambda: pl.semaphore_wait(barrier, 2)


def remote(src, dst, send, recv, target):
    return pltpu.make_async_remote_copy(
        src_ref=src, dst_ref=dst, send_sem=send, recv_sem=recv,
        device_id={"grp": target}, device_id_type=MESH,
    )


class Gather:
    def __init__(self, full, send, recv, size):
        self.full, self.send, self.recv, self.size = full, send, recv, size
        self.y, self.c = place()

    def piece(self, kind, i):
        y, c = self.y, self.c
        rows = shard_rows(1 - y if kind == 2 else y, c, i, self.size)
        target = 2 * (1 - y) + c if kind == 1 else 2 * y + 1 - c
        view = self.full.at[rows]
        return remote(view, view, self.send.at[kind, i], self.recv.at[kind, i], target)

    def own(self, i):
        return shard_rows(self.y, self.c, i, self.size)

    def start(self, i):
        self.piece(0, i).start()
        self.piece(1, i).start()

    def sibling(self, i):
        self.piece(0, i).wait_recv()
        return shard_rows(self.y, 1 - self.c, i, self.size)

    def across(self, i):
        self.piece(1, i).wait_recv()
        self.piece(2, i).start()
        return shard_rows(1 - self.y, self.c, i, self.size)

    def diagonal(self, i):
        self.piece(2, i).wait_recv()
        return shard_rows(1 - self.y, 1 - self.c, i, self.size)

    def finish(self):
        for kind in range(3):
            for i in range(self.size // SUB):
                self.piece(kind, i).wait_send()


class Scatter:
    def __init__(self, out, core, keep, relay, far, send, recv, size):
        self.out, self.core, self.keep, self.relayed, self.far = out, core, keep, relay, far
        self.send, self.recv, self.size = send, recv, size
        self.y, self.c = place()

    def to_sibling(self, part, i):
        rows = pl.ds(i * SUB, SUB)
        return remote(
            self.out.at[part, rows], self.core.at[part, rows],
            self.send.at[part, i], self.recv.at[part, i], 2 * self.y + 1 - self.c,
        )

    def to_across(self, i):
        rows = pl.ds(i * SUB, SUB)
        return remote(
            self.relayed.at[rows], self.far.at[rows],
            self.send.at[2, i], self.recv.at[2, i], 2 * (1 - self.y) + self.c,
        )

    def give(self, part, i, value):
        self.out[part, i * SUB : (i + 1) * SUB, :] = value.astype(bf16)
        self.to_sibling(part, i).start()

    def hold(self, part, i, value):
        self.keep[part, i * SUB : (i + 1) * SUB, :] = value

    def relay(self, i):
        rows = slice(i * SUB, (i + 1) * SUB)
        self.to_sibling(0, i).wait_recv()
        self.relayed[rows, :] = (self.keep[0, rows, :] + self.core[0, rows, :].astype(f32)).astype(bf16)
        self.to_across(i).start()

    def total(self, i):
        rows = slice(i * SUB, (i + 1) * SUB)
        self.to_sibling(1, i).wait_recv()
        near = self.keep[1, rows, :] + self.core[1, rows, :].astype(f32)
        self.to_across(i).wait_recv()
        return near + self.far[rows, :].astype(f32)

    def finish(self):
        for i in range(self.size // SUB):
            self.to_sibling(0, i).wait_send()
            self.to_sibling(1, i).wait_send()
            self.to_across(i).wait_send()

    @staticmethod
    def scratch(size, width):
        return [
            pltpu.VMEM((2, size, width), bf16),
            pltpu.VMEM((2, size, width), bf16),
            pltpu.VMEM((2, size, width), f32),
            pltpu.VMEM((size, width), bf16),
            pltpu.VMEM((size, width), bf16),
            pltpu.SemaphoreType.DMA((3, size // SUB)),
            pltpu.SemaphoreType.DMA((3, size // SUB)),
        ]


def gather_sems(size):
    return [pltpu.SemaphoreType.DMA((3, size // SUB)), pltpu.SemaphoreType.DMA((3, size // SUB))]


def in_order(gather):
    count = gather.size // SUB
    for i in range(count):
        yield gather.own(i)
    for i in range(count):
        yield gather.sibling(i)
    for i in range(count):
        yield gather.across(i)
        yield gather.diagonal(i)


def call(kernel, out_shape, inputs, scratch, collective, name, spots=(), out_spots=()):
    vmem = pl.BlockSpec(memory_space=pltpu.VMEM)
    spot = pl.BlockSpec(memory_space=pl.ANY)
    return pl.pallas_call(
        kernel,
        out_shape=out_shape,
        in_specs=[vmem] * len(inputs) + [spot] * len(spots),
        out_specs=tuple(spot if k in out_spots else vmem for k in range(len(out_shape))),
        scratch_shapes=scratch,
        compiler_params=pltpu.CompilerParams(
            collective_id=collective, has_side_effects=True, vmem_limit_bytes=LIMIT
        ),
        cost_estimate=pl.CostEstimate(flops=1000, bytes_accessed=1000, transcendentals=0),
        name=name,
    )(*inputs, *spots)


def relative(y, c, d):
    dy, dc = d // 2, d % 2
    return 2 * (y + dy - 2 * y * dy) + c + dc - 2 * c * dc


def load_whole(src, whole, sem):
    copy = pltpu.make_async_copy(src, whole, sem)
    copy.start()
    return copy.wait


class Outgoing:
    def __init__(self, sems):
        self.sems, self.copies = sems, []

    def put(self, src, dst):
        copy = pltpu.make_async_copy(src, dst, self.sems.at[len(self.copies)])
        copy.start()
        self.copies.append(copy)

    def wait(self):
        for copy in self.copies:
            copy.wait()


def load_down(src, whole, sem):
    y, c = place()
    rows, extra = src.shape[0], whole.shape[0] - src.shape[0]
    whole[:extra, :] = jnp.zeros((extra, whole.shape[1]), bf16)
    whole[rows:, :] = jnp.zeros((extra, whole.shape[1]), bf16)
    spot = pl.ds(pl.multiple_of(extra * c, extra), rows)
    copy = pltpu.make_async_copy(src, whole.at[spot], sem)
    copy.start()
    return copy.wait


def flip(rank):
    return rank + 1 - 2 * (rank % 2)


def greet_wide(y, c):
    barrier = pltpu.get_barrier_semaphore()
    for d in range(1, 4):
        pl.semaphore_signal(
            barrier, inc=1, device_id={"grp": relative(y, c, d)}, device_id_type=MESH
        )
    pl.semaphore_signal(
        barrier, inc=1, device_id={"rep": flip(lax.axis_index("rep"))}, device_id_type=MESH
    )
    return lambda: pl.semaphore_wait(barrier, 4)


PART = 64


def in_lanes(t):
    return (
        (256 * t, 256, 0),
        (HK + 256 * t, 256, 256),
        (2 * HK + 512 * t, 512, 512),
        (CH + 512 * t, 512, 1024),
    )


def up_lanes(t):
    first = 1408 * (t // 2) + 640 * (t % 2)
    return ((first, 768, 0), (FF + first, 768, 768))


class Reshard:
    def __init__(self, source, lanes, whole, send, recv, passed, arrived, local):
        self.source, self.lanes, self.whole = source, lanes, whole
        self.send, self.recv, self.passed, self.arrived = send, recv, passed, arrived
        self.local = local
        self.y, self.c = place()
        rank = lax.axis_index("rep")
        self.x, self.other = rank % 2, flip(rank)
        self.size = source.shape[0]

    def at(self, index, offset, count):
        return pl.ds(pl.multiple_of(index * self.size + offset, PART), count)

    def pieces(self, d, q):
        y, c = self.y, self.c
        target = relative(y, c, d)
        start = 0 if d < 2 else self.size // 2 * self.x + PART * q
        count = self.size if d < 2 else PART
        copies = []
        for k, (lane, wide, to) in enumerate(self.lanes(target)):
            src = self.source.at[
                pl.ds(pl.multiple_of(start, PART), count) if d >= 2 else pl.ds(0, count),
                pl.ds(pl.multiple_of(lane, 128), wide),
            ]
            dst = self.whole.at[self.at(2 * y + c, start, count), pl.ds(to, wide)]
            if d == 0:
                copies.append(pltpu.make_async_copy(src, dst, self.local.at[k]))
            else:
                copies.append(
                    pltpu.make_async_remote_copy(
                        src_ref=src, dst_ref=dst,
                        send_sem=self.send.at[d, q, k], recv_sem=self.recv.at[d, q, k],
                        device_id={"grp": target}, device_id_type=MESH,
                    )
                )
        return copies

    def onward(self, d, q):
        source = relative(self.y, self.c, d)
        rows = self.at(source, self.size // 2 * self.x + PART * q, PART)
        return pltpu.make_async_remote_copy(
            src_ref=self.whole.at[rows], dst_ref=self.whole.at[rows],
            send_sem=self.passed.at[d - 2, q], recv_sem=self.arrived.at[d - 2, q],
            device_id={"rep": self.other}, device_id_type=MESH,
        )

    def parts(self):
        return range(self.size // 2 // PART)

    def start_far(self, q):
        for d in (2, 3):
            for copy in self.pieces(d, q):
                copy.start()

    def start_near(self):
        for copy in self.pieces(1, 0):
            copy.start()

    def start_own(self):
        for copy in self.pieces(0, 0):
            copy.start()

    def forward(self, q):
        for d in (2, 3):
            for copy in self.pieces(d, q):
                copy.wait_recv()
            self.onward(d, q).start()

    def wait_own(self):
        for copy in self.pieces(0, 0):
            copy.wait()

    def wait(self):
        for copy in self.pieces(1, 0):
            copy.wait_recv()
        for q in self.parts():
            for d in (2, 3):
                self.onward(d, q).wait_recv()

    def finish(self):
        for copy in self.pieces(1, 0):
            copy.wait_send()
        for q in self.parts():
            for d in (2, 3):
                for copy in self.pieces(d, q):
                    copy.wait_send()
                self.onward(d, q).wait_send()

    @staticmethod
    def scratch():
        dma = pltpu.SemaphoreType.DMA
        return [dma((4, 2, 4)), dma((4, 2, 4)), dma((2, 2)), dma((2, 2)), dma((4,))]


def like(*shape, dtype=f32):
    return jax.ShapeDtypeStruct(shape, dtype)


def normalise(x, gain):
    return x * lax.rsqrt(jnp.mean(x * x, axis=-1, keepdims=True) + epsilon) * gain


def normalise_back(x, gain, d_out):
    scale = lax.rsqrt(jnp.mean(x * x, axis=-1, keepdims=True) + epsilon)
    unit = x * scale
    d_unit = d_out * gain
    d_x = scale * (d_unit - unit * jnp.mean(d_unit * unit, axis=-1, keepdims=True))
    return d_x, jnp.sum(d_out * unit, axis=0, keepdims=True)


class Quarter(Reshard):
    def __init__(self, source, lanes, whole, far, *sems):
        super().__init__(source, lanes, whole, *sems)
        self.far = far
        self.z = (lax.axis_index("rep") % 8) // 2

    def quarters(self, d):
        target = relative(self.y, self.c, d)
        copies = []
        for k, (lane, wide, to) in enumerate(self.lanes(target)):
            copies.append(
                pltpu.make_async_remote_copy(
                    src_ref=self.source.at[
                        pl.ds(pl.multiple_of(PART * self.z, PART), PART),
                        pl.ds(pl.multiple_of(lane, 128), wide),
                    ],
                    dst_ref=self.far.at[d - 2, :, pl.ds(to, wide)],
                    send_sem=self.send.at[d, 0, k], recv_sem=self.recv.at[d, 0, k],
                    device_id={"grp": target}, device_id_type=MESH,
                )
            )
        return copies

    def start_quarter(self):
        for d in (2, 3):
            for copy in self.quarters(d):
                copy.start()

    def wait_quarter(self):
        for copy in self.pieces(1, 0):
            copy.wait_recv()
            copy.wait_send()
        for d in (2, 3):
            for copy in self.quarters(d):
                copy.wait_recv()
                copy.wait_send()


def load_shard(parts, whole, sems):
    y, c = place()
    copies = []

    def add(src, dst):
        copies.append(pltpu.make_async_copy(src, dst, sems.at[len(copies)]))

    if len(parts) == 1:
        add(parts[0], whole)
    else:
        raw, lanes, near, *far = parts
        size = whole.shape[0] // 4

        def block(index, count):
            return pl.ds(pl.multiple_of(index * size, size), count * size)

        own, sibling, across = block(2 * y + c, 1), block(2 * y + 1 - c, 1), block(2 - 2 * y, 2)
        for lane, wide, to in lanes(2 * y + c):
            src = raw.at[pl.ds(0, size), pl.ds(pl.multiple_of(lane, 128), wide)]
            add(src, whole.at[own, pl.ds(to, wide)])
        add(near.at[sibling], whole.at[sibling])
        if not far:
            add(near.at[across], whole.at[across])
        else:
            for z in range(4):
                for d in (2, 3):
                    at = relative(y, c, d) * size + PART * z
                    spot = pl.ds(pl.multiple_of(at, PART), PART)
                    add(far[0].at[z, d - 2], whole.at[spot])
    for copy in copies:
        copy.start()

    def wait():
        for copy in copies:
            copy.wait()

    return wait


def in_parts(parts):
    return parts if len(parts) == 1 else (parts[0].at[1], in_lanes) + tuple(parts[1:])


GAIN_AT, TAPS_AT, AB_AT, OUT_GAIN_AT, PACK_ROWS = 0, 8, 72, 136, 144


def start_kernel(
    x_ref, pack_ref, win_ref,
    normed_hbm, proj_hbm, small_ref, whole_hbm,
    gain0, gain1, gain2, gain3, taps0, taps1, ab0, ab1, out0, out1,
    everyone, ab_rows, normed_ref, proj_ref, whole_ref, out_sems, *scratch,
):
    outgoing = Outgoing(out_sems)
    size = x_ref.shape[0]
    y, c = place()
    me = 2 * y + c
    ready = greet_wide(y, c)
    shard = Reshard(win_ref.at[0], in_lanes, whole_ref, *scratch[:5])
    psend, precv = scratch[5:7]
    gather = Gather(normed_ref, *scratch[7:], size)
    everyone[me] = pack_ref[...]
    ready()

    def share(d):
        return pltpu.make_async_remote_copy(
            src_ref=pack_ref, dst_ref=everyone.at[me],
            send_sem=psend.at[d], recv_sem=precv.at[d],
            device_id={"grp": relative(y, c, d)}, device_id_type=MESH,
        )

    for d in (2, 3, 1):
        share(d).start()
    for q in shard.parts():
        shard.start_far(q)
    shard.start_near()
    shard.start_own()
    for d in (1, 2, 3):
        share(d).wait_recv()
    for k, ref in enumerate((gain0, gain1, gain2, gain3)):
        for s in range(4):
            for b in range(2):
                row = GAIN_AT + 2 * k + b
                ref[0:1, 256 * s + 128 * b : 256 * s + 128 * b + 128] = everyone[s, row : row + 1, :]
    for i in range(size // SUB):
        rows = slice(i * SUB, (i + 1) * SUB)
        normed = normalise(x_ref[rows, :].astype(f32), gain0[...])
        normed_ref[gather.own(i), :] = normed.astype(bf16)
        gather.start(i)
    for l, (taps, ab, out) in enumerate(((taps0, ab0, out0), (taps1, ab1, out1))):
        taps[...] = jnp.zeros_like(taps)
        out[...] = jnp.zeros_like(out)
        ab_rows[...] = jnp.zeros_like(ab_rows)
        for j in range(4):
            base = TAPS_AT + (4 * l + j) * 8
            for b in range(8):
                if b < 2:
                    s, row = 0, base + 2 * me + b
                elif b < 4:
                    s, row = 1, base + 2 * me + b - 2
                else:
                    s, row = 2 + y, base + 4 * c + b - 4
                taps[j : j + 1, 128 * b : 128 * b + 128] = everyone[s, pl.ds(row, 1), :]
            column = 2 * me + j if j < 2 else H + 2 * me + j - 2
            for s in range(4):
                for b in range(2):
                    row = AB_AT + (16 * l + column) * 2 + b
                    ab_rows[j : j + 1, 256 * s + 128 * b : 256 * s + 128 * b + 128] = everyone[
                        s, pl.ds(row, 1), :
                    ]
        ab[...] = ab_rows[...].T.astype(bf16)
        for s in range(4):
            out[0:1, 64 * s : 64 * s + 64] = everyone[
                s, OUT_GAIN_AT : OUT_GAIN_AT + 1, 64 * l : 64 * l + 64
            ]
    for q in shard.parts():
        shard.forward(q)
    shard.wait()
    shard.wait_own()
    outgoing.put(whole_ref, whole_hbm)
    for rows in in_order(gather):
        normed = normed_ref[rows, :]
        proj_ref[rows, :] = mm(normed, whole_ref[...]).astype(bf16)
        small_ref[rows, :] = mm(normed, ab0[...])
        outgoing.put(proj_ref.at[rows], proj_hbm.at[rows])
        outgoing.put(normed_ref.at[rows], normed_hbm.at[rows])
    gather.finish()
    outgoing.wait()
    shard.finish()
    for d in (1, 2, 3):
        share(d).wait_send()


def start(x, pack, w_in):
    size, width = x.shape
    tokens = 4 * size
    row = like(1, width)
    dma = pltpu.SemaphoreType.DMA
    return call(
        start_kernel,
        (
            like(tokens, width, dtype=bf16),
            like(tokens, 1536, dtype=bf16),
            like(tokens, 128),
            like(width, 1536, dtype=bf16),
            row, row, row, row,
            like(8, width), like(8, width),
            like(width, 128, dtype=bf16), like(width, 128, dtype=bf16),
            like(8, DV), like(8, DV),
        ),
        (x, pack),
        [
            pltpu.VMEM((4, PACK_ROWS, 128), f32),
            pltpu.VMEM((128, width), f32),
            pltpu.VMEM((tokens, width), bf16),
            pltpu.VMEM((tokens, 1536), bf16),
            pltpu.VMEM((width, 1536), bf16),
            dma((17,)),
        ]
        + Reshard.scratch()
        + [dma((4,)), dma((4,))]
        + gather_sems(size),
        1,
        "start",
        (w_in,),
        (0, 1, 3),
    )


def project_kernel(count, res_ref, gain_ref, ab_ref, *refs):
    parts, refs = refs[:count], refs[count:]
    normed_hbm, proj_hbm, small_ref, w_ref, loads, normed_ref, proj_ref, out_sems, send, recv = refs
    outgoing = Outgoing(out_sems)
    loaded = load_shard(in_parts(parts), w_ref, loads)
    size = res_ref.shape[0]
    y, c = place()
    ready = greet(y, c)
    gather = Gather(normed_ref, send, recv, size)
    for i in range(size // SUB):
        rows = slice(i * SUB, (i + 1) * SUB)
        normed_ref[gather.own(i), :] = normalise(res_ref[rows, :], gain_ref[...]).astype(bf16)
        if i == 0:
            ready()
        gather.start(i)
    loaded()
    for rows in in_order(gather):
        normed = normed_ref[rows, :]
        proj_ref[rows, :] = mm(normed, w_ref[...]).astype(bf16)
        small_ref[rows, :] = mm(normed, ab_ref[...])
        outgoing.put(proj_ref.at[rows], proj_hbm.at[rows])
        outgoing.put(normed_ref.at[rows], normed_hbm.at[rows])
    gather.finish()
    outgoing.wait()


def project(residual, gain, ab, weight):
    size, width = residual.shape
    tokens = 4 * size
    return call(
        partial(project_kernel, len(weight)),
        (like(tokens, width, dtype=bf16), like(tokens, 1536, dtype=bf16), like(tokens, 128)),
        (residual, gain, ab),
        [
            pltpu.VMEM((width, 1536), bf16),
            pltpu.SemaphoreType.DMA((13,)),
            pltpu.VMEM((tokens, width), bf16),
            pltpu.VMEM((tokens, 1536), bf16),
            pltpu.SemaphoreType.DMA((16,)),
        ]
        + gather_sems(size),
        6,
        "project",
        weight,
        (0, 1),
    )


def swiglu(up):
    gate, value = up[:, :768], up[:, 768:]
    return gate * jax.nn.sigmoid(gate) * value


def swiglu_back(up, d_hidden):
    gate, value = up[:, :768], up[:, 768:]
    sig = jax.nn.sigmoid(gate)
    d_gate = d_hidden * value * (sig * (1.0 + gate * (1.0 - sig)))
    return jnp.concatenate([d_gate, d_hidden * gate * sig], axis=1)


def ffn_forward_kernel(
    layer, gated_ref, res_ref, gain_ref, raw_ref, down_ref, ffn_ref, whole_ref,
    mid_hbm, normed_hbm, up_hbm, hidden_hbm, *refs
):
    last = layer == LAYERS - 1
    if not last:
        out_ref, *refs = refs
    wup_ref, wdown_ref, wout_ref, loads, shard_loads, *refs = refs
    mid_ref, normed_ref, up_ref, hidden_ref, out_sems, *scratch = refs
    outgoing = Outgoing(out_sems)
    loaded_out = load_whole(raw_ref.at[layer], wout_ref, loads.at[2])
    loaded = load_shard((ffn_ref.at[layer], up_lanes, whole_ref), wup_ref, shard_loads)
    if not last:
        loaded_down = load_down(down_ref.at[layer], wdown_ref, loads.at[1])
    size = res_ref.shape[0]
    count = size // SUB
    y, c = place()
    ready = greet(y, c)
    first = Scatter(*scratch[:7], size)
    second = Scatter(*scratch[7:14], size)
    gather = Gather(normed_ref, *scratch[14:], size)

    loaded_out()

    def branch(rows):
        return mm(gated_ref[rows, :], wout_ref[...])

    for part in range(2):
        yy = 1 - y if part == 0 else y
        for i in range(count):
            value = branch(shard_rows(yy, 1 - c, i, size))
            if part == 0 and i == 0:
                ready()
            first.give(part, i, value)
            first.hold(part, i, branch(shard_rows(yy, c, i, size)))
            if part == 0:
                first.relay(i)
    for i in range(count):
        rows = slice(i * SUB, (i + 1) * SUB)
        mid = res_ref[rows, :].astype(f32) + first.total(i)
        mid_ref[rows, :] = mid
        normed_ref[gather.own(i), :] = normalise(mid, gain_ref[...]).astype(bf16)
        gather.start(i)

    def feed(rows):
        up = mm(normed_ref[rows, :], wup_ref[...])
        up_ref[rows, :] = up.astype(bf16)
        hidden = swiglu(up).astype(bf16)
        hidden_ref[rows, :] = hidden
        outgoing.put(normed_ref.at[rows], normed_hbm.at[rows])
        outgoing.put(up_ref.at[rows], up_hbm.at[rows])
        outgoing.put(hidden_ref.at[rows], hidden_hbm.at[rows])
        return None if last else mm(hidden, wdown_ref[...])

    outgoing.put(mid_ref, mid_hbm)
    loaded()
    if last:
        for rows in in_order(gather):
            feed(rows)
    else:
        loaded_down()
        for i in range(count):
            second.hold(1, i, feed(gather.own(i)))
        for i in range(count):
            second.give(1, i, feed(gather.sibling(i)))
        for i in range(count):
            near = gather.across(i)
            second.hold(0, i, feed(near))
            second.give(0, i, feed(gather.diagonal(i)))
            second.relay(i)
        for i in range(count):
            rows = slice(i * SUB, (i + 1) * SUB)
            out_ref[rows, :] = mid_ref[rows, :] + second.total(i)
    first.finish()
    if not last:
        second.finish()
    gather.finish()
    outgoing.wait()


def ffn_forward(layer, gated, residual, gain, w_out, w_down, w_up):
    size, width = residual.shape
    tokens = 4 * size
    return call(
        partial(ffn_forward_kernel, layer),
        (
            like(size, width),
            like(tokens, width, dtype=bf16),
            like(tokens, 1536, dtype=bf16),
            like(tokens, 768, dtype=bf16),
        )
        + (like(size, width),) * (layer < LAYERS - 1),
        (gated, residual, gain),
        [
            pltpu.VMEM((width, 1536), bf16),
            pltpu.VMEM((768, width), bf16),
            pltpu.VMEM((512, width), bf16),
            pltpu.SemaphoreType.DMA((3,)),
            pltpu.SemaphoreType.DMA((13,)),
            pltpu.VMEM((size, width), f32),
            pltpu.VMEM((tokens, width), bf16),
            pltpu.VMEM((tokens, 1536), bf16),
            pltpu.VMEM((tokens, 768), bf16),
            pltpu.SemaphoreType.DMA((25,)),
        ]
        + Scatter.scratch(size, width)
        + Scatter.scratch(size, width)
        + gather_sems(size),
        (2, 12)[layer],
        "ffn_forward",
        (w_out, w_down) + w_up,
        (0, 1, 2, 3),
    )


class Owners:
    def __init__(self, keep, send):
        self.keep, self.send = keep, send
        self.x = lax.axis_index("rep") % 2

    def put(self, r, store):
        @pl.when(self.x == r % 2)
        def _():
            store(self.keep.at[r // 2])

        @pl.when(self.x != r % 2)
        def _():
            store(self.send.at[r // 2])


def store_columns(buf, value, at):
    rows = pl.ds(at, value.shape[0])
    for r in range(8):

        def store(ref):
            ref[rows, :] = value[:, 128 * r : 128 * r + 128].astype(bf16)

        buf.put(r, store)


def store_up(buf, staged, d, c):
    own_half = (grid_of((32, 128), 1) >> 6) == c
    for r in range(8):
        rows = slice(32 * r, 32 * r + 32)

        def tile(side, j):
            lane = pl.multiple_of(768 * side + 128 * j, 128)
            return staged[rows, pl.ds(lane, 128)]

        tiles = [tile(j // 5, j % 5 + c) for j in range(10)]
        turned = pltpu.roll(tile(1, 5 - 5 * c), 64, 1)
        tiles.append(jnp.where(own_half, tile(0, 5 - 5 * c), turned))

        def store(ref):
            for j, value in enumerate(tiles):
                at = UP_AT + (d * 11 + j) * 32
                ref[at : at + 32, :] = value.astype(bf16)

        buf.put(r, store)


def store_rows(buf, value, d, base):
    blocks = value.shape[1] // 128
    for r in range(8):

        def store(ref):
            for j in range(blocks):
                at = base + (d * blocks + j) * 32
                ref[at : at + 32, :] = value[
                    32 * r : 32 * r + 32, 128 * j : 128 * j + 128
                ].astype(bf16)

        buf.put(r, store)


UP_AT, DOWN_AT, OUT_AT, FFN_ROWS = 0, 1408, 2112, 2624
SMALL_AT, IN_ROWS = 1536, 1552


def ffn_backward_kernel(
    layer, dres_ref, gain_ref, ddown_hbm, up_hbm, hidden_hbm, normed_hbm, mid_hbm, gated_hbm,
    raw_ref, down_ref, ffn_ref, whole_ref,
    dmid_ref, dgated_hbm, ggain_ref, keep_hbm, send_hbm,
    wup_ref, wdown_ref, wout_ref, loads, shard_loads, ddown_ref, dup_ref, dbranch_ref, staged,
    up_ref, hidden_ref, normed_ref, mid_ref, gated_ref, dgated_ref, keep_ref, send_ref,
    late_sems, out_sems, *scratch,
):
    buf_ref = Owners(keep_ref, send_ref)
    outgoing = Outgoing(out_sems)
    loaded_out = load_whole(raw_ref.at[layer], wout_ref, loads.at[2])
    loaded = load_shard((ffn_ref.at[layer], up_lanes, whole_ref), wup_ref, shard_loads)
    loaded_down = load_down(down_ref.at[layer], wdown_ref, loads.at[1])
    size = dres_ref.shape[0]
    count = size // SUB
    y, c = place()
    ready = greet(y, c)
    gathered = layer == LAYERS - 1
    if gathered:
        loaded_rows = load_whole(ddown_hbm, ddown_ref, late_sems.at[5])
    else:
        first = Gather(ddown_ref, *scratch[:2], size)
    second = Gather(dbranch_ref, *scratch[2:4], size)
    scatter = Scatter(*scratch[4:], size)
    late = [
        load_whole(src, dst, late_sems.at[k])
        for k, (src, dst) in enumerate(
            (
                (up_hbm, up_ref),
                (hidden_hbm, hidden_ref),
                (mid_hbm, mid_ref),
                (normed_hbm, normed_ref),
                (gated_hbm, gated_ref),
            )
        )
    ]
    if not gathered:
        for i in range(count):
            ddown_ref[first.own(i), :] = dres_ref[i * SUB : (i + 1) * SUB, :].astype(bf16)
            if i == 0:
                ready()
            first.start(i)

    def feed(rows):
        d_hidden = mm(ddown_ref[rows, :], wdown_ref[...], NT)
        d_up = swiglu_back(up_ref[rows, :].astype(f32), d_hidden).astype(bf16)
        dup_ref[rows, :] = d_up
        return mm(d_up, wup_ref[...], NT)

    loaded()
    loaded_down()
    late[0]()
    if gathered:
        loaded_rows()
        for part in range(2):
            yy = 1 - y if part == 0 else y
            for i in range(count):
                value = feed(shard_rows(yy, 1 - c, i, size))
                if part == 0 and i == 0:
                    ready()
                scatter.give(part, i, value)
                scatter.hold(part, i, feed(shard_rows(yy, c, i, size)))
                if part == 0:
                    scatter.relay(i)
    else:
        for i in range(count):
            scatter.hold(1, i, feed(first.own(i)))
        for i in range(count):
            scatter.give(1, i, feed(first.sibling(i)))
        for i in range(count):
            near = first.across(i)
            scatter.hold(0, i, feed(near))
            scatter.give(0, i, feed(first.diagonal(i)))
            scatter.relay(i)
    late[1]()
    for m in range(6):
        value = mm(hidden_ref[:, 128 * m : 128 * m + 128], ddown_ref[...], TN)
        store_columns(buf_ref, value, pl.multiple_of(DOWN_AT + 128 * m - 64 * c, 64))
    ggain_ref[...] = jnp.zeros_like(ggain_ref)
    late[2]()
    for i in range(count):
        rows = slice(i * SUB, (i + 1) * SUB)
        d_norm, g_gain = normalise_back(mid_ref[rows, :], gain_ref[...], scatter.total(i))
        d_mid = dres_ref[rows, :].astype(f32) + d_norm
        dmid_ref[rows, :] = d_mid
        ggain_ref[0:1, :] += g_gain
        dbranch_ref[second.own(i), :] = d_mid.astype(bf16)
        second.start(i)
    late[3]()
    for d in range(4):
        lanes = pl.ds(pl.multiple_of(relative(y, c, d) * 256, 256), 256)
        staged[...] = mm(normed_ref[:, lanes], dup_ref[...], TN)
        store_up(buf_ref, staged, d, c)
    for keep, hbm in ((keep_ref, keep_hbm), (send_ref, send_hbm)):
        rows = pl.ds(0, OUT_AT)
        outgoing.put(keep.at[:, rows], hbm.at[:, rows])
    loaded_out()
    for rows in in_order(second):
        dgated_ref[rows, :] = mm(dbranch_ref[rows, :], wout_ref[...], NT).astype(bf16)
    outgoing.put(dgated_ref, dgated_hbm)
    late[4]()
    for m in range(4):
        value = mm(gated_ref[:, 128 * m : 128 * m + 128], dbranch_ref[...], TN)
        store_columns(buf_ref, value, OUT_AT + 128 * m)
    for keep, hbm in ((keep_ref, keep_hbm), (send_ref, send_hbm)):
        rows = pl.ds(OUT_AT, FFN_ROWS - OUT_AT)
        outgoing.put(keep.at[:, rows], hbm.at[:, rows])
    if not gathered:
        first.finish()
    second.finish()
    scatter.finish()
    outgoing.wait()


def ffn_backward(layer, d_res, d_down, up, hidden, normed, mid, gain, gated, w_out, w_down, w_up):
    size, width = d_res.shape
    tokens = 4 * size
    return call(
        partial(ffn_backward_kernel, layer),
        (
            like(size, width),
            like(tokens, 512, dtype=bf16),
            like(8, width),
            like(4, FFN_ROWS, 128, dtype=bf16),
            like(4, FFN_ROWS, 128, dtype=bf16),
        ),
        (d_res, gain),
        [
            pltpu.VMEM((width, 1536), bf16),
            pltpu.VMEM((768, width), bf16),
            pltpu.VMEM((512, width), bf16),
            pltpu.SemaphoreType.DMA((3,)),
            pltpu.SemaphoreType.DMA((13,)),
            pltpu.VMEM((tokens, width), bf16),
            pltpu.VMEM((tokens, 1536), bf16),
            pltpu.VMEM((tokens, width), bf16),
            pltpu.VMEM((256, 1536), f32),
        ]
        + [pltpu.VMEM(array.shape, array.dtype) for array in (up, hidden, normed, mid, gated, gated)]
        + [pltpu.VMEM((4, FFN_ROWS, 128), bf16)] * 2
        + [pltpu.SemaphoreType.DMA((6,)), pltpu.SemaphoreType.DMA((5,))]
        + gather_sems(size)
        + gather_sems(size)
        + Scatter.scratch(size, width),
        (3, 13)[layer],
        "ffn_backward",
        (d_down, up, hidden, normed, mid, gated, w_out, w_down) + w_up,
        (1, 3, 4),
    )


def project_backward_kernel(
    parts, dproj_ref, dsmall_ref, ab_ref, gain_ref, gtwo_ref, gtaps_ref, gheads_ref, *refs
):
    normed_hbm, res_hbm, dmid_hbm, *refs = refs
    parts, refs = refs[:parts], refs[parts:]
    dres_ref, keep_hbm, send_hbm, w_ref, loads, table, *refs = refs
    normed_ref, res_ref, dmid_ref, keep_ref, send_ref, late_sems, out_sems, *scratch = refs
    buf_ref = Owners(keep_ref, send_ref)
    outgoing = Outgoing(out_sems)
    loaded = load_shard(in_parts(parts), w_ref, loads)
    late = [
        load_whole(src, dst, late_sems.at[k])
        for k, (src, dst) in enumerate(
            ((normed_hbm, normed_ref), (res_hbm, res_ref), (dmid_hbm, dmid_ref))
        )
    ]
    size = res_ref.shape[0]
    count = size // SUB
    y, c = place()
    ready = greet(y, c)
    scatter = Scatter(*scratch, size)

    def back(rows):
        return mm(dproj_ref[rows, :], w_ref[...], NT) + mm(dsmall_ref[rows, :], ab_ref[...], NT)

    def weight_grad(d):
        lanes = pl.ds(pl.multiple_of(relative(y, c, d) * 256, 256), 256)
        value = mm(normed_ref[:, lanes], dproj_ref[...], TN)
        store_rows(buf_ref, value, d, 0)

    loaded()
    for part in range(2):
        yy = 1 - y if part == 0 else y
        for i in range(count):
            value = back(shard_rows(yy, 1 - c, i, size))
            if part == 0 and i == 0:
                ready()
            scatter.give(part, i, value)
            scatter.hold(part, i, back(shard_rows(yy, c, i, size)))
            if part == 0:
                scatter.relay(i)
    late[0]()
    for d in range(4):
        weight_grad(d)
    for keep, hbm in ((keep_ref, keep_hbm), (send_ref, send_hbm)):
        rows = pl.ds(0, SMALL_AT)
        outgoing.put(keep.at[:, rows], hbm.at[:, rows])
    ab_grad = mm(dsmall_ref[...], normed_ref[...], TN)
    table[...] = jnp.zeros_like(table)
    for k in range(8):
        lanes = slice(128 * k, 128 * k + 128)
        for j in range(4):
            table[8 * j + k : 8 * j + k + 1, :] = gtaps_ref[j : j + 1, lanes]
            table[32 + 8 * j + k : 33 + 8 * j + k, :] = ab_grad[j : j + 1, lanes]
        table[72 + k : 73 + k, :] = gtwo_ref[0:1, lanes]
    table[80:81, :] = gheads_ref[0:1, 0:128]
    table[81:82, :] = gheads_ref[0:1, 128:256]
    table[82:83, :] = gheads_ref[1:2, 0:128]
    table[83:84, :] = gheads_ref[2:3, 0:128]
    gain_sum = jnp.zeros((1, res_ref.shape[1]), f32)
    late[1]()
    late[2]()
    for i in range(count):
        rows = slice(i * SUB, (i + 1) * SUB)
        d_norm, g_gain = normalise_back(
            res_ref[rows, :].astype(f32), gain_ref[...], scatter.total(i)
        )
        dres_ref[rows, :] = dmid_ref[rows, :] + d_norm
        gain_sum = gain_sum + g_gain
    for k in range(8):
        table[64 + k : 65 + k, :] = gain_sum[:, 128 * k : 128 * k + 128]
    for r in range(8):

        def store(ref):
            ref[SMALL_AT:IN_ROWS, :] = table[16 * r : 16 * r + 16, :].astype(bf16)

        buf_ref.put(r, store)
    for keep, hbm in ((keep_ref, keep_hbm), (send_ref, send_hbm)):
        rows = pl.ds(SMALL_AT, IN_ROWS - SMALL_AT)
        outgoing.put(keep.at[:, rows], hbm.at[:, rows])
    scatter.finish()
    outgoing.wait()


def project_backward(d_proj, d_small, weight, ab, normed, residual, gain, d_mid, g_two, g_taps, g_heads):
    size, width = residual.shape
    return call(
        partial(project_backward_kernel, len(weight)),
        (like(size, width),) + (like(4, IN_ROWS, 128, dtype=bf16),) * 2,
        (d_proj, d_small, ab, gain, g_two, g_taps, g_heads),
        [
            pltpu.VMEM((width, 1536), bf16),
            pltpu.SemaphoreType.DMA((13,)),
            pltpu.VMEM((128, 128), f32),
        ]
        + [pltpu.VMEM(array.shape, array.dtype) for array in (normed, residual, d_mid)]
        + [pltpu.VMEM((4, IN_ROWS, 128), bf16)] * 2
        + [pltpu.SemaphoreType.DMA((3,)), pltpu.SemaphoreType.DMA((4,))]
        + Scatter.scratch(size, width),
        4 if len(weight) == 1 else 7,
        "project_backward",
        (normed, residual, d_mid) + tuple(weight),
        (1, 2),
    )


def assemble_kernel(
    f1, f2, f3, f4, last_ref, grad_ref,
    down_ref, out_ref, up_ref, in_ref, table_ref, block_ref, input_ref,
    p1, p2, p3, p4, down, out, up, whole, loads, stores,
):
    y, c = place()
    copies = [
        pltpu.make_async_copy(src, dst, loads.at[k])
        for k, (src, dst) in enumerate(((f1, p1), (f2, p2), (f3, p3), (f4, p4)))
    ]
    copies[0].start()
    copies[1].start()
    block_ref[...] = last_ref[...].astype(bf16)
    input_ref[...] = grad_ref[...].astype(bf16)
    left = grid_of((32, 128), 1) < 64

    def ffn(layer, pieces):
        def up_rows(r, carry):
            rows = pl.ds(pl.multiple_of(32 * r, 32), 32)
            for m in range(2):
                tiles = []
                for s in (2 * m, 2 * m + 1):
                    at = UP_AT + offset_of(y, c, s) * 352
                    tiles.append(
                        [
                            pieces[r, pl.ds(pl.multiple_of(at + 32 * j, 32), 32), :].astype(f32)
                            for j in range(11)
                        ]
                    )
                even, odd = tiles
                middle = (
                    jnp.where(left, even[10], odd[10]),
                    pltpu.roll(jnp.where(left, odd[10], even[10]), 64, 1),
                )
                for side in range(2):
                    part = slice(5 * side, 5 * side + 5)
                    base = FF * side + 1408 * m
                    for j, tile in enumerate(even[part] + [middle[side]] + odd[part]):
                        up[layer, rows, base + 128 * j : base + 128 * j + 128] = tile
            return carry

        lax.fori_loop(0, 8, up_rows, 0)
        done = [pltpu.make_async_copy(up.at[layer], up_ref.at[layer], stores.at[layer, 0])]
        done[0].start()
        for r in range(8):
            lanes = slice(128 * r, 128 * r + 128)
            down[layer, :, lanes] = pieces[r, DOWN_AT:OUT_AT, :].astype(f32)
            out[layer, :, lanes] = pieces[r, OUT_AT:FFN_ROWS, :].astype(f32)
        done.append(pltpu.make_async_copy(down.at[layer], down_ref.at[layer], stores.at[layer, 1]))
        done.append(pltpu.make_async_copy(out.at[layer], out_ref.at[layer], stores.at[layer, 2]))
        done[1].start()
        done[2].start()
        return done

    def projection(layer, pieces):
        def in_rows(r, carry):
            rows = pl.ds(pl.multiple_of(32 * r, 32), 32)
            for s in range(4):
                at = offset_of(y, c, s) * 384
                for lane, wide, to in in_lanes(s):
                    for k in range(wide // 128):
                        j = to // 128 + k
                        tile = pieces[r, pl.ds(pl.multiple_of(at + 32 * j, 32), 32), :]
                        column = lane + 128 * k
                        whole[layer, rows, column : column + 128] = tile.astype(f32)
            return carry

        lax.fori_loop(0, 8, in_rows, 0)
        done = pltpu.make_async_copy(whole.at[layer], in_ref.at[layer], stores.at[layer, 3])
        done.start()
        for s in range(4):
            at = pl.ds(pl.multiple_of(SMALL_AT + 16 * offset_of(y, c, s), 16), 16)
            for r in range(8):
                table_ref[s, layer, 16 * r : 16 * r + 16, :] = pieces[r, at, :].astype(f32)
        return [done]

    waiting = []
    copies[0].wait()
    copies[2].start()
    waiting += ffn(1, p1)
    copies[1].wait()
    copies[3].start()
    waiting += projection(1, p2)
    copies[2].wait()
    waiting += ffn(0, p3)
    copies[3].wait()
    waiting += projection(0, p4)
    for store in waiting:
        store.wait()


def offset_of(y, c, s):
    sy, sc = s // 2, s % 2
    return 2 * (y + sy - 2 * y * sy) + c + sc - 2 * c * sc


def assemble(finals, last, grad):
    spot = pl.BlockSpec(memory_space=pl.ANY)
    vmem = pl.BlockSpec(memory_space=pltpu.VMEM)
    shapes = [(LAYERS, 704, 1024), (LAYERS, 512, 1024), (LAYERS, 256, 2 * FF), (LAYERS, 256, CH + HV)]
    return pl.pallas_call(
        assemble_kernel,
        out_shape=tuple(like(*shape) for shape in shapes)
        + (like(4, LAYERS, 128, 128),)
        + (like(*last.shape, dtype=bf16),) * 2,
        in_specs=[spot] * 4 + [vmem] * 2,
        out_specs=(spot,) * 4 + (vmem,) * 3,
        scratch_shapes=[pltpu.VMEM(final.shape, bf16) for final in finals]
        + [pltpu.VMEM(shape, f32) for shape in shapes]
        + [pltpu.SemaphoreType.DMA((4,)), pltpu.SemaphoreType.DMA((2, 4))],
        compiler_params=pltpu.CompilerParams(vmem_limit_bytes=LIMIT),
        name="assemble",
    )(*finals, last, grad)


FFN_MOVE, IN_MOVE = (UP_AT, 352), (0, 384)
GATHERED_ROWS = SMALL_AT + 4 * 16


def add_into(dst, left, right):
    dst[...] = (left[...].astype(f32) + right[...].astype(f32)).astype(bf16)


class Group:
    def __init__(self, number, piece, moved, final, move, sems, x_first=False):
        self.number, self.piece, self.moved, self.final = number, piece, moved, final
        self.at, self.part = move
        self.send, self.recv, self.local = sems
        self.x_first = x_first
        rank = lax.axis_index("rep")
        self.rank, self.x, self.z = rank, rank % 2, (rank % 8) // 2
        self.y, self.c = place()
        self.extra = moved.shape[0] > piece.shape[0]

    def swaps(self, d):
        target = relative(self.y, self.c, d)
        rows = pl.ds(self.at + d * self.part, self.part)
        spans = [(rows, rows, d)]
        if self.extra:
            spans.append((pl.ds(SMALL_AT, 16), pl.ds(SMALL_AT + 16 * d, 16), 20 + d))
        return [
            pltpu.make_async_remote_copy(
                src_ref=self.piece.at[src], dst_ref=self.moved.at[dst],
                send_sem=self.send.at[self.number, k], recv_sem=self.recv.at[self.number, k],
                device_id={"grp": target}, device_id_type=MESH,
            )
            for src, dst, k in spans
        ]

    def start_swap(self):
        for d in range(1, 4):
            for copy in self.swaps(d):
                copy.start()
        first = self.at + self.part
        self.moved[0:first, :] = self.piece[0:first, :]
        rest, last = self.at + 4 * self.part, self.piece.shape[0]
        if rest < last:
            self.moved[rest:last, :] = self.piece[rest:last, :]

    def wait_swap(self):
        for d in range(1, 4):
            for copy in self.swaps(d):
                copy.wait_recv()

    def owner(self, source_z, which):
        return 2 * source_z + (self.x if which == 0 else 1 - self.x)

    def move(self, step, source_z, kind, which=0):
        owner = self.owner(source_z, which)
        src = self.moved if step == 0 and which == 0 else self.final.at[owner]
        number = self.number if which == 0 else 4
        slot = 4 + 4 * kind + step
        return pltpu.make_async_remote_copy(
            src_ref=src, dst_ref=self.final.at[owner],
            send_sem=self.send.at[number, slot], recv_sem=self.recv.at[number, slot],
            device_id={"rep": self.rank + 2 - 4 * kind}, device_id_type=MESH,
        )

    def x_move(self, step, source_z):
        owner = self.owner(source_z, 0)
        src = self.moved if step == 0 else self.final.at[owner]
        return pltpu.make_async_remote_copy(
            src_ref=src, dst_ref=self.final.at[owner],
            send_sem=self.send.at[self.number, 12 + step + 3],
            recv_sem=self.recv.at[self.number, 12 + source_z],
            device_id={"rep": flip(self.rank)}, device_id_type=MESH,
        )

    def own_copy(self):
        return pltpu.make_async_copy(
            self.moved, self.final.at[self.owner(self.z, 0)], self.local.at[self.number]
        )

    def both_ways(self, which, act):
        @pl.when(self.z < 3)
        def _():
            act(self.move(0, self.z, 0, which))

        @pl.when(self.z > 0)
        def _():
            act(self.move(0, self.z, 1, which))

    def begin(self):
        self.both_ways(0, lambda copy: copy.start())
        self.x_move(0, self.z).start()
        self.own_copy().start()

    def begin_other(self):
        self.x_move(0, self.z).wait_recv()
        self.both_ways(1, lambda copy: copy.start())

    def passes(self, k, which, arrive, onward):
        z = self.z

        @pl.when(z >= k)
        def _():
            arrive(k, z - k, 0)

            @pl.when(z < 3)
            def _():
                onward(self.move(k, z - k, 0, which))

        @pl.when(z + k <= 3)
        def _():
            arrive(-k, z + k, 1)

            @pl.when(z > 0)
            def _():
                onward(self.move(k, z + k, 1, which))

    def relay(self, k, which=0):
        def arrive(step, source, kind):
            self.move(abs(step) - 1, source, kind, which).wait_recv()
            if not self.x_first:
                self.x_move(step, source).start()

        self.passes(k, which, arrive, lambda copy: copy.start())

    def finish(self):
        for which in range(2 if self.x_first else 1):

            def arrive(step, source, kind):
                if not self.x_first:
                    self.x_move(step, source).wait_send()

            for k in range(1, 4):
                self.passes(k, which, arrive, lambda copy: copy.wait_send())
            self.both_ways(which, lambda copy: copy.wait_send())
        self.x_move(0, self.z).wait_send()
        if not self.x_first:
            for source in range(4):
                self.x_move(0, source).wait_recv()
        self.own_copy().wait()
        for d in range(1, 4):
            for copy in self.swaps(d):
                copy.wait_send()


class Line:
    def __init__(self, values, right, left, send, recv):
        self.values, self.right, self.left = values, right, left
        self.send, self.recv = send, recv
        self.rank = lax.axis_index("rep")
        self.z = (self.rank % 8) // 2

    def go(self, o, toward):
        land = self.right if toward == 0 else self.left
        return pltpu.make_async_remote_copy(
            src_ref=self.values.at[o], dst_ref=land.at[o],
            send_sem=self.send.at[toward, o], recv_sem=self.recv.at[toward, o],
            device_id={"rep": self.rank + 2 - 4 * toward}, device_id_type=MESH,
        )

    def edge(self, step, act):
        @pl.when(self.z == 0)
        def _():
            act(self.go(3 - step, 0))

        @pl.when(self.z == 3)
        def _():
            act(self.go(step, 1))

    def start_edge(self, step):
        if step > 0:
            self.edge(step - 1, lambda copy: copy.wait_send())
        self.edge(step, lambda copy: copy.start())

    def inner(self, step):
        z, o = self.z, 3 - step

        @pl.when((z > 0) & (z < o))
        def _():
            self.go(o, 0).wait_recv()
            add_into(self.values.at[o], self.values.at[o], self.right.at[o])
            self.go(o, 0).start()

        @pl.when((z < 3) & (z > step))
        def _():
            self.go(step, 1).wait_recv()
            add_into(self.values.at[step], self.values.at[step], self.left.at[step])
            self.go(step, 1).start()

    def total(self, out):
        z = self.z
        for o in range(4):

            @pl.when(z == o)
            def _():
                value = self.values[o].astype(f32)
                if o > 0:
                    self.go(o, 0).wait_recv()
                    value = value + self.right[o].astype(f32)
                if o < 3:
                    self.go(o, 1).wait_recv()
                    value = value + self.left[o].astype(f32)
                out[...] = value.astype(bf16)

    def finish(self):
        self.edge(2, lambda copy: copy.wait_send())
        for o in range(4):

            @pl.when((self.z > 0) & (self.z < o))
            def _():
                self.go(o, 0).wait_send()

            @pl.when((self.z < 3) & (self.z > o))
            def _():
                self.go(o, 1).wait_send()


def finish_kernel(
    p1, p2, k3, a3, k4, b4, hidden_hbm, down_raw, mid_ref, f1, f2, f3, f4, last_ref,
    q1, q2, q3, q4, e1, e2, e3, e4, v3, x3, r3, l3, v4, x4, r4, l4,
    send, recv, local, send3, recv3, send4, recv4, send5, recv5, loads,
    hidden_ref, wdown_ref, down_loads, *scratch,
):
    loaded_hidden = load_whole(hidden_hbm, hidden_ref, down_loads.at[0])
    loaded_down = load_down(down_raw.at[LAYERS - 1], wdown_ref, down_loads.at[1])
    scatter = Scatter(*scratch, mid_ref.shape[0])
    count = scatter.size // SUB
    rank = lax.axis_index("rep")
    x, z = rank % 2, (rank % 8) // 2
    y, c = place()
    loaded = [
        pltpu.make_async_copy(p1, q1, loads.at[0]),
        pltpu.make_async_copy(p2, q2, loads.at[1]),
        pltpu.make_async_copy(k3, v3, loads.at[2]),
        pltpu.make_async_copy(k4, v4, loads.at[3]),
        pltpu.make_async_copy(a3, x3, loads.at[4]),
    ]
    for load in loaded:
        load.start()
    barrier = pltpu.get_barrier_semaphore()
    pl.semaphore_signal(
        barrier, inc=1, device_id={"rep": rank + 1 - 2 * x}, device_id_type=MESH
    )
    for d in range(1, 4):
        dy, dc = d // 2, d % 2
        target = 2 * (y + dy - 2 * y * dy) + c + dc - 2 * c * dc
        pl.semaphore_signal(barrier, inc=1, device_id={"grp": target}, device_id_type=MESH)

    @pl.when(z > 0)
    def _():
        pl.semaphore_signal(barrier, inc=1, device_id={"rep": rank - 2}, device_id_type=MESH)

    @pl.when(z < 3)
    def _():
        pl.semaphore_signal(barrier, inc=1, device_id={"rep": rank + 2}, device_id_type=MESH)

    @pl.when((z > 0) & (z < 3))
    def _():
        pl.semaphore_wait(barrier, 6)

    @pl.when((z == 0) | (z == 3))
    def _():
        pl.semaphore_wait(barrier, 5)

    def halves(o):
        return pltpu.make_async_remote_copy(
            src_ref=b4.at[o], dst_ref=x4.at[o], send_sem=send5.at[o], recv_sem=recv5.at[o],
            device_id={"rep": rank + 1 - 2 * x}, device_id_type=MESH,
        )

    for o in (3, 0, 2, 1):
        halves(o).start()
    sems = (send, recv, local)

    def down_begin():
        loaded_hidden()
        loaded_down()
        for part in range(2):
            yy = 1 - y if part == 0 else y
            for i in range(count):
                for cc, take in ((1 - c, scatter.give), (c, scatter.hold)):
                    rows = shard_rows(yy, cc, i, scatter.size)
                    take(part, i, mm(hidden_ref[rows, :], wdown_ref[...]))
                if part == 0:
                    scatter.relay(i)

    def down_end():
        for i in range(count):
            rows = slice(i * SUB, (i + 1) * SUB)
            last_ref[rows, :] = mid_ref[rows, :] + scatter.total(i)
        scatter.finish()

    def merge(*owners):
        for o in owners:
            add_into(v3.at[o], v3.at[o], x3.at[o])

    def arrive(*owners):
        for o in owners:
            halves(o).wait_recv()
            add_into(v4.at[o], v4.at[o], x4.at[o])

    g1 = Group(0, q1, e1, f1, FFN_MOVE, sems)
    g2 = Group(1, q2, e2, f2, IN_MOVE, sems)
    g3 = Group(2, q3, e3, f3, FFN_MOVE, sems)
    g4 = Group(3, q4, e4, f4, IN_MOVE, sems)
    line3 = Line(v3, r3, l3, send3, recv3)
    line4 = Line(v4, r4, l4, send4, recv4)
    loaded[0].wait()
    g1.start_swap()
    loaded[1].wait()
    g2.start_swap()
    g1.wait_swap()
    g1.begin()
    down_begin()
    loaded[3].wait()
    arrive(3, 0)
    loaded[2].wait()
    loaded[4].wait()
    merge(3, 0)
    line3.start_edge(0)
    g2.wait_swap()
    g2.begin()
    merge(2, 1)
    line3.start_edge(1)
    g1.relay(1)
    line3.inner(0)
    line3.inner(1)
    line4.start_edge(0)
    g2.relay(1)
    g1.relay(2)
    line3.start_edge(2)
    arrive(2, 1)
    line3.total(q3)
    g3.start_swap()
    g2.relay(2)
    g3.wait_swap()
    g3.begin()
    line4.inner(0)
    line4.start_edge(1)
    line4.inner(1)
    line4.start_edge(2)
    g2.relay(3)
    g1.relay(3)
    g3.relay(1)
    line4.total(q4)
    g4.start_swap()
    g4.wait_swap()
    g4.begin()
    down_end()
    g3.relay(2)
    g4.relay(1)
    g4.relay(2)
    g3.relay(3)
    g4.relay(3)
    for group in (g1, g2, g3, g4):
        group.finish()
    line3.finish()
    line4.finish()
    for o in range(4):
        halves(o).wait_send()


def finish_reduction(p1, p2, k3, a3, k4, b4, hidden, w_down, mid):
    spot = pl.BlockSpec(memory_space=pl.ANY)
    vmem = pl.BlockSpec(memory_space=pltpu.VMEM)
    big, small = p1.shape, p2.shape
    wide = (GATHERED_ROWS, 128)
    dma = pltpu.SemaphoreType.DMA
    return pl.pallas_call(
        finish_kernel,
        out_shape=tuple(like(8, *shape, dtype=bf16) for shape in (big, wide, big, wide))
        + (like(*mid.shape),),
        in_specs=[spot] * 8 + [vmem],
        out_specs=(spot,) * 4 + (vmem,),
        scratch_shapes=[
            pltpu.VMEM(shape, bf16)
            for shape in [big, small] * 2 + [big, wide] * 2
            + [(4,) + big] * 4
            + [(4,) + small] * 4
        ]
        + [dma((5, 24)), dma((5, 24)), dma((4,))]
        + [dma((2, 4))] * 4
        + [dma((4,)), dma((4,)), dma((5,))]
        + [pltpu.VMEM(hidden.shape, bf16), pltpu.VMEM((768, mid.shape[1]), bf16), dma((2,))]
        + Scatter.scratch(*mid.shape),
        compiler_params=pltpu.CompilerParams(
            collective_id=5, has_side_effects=True, vmem_limit_bytes=LIMIT
        ),
        cost_estimate=pl.CostEstimate(flops=1000, bytes_accessed=1000, transcendentals=0),
        name="finish_reduction",
    )(p1, p2, k3, a3, k4, b4, hidden, w_down, mid)


def swap_route(bit, count):
    return [(i, i ^ bit) for i in range(count)]


def planes_of(replicas):
    return [
        [8 * b + 2 * z + x for z in range(4)] for b in range(replicas // 8) for x in range(2)
    ]


def swap_x(array, replicas):
    return lax.ppermute(array, "rep", swap_route(1, replicas))


def add_arrived(kept, arrived):
    return (kept.astype(f32) + arrived.astype(f32)).astype(bf16)


def reduce_z(summed, replicas):
    piece = lax.psum_scatter(
        summed, "rep", scatter_dimension=0, tiled=False, axis_index_groups=planes_of(replicas)
    )
    blocks = replicas // 8
    if blocks > 1:
        piece = lax.psum(
            piece, "rep", axis_index_groups=[[8 * b + r for b in range(blocks)] for r in range(8)]
        )
    return piece


def exchange(piece, at, part):
    moved = [piece[: at + part]]
    for d in range(1, 4):
        moved.append(swap(piece[at + d * part : at + (d + 1) * part], d))
    moved.append(piece[at + 4 * part :])
    if piece.shape[0] == IN_ROWS:
        moved += [swap(piece[SMALL_AT:], d) for d in range(1, 4)]
    return jnp.concatenate(moved, axis=0)


def gather_z(piece, replicas):
    return lax.all_gather(piece, "rep", axis=0, axis_index_groups=planes_of(replicas))


def spread(piece, replicas):
    owned = gather_z(piece, replicas)
    other = swap_x(owned, replicas)
    odd = lax.axis_index("rep") % 2 == 1
    pair = jnp.stack([jnp.where(odd, other, owned), jnp.where(odd, owned, other)], axis=1)
    return pair.reshape((8,) + piece.shape)


def finish_all(
    piece1, piece2, keep3, arrived3, keep4, send4, hidden, w_down, mid, replicas
):
    if replicas == 8:
        return finish_reduction(
            piece1, piece2, keep3, arrived3, keep4, send4, hidden, w_down, mid
        )
    piece3 = reduce_z(add_arrived(keep3, arrived3), replicas)
    piece4 = reduce_z(add_arrived(keep4, swap_x(send4, replicas)), replicas)
    finals = [
        spread(exchange(piece, *move), replicas)
        for piece, move in (
            (piece1, FFN_MOVE), (piece2, IN_MOVE), (piece3, FFN_MOVE), (piece4, IN_MOVE)
        )
    ]
    padded = jnp.zeros((hidden.shape[1], mid.shape[1]), bf16)
    offset = 64 * (lax.axis_index("grp") % 2)
    padded = lax.dynamic_update_slice_in_dim(padded, w_down[LAYERS - 1], offset, 0)
    partial_sum = mm(hidden, padded).astype(bf16)
    down = lax.psum_scatter(partial_sum, "grp", scatter_dimension=0, tiled=True)
    return finals + [mid + down.astype(f32)]


def tie(*values):
    return lax.optimization_barrier(values)


def swap(array, d):
    return lax.ppermute(array, "grp", swap_route(d, 4))


def per_device(
    x_input, norm_gain, w_in, w_ab, conv_w, a_log, dt_bias, out_gain, w_out, ffn_in, ffn_out,
    cotangent,
):
    parts = lax.axis_size("grp")
    replicas = lax.axis_size("rep")
    mine = lax.axis_index("grp")
    rows, width = x_input.shape[1], x_input.shape[2]
    shard = w_in.shape[1]

    pack = jnp.concatenate(
        [
            norm_gain.reshape(-1, 128),
            conv_w.reshape(-1, 128),
            jnp.swapaxes(w_ab, 1, 2).reshape(-1, 128),
            out_gain.reshape(-1, 128),
            jnp.zeros((PACK_ROWS - OUT_GAIN_AT - 1, 128), bf16),
        ]
    ).astype(f32)
    normed, projected, small, in_weight, *rest = start(x_input[0], pack, w_in)
    gains, taps_pair, ab_pair, out_pair = rest[0:4], rest[4:6], rest[6:8], rest[8:10]
    small_weights = []
    for l in range(LAYERS):
        heads = jnp.pad(jnp.stack([a_log[l], dt_bias[l]]).astype(f32), ((0, 6), (2, 124)))
        small_weights.append(
            (
                gains[2 * l], gains[2 * l + 1], ab_pair[l], taps_pair[l], heads, out_pair[l],
            )
        )

    residual = x_input[0]
    kept = []
    in_weights, up_weights = [(in_weight,)], []
    for l in range(LAYERS):
        gain_one, gain_two, ab, taps, heads, gain = small_weights[l]
        if l > 0:
            normed, projected, small = project(residual, gain_one, ab, in_weights[l])
        gated, *saved = mixer_forward(
            l, projected, small, taps, heads, gain, (ffn_in, (w_in, cotangent[0])[l])
        )
        up_weights.append((ffn_in, saved[4]))
        if l == 0:
            near, far = saved[5:]
            in_weights.append(
                (
                    w_in,
                    near,
                    lax.all_gather(far, "rep", axis=0, axis_index_groups=planes_of(replicas)),
                )
            )
        else:
            d_down = saved[5]
        saved = saved[:4]
        mid, normed_two, up, hidden, *residual_out = ffn_forward(
            l, gated, residual, gain_two, w_out, ffn_out, up_weights[l]
        )
        kept.append((residual, normed, projected, small, gated, saved, mid, normed_two, up, hidden))
        if l == 0:
            (residual,) = residual_out

    d_residual = cotangent[0]

    def ffn_part(l, d_residual):
        gain_one, gain_two, ab, taps, heads, gain = small_weights[l]
        residual, normed, projected, small, gated, saved, mid, normed_two, up, hidden = kept[l]
        return ffn_backward(
            l, d_residual, d_down, up, hidden, normed_two, mid, gain_two, gated, w_out, ffn_out,
            up_weights[l],
        )

    def mixer_part(l, d_gated):
        gain_one, gain_two, ab, taps, heads, gain = small_weights[l]
        residual, normed, projected, small, gated, saved, mid, normed_two, up, hidden = kept[l]
        return mixer_backward(projected, small, taps, heads, gain, saved, d_gated)

    def project_part(l, d_mid, g_gain_two, mixed):
        gain_one, gain_two, ab, taps, heads, gain = small_weights[l]
        residual, normed, projected, small, gated, saved, mid, normed_two, up, hidden = kept[l]
        d_projected, d_small, g_taps, g_heads = mixed
        return project_backward(
            d_projected, d_small, in_weights[l], ab, normed, residual, gain_one, d_mid,
            g_gain_two, g_taps, g_heads,
        )

    d_mid, d_gated, g_gain_two, keep1, send1 = ffn_part(1, d_residual)
    arrived1 = swap_x(send1, replicas)
    mixed = mixer_part(1, d_gated)
    d_residual, keep2, send2 = project_part(1, d_mid, g_gain_two, mixed)
    d_residual, arrived1 = tie(d_residual, arrived1)
    piece1 = reduce_z(add_arrived(keep1, arrived1), replicas)
    arrived2 = swap_x(send2, replicas)
    d_mid, d_gated, g_gain_two, keep3, send3 = ffn_part(0, d_residual)
    d_gated, piece1, arrived2 = tie(d_gated, piece1, arrived2)
    piece2 = reduce_z(add_arrived(keep2, arrived2), replicas)
    arrived3 = swap_x(send3, replicas)
    mixed = mixer_part(0, d_gated)
    d_residual, keep4, send4 = project_part(0, d_mid, g_gain_two, mixed)
    d_residual, arrived3 = tie(d_residual, arrived3)
    final1, final2, final3, final4, last = finish_all(
        piece1, piece2, keep3, arrived3, keep4, send4, kept[-1][-1], ffn_out, kept[-1][6], replicas
    )
    finals = (final1, final2, final3, final4)
    residual = last
    down_grads, out_grads, up_grads, w_in_grads, everyone, *ends = assemble(
        finals, residual, d_residual
    )
    block_output, input_grad = (end[None] for end in ends)

    tables = lax.dynamic_index_in_dim(everyone, mine, 0, keepdims=False)
    sums = jnp.sum(everyone[:, :, 64:82], axis=0)
    grad_gain = lax.dynamic_slice_in_dim(
        sums[:, :16].reshape(LAYERS, 2, width), mine * shard, shard, 2
    )
    grad_out_gain = lax.dynamic_slice_in_dim(
        sums[:, 16:18].reshape(LAYERS, DV), mine * (DV // 4), DV // 4, 1
    )
    grad_a_log = tables[:, 82, 2:4]
    grad_dt = tables[:, 83, 2:4]
    taps_sum = everyone[:, :, 0:32].reshape(4, LAYERS, 4, 1024)

    def side_by_side(array):
        return jnp.moveaxis(array, 0, 2).reshape(LAYERS, 4, -1)

    conv_full = jnp.concatenate(
        [
            side_by_side(taps_sum[..., :256]),
            side_by_side(taps_sum[..., 256:512]),
            side_by_side(taps_sum[..., 512:]),
        ],
        axis=2,
    )
    grad_conv = lax.dynamic_slice_in_dim(conv_full, mine * 1024, 1024, 2)
    ab_sum = everyone[:, :, 32:64].reshape(4, LAYERS, 4, width)
    ab_sum = lax.dynamic_slice_in_dim(ab_sum, mine * shard, shard, 3)
    grad_ab = jnp.transpose(ab_sum.reshape(4, LAYERS, 2, 2, shard), (1, 4, 2, 0, 3)).reshape(
        LAYERS, shard, 2 * H
    )
    return (
        block_output,
        input_grad,
        grad_gain,
        w_in_grads,
        grad_ab,
        grad_conv,
        grad_a_log,
        grad_dt,
        grad_out_gain,
        out_grads,
        up_grads,
        down_grads,
    )


def solution(mesh):
    rows = P("rep", "grp", None)
    first = P(None, "grp")
    middle = P(None, "grp", None)
    last = P(None, None, "grp")
    in_specs = (rows, last, middle, middle, last, first, first, first, middle, middle, middle, rows)
    out_specs = (rows, rows, last, middle, middle, last, first, first, first, middle, middle, middle)
    return jax.shard_map(
        per_device, mesh=mesh, in_specs=in_specs, out_specs=out_specs, check_vma=False
    )
```
